32 devices in a mesh: dp: 8 (over y, x, core), seq: 4 (over z).
Axes of the slice: x: 2, y: 2, z: 4, core: 2. Of those that a mesh axis runs over, the one named last changes fastest.
Arguments:
- inputs: bfloat16 [2, 8, 1024, 768], P(None, 'dp', 'seq'), may hold values from -6 to 6
- segments: int32 [2, 8, 1024], P(None, 'dp', 'seq'), may hold values from 0 to 1023, as said below
- attn_params: bfloat16 [2363392], P(('dp', 'seq'))
- mlp_params: bfloat16 [4726784], P(('dp', 'seq'))
- cotangent: bfloat16 [2, 8, 1024, 768], P(None, 'dp', 'seq'), may hold values from -6 to 6
Outputs:
- outputs: bfloat16 [2, 8, 1024, 768], P(None, 'dp', 'seq')
- input_grad: float32 [2, 8, 1024, 768], P(None, 'dp', 'seq')
- attn_grad: float32 [2363392], P(('dp', 'seq'))
- mlp_grad: float32 [4726784], P(('dp', 'seq'))
The draws below stay inside these ranges and needn't reach their ends.
Inputs may be any that keep to these rules, and one draw needn't show every extreme that they name: `segments`: along each sequence the segment numbers never fall, and equal numbers mark one document. In each micro-batch one sequence, chosen by the seed, is a single document with all numbers 1024 - 1; every other document has at most 512 tokens.
All inputs are finite; a program needn't handle non-finite values.
Results may differ from the reference program's by a relative error of at most 0.012.
The reference program's roundings to bfloat16 on the way count: a program that leaves them out, or rounds other values in their place, can miss the bound.
Values may be sent and summed in bfloat16 or wider, within the bound.
A program may use at most 256 MiB of HBM per device.

```python
import math
import jax
import jax.numpy as jnp
from jax import lax

D = 768
H = 12
HD = 64
FF = 3072
MICRO = 2
LENGTH = 1024
SEQS = 8
DOC_MOST = 512
BREAK = 256
ATTN_FLAT = 2363392
MLP_FLAT = 4726784


def flat_draw(key, layout_specs, total_size):
    pieces = []
    used_total = 0
    for index_spec, spec_entry in enumerate(layout_specs):
        amount, center, spread = spec_entry
        piece_key = jax.random.fold_in(key, index_spec)
        normal_part = jnp.clip(jax.random.normal(piece_key, (amount,), jnp.float32), -5.0, 5.0)
        noise_part = normal_part
        pieces.append(center + spread * noise_part)
        used_total += amount
    pad_key = jax.random.fold_in(key, 999)
    pieces.append(0.02 * jax.random.normal(pad_key, (total_size - used_total,), jnp.float32))
    return jnp.concatenate(pieces)


def draw_attn_params(key, part):
    key = jax.random.fold_in(key, 3)
    layout_specs = [(D, 1.0, 0.25), (D, 0.0, 0.3), (3 * D * D, 0.0, 1.4 / math.sqrt(D)), (D, 0.0, 0.3), (D, 0.0, 0.3), (D * D, 0.0, 4.0 / math.sqrt(D)), (D, 0.0, 0.3)]
    return flat_draw(key, layout_specs, ATTN_FLAT).astype(jnp.bfloat16)


def draw_mlp_params(key, part):
    key = jax.random.fold_in(key, 5)
    layout_specs = [(D, 1.0, 0.25), (D, 0.0, 0.3), (D * FF, 0.0, 1.0 / math.sqrt(D)), (FF, 0.0, 0.3), (FF * D, 0.0, 1.5 / math.sqrt(FF)), (D, 0.0, 0.3)]
    return flat_draw(key, layout_specs, MLP_FLAT).astype(jnp.bfloat16)


def draw_segments(key, part):
    key = jax.random.fold_in(key, 7)
    offset_key, break_key, whole_key = jax.random.split(key, 3)
    position = jnp.arange(LENGTH, dtype=jnp.int32)
    offsets = jax.random.randint(offset_key, (MICRO, SEQS, 1), 0, LENGTH - DOC_MOST + 1, dtype=jnp.int32)
    relative = position[None, None, :] - offsets
    inside = (relative > 0) & (relative < DOC_MOST)
    forced = relative % DOC_MOST == 0
    extra = jax.random.randint(break_key, (MICRO, SEQS, LENGTH), 0, BREAK, dtype=jnp.int32) == 0
    starts = (position[None, None, :] == 0) | forced | extra & jnp.logical_not(inside)
    numbers = jnp.cumsum(starts.astype(jnp.int32), axis=-1) - 1
    whole_seq = jax.random.randint(whole_key, (MICRO, 1, 1), 0, SEQS, dtype=jnp.int32)
    chosen = jnp.arange(SEQS, dtype=jnp.int32)[None, :, None] == whole_seq
    return jnp.where(chosen, LENGTH - 1, numbers).astype(jnp.int32)


def level_of(stream_key, extent, cuts, low, high):
    level, own = 1.0, jax.random.fold_in(stream_key, 6)
    for dim, shards_of in cuts:
        steps = jnp.exp(jax.random.uniform(jax.random.fold_in(own, dim), (shards_of,), jnp.float32, low / len(cuts), high / len(cuts)))
        level = level * jnp.repeat(steps, extent[dim] // shards_of).reshape([-1 if axis == dim else 1 for axis in range(len(extent))])
    return level


def gaussian(key, dims, width, reach, cuts=(), held_as=jnp.bfloat16):
    drawn = jax.random.normal(key, dims, jnp.float32) * width
    if len(cuts) > 0:
        drawn = level_of(key, dims, cuts, -0.22, 0.18) * drawn
    return jnp.clip(drawn, min=-reach, max=reach).astype(held_as)


def setup_inputs(seed: int = 0) -> dict:
    arg_keys = jax.random.split(jax.random.key(seed), 6)
    inputs = gaussian(arg_keys[0], (MICRO, SEQS, LENGTH, D), 1.0, 6.0, ((1, 8), (2, 4)))
    segments = draw_segments(jax.random.fold_in(arg_keys[5], 71), 0)
    attn_params = draw_attn_params(jax.random.fold_in(arg_keys[5], 71), 0)
    mlp_params = draw_mlp_params(jax.random.fold_in(arg_keys[5], 71), 0)
    cotangent = gaussian(arg_keys[4], (MICRO, SEQS, LENGTH, D), 1.0, 6.0, ((1, 8), (2, 4)))
    return {"inputs": inputs, "segments": segments, "attn_params": attn_params, "mlp_params": mlp_params, "cotangent": cotangent}


@jax.custom_vjp
def low(v):
    return lax.optimization_barrier(v.astype(jnp.bfloat16)).astype(jnp.float32)

@jax.custom_vjp
def low_back(v):
    return v

def low_keep(v):
    return (low(v), None)

def low_pass(kept, grad):
    return (grad,)

def back_keep(v):
    return (v, None)

def back_low(kept, grad):
    return (low(grad),)
low.defvjp(low_keep, low_pass)
low_back.defvjp(back_keep, back_low)
highest = lax.Precision.HIGHEST
norm_eps = 1e-05
score_floor = -1e+30

def attention_layout():
    return [(D,), (D,), (D, 3 * D), (D,), (D,), (D, D), (D,)]

def mlp_layout():
    return [(D,), (D,), (D, FF), (FF,), (FF, D), (D,)]

def unpack_params(flat_vector, layout):
    offset = 0
    result = []
    for dims_entry in layout:
        amount = math.prod(dims_entry)
        result.append(lax.slice_in_dim(flat_vector, offset, offset + amount).reshape(dims_entry))
        offset += amount
    return result

def layer_norm(values, gain, shift):
    average = lax.optimization_barrier(jnp.mean(values, axis=-1, keepdims=True))
    centred = values - average
    spread = lax.optimization_barrier(jnp.mean(centred * centred, axis=-1, keepdims=True))
    return centred * lax.rsqrt(spread + norm_eps) * gain + shift

def rounded_both(values):
    return low_back(low(values))

def forward_sequence(input_row, seg_row, attn_flat, mlp_flat):
    gain_one, shift_one, w_qkv, bias_query, bias_value, w_proj, bias_proj = unpack_params(attn_flat, attention_layout())
    gain_two, shift_two, w_up, bias_up, w_down, bias_down = unpack_params(mlp_flat, mlp_layout())
    normed_one = low(layer_norm(input_row, gain_one, shift_one))
    merged_rows = jnp.dot(normed_one, w_qkv, precision=highest)
    query_heads = rounded_both(merged_rows[:, :D] + bias_query).reshape(LENGTH, H, HD)
    key_heads = rounded_both(merged_rows[:, D:2 * D]).reshape(LENGTH, H, HD)
    value_heads = rounded_both(merged_rows[:, 2 * D:] + bias_value).reshape(LENGTH, H, HD)
    block_rows = min(512, LENGTH)
    count_blocks = LENGTH // block_rows
    key_pos = jnp.arange(LENGTH, dtype=jnp.int32)
    score_scale = 1.0 / math.sqrt(HD)

    def one_block(block_args):
        query_block, seg_block, block_start = block_args
        scores = jnp.einsum('qhd,khd->hqk', query_block, key_heads, precision=highest) * score_scale
        query_pos = block_start + jnp.arange(block_rows, dtype=jnp.int32)
        allowed = (seg_block[:, None] == seg_row[None, :]) & (key_pos[None, :] <= query_pos[:, None])
        scores = low_back(jnp.where(allowed[None], scores, score_floor))
        row_top = lax.optimization_barrier(jnp.max(scores, axis=-1, keepdims=True))
        exp_scores = jnp.exp(scores - row_top)
        probs = low(exp_scores / lax.optimization_barrier(jnp.sum(exp_scores, axis=-1, keepdims=True)))
        return jnp.einsum('hqk,khd->qhd', probs, value_heads, precision=highest)
    starts = jnp.arange(count_blocks, dtype=jnp.int32) * block_rows
    attended = lax.map(jax.checkpoint(one_block), (query_heads.reshape(count_blocks, block_rows, H, HD), seg_row.reshape(count_blocks, block_rows), starts))
    attended = rounded_both(attended.reshape(LENGTH, D))
    middle = input_row + low_back(jnp.dot(attended, w_proj, precision=highest) + bias_proj)
    normed_two = low(layer_norm(middle, gain_two, shift_two))
    hidden = low_back(jnp.dot(normed_two, w_up, precision=highest) + bias_up)
    active = low(jax.nn.gelu(hidden, approximate=True))
    return middle + low_back(jnp.dot(active, w_down, precision=highest) + bias_down)

def reference(inputs, segments, attn_params, mlp_params, cotangent):
    attn_flat = attn_params.astype(jnp.float32)
    mlp_flat = mlp_params.astype(jnp.float32)
    total_seqs = MICRO * SEQS
    rows_in = inputs.astype(jnp.float32).reshape(total_seqs, LENGTH, D)
    seg_in = segments.reshape(total_seqs, LENGTH).astype(jnp.int32)
    cot_in = cotangent.astype(jnp.float32).reshape(total_seqs, LENGTH, D)

    def step_seq(running, seq_args):
        input_row, seg_row, cot_row = seq_args

        def closed(row_vals, attn_vals, mlp_vals):
            return forward_sequence(row_vals, seg_row, attn_vals, mlp_vals)
        result, pullback = jax.vjp(closed, input_row, attn_flat, mlp_flat)
        grad_input, grad_attn, grad_mlp = pullback(cot_row)
        return ((running[0] + grad_attn, running[1] + grad_mlp), (result.astype(jnp.bfloat16), grad_input))
    start_sums = (jnp.zeros((ATTN_FLAT,), jnp.float32), jnp.zeros((MLP_FLAT,), jnp.float32))
    (grad_attn, grad_mlp), (outputs, input_grad) = lax.scan(step_seq, start_sums, (rows_in, seg_in, cot_in))
    return (outputs.reshape(MICRO, SEQS, LENGTH, D), input_grad.reshape(MICRO, SEQS, LENGTH, D), grad_attn, grad_mlp)
```

```python
import functools
from functools import partial
import math

import jax
import jax.numpy as jnp
from jax import lax
from jax.experimental import pallas as pl
from jax.experimental.pallas import tpu as pltpu
from jax.sharding import PartitionSpec as P

D = 768
H = 12
HD = 64
FF = 3072


norm_eps = 1e-05
score_floor = -1e30
key_block = 512


def attention_layout():
    return [(D,), (D,), (D, 3 * D), (D,), (D,), (D, D), (D,)]


def mlp_layout():
    return [(D,), (D,), (D, FF), (FF,), (FF, D), (D,)]


def unpack_params(flat_vector, layout):
    offset = 0
    result = []
    for dims_entry in layout:
        amount = math.prod(dims_entry)
        result.append(lax.slice_in_dim(flat_vector, offset, offset + amount).reshape(dims_entry))
        offset += amount
    return result


def layer_norm(values, gain, shift):
    average = jnp.mean(values, axis=-1, keepdims=True)
    centred = values - average
    spread = jnp.mean(centred * centred, axis=-1, keepdims=True)
    return centred * lax.rsqrt(spread + norm_eps) * gain + shift


def gelu_tanh(values):
    return jax.nn.gelu(values, approximate=True)


def pack_grads(grad_list, total_size):
    flat_parts = [part_grad.reshape(-1) for part_grad in grad_list]
    used_total = sum((part_grad.size for part_grad in grad_list))
    flat_parts.append(jnp.zeros((total_size - used_total,), jnp.float32))
    return jnp.concatenate(flat_parts)


def fetch_params(attn_params, mlp_params):
    gathered = (
        lax.all_gather(attn_params, ("dp", "seq"), axis=0, tiled=True),
        lax.all_gather(mlp_params, ("dp", "seq"), axis=0, tiled=True),
    )
    return (
        unpack_params(gathered[0], attention_layout()),
        unpack_params(gathered[1], mlp_layout()),
    )


def send_grads(attn_list, mlp_list, attn_total, mlp_total):
    return (
        lax.psum_scatter(
            pack_grads(attn_list, attn_total), ("dp", "seq"), scatter_dimension=0, tiled=True
        ),
        lax.psum_scatter(
            pack_grads(mlp_list, mlp_total), ("dp", "seq"), scatter_dimension=0, tiled=True
        ),
    )


def fold_keys(key_rows, key_segs, fold_step, start_carry):
    return fold_step(
        start_carry,
        (
            lax.all_gather(key_rows, "seq", axis=0, tiled=True),
            lax.all_gather(key_segs, "seq", axis=0, tiled=True),
        ),
        jnp.int32(0),
    )


def over_blocks(block_step, carry_now, key_piece, key_start):
    piece_rows = key_piece[0].shape[0]
    step_rows = math.gcd(piece_rows, key_block)

    def loop_step(index_block, carry_in):
        offset = index_block * step_rows
        sub_piece = tuple(
            (lax.dynamic_slice_in_dim(member, offset, step_rows, 0) for member in key_piece)
        )
        return block_step(carry_in, sub_piece, offset)

    return lax.fori_loop(0, piece_rows // step_rows, loop_step, carry_now)


def block_scores(query_heads, query_segs, query_pos, kv_rows, key_segs, key_start):
    key_heads = kv_rows[:, :D].reshape(-1, H, HD)
    scores = jnp.einsum(
        "qhd,khd->hqk", query_heads, key_heads, preferred_element_type=jnp.float32
    ) * (1.0 / math.sqrt(HD))
    key_pos = key_start + jnp.arange(kv_rows.shape[0], dtype=jnp.int32)
    allowed = (query_segs[:, None] == key_segs[None, :]) & (key_pos[None, :] <= query_pos[:, None])
    return (jnp.where(allowed[None], scores, score_floor), key_heads)


MESH = pl.DeviceIdType.MESH
LANES = 128

def pad_rows(rows):
    return -(-rows // 16) * 16


class Gather:
    def __init__(self, dp_size, seq_size, own, slots, send_sems, recv_sems):
        self.n = seq_size
        self.bits = [b for b in range(1, dp_size.bit_length() - 1)]
        self.dp = lax.axis_index("dp")
        self.z = lax.axis_index("seq")
        self.own, self.slots = own, slots
        self.rows = own.shape[0]
        half = self.rows // 32 * 16
        self.parts = [(0, half), (half, self.rows - half)]
        self.orders = [self.bits, self.bits[::-1]]
        self.send_sems, self.recv_sems = send_sems, recv_sems
        self.started = []

    def peers(self):
        out = [(self.dp, lax.rem(self.z + k, self.n)) for k in range(1, self.n)]
        out += [(self.dp ^ (1 << b), self.z) for b in [0] + self.bits]
        return out

    def slot(self, mask, k):
        return (self.dp ^ mask) * self.n + lax.rem(self.z + self.n - k, self.n)

    def view(self, mask, k, part):
        index = self.slot(mask, k)
        if part is None:
            return self.slots.at[index]
        start, size = self.parts[part]
        return self.slots.at[index, pl.ds(start, size)]

    def source(self, mask, k, part):
        if mask == 0 and k == 0:
            if part is None:
                return self.own
            start, size = self.parts[part]
            return self.own.at[pl.ds(start, size)]
        return self.view(mask, k, part)

    def send(self, mask, k, part, to, kind, recv_index):
        copy = pltpu.make_async_remote_copy(
            src_ref=self.source(mask, k, part),
            dst_ref=self.view(mask, k, part),
            send_sem=self.send_sems.at[len(self.started)],
            recv_sem=self.recv_sems.at[recv_index],
            device_id=to,
            device_id_type=MESH,
        )
        copy.start()
        self.started.append(copy)

    def recv_index(self, sibling, part, mask, k):
        part = 0 if part is None else part
        return ((sibling * 2 + part) * (2 << len(self.bits)) // 2 + (mask >> 1)) * self.n + k

    def wait(self, sibling, part, mask, k):
        view = self.view(mask ^ sibling, k, part)
        pltpu.make_async_remote_copy(
            src_ref=view, dst_ref=view, send_sem=self.send_sems.at[0],
            recv_sem=self.recv_sems.at[self.recv_index(sibling, part, mask, k)],
            device_id=(self.dp, self.z), device_id_type=MESH,
        ).wait_recv()

    def forward(self, part, mask, k):
        for p in ((0, 1) if part is None else (part,)):
            order = self.orders[p]
            last = max([order.index(b) for b in self.bits if mask >> b & 1], default=-1)
            for b in order[last + 1 :]:
                self.send(mask, k, p, (self.dp ^ (1 << b), self.z), 0, self.recv_index(0, p, mask | 1 << b, k))
        self.send(mask, k, part, (self.dp ^ 1, self.z), 1, self.recv_index(1, part, mask, k))

    def begin(self):
        for k in range(1, self.n):
            self.send(0, 0, None, (self.dp, lax.rem(self.z + k, self.n)), 0, self.recv_index(0, None, 0, k))
        self.forward(None, 0, 0)

    def events(self):
        out = []
        for k in range(1, self.n):
            out.append((k, None, 0, k))
        for k in range(self.n):
            for p in (0, 1):
                for level in range(len(self.bits)):
                    order = self.orders[p]
                    for low in range(1 << level):
                        mask = 1 << order[level]
                        for i in range(level):
                            if low >> i & 1:
                                mask |= 1 << order[i]
                        out.append(((level + 1) * 4 + k, p, mask, k))
        out.sort(key=lambda e: e[0])
        return [e[1:] for e in out]

    def step(self, event):
        part, mask, k = event
        self.wait(0, part, mask, k)
        self.forward(part, mask, k)

    def sibling_events(self):
        return [(None, 0, 0)] + self.events()

    def finish_sibling(self):
        for part, mask, k in self.sibling_events():
            self.wait(1, part, mask, k)

    def finish_sends(self):
        for copy in self.started:
            copy.wait_send()


def gather_counts(dp_size, seq_size):
    bits = dp_size.bit_length() - 2
    recv = 4 * (1 << bits) * seq_size
    send = 0
    send += seq_size - 1
    for p in range(2):
        for mask in range(1 << bits):
            top = mask.bit_length()
            send += (bits - top) * seq_size
    send += seq_size + 2 * ((1 << bits) - 1) * seq_size
    return send, recv


def gather_kernel(dp_size, seq_size, a_own, m_own, a_slots, m_slots, a_send, a_recv, m_send, m_recv, own_sems):
    ga = Gather(dp_size, seq_size, a_own, a_slots, a_send, a_recv)
    gm = Gather(dp_size, seq_size, m_own, m_slots, m_send, m_recv)
    barrier = pltpu.get_barrier_semaphore()
    peers = ga.peers()
    for peer in peers:
        pl.semaphore_signal(barrier, inc=1, device_id=peer, device_id_type=MESH)
    pl.semaphore_wait(barrier, len(peers))
    ca = pltpu.make_async_copy(a_own, a_slots.at[ga.slot(0, 0)], own_sems.at[0])
    cm = pltpu.make_async_copy(m_own, m_slots.at[gm.slot(0, 0)], own_sems.at[1])
    ca.start()
    cm.start()
    ga.begin()
    gm.begin()
    for e in ga.events():
        ga.step(e)
    for e in gm.events():
        gm.step(e)
    ca.wait()
    cm.wait()
    ga.finish_sibling()
    gm.finish_sibling()
    ga.finish_sends()
    gm.finish_sends()


def to_rows(flat):
    rows = flat.shape[0] // LANES
    return jnp.pad(flat.reshape(rows, LANES), ((0, pad_rows(rows) - rows), (0, 0)))


def gather_params(attn, mlp, dp_size, seq_size):
    a, m = to_rows(attn), to_rows(mlp)
    devices = dp_size * seq_size
    send, recv = gather_counts(dp_size, seq_size)
    return pl.pallas_call(
        functools.partial(gather_kernel, dp_size, seq_size),
        out_shape=[jax.ShapeDtypeStruct((devices,) + a.shape, jnp.bfloat16), jax.ShapeDtypeStruct((devices,) + m.shape, jnp.bfloat16)],
        in_specs=[pl.BlockSpec(memory_space=pl.ANY)] * 2,
        out_specs=[pl.BlockSpec(memory_space=pl.ANY)] * 2,
        scratch_shapes=[pltpu.SemaphoreType.DMA((send,)), pltpu.SemaphoreType.DMA((recv,)),
                        pltpu.SemaphoreType.DMA((send,)), pltpu.SemaphoreType.DMA((recv,)), pltpu.SemaphoreType.DMA((2,))],
        compiler_params=pltpu.CompilerParams(collective_id=0, has_side_effects=True),
    )(a, m)


def per_device(inputs, segments, attn_params, mlp_params, cotangent):
    micro_count = inputs.shape[0]
    local_rows = inputs.shape[2]
    seq_length = local_rows * lax.axis_size("seq")
    attn_total = attn_params.shape[0] * lax.axis_size(("dp", "seq"))
    mlp_total = mlp_params.shape[0] * lax.axis_size(("dp", "seq"))
    query_pos = lax.axis_index("seq") * local_rows + jnp.arange(local_rows, dtype=jnp.int32)
    score_scale = 1.0 / math.sqrt(HD)
    out_rows = []
    grad_rows = []
    attn_sums = None
    mlp_sums = None
    shard_sums = None
    attn_slots, mlp_slots = gather_params(attn_params, mlp_params, lax.axis_size("dp"), lax.axis_size("seq"))
    attn_set = unpack_params(
        attn_slots[:, : attn_params.shape[0] // LANES].reshape(-1), attention_layout()
    )
    mlp_set = unpack_params(
        mlp_slots[:, : mlp_params.shape[0] // LANES].reshape(-1), mlp_layout()
    )
    for micro_index in range(micro_count):
        gain_one, shift_one, w_qkv, bias_query, bias_value, w_proj, bias_proj = attn_set
        gain_two, shift_two, w_up, bias_up, w_down, bias_down = mlp_set
        input_rows = inputs[micro_index, 0].astype(jnp.float32)
        query_segs = segments[micro_index, 0]
        normed_one, norm_one_back = jax.vjp(
            layer_norm, input_rows, gain_one.astype(jnp.float32), shift_one.astype(jnp.float32)
        )
        normed_one_low = normed_one.astype(jnp.bfloat16)
        merged_rows = jnp.dot(normed_one_low, w_qkv, preferred_element_type=jnp.float32)
        query_low = (merged_rows[:, :D] + bias_query.astype(jnp.float32)).astype(jnp.bfloat16)
        kv_local = jnp.concatenate(
            [merged_rows[:, D : 2 * D], merged_rows[:, 2 * D :] + bias_value.astype(jnp.float32)],
            axis=1,
        ).astype(jnp.bfloat16)
        query_heads = query_low.reshape(local_rows, H, HD)

        def max_step(carry_in, sub_piece, key_start):
            scores, key_heads = block_scores(
                query_heads, query_segs, query_pos, sub_piece[0], sub_piece[1], key_start
            )
            running_top, running_total = carry_in
            new_top = jnp.maximum(running_top, jnp.max(scores, axis=-1))
            new_total = running_total * jnp.exp(running_top - new_top) + jnp.sum(
                jnp.exp(scores - new_top[..., None]), axis=-1
            )
            return (new_top, new_total)

        top_start = jnp.full((H, local_rows), score_floor, jnp.float32)
        row_top, row_total = fold_keys(
            kv_local,
            query_segs,
            partial(over_blocks, max_step),
            (top_start, jnp.zeros((H, local_rows), jnp.float32)),
        )
        log_total = row_top + jnp.log(row_total)

        def value_step(carry_in, sub_piece, key_start):
            scores, key_heads = block_scores(
                query_heads, query_segs, query_pos, sub_piece[0], sub_piece[1], key_start
            )
            probs = jnp.exp(scores - log_total[..., None])
            probs_low = probs.astype(jnp.bfloat16)
            probs_rest = (probs - probs_low.astype(jnp.float32)).astype(jnp.bfloat16)
            value_heads = sub_piece[0][:, D:].reshape(-1, H, HD)
            main_part, rest_part = carry_in
            main_part = main_part + jnp.einsum(
                "hqk,khd->qhd", probs_low, value_heads, preferred_element_type=jnp.float32
            )
            rest_part = rest_part + jnp.einsum(
                "hqk,khd->qhd", probs_rest, value_heads, preferred_element_type=jnp.float32
            )
            return (main_part, rest_part)

        zero_heads = jnp.zeros((local_rows, H, HD), jnp.float32)
        main_sum, rest_sum = fold_keys(
            kv_local, query_segs, partial(over_blocks, value_step), (zero_heads, zero_heads)
        )
        attended_low = main_sum.reshape(local_rows, D).astype(jnp.bfloat16)
        attended_full = main_sum + rest_sum
        middle = (
            input_rows
            + jnp.dot(attended_low, w_proj, preferred_element_type=jnp.float32)
            + bias_proj.astype(jnp.float32)
        )
        normed_two, norm_two_back = jax.vjp(
            layer_norm, middle, gain_two.astype(jnp.float32), shift_two.astype(jnp.float32)
        )
        normed_two_low = normed_two.astype(jnp.bfloat16)
        hidden = jnp.dot(normed_two_low, w_up, preferred_element_type=jnp.float32) + bias_up.astype(
            jnp.float32
        )
        active, gelu_back = jax.vjp(gelu_tanh, hidden)
        active_low = active.astype(jnp.bfloat16)
        result = (
            middle
            + jnp.dot(active_low, w_down, preferred_element_type=jnp.float32)
            + bias_down.astype(jnp.float32)
        )
        out_rows.append(result.astype(jnp.bfloat16))
        w_qkv, w_proj = (attn_set[2], attn_set[5])
        w_up, w_down = (mlp_set[2], mlp_set[4])
        cot_low = cotangent[micro_index, 0]
        cot_rows = cot_low.astype(jnp.float32)
        grad_w_down = jnp.einsum(
            "rf,rd->fd", active_low, cot_low, preferred_element_type=jnp.float32
        )
        grad_b_down = jnp.sum(cot_rows, axis=0)
        grad_active = jnp.einsum("rd,fd->rf", cot_low, w_down, preferred_element_type=jnp.float32)
        grad_hidden = gelu_back(grad_active)[0].astype(jnp.bfloat16)
        grad_w_up = jnp.einsum(
            "rd,rf->df", normed_two_low, grad_hidden, preferred_element_type=jnp.float32
        )
        grad_b_up = jnp.sum(grad_hidden.astype(jnp.float32), axis=0)
        grad_normed_two = jnp.einsum(
            "rf,df->rd", grad_hidden, w_up, preferred_element_type=jnp.float32
        )
        grad_middle_norm, grad_gain_two, grad_shift_two = norm_two_back(grad_normed_two)
        grad_middle = cot_rows + grad_middle_norm
        grad_branch = grad_middle.astype(jnp.bfloat16)
        grad_w_proj = jnp.einsum(
            "rd,re->de", attended_low, grad_branch, preferred_element_type=jnp.float32
        )
        grad_b_proj = jnp.sum(grad_branch.astype(jnp.float32), axis=0)
        grad_attended = jnp.einsum(
            "re,de->rd", grad_branch, w_proj, preferred_element_type=jnp.float32
        ).astype(jnp.bfloat16)
        grad_heads = grad_attended.reshape(local_rows, H, HD)
        row_delta = jnp.einsum("qhd,qhd->hq", grad_heads.astype(jnp.float32), attended_full)

        def grad_step(carry_in, sub_piece, key_start):
            scores, key_heads = block_scores(
                query_heads, query_segs, query_pos, sub_piece[0], sub_piece[1], key_start
            )
            value_heads = sub_piece[0][:, D:].reshape(-1, H, HD)
            probs = jnp.exp(scores - log_total[..., None])
            grad_probs = jnp.einsum(
                "qhd,khd->hqk", grad_heads, value_heads, preferred_element_type=jnp.float32
            )
            grad_scores = (probs * (grad_probs - row_delta[..., None])).astype(jnp.bfloat16)
            query_part, kv_part = carry_in
            query_part = (
                query_part
                + jnp.einsum(
                    "hqk,khd->qhd", grad_scores, key_heads, preferred_element_type=jnp.float32
                )
                * score_scale
            )
            key_grad = (
                jnp.einsum(
                    "hqk,qhd->khd", grad_scores, query_heads, preferred_element_type=jnp.float32
                )
                * score_scale
            )
            value_grad = jnp.einsum(
                "hqk,qhd->khd",
                probs.astype(jnp.bfloat16),
                grad_heads,
                preferred_element_type=jnp.float32,
            )
            block_grads = jnp.concatenate(
                [key_grad.reshape(-1, D), value_grad.reshape(-1, D)], axis=1
            )
            kv_part = lax.dynamic_update_slice_in_dim(kv_part, block_grads, key_start, 0)
            return (query_part, kv_part)

        query_sum, kv_sums = fold_keys(
            kv_local,
            query_segs,
            partial(over_blocks, grad_step),
            (zero_heads, jnp.zeros((seq_length, 2 * D), jnp.float32)),
        )
        kv_grads = lax.psum_scatter(
            kv_sums.astype(jnp.bfloat16), "seq", scatter_dimension=0, tiled=True
        ).astype(jnp.float32)
        grad_merged = jnp.concatenate([query_sum.reshape(local_rows, D), kv_grads], axis=1).astype(
            jnp.bfloat16
        )
        grad_merged_wide = grad_merged.astype(jnp.float32)
        grad_w_qkv = jnp.einsum(
            "rd,re->de", normed_one_low, grad_merged, preferred_element_type=jnp.float32
        )
        grad_b_query = jnp.sum(grad_merged_wide[:, :D], axis=0)
        grad_b_value = jnp.sum(grad_merged_wide[:, 2 * D :], axis=0)
        grad_normed_one = jnp.einsum(
            "re,de->rd", grad_merged, w_qkv, preferred_element_type=jnp.float32
        )
        grad_input_norm, grad_gain_one, grad_shift_one = norm_one_back(grad_normed_one)
        grad_rows.append(grad_middle + grad_input_norm)
        attn_list = [
            grad_gain_one,
            grad_shift_one,
            grad_w_qkv,
            grad_b_query,
            grad_b_value,
            grad_w_proj,
            grad_b_proj,
        ]
        mlp_list = [grad_gain_two, grad_shift_two, grad_w_up, grad_b_up, grad_w_down, grad_b_down]
        attn_sums = (
            attn_list
            if attn_sums is None
            else [left_sum + right_sum for left_sum, right_sum in zip(attn_sums, attn_list)]
        )
        mlp_sums = (
            mlp_list
            if mlp_sums is None
            else [left_sum + right_sum for left_sum, right_sum in zip(mlp_sums, mlp_list)]
        )
    shard_sums = send_grads(attn_sums, mlp_sums, attn_total, mlp_total)
    outputs = jnp.stack(out_rows)[:, None]
    input_grad = jnp.stack(grad_rows)[:, None]
    return (outputs, input_grad, shard_sums[0], shard_sums[1])


def solution(mesh):
    in_specs = (
        P(None, "dp", "seq", None),
        P(None, "dp", "seq"),
        P(("dp", "seq")),
        P(("dp", "seq")),
        P(None, "dp", "seq", None),
    )
    out_specs = (
        P(None, "dp", "seq", None),
        P(None, "dp", "seq", None),
        P(("dp", "seq")),
        P(("dp", "seq")),
    )
    return jax.shard_map(
        per_device, mesh=mesh, in_specs=in_specs, out_specs=out_specs, check_vma=False
    )
```

```python
import functools
from functools import partial
import math

import jax
import jax.numpy as jnp
from jax import lax
from jax.experimental import pallas as pl
from jax.experimental.pallas import tpu as pltpu
from jax.sharding import PartitionSpec as P

D = 768
H = 12
HD = 64
FF = 3072


norm_eps = 1e-05
score_floor = -1e30
key_block = 512


def attention_layout():
    return [(D,), (D,), (D, 3 * D), (D,), (D,), (D, D), (D,)]


def mlp_layout():
    return [(D,), (D,), (D, FF), (FF,), (FF, D), (D,)]


def unpack_params(flat_vector, layout):
    offset = 0
    result = []
    for dims_entry in layout:
        amount = math.prod(dims_entry)
        result.append(lax.slice_in_dim(flat_vector, offset, offset + amount).reshape(dims_entry))
        offset += amount
    return result


def layer_norm(values, gain, shift):
    average = jnp.mean(values, axis=-1, keepdims=True)
    centred = values - average
    spread = jnp.mean(centred * centred, axis=-1, keepdims=True)
    return centred * lax.rsqrt(spread + norm_eps) * gain + shift


def gelu_tanh(values):
    return jax.nn.gelu(values, approximate=True)


def pack_grads(grad_list, total_size):
    flat_parts = [part_grad.reshape(-1) for part_grad in grad_list]
    used_total = sum((part_grad.size for part_grad in grad_list))
    flat_parts.append(jnp.zeros((total_size - used_total,), jnp.float32))
    return jnp.concatenate(flat_parts)


def fetch_params(attn_params, mlp_params):
    gathered = (
        lax.all_gather(attn_params, ("dp", "seq"), axis=0, tiled=True),
        lax.all_gather(mlp_params, ("dp", "seq"), axis=0, tiled=True),
    )
    return (
        unpack_params(gathered[0], attention_layout()),
        unpack_params(gathered[1], mlp_layout()),
    )


def send_grads(attn_list, mlp_list, attn_total, mlp_total):
    return (
        lax.psum_scatter(
            pack_grads(attn_list, attn_total), ("dp", "seq"), scatter_dimension=0, tiled=True
        ),
        lax.psum_scatter(
            pack_grads(mlp_list, mlp_total), ("dp", "seq"), scatter_dimension=0, tiled=True
        ),
    )


def fold_keys(key_rows, key_segs, fold_step, start_carry):
    return fold_step(
        start_carry,
        (
            lax.all_gather(key_rows, "seq", axis=0, tiled=True),
            lax.all_gather(key_segs, "seq", axis=0, tiled=True),
        ),
        jnp.int32(0),
    )


def over_blocks(block_step, carry_now, key_piece, key_start):
    piece_rows = key_piece[0].shape[0]
    step_rows = math.gcd(piece_rows, key_block)

    def loop_step(index_block, carry_in):
        offset = index_block * step_rows
        sub_piece = tuple(
            (lax.dynamic_slice_in_dim(member, offset, step_rows, 0) for member in key_piece)
        )
        return block_step(carry_in, sub_piece, offset)

    return lax.fori_loop(0, piece_rows // step_rows, loop_step, carry_now)


def block_scores(query_heads, query_segs, query_pos, kv_rows, key_segs, key_start):
    key_heads = kv_rows[:, :D].reshape(-1, H, HD)
    scores = jnp.einsum(
        "qhd,khd->hqk", query_heads, key_heads, preferred_element_type=jnp.float32
    ) * (1.0 / math.sqrt(HD))
    key_pos = key_start + jnp.arange(kv_rows.shape[0], dtype=jnp.int32)
    allowed = (query_segs[:, None] == key_segs[None, :]) & (key_pos[None, :] <= query_pos[:, None])
    return (jnp.where(allowed[None], scores, score_floor), key_heads)


MESH = pl.DeviceIdType.MESH
LANES = 128

def pad_rows(rows):
    return -(-rows // 16) * 16


class Gather:
    def __init__(self, dp_size, seq_size, own, slots, send_sems, recv_sems):
        self.n = seq_size
        self.bits = [b for b in range(1, dp_size.bit_length() - 1)]
        self.dp = lax.axis_index("dp")
        self.z = lax.axis_index("seq")
        self.own, self.slots = own, slots
        self.rows = own.shape[0]
        half = self.rows // 32 * 16
        self.parts = [(0, half), (half, self.rows - half)]
        self.orders = [self.bits, self.bits[::-1]]
        self.send_sems, self.recv_sems = send_sems, recv_sems
        self.started = []

    def peers(self):
        out = [(self.dp, lax.rem(self.z + k, self.n)) for k in range(1, self.n)]
        out += [(self.dp ^ (1 << b), self.z) for b in [0] + self.bits]
        return out

    def slot(self, mask, k):
        return (self.dp ^ mask) * self.n + lax.rem(self.z + self.n - k, self.n)

    def view(self, mask, k, part):
        index = self.slot(mask, k)
        if part is None:
            return self.slots.at[index]
        start, size = self.parts[part]
        return self.slots.at[index, pl.ds(start, size)]

    def source(self, mask, k, part):
        if mask == 0 and k == 0:
            if part is None:
                return self.own
            start, size = self.parts[part]
            return self.own.at[pl.ds(start, size)]
        return self.view(mask, k, part)

    def send(self, mask, k, part, to, kind, recv_index):
        copy = pltpu.make_async_remote_copy(
            src_ref=self.source(mask, k, part),
            dst_ref=self.view(mask, k, part),
            send_sem=self.send_sems.at[len(self.started)],
            recv_sem=self.recv_sems.at[recv_index],
            device_id=to,
            device_id_type=MESH,
        )
        copy.start()
        self.started.append(part)

    def recv_index(self, sibling, part, mask, k):
        part = 0 if part is None else part
        return ((sibling * 2 + part) * (2 << len(self.bits)) // 2 + (mask >> 1)) * self.n + k

    def wait(self, sibling, part, mask, k):
        view = self.view(mask ^ sibling, k, part)
        pltpu.make_async_remote_copy(
            src_ref=view, dst_ref=view, send_sem=self.send_sems.at[0],
            recv_sem=self.recv_sems.at[self.recv_index(sibling, part, mask, k)],
            device_id=(self.dp, self.z), device_id_type=MESH,
        ).wait_recv()

    def forward(self, part, mask, k):
        for p in ((0, 1) if part is None else (part,)):
            order = self.orders[p]
            last = max([order.index(b) for b in self.bits if mask >> b & 1], default=-1)
            for b in order[last + 1 :]:
                self.send(mask, k, p, (self.dp ^ (1 << b), self.z), 0, self.recv_index(0, p, mask | 1 << b, k))
        self.send(mask, k, part, (self.dp ^ 1, self.z), 1, self.recv_index(1, part, mask, k))

    def begin(self):
        for k in range(1, self.n):
            self.send(0, 0, None, (self.dp, lax.rem(self.z + k, self.n)), 0, self.recv_index(0, None, 0, k))
        self.forward(None, 0, 0)

    def events(self):
        out = []
        for k in range(1, self.n):
            out.append((k, None, 0, k))
        for k in range(self.n):
            for p in (0, 1):
                for level in range(len(self.bits)):
                    order = self.orders[p]
                    for low in range(1 << level):
                        mask = 1 << order[level]
                        for i in range(level):
                            if low >> i & 1:
                                mask |= 1 << order[i]
                        out.append(((level + 1) * 4 + k, p, mask, k))
        out.sort(key=lambda e: e[0])
        return [e[1:] for e in out]

    def step(self, event):
        part, mask, k = event
        self.wait(0, part, mask, k)
        self.forward(part, mask, k)

    def sibling_events(self):
        return [(None, 0, 0)] + self.events()

    def finish_sibling(self):
        for part, mask, k in self.sibling_events():
            self.wait(1, part, mask, k)

    def finish_sends(self):
        for index, part in enumerate(self.started):
            start, size = (0, self.rows) if part is None else self.parts[part]
            view = self.slots.at[0, pl.ds(start, size)]
            pltpu.make_async_remote_copy(
                src_ref=view, dst_ref=view, send_sem=self.send_sems.at[index], recv_sem=self.recv_sems.at[0],
                device_id=(self.dp, self.z), device_id_type=MESH,
            ).wait_send()


def gather_counts(dp_size, seq_size):
    bits = dp_size.bit_length() - 2
    recv = 4 * (1 << bits) * seq_size
    send = 0
    send += seq_size - 1
    for p in range(2):
        for mask in range(1 << bits):
            top = mask.bit_length()
            send += (bits - top) * seq_size
    send += seq_size + 2 * ((1 << bits) - 1) * seq_size
    return send, recv


def gather_kernel(dp_size, seq_size, a_own, m_own, a_slots, m_slots, a_send, a_recv, m_send, m_recv, own_sems):
    ga = Gather(dp_size, seq_size, a_own, a_slots, a_send, a_recv)
    gm = Gather(dp_size, seq_size, m_own, m_slots, m_send, m_recv)
    barrier = pltpu.get_barrier_semaphore()
    peers = ga.peers()
    for peer in peers:
        pl.semaphore_signal(barrier, inc=1, device_id=peer, device_id_type=MESH)
    pl.semaphore_wait(barrier, len(peers))
    ca = pltpu.make_async_copy(a_own, a_slots.at[ga.slot(0, 0)], own_sems.at[0])
    cm = pltpu.make_async_copy(m_own, m_slots.at[gm.slot(0, 0)], own_sems.at[1])
    ca.start()
    cm.start()
    ga.begin()
    gm.begin()
    for e in ga.events():
        ga.step(e)
    for e in gm.events():
        gm.step(e)
    ca.wait()
    cm.wait()
    ga.finish_sibling()
    gm.finish_sibling()
    ga.finish_sends()
    gm.finish_sends()


def to_rows(flat):
    rows = flat.shape[0] // LANES
    return jnp.pad(flat.reshape(rows, LANES), ((0, pad_rows(rows) - rows), (0, 0)))


def gather_params(attn, mlp, dp_size, seq_size):
    a, m = to_rows(attn), to_rows(mlp)
    devices = dp_size * seq_size
    send, recv = gather_counts(dp_size, seq_size)
    return pl.pallas_call(
        functools.partial(gather_kernel, dp_size, seq_size),
        out_shape=[jax.ShapeDtypeStruct((devices,) + a.shape, jnp.bfloat16), jax.ShapeDtypeStruct((devices,) + m.shape, jnp.bfloat16)],
        in_specs=[pl.BlockSpec(memory_space=pl.ANY)] * 2,
        out_specs=[pl.BlockSpec(memory_space=pl.ANY)] * 2,
        scratch_shapes=[pltpu.SemaphoreType.DMA((send,)), pltpu.SemaphoreType.DMA((recv,)),
                        pltpu.SemaphoreType.DMA((send,)), pltpu.SemaphoreType.DMA((recv,)), pltpu.SemaphoreType.DMA((2,))],
        compiler_params=pltpu.CompilerParams(collective_id=0, has_side_effects=True),
    )(a, m)


def per_device(inputs, segments, attn_params, mlp_params, cotangent):
    micro_count = inputs.shape[0]
    local_rows = inputs.shape[2]
    seq_length = local_rows * lax.axis_size("seq")
    attn_total = attn_params.shape[0] * lax.axis_size(("dp", "seq"))
    mlp_total = mlp_params.shape[0] * lax.axis_size(("dp", "seq"))
    query_pos = lax.axis_index("seq") * local_rows + jnp.arange(local_rows, dtype=jnp.int32)
    score_scale = 1.0 / math.sqrt(HD)
    out_rows = []
    grad_rows = []
    attn_sums = None
    mlp_sums = None
    shard_sums = None
    attn_slots, mlp_slots = gather_params(attn_params, mlp_params, lax.axis_size("dp"), lax.axis_size("seq"))
    attn_set = unpack_params(
        attn_slots[:, : attn_params.shape[0] // LANES].reshape(-1), attention_layout()
    )
    mlp_set = unpack_params(
        mlp_slots[:, : mlp_params.shape[0] // LANES].reshape(-1), mlp_layout()
    )
    for micro_index in range(micro_count):
        gain_one, shift_one, w_qkv, bias_query, bias_value, w_proj, bias_proj = attn_set
        gain_two, shift_two, w_up, bias_up, w_down, bias_down = mlp_set
        input_rows = inputs[micro_index, 0].astype(jnp.float32)
        query_segs = segments[micro_index, 0]
        normed_one, norm_one_back = jax.vjp(
            layer_norm, input_rows, gain_one.astype(jnp.float32), shift_one.astype(jnp.float32)
        )
        normed_one_low = normed_one.astype(jnp.bfloat16)
        merged_rows = jnp.dot(normed_one_low, w_qkv, preferred_element_type=jnp.float32)
        query_low = (merged_rows[:, :D] + bias_query.astype(jnp.float32)).astype(jnp.bfloat16)
        kv_local = jnp.concatenate(
            [merged_rows[:, D : 2 * D], merged_rows[:, 2 * D :] + bias_value.astype(jnp.float32)],
            axis=1,
        ).astype(jnp.bfloat16)
        query_heads = query_low.reshape(local_rows, H, HD)

        def max_step(carry_in, sub_piece, key_start):
            scores, key_heads = block_scores(
                query_heads, query_segs, query_pos, sub_piece[0], sub_piece[1], key_start
            )
            running_top, running_total = carry_in
            new_top = jnp.maximum(running_top, jnp.max(scores, axis=-1))
            new_total = running_total * jnp.exp(running_top - new_top) + jnp.sum(
                jnp.exp(scores - new_top[..., None]), axis=-1
            )
            return (new_top, new_total)

        top_start = jnp.full((H, local_rows), score_floor, jnp.float32)
        row_top, row_total = fold_keys(
            kv_local,
            query_segs,
            partial(over_blocks, max_step),
            (top_start, jnp.zeros((H, local_rows), jnp.float32)),
        )
        log_total = row_top + jnp.log(row_total)

        def value_step(carry_in, sub_piece, key_start):
            scores, key_heads = block_scores(
                query_heads, query_segs, query_pos, sub_piece[0], sub_piece[1], key_start
            )
            probs = jnp.exp(scores - log_total[..., None])
            probs_low = probs.astype(jnp.bfloat16)
            probs_rest = (probs - probs_low.astype(jnp.float32)).astype(jnp.bfloat16)
            value_heads = sub_piece[0][:, D:].reshape(-1, H, HD)
            main_part, rest_part = carry_in
            main_part = main_part + jnp.einsum(
                "hqk,khd->qhd", probs_low, value_heads, preferred_element_type=jnp.float32
            )
            rest_part = rest_part + jnp.einsum(
                "hqk,khd->qhd", probs_rest, value_heads, preferred_element_type=jnp.float32
            )
            return (main_part, rest_part)

        zero_heads = jnp.zeros((local_rows, H, HD), jnp.float32)
        main_sum, rest_sum = fold_keys(
            kv_local, query_segs, partial(over_blocks, value_step), (zero_heads, zero_heads)
        )
        attended_low = main_sum.reshape(local_rows, D).astype(jnp.bfloat16)
        attended_full = main_sum + rest_sum
        middle = (
            input_rows
            + jnp.dot(attended_low, w_proj, preferred_element_type=jnp.float32)
            + bias_proj.astype(jnp.float32)
        )
        normed_two, norm_two_back = jax.vjp(
            layer_norm, middle, gain_two.astype(jnp.float32), shift_two.astype(jnp.float32)
        )
        normed_two_low = normed_two.astype(jnp.bfloat16)
        hidden = jnp.dot(normed_two_low, w_up, preferred_element_type=jnp.float32) + bias_up.astype(
            jnp.float32
        )
        active, gelu_back = jax.vjp(gelu_tanh, hidden)
        active_low = active.astype(jnp.bfloat16)
        result = (
            middle
            + jnp.dot(active_low, w_down, preferred_element_type=jnp.float32)
            + bias_down.astype(jnp.float32)
        )
        out_rows.append(result.astype(jnp.bfloat16))
        w_qkv, w_proj = (attn_set[2], attn_set[5])
        w_up, w_down = (mlp_set[2], mlp_set[4])
        cot_low = cotangent[micro_index, 0]
        cot_rows = cot_low.astype(jnp.float32)
        grad_w_down = jnp.einsum(
            "rf,rd->fd", active_low, cot_low, preferred_element_type=jnp.float32
        )
        grad_b_down = jnp.sum(cot_rows, axis=0)
        grad_active = jnp.einsum("rd,fd->rf", cot_low, w_down, preferred_element_type=jnp.float32)
        grad_hidden = gelu_back(grad_active)[0].astype(jnp.bfloat16)
        grad_w_up = jnp.einsum(
            "rd,rf->df", normed_two_low, grad_hidden, preferred_element_type=jnp.float32
        )
        grad_b_up = jnp.sum(grad_hidden.astype(jnp.float32), axis=0)
        grad_normed_two = jnp.einsum(
            "rf,df->rd", grad_hidden, w_up, preferred_element_type=jnp.float32
        )
        grad_middle_norm, grad_gain_two, grad_shift_two = norm_two_back(grad_normed_two)
        grad_middle = cot_rows + grad_middle_norm
        grad_branch = grad_middle.astype(jnp.bfloat16)
        grad_w_proj = jnp.einsum(
            "rd,re->de", attended_low, grad_branch, preferred_element_type=jnp.float32
        )
        grad_b_proj = jnp.sum(grad_branch.astype(jnp.float32), axis=0)
        grad_attended = jnp.einsum(
            "re,de->rd", grad_branch, w_proj, preferred_element_type=jnp.float32
        ).astype(jnp.bfloat16)
        grad_heads = grad_attended.reshape(local_rows, H, HD)
        row_delta = jnp.einsum("qhd,qhd->hq", grad_heads.astype(jnp.float32), attended_full)

        def grad_step(carry_in, sub_piece, key_start):
            scores, key_heads = block_scores(
                query_heads, query_segs, query_pos, sub_piece[0], sub_piece[1], key_start
            )
            value_heads = sub_piece[0][:, D:].reshape(-1, H, HD)
            probs = jnp.exp(scores - log_total[..., None])
            grad_probs = jnp.einsum(
                "qhd,khd->hqk", grad_heads, value_heads, preferred_element_type=jnp.float32
            )
            grad_scores = (probs * (grad_probs - row_delta[..., None])).astype(jnp.bfloat16)
            query_part, kv_part = carry_in
            query_part = (
                query_part
                + jnp.einsum(
                    "hqk,khd->qhd", grad_scores, key_heads, preferred_element_type=jnp.float32
                )
                * score_scale
            )
            key_grad = (
                jnp.einsum(
                    "hqk,qhd->khd", grad_scores, query_heads, preferred_element_type=jnp.float32
                )
                * score_scale
            )
            value_grad = jnp.einsum(
                "hqk,qhd->khd",
                probs.astype(jnp.bfloat16),
                grad_heads,
                preferred_element_type=jnp.float32,
            )
            block_grads = jnp.concatenate(
                [key_grad.reshape(-1, D), value_grad.reshape(-1, D)], axis=1
            )
            kv_part = lax.dynamic_update_slice_in_dim(kv_part, block_grads, key_start, 0)
            return (query_part, kv_part)

        query_sum, kv_sums = fold_keys(
            kv_local,
            query_segs,
            partial(over_blocks, grad_step),
            (zero_heads, jnp.zeros((seq_length, 2 * D), jnp.float32)),
        )
        kv_grads = lax.psum_scatter(
            kv_sums.astype(jnp.bfloat16), "seq", scatter_dimension=0, tiled=True
        ).astype(jnp.float32)
        grad_merged = jnp.concatenate([query_sum.reshape(local_rows, D), kv_grads], axis=1).astype(
            jnp.bfloat16
        )
        grad_merged_wide = grad_merged.astype(jnp.float32)
        grad_w_qkv = jnp.einsum(
            "rd,re->de", normed_one_low, grad_merged, preferred_element_type=jnp.float32
        )
        grad_b_query = jnp.sum(grad_merged_wide[:, :D], axis=0)
        grad_b_value = jnp.sum(grad_merged_wide[:, 2 * D :], axis=0)
        grad_normed_one = jnp.einsum(
            "re,de->rd", grad_merged, w_qkv, preferred_element_type=jnp.float32
        )
        grad_input_norm, grad_gain_one, grad_shift_one = norm_one_back(grad_normed_one)
        grad_rows.append(grad_middle + grad_input_norm)
        attn_list = [
            grad_gain_one,
            grad_shift_one,
            grad_w_qkv,
            grad_b_query,
            grad_b_value,
            grad_w_proj,
            grad_b_proj,
        ]
        mlp_list = [grad_gain_two, grad_shift_two, grad_w_up, grad_b_up, grad_w_down, grad_b_down]
        attn_sums = (
            attn_list
            if attn_sums is None
            else [left_sum + right_sum for left_sum, right_sum in zip(attn_sums, attn_list)]
        )
        mlp_sums = (
            mlp_list
            if mlp_sums is None
            else [left_sum + right_sum for left_sum, right_sum in zip(mlp_sums, mlp_list)]
        )
    shard_sums = send_grads(attn_sums, mlp_sums, attn_total, mlp_total)
    outputs = jnp.stack(out_rows)[:, None]
    input_grad = jnp.stack(grad_rows)[:, None]
    return (outputs, input_grad, shard_sums[0], shard_sums[1])


HALF_HEADS = H // 2
HALF_COLS = D // 2
ROW_D = D // LANES
ROW_FF = FF // LANES
ROW_QKV = 3 * ROW_D
ROW_HALF = HALF_COLS // LANES
FF_STEP = 512
VMEM_LIMIT = 62 * 2**20

ATTN_QKV = 2 * ROW_D
ATTN_BQ = ATTN_QKV + D * ROW_QKV
ATTN_BV = ATTN_BQ + ROW_D
ATTN_PROJ = ATTN_BV + ROW_D
ATTN_BPROJ = ATTN_PROJ + D * ROW_D
MLP_UP = 2 * ROW_D
MLP_BUP = MLP_UP + D * ROW_FF
MLP_DOWN = MLP_BUP + ROW_FF
MLP_BDOWN = MLP_DOWN + FF * ROW_D

f32 = jnp.float32
bf16 = jnp.bfloat16


def dot_nn(left, right):
    return jnp.dot(left, right, preferred_element_type=f32)


def dot_nt(left, right):
    return lax.dot_general(left, right, (((1,), (1,)), ((), ())), preferred_element_type=f32)


def dot_tn(left, right):
    return lax.dot_general(left, right, (((0,), (0,)), ((), ())), preferred_element_type=f32)


def remote(src, dst, send_sem, recv_sem, to):
    return pltpu.make_async_remote_copy(
        src_ref=src, dst_ref=dst, send_sem=send_sem, recv_sem=recv_sem, device_id=to, device_id_type=MESH
    )


class Place:
    def __init__(self, seq_size):
        self.n = seq_size
        self.dp = lax.axis_index("dp")
        self.z = lax.axis_index("seq")
        self.core = lax.rem(self.dp, 2)
        self.base = self.dp - self.core
        self.sibling = (self.base + 1 - self.core, self.z)

    def line_peers(self):
        out = [self.sibling]
        for k in range(1, self.n):
            other = lax.rem(self.z + k, self.n)
            out += [(self.base, other), (self.base + 1, other)]
        return out

    def own_block(self, j):
        return 1 - self.core + 2 * j

    def other_block(self, j):
        return self.core + 2 * j

    def worker(self, micro):
        return (self.base + 1 - lax.rem(self.z, 2), 2 * micro + self.core)

    def home(self, j):
        return (self.base + lax.rem(self.z, 2), self.own_block(j)), self.z // 2


def greet(peers):
    barrier = pltpu.get_barrier_semaphore()
    for peer in peers:
        pl.semaphore_signal(barrier, inc=1, device_id=peer, device_id_type=MESH)
    pl.semaphore_wait(barrier, len(peers))


def unflatten(slots, flat, rows):
    def body(s, carry):
        flat[pl.ds(s * rows, rows), :] = slots[s, :rows, :].astype(f32)
        return carry

    lax.fori_loop(0, slots.shape[0], body, 0)


def flatten(flat, slots, rows):
    def body(s, carry):
        slots[s, :rows, :] = flat[pl.ds(s * rows, rows), :].astype(bf16)
        return carry

    lax.fori_loop(0, slots.shape[0], body, 0)


def load_matrix(flat, start, stride, columns, out, step):
    def body(i, carry):
        rows = pl.ds(pl.multiple_of(i * step, step), step)
        for j in range(columns):
            piece = flat[pl.ds(start + j + i * (step * stride), step, stride=stride), :]
            out[rows, j * LANES : (j + 1) * LANES] = piece.astype(bf16)
        return carry

    lax.fori_loop(0, out.shape[0] // step, body, 0)


def load_vector(flat, start, blocks):
    return jnp.concatenate([flat[pl.ds(start + j, 1), :] for j in range(blocks)], axis=1)


def store_vector(flat, start, value):
    for j in range(value.shape[1] // LANES):
        flat[pl.ds(start + j, 1), :] = value[:, j * LANES : (j + 1) * LANES]


def norm_parts(values):
    average = jnp.mean(values, axis=-1, keepdims=True)
    centred = values - average
    spread = jnp.mean(centred * centred, axis=-1, keepdims=True)
    scale = lax.rsqrt(spread + norm_eps)
    return centred * scale, scale


def norm_back(normal, scale, grad, gain):
    scaled = grad * gain
    return scale * (
        scaled
        - jnp.mean(scaled, axis=-1, keepdims=True)
        - normal * jnp.mean(scaled * normal, axis=-1, keepdims=True)
    )


def forward_kernel(
    dp_size, seq_size, a_rows,
    x_in, seg_in, cot_in, a_own, m_own,
    m_slots, cot_own, x_own, n1, wqkv, w_proj, vec, qt, kt, vt, qh, kh, vh, bias, lse, att,
    a_slots, flat, x_all, seg_all, seg_col, scores, ot, att_out,
    a_send, a_recv, m_send, m_recv, own_sems, move_send, move_recv, cot_sems, swap_sems,
):
    place = Place(seq_size)
    block = x_in.shape[1]
    ga = Gather(dp_size, seq_size, a_own, a_slots, a_send, a_recv)
    gm = Gather(dp_size, seq_size, m_own, m_slots, m_send, m_recv)
    greet(place.line_peers() + [(place.dp ^ (1 << b), place.z) for b in ga.bits])

    own_copies = [
        pltpu.make_async_copy(a_own, a_slots.at[ga.slot(0, 0)], own_sems.at[0]),
        pltpu.make_async_copy(m_own, m_slots.at[gm.slot(0, 0)], own_sems.at[1]),
    ]
    for copy in own_copies:
        copy.start()
    sent = []
    for micro in range(2):
        to = place.worker(micro)
        sent.append(
            remote(x_in.at[micro], x_all.at[place.z], move_send.at[0, micro], move_recv.at[0, place.z], to)
        )
        sent.append(
            remote(seg_in.at[micro], seg_all.at[place.z], move_send.at[1, micro], move_recv.at[1, place.z], to)
        )
    for copy in sent:
        copy.start()
    ga.begin()
    for micro in range(2):
        copy = remote(
            cot_in.at[micro], cot_own.at[place.z // 2], cot_sems.at[0, micro], cot_sems.at[1, place.z // 2],
            place.worker(micro),
        )
        copy.start()
        sent.append(copy)
    gm.begin()

    def arrival(t, kind):
        ref = (x_all, seg_all)[kind].at[t]
        return remote(ref, ref, move_send.at[kind, 0], move_recv.at[kind, t], place.sibling)

    for j in range(2):
        t = place.own_block(j)
        for kind in range(2):
            ref = (x_all, seg_all)[kind].at[t]
            arrival(t, kind).wait_recv()
            copy = remote(ref, ref, move_send.at[kind, 2 + j], move_recv.at[kind, t], place.sibling)
            copy.start()
            sent.append(copy)
    for event in ga.events():
        ga.step(event)
    for j in range(2):
        for kind in range(2):
            arrival(place.other_block(j), kind).wait_recv()
        x_own[j] = x_all[place.own_block(j)]

    for t in range(seq_size):
        for r in range(block // LANES):
            row = jnp.broadcast_to(seg_all[t, r : r + 1, :], (LANES, LANES))
            seg_col[pl.ds(t * block + r * LANES, LANES), :] = row.T
    chunks = seq_size * block // LANES
    key_pos = lax.broadcasted_iota(jnp.int32, (LANES, LANES), 0)
    query_pos = lax.broadcasted_iota(jnp.int32, (LANES, LANES), 1)
    for q in range(chunks):
        row = seg_all[q * LANES // block, q % (block // LANES) : q % (block // LANES) + 1, :]
        top = (q * LANES // block + 1) * block // LANES
        for k in range(top):
            rows = slice(k * LANES, (k + 1) * LANES)
            if k > q:
                value = jnp.full((LANES, LANES), score_floor, f32)
            else:
                allowed = seg_col[rows, :] == row
                if k == q:
                    allowed = allowed & (key_pos <= query_pos)
                value = jnp.where(allowed, 0.0, score_floor)
            bias[rows, q * LANES : (q + 1) * LANES] = value

    own_copies[0].wait()
    ga.finish_sibling()
    unflatten(a_slots, flat, a_rows)
    for section in range(3):
        load_matrix(
            flat, ATTN_QKV + section * ROW_D + place.core * ROW_HALF, ROW_QKV, ROW_HALF, wqkv.at[section], LANES
        )
    load_matrix(flat, ATTN_PROJ, ROW_D, ROW_D, w_proj, LANES)
    gain = load_vector(flat, 0, ROW_D)
    shift = load_vector(flat, ROW_D, ROW_D)
    vec[...] = jnp.zeros_like(vec)
    vec[0:1, :] = gain
    vec[1:2, :] = load_vector(flat, ATTN_BPROJ, ROW_D)
    bias_query = load_vector(flat, ATTN_BQ + place.core * ROW_HALF, ROW_HALF)
    bias_value = load_vector(flat, ATTN_BV + place.core * ROW_HALF, ROW_HALF)

    def project(t, carry):
        rows = pl.ds(pl.multiple_of(t * block, block), block)
        normal, _ = norm_parts(x_all[t].astype(f32))
        low = (normal * gain + shift).astype(bf16)
        n1[rows, :] = low
        query = (dot_nn(low, wqkv[0]) + bias_query).astype(bf16).astype(f32) * (1.0 / math.sqrt(HD))
        key = dot_nn(low, wqkv[1])
        value = dot_nn(low, wqkv[2]) + bias_value
        for result, across, heads in ((query, qt, qh), (key, kt, kh), (value, vt, vh)):
            across[:, rows] = result.T.astype(bf16)
            rounded = result.astype(bf16)
            for h in range(HALF_HEADS):
                heads[h, rows, :] = rounded[:, h * HD : (h + 1) * HD]
        return carry

    lax.fori_loop(0, seq_size, project, 0)
    lse[...] = jnp.zeros_like(lse)

    m_events = gm.events()
    per_head = -(-len(m_events) // HALF_HEADS)

    def one_head(h, carry):
        for c in range(HALF_HEADS):

            @pl.when(h == c)
            def _():
                for event in m_events[c * per_head : (c + 1) * per_head]:
                    gm.step(event)

        head_rows = pl.ds(pl.multiple_of(h * HD, HD), HD)
        for i in range(seq_size):
            columns = slice(i * block, (i + 1) * block)
            query = qt[head_rows, columns]
            top = jnp.full((1, block), -jnp.inf, f32)
            for b in range(i + 1):
                rows = slice(b * block, (b + 1) * block)
                piece = dot_nn(kh[h, rows, :], query) + bias[rows, columns]
                scores[rows, :] = piece
                top = jnp.maximum(top, jnp.max(piece, axis=0, keepdims=True))
            total = jnp.zeros((1, block), f32)
            for b in range(i + 1):
                rows = slice(b * block, (b + 1) * block)
                piece = jnp.exp(scores[rows, :] - top)
                scores[rows, :] = piece
                total = total + jnp.sum(piece, axis=0, keepdims=True)
            inverse = 1.0 / total
            result = jnp.zeros((HD, block), f32)
            for b in range(i + 1):
                rows = slice(b * block, (b + 1) * block)
                result = result + dot_nn(vt[head_rows, rows], (scores[rows, :] * inverse).astype(bf16))
            ot[head_rows, columns] = result
            lse[pl.ds(h, 1), columns] = top + jnp.log(total)
        return carry

    lax.fori_loop(0, HALF_HEADS, one_head, 0)

    for j in range(2):
        columns = pl.ds(pl.multiple_of(place.other_block(j) * block, block), block)
        att_out[j] = ot[:, columns].T.astype(bf16)
        copy = remote(
            att_out.at[j], att.at[place.core, j], swap_sems.at[0, j], swap_sems.at[1, j], place.sibling
        )
        copy.start()
        sent.append(copy)
    for j in range(2):
        columns = pl.ds(pl.multiple_of(place.own_block(j) * block, block), block)
        att[place.core, j] = ot[:, columns].T.astype(bf16)
    for j in range(2):
        ref = att.at[1 - place.core, j]
        remote(ref, ref, swap_sems.at[0, j], swap_sems.at[1, j], place.sibling).wait_recv()
        ref = cot_own.at[j]
        remote(ref, ref, cot_sems.at[0, j], cot_sems.at[1, j], place.sibling).wait_recv()
    own_copies[1].wait()
    gm.finish_sibling()
    for copy in sent:
        copy.wait_send()
    ga.finish_sends()
    gm.finish_sends()


def mlp_kernel(
    m_rows,
    m_slots, x_own, cot, att, w_proj, vec,
    out, d_mid, d_att, g_slots, g_proj, g_bias,
    flat, w_up, w_down, mid, n2, d_n2, total, b_up, gb_up, sem,
):
    rows_all = x_own.shape[0]
    half = rows_all // 2
    copy = pltpu.make_async_copy(m_slots, g_slots, sem)
    copy.start()
    blocks = [slice(0, half), slice(half, rows_all)]
    for rows in blocks:
        mid[rows, :] = (
            x_own[rows, :].astype(f32)
            + dot_nn(att[0, rows, :], w_proj[:HALF_COLS, :])
            + dot_nn(att[1, rows, :], w_proj[HALF_COLS:, :])
            + vec[1:2, :]
        )
    copy.wait()
    unflatten(g_slots, flat, m_rows)
    load_matrix(flat, MLP_UP, ROW_FF, ROW_FF, w_up, 64)
    load_matrix(flat, MLP_DOWN, ROW_D, ROW_D, w_down, LANES)
    gain = load_vector(flat, 0, ROW_D)
    shift = load_vector(flat, ROW_D, ROW_D)
    b_down = load_vector(flat, MLP_BDOWN, ROW_D)
    b_up[...] = load_vector(flat, MLP_BUP, ROW_FF)
    for rows in blocks:
        normal, _ = norm_parts(mid[rows, :])
        n2[rows, :] = (normal * gain + shift).astype(bf16)
    total[...] = jnp.zeros_like(total)
    d_n2[...] = jnp.zeros_like(d_n2)
    inner = math.sqrt(2.0 / math.pi)

    def step(f, carry):
        start = pl.multiple_of(f * FF_STEP, FF_STEP)
        columns = pl.ds(start, FF_STEP)
        hidden = dot_nn(n2[...], w_up[:, columns]) + b_up[:, columns]
        square = hidden * hidden
        tanh = jnp.tanh(inner * (hidden + 0.044715 * (square * hidden)))
        cdf = 0.5 * (1.0 + tanh)
        active = (hidden * cdf).astype(bf16)
        slope = cdf + (0.5 * inner) * hidden * (1.0 - tanh * tanh) * (1.0 + (3 * 0.044715) * square)
        d_hidden = dot_nt(cot[...], w_down[columns, :]) * slope
        low = d_hidden.astype(bf16)
        gb_up[:, columns] = jnp.sum(low.astype(f32), axis=0, keepdims=True)
        total[...] += dot_nn(active, w_down[columns, :])
        d_n2[...] += dot_nt(low, w_up[:, columns])
        g_down = dot_tn(active, cot[...])
        for j in range(ROW_D):
            flat[pl.ds(MLP_DOWN + j + f * (FF_STEP * ROW_D), FF_STEP, stride=ROW_D), :] = g_down[
                :, j * LANES : (j + 1) * LANES
            ]
        g_up = dot_tn(n2[...], low)
        for j in range(FF_STEP // LANES):
            flat[pl.ds(MLP_UP + j + f * (FF_STEP // LANES), D, stride=ROW_FF), :] = g_up[
                :, j * LANES : (j + 1) * LANES
            ]
        return carry

    lax.fori_loop(0, FF // FF_STEP, step, 0)

    gain_sum = jnp.zeros((1, D), f32)
    shift_sum = jnp.zeros((1, D), f32)
    down_sum = jnp.zeros((1, D), f32)
    proj_sum = jnp.zeros((1, D), f32)
    for rows in blocks:
        out[rows, :] = (mid[rows, :] + total[rows, :] + b_down).astype(bf16)
        normal, scale = norm_parts(mid[rows, :])
        grad = d_n2[rows, :]
        cot_rows = cot[rows, :].astype(f32)
        gain_sum += jnp.sum(grad * normal, axis=0, keepdims=True)
        shift_sum += jnp.sum(grad, axis=0, keepdims=True)
        down_sum += jnp.sum(cot_rows, axis=0, keepdims=True)
        d_rows = cot_rows + norm_back(normal, scale, grad, gain)
        d_mid[rows, :] = d_rows
        low = d_rows.astype(bf16)
        n2[rows, :] = low
        proj_sum += jnp.sum(low.astype(f32), axis=0, keepdims=True)
        for c in range(2):
            d_att[c, rows, :] = dot_nt(low, w_proj[c * HALF_COLS : (c + 1) * HALF_COLS, :]).astype(bf16)
    for c in range(2):
        g_part = dot_tn(att[c], n2[...])
        for j in range(ROW_D):
            g_proj[pl.ds(c * HALF_COLS * ROW_D + j, HALF_COLS, stride=ROW_D), :] = g_part[
                :, j * LANES : (j + 1) * LANES
            ]
    g_bias[...] = proj_sum
    store_vector(flat, 0, gain_sum)
    store_vector(flat, ROW_D, shift_sum)
    store_vector(flat, MLP_BUP, gb_up[...])
    store_vector(flat, MLP_BDOWN, down_sum)
    used = MLP_BDOWN + ROW_D
    flat[used:, :] = jnp.zeros((flat.shape[0] - used, LANES), f32)
    flatten(flat, g_slots, m_rows)


def backward_kernel(
    seq_size, a_rows,
    out_own, d_mid, d_att, g_proj, g_bias, x_own, n1, wqkv, vec, qt, kt, qh, kh, vh, bias, lse,
    out_back, grad_back, a_grads,
    flat, d_all, dt, dh, p_piece, d_piece, dk, dv, dqt, dm, d_n1, d_n1_in, g_out,
    move_sems, swap_sems, norm_sems, proj_sem,
):
    place = Place(seq_size)
    block = x_own.shape[1]
    length = seq_size * block
    greet(place.line_peers())
    sent = []
    for j in range(2):
        t = place.own_block(j)
        src = d_att.at[1 - place.core, pl.ds(j * block, block)]
        copy = remote(src, d_all.at[t], swap_sems.at[0, j], swap_sems.at[1, j], place.sibling)
        copy.start()
        sent.append(copy)
        to, micro = place.home(j)
        copy = remote(
            out_own.at[pl.ds(j * block, block)], out_back.at[micro], move_sems.at[0, j], move_sems.at[1, micro], to
        )
        copy.start()
        sent.append(copy)
    flat[...] = jnp.zeros_like(flat)
    proj_copy = pltpu.make_async_copy(g_proj, flat.at[pl.ds(ATTN_PROJ, D * ROW_D)], proj_sem)
    proj_copy.start()
    for j in range(2):
        d_all[place.own_block(j)] = d_att[place.core, j * block : (j + 1) * block, :]
    for j in range(2):
        ref = d_all.at[place.other_block(j)]
        remote(ref, ref, swap_sems.at[0, j], swap_sems.at[1, j], place.sibling).wait_recv()

    def spread(t, carry):
        rows = pl.ds(pl.multiple_of(t * block, block), block)
        piece = d_all[t]
        dt[:, rows] = piece.astype(f32).T.astype(bf16)
        for h in range(HALF_HEADS):
            dh[h, rows, :] = piece[:, h * HD : (h + 1) * HD]
        return carry

    lax.fori_loop(0, seq_size, spread, 0)

    def one_head(h, carry):
        head_rows = pl.ds(pl.multiple_of(h * HD, HD), HD)
        for i in range(seq_size):
            columns = slice(i * block, (i + 1) * block)
            query = qt[head_rows, columns]
            d_query = dt[head_rows, columns]
            level = lse[pl.ds(h, 1), columns]
            delta = jnp.zeros((1, block), f32)
            for b in range(i + 1):
                rows = slice(b * block, (b + 1) * block)
                probs = jnp.exp(dot_nn(kh[h, rows, :], query) + bias[rows, columns] - level)
                d_probs = dot_nn(vh[h, rows, :], d_query)
                delta = delta + jnp.sum(probs * d_probs, axis=0, keepdims=True)
                p_piece[rows, :] = probs
                d_piece[rows, :] = d_probs
            result = jnp.zeros((HD, block), f32)
            for b in range(i + 1):
                rows = slice(b * block, (b + 1) * block)
                probs = p_piece[rows, :]
                d_scores = (probs * (d_piece[rows, :] - delta)).astype(bf16)
                key_part = dot_nn(d_scores, qh[h, columns, :])
                value_part = dot_nn(probs.astype(bf16), dh[h, columns, :])
                if b == i:
                    dk[h, rows, :] = key_part
                    dv[h, rows, :] = value_part
                else:
                    dk[h, rows, :] += key_part
                    dv[h, rows, :] += value_part
                result = result + dot_nn(kt[head_rows, rows], d_scores)
            dqt[head_rows, columns] = result * (1.0 / math.sqrt(HD))
        return carry

    lax.fori_loop(0, HALF_HEADS, one_head, 0)

    query_sum = jnp.zeros((1, HALF_COLS), f32)
    value_sum = jnp.zeros((1, HALF_COLS), f32)
    for t in range(seq_size):
        rows = slice(t * block, (t + 1) * block)
        low = dqt[:, rows].T.astype(bf16)
        dm[0, rows, :] = low
        query_sum += jnp.sum(low.astype(f32), axis=0, keepdims=True)
        for section, part in ((1, dk), (2, dv)):
            low = jnp.concatenate([part[h, rows, :] for h in range(HALF_HEADS)], axis=1).astype(bf16)
            dm[section, rows, :] = low
        value_sum += jnp.sum(low.astype(f32), axis=0, keepdims=True)

    def to_norm(t):
        rows = pl.ds(pl.multiple_of(t * block, block), block)
        return dot_nt(dm[0, rows, :], wqkv[0]) + dot_nt(dm[1, rows, :], wqkv[1]) + dot_nt(dm[2, rows, :], wqkv[2])

    for j in range(2):
        d_n1[j] = to_norm(place.other_block(j))
        copy = remote(d_n1.at[j], d_n1_in.at[j], norm_sems.at[0, j], norm_sems.at[1, j], place.sibling)
        copy.start()
        sent.append(copy)
    proj_copy.wait()
    for section in range(3):
        part = dot_tn(n1[...], dm[section])
        for j in range(ROW_HALF):
            start = ATTN_QKV + section * ROW_D + place.core * ROW_HALF + j
            flat[pl.ds(start, D, stride=ROW_QKV), :] = part[:, j * LANES : (j + 1) * LANES]
    store_vector(flat, ATTN_BQ + place.core * ROW_HALF, query_sum)
    store_vector(flat, ATTN_BV + place.core * ROW_HALF, value_sum)
    store_vector(flat, ATTN_BPROJ, g_bias[...])
    gain = vec[0:1, :]
    gain_sum = jnp.zeros((1, D), f32)
    shift_sum = jnp.zeros((1, D), f32)
    for j in range(2):
        grad = to_norm(place.own_block(j))
        ref = d_n1_in.at[j]
        remote(ref, ref, norm_sems.at[0, j], norm_sems.at[1, j], place.sibling).wait_recv()
        grad = grad + d_n1_in[j]
        normal, scale = norm_parts(x_own[j].astype(f32))
        gain_sum += jnp.sum(grad * normal, axis=0, keepdims=True)
        shift_sum += jnp.sum(grad, axis=0, keepdims=True)
        g_out[j] = (d_mid[j * block : (j + 1) * block, :] + norm_back(normal, scale, grad, gain)).astype(bf16)
        to, micro = place.home(j)
        copy = remote(g_out.at[j], grad_back.at[micro], move_sems.at[2, j], move_sems.at[3, micro], to)
        copy.start()
        sent.append(copy)
    store_vector(flat, 0, gain_sum)
    store_vector(flat, ROW_D, shift_sum)
    flatten(flat, a_grads, a_rows)
    for micro in range(2):
        for kind, ref in ((1, out_back), (3, grad_back)):
            remote(
                ref.at[micro], ref.at[micro], move_sems.at[0, micro], move_sems.at[kind, micro], place.sibling
            ).wait_recv()
    for copy in sent:
        copy.wait_send()


class Scatter:
    def __init__(self, dp_size, seq_size, slots, out, acc, core_in, level_in, seq_in, load_sems, send_sems, recv_sems):
        self.n = seq_size
        self.bits = list(range(1, dp_size.bit_length() - 1))
        self.masks = [m << 1 for m in range(1 << len(self.bits))]
        self.dp = lax.axis_index("dp")
        self.z = lax.axis_index("seq")
        self.slots, self.out, self.acc = slots, out, acc
        self.core_in, self.level_in, self.seq_in = core_in, level_in, seq_in
        rows = slots.shape[1]
        half = rows // 32 * 16
        self.parts = [(0, half), (half, rows - half)]
        self.orders = [self.bits[::-1], self.bits]
        self.load_sems, self.send_sems, self.recv_sems = load_sems, send_sems, recv_sems
        self.started = []
        self.indices = {}

    def index(self, *key):
        return self.indices.setdefault(key, len(self.indices))

    def slot(self, mask, k):
        return (self.dp ^ mask) * self.n + lax.rem(self.z + k, self.n)

    def send(self, src, dst, to, key):
        copy = remote(src, dst, self.send_sems.at[len(self.started)], self.recv_sems.at[self.index(*key)], to)
        copy.start()
        self.started.append(copy)

    def wait(self, ref, key):
        remote(ref, ref, self.send_sems.at[0], self.recv_sems.at[self.index(*key)], (self.dp, self.z)).wait_recv()

    def turn(self):
        return list(range(1, self.n)) + [0]

    def begin(self):
        for k in self.turn():
            for mask in self.masks[::-1]:
                i = self.masks.index(mask)
                pltpu.make_async_copy(
                    self.slots.at[self.slot(mask, k)], self.acc.at[i, k], self.load_sems.at[i, k]
                ).start()
                self.send(
                    self.slots.at[self.slot(mask ^ 1, k)], self.core_in.at[i, k], (self.dp ^ 1, self.z), ("c", i, k)
                )

    def cell(self, part, level, mask):
        free = [b for b in self.bits if b not in self.orders[part][: level + 1]]
        return sum(1 << n for n, b in enumerate(free) if mask >> b & 1)

    def pass_on(self, part, level, mask, k):
        order = self.orders[part]
        i = self.masks.index(mask)
        start, size = self.parts[part]
        src = self.acc.at[i, k, pl.ds(start, size)]
        if level == len(order):
            if k:
                to = (self.dp, lax.rem(self.z + k, self.n))
                self.send(src, self.seq_in[part].at[k - 1], to, ("z", part, k))
            return
        bit = 1 << order[level]
        if mask & bit:
            rest = mask ^ bit
            dst = self.level_in[part][level].at[self.cell(part, level, rest), k]
            self.send(src, dst, (self.dp ^ bit, self.z), ("l", part, level, rest, k))

    def events(self):
        out = []
        for turn, k in enumerate(self.turn()):
            for mask in self.masks[::-1]:
                out.append((turn, ("c", mask, k)))
            for level in range(len(self.bits)):
                for part in (0, 1):
                    past = self.orders[part][: level + 1]
                    for mask in self.masks[::-1]:
                        if not any(mask >> b & 1 for b in past):
                            out.append((turn + (level + 1) * 1.0 + 0.5, ("l", part, level, mask, k)))
        out.sort(key=lambda e: e[0])
        return [e[1] for e in out]

    def step(self, event):
        if event[0] == "c":
            _, mask, k = event
            i = self.masks.index(mask)
            pltpu.make_async_copy(
                self.slots.at[self.slot(mask, k)], self.acc.at[i, k], self.load_sems.at[i, k]
            ).wait()
            self.wait(self.core_in.at[i, k], ("c", i, k))
            self.acc[i, k] = (self.acc[i, k].astype(f32) + self.core_in[i, k].astype(f32)).astype(bf16)
            for part in (0, 1):
                self.pass_on(part, 0, mask, k)
            return
        _, part, level, mask, k = event
        i = self.masks.index(mask)
        start, size = self.parts[part]
        cell = self.level_in[part][level].at[self.cell(part, level, mask), k]
        self.wait(cell, ("l", part, level, mask, k))
        rows = pl.ds(start, size)
        self.acc[i, k, rows] = (self.acc[i, k, rows].astype(f32) + cell[...].astype(f32)).astype(bf16)
        self.pass_on(part, level + 1, mask, k)

    def finish(self):
        used = self.out.shape[0]
        for part in (0, 1):
            start, size = self.parts[part]
            size = min(size, used - start)
            total = self.acc[0, 0, pl.ds(start, size)].astype(f32)
            for k in range(1, self.n):
                self.wait(self.seq_in[part].at[k - 1], ("z", part, k))
                total = total + self.seq_in[part][k - 1, :size].astype(f32)
            self.out[start : start + size, :] = total
        for copy in self.started:
            copy.wait_send()

    def peers(self):
        out = [(self.dp, lax.rem(self.z + k, self.n)) for k in range(1, self.n)]
        return out + [(self.dp ^ (1 << b), self.z) for b in [0] + self.bits]


def scatter_scratch(dp_size, seq_size, rows):
    bits = dp_size.bit_length() - 2
    masks = 1 << bits
    half = rows // 32 * 16
    sizes = [half, rows - half]
    shapes = [
        pltpu.VMEM((masks, seq_size, rows, LANES), bf16),
        pltpu.VMEM((masks, seq_size, rows, LANES), bf16),
    ]
    for size in sizes:
        for level in range(bits):
            shapes.append(pltpu.VMEM((masks >> (level + 1), seq_size, size, LANES), bf16))
    for size in sizes:
        shapes.append(pltpu.VMEM((seq_size - 1, size, LANES), bf16))
    count = masks * seq_size + 2 * (masks - 1) * seq_size + 2 * (seq_size - 1)
    shapes += [
        pltpu.SemaphoreType.DMA((masks, seq_size)),
        pltpu.SemaphoreType.DMA((count,)),
        pltpu.SemaphoreType.DMA((count,)),
    ]
    return shapes


def make_scatter(dp_size, seq_size, slots, out, refs):
    bits = dp_size.bit_length() - 2
    acc, core_in, *rest = refs
    level_in = [rest[:bits], rest[bits : 2 * bits]]
    rest = rest[2 * bits :]
    return Scatter(dp_size, seq_size, slots, out, acc, core_in, level_in, rest[:2], *rest[2:])


def scatter_kernel(dp_size, seq_size, a_slots, m_slots, a_out, m_out, *refs):
    count = len(refs) // 2
    sa = make_scatter(dp_size, seq_size, a_slots, a_out, refs[:count])
    sm = make_scatter(dp_size, seq_size, m_slots, m_out, refs[count:])
    greet(sa.peers())
    sm.begin()
    sa.begin()
    for event in sm.events():
        sm.step(event)
    for event in sa.events():
        sa.step(event)
    sm.finish()
    sa.finish()


ANY = pl.BlockSpec(memory_space=pl.ANY)
LOCAL = pl.BlockSpec(memory_space=pltpu.VMEM)


def shape_of(dims, dtype):
    return jax.ShapeDtypeStruct(dims, dtype)


def per_chip_sequence(inputs, segments, attn_params, mlp_params, cotangent):
    dp_size, n = lax.axis_size("dp"), lax.axis_size("seq")
    devices = dp_size * n
    block = inputs.shape[2]
    length = n * block
    a_rows, m_rows = attn_params.shape[0] // LANES, mlp_params.shape[0] // LANES
    a_own, m_own = to_rows(attn_params), to_rows(mlp_params)
    a_pad, m_pad = a_own.shape[0], m_own.shape[0]
    seg_rows = jnp.pad(segments.reshape(2, block // LANES, LANES), ((0, 0), (0, 8 - block // LANES), (0, 0)))
    send, recv = gather_counts(dp_size, n)
    dma = pltpu.SemaphoreType.DMA
    across = shape_of((HALF_COLS, length), bf16)
    heads = shape_of((HALF_HEADS, length, HD), bf16)
    own = shape_of((2, block, D), bf16)
    (
        m_slots, cot_own, x_own, n1, wqkv, w_proj, vec, qt, kt, vt, qh, kh, vh, bias, lse, att,
    ) = pl.pallas_call(
        functools.partial(forward_kernel, dp_size, n, a_rows),
        out_shape=[
            shape_of((devices, m_pad, LANES), bf16), own, own, shape_of((length, D), bf16),
            shape_of((3, D, HALF_COLS), bf16), shape_of((D, D), bf16), shape_of((8, D), f32),
            across, across, across, heads, heads, heads,
            shape_of((length, length), f32), shape_of((8, length), f32), shape_of((2, 2, block, HALF_COLS), bf16),
        ],
        in_specs=[ANY] * 5,
        out_specs=[ANY] * 2 + [LOCAL] * 14,
        scratch_shapes=[
            pltpu.VMEM((devices, a_pad, LANES), bf16),
            pltpu.VMEM((devices * a_rows, LANES), f32),
            pltpu.VMEM((n, block, D), bf16),
            pltpu.VMEM((n, 8, LANES), jnp.int32),
            pltpu.VMEM((length, LANES), jnp.int32),
            pltpu.VMEM((length, block), f32),
            pltpu.VMEM((HALF_COLS, length), f32),
            pltpu.VMEM((2, block, HALF_COLS), bf16),
            dma((send,)), dma((recv,)), dma((send,)), dma((recv,)), dma((2,)),
            dma((2, 4)), dma((2, n)), dma((2, 2)), dma((2, 2)),
        ],
        compiler_params=pltpu.CompilerParams(collective_id=0, has_side_effects=True, vmem_limit_bytes=VMEM_LIMIT),
    )(inputs[:, 0], seg_rows, cotangent[:, 0], a_own, m_own)

    tokens = 2 * block
    out_own, d_mid, d_att, m_grads, g_proj, g_bias = pl.pallas_call(
        functools.partial(mlp_kernel, m_rows),
        out_shape=[
            shape_of((tokens, D), bf16), shape_of((tokens, D), f32), shape_of((2, tokens, HALF_COLS), bf16),
            shape_of((devices, m_pad, LANES), bf16), shape_of((D * ROW_D, LANES), f32), shape_of((1, D), f32),
        ],
        in_specs=[ANY] + [LOCAL] * 5,
        out_specs=[LOCAL] * 6,
        scratch_shapes=[
            pltpu.VMEM((devices * m_rows, LANES), f32),
            pltpu.VMEM((D, FF), bf16), pltpu.VMEM((FF, D), bf16),
            pltpu.VMEM((tokens, D), f32), pltpu.VMEM((tokens, D), bf16),
            pltpu.VMEM((tokens, D), f32), pltpu.VMEM((tokens, D), f32),
            pltpu.VMEM((1, FF), f32), pltpu.VMEM((1, FF), f32),
            dma(()),
        ],
        compiler_params=pltpu.CompilerParams(vmem_limit_bytes=VMEM_LIMIT),
    )(m_slots, x_own.reshape(tokens, D), cot_own.reshape(tokens, D), att.reshape(2, tokens, HALF_COLS), w_proj, vec)

    out_back, grad_back, a_grads = pl.pallas_call(
        functools.partial(backward_kernel, n, a_rows),
        out_shape=[own, own, shape_of((devices, a_pad, LANES), bf16)],
        in_specs=[ANY] + [LOCAL] * 2 + [ANY] + [LOCAL] * 12,
        out_specs=[ANY] * 2 + [LOCAL],
        scratch_shapes=[
            pltpu.VMEM((devices * a_rows, LANES), f32),
            pltpu.VMEM((n, block, HALF_COLS), bf16),
            pltpu.VMEM((HALF_COLS, length), bf16),
            pltpu.VMEM((HALF_HEADS, length, HD), bf16),
            pltpu.VMEM((length, block), f32),
            pltpu.VMEM((length, block), f32),
            pltpu.VMEM((HALF_HEADS, length, HD), f32),
            pltpu.VMEM((HALF_HEADS, length, HD), f32),
            pltpu.VMEM((HALF_COLS, length), f32),
            pltpu.VMEM((3, length, HALF_COLS), bf16),
            pltpu.VMEM((2, block, D), f32),
            pltpu.VMEM((2, block, D), f32),
            pltpu.VMEM((2, block, D), bf16),
            dma((4, 2)), dma((2, 2)), dma((2, 2)), dma(()),
        ],
        compiler_params=pltpu.CompilerParams(collective_id=1, has_side_effects=True, vmem_limit_bytes=VMEM_LIMIT),
    )(out_own, d_mid, d_att, g_proj, g_bias, x_own, n1, wqkv, vec, qt, kt, qh, kh, vh, bias, lse)

    a_sum, m_sum = pl.pallas_call(
        functools.partial(scatter_kernel, dp_size, n),
        out_shape=[shape_of((a_rows, LANES), f32), shape_of((m_rows, LANES), f32)],
        in_specs=[ANY] * 2,
        out_specs=[LOCAL] * 2,
        scratch_shapes=scatter_scratch(dp_size, n, a_pad) + scatter_scratch(dp_size, n, m_pad),
        compiler_params=pltpu.CompilerParams(collective_id=2, has_side_effects=True, vmem_limit_bytes=VMEM_LIMIT),
    )(a_grads, m_grads)
    return (
        out_back[:, None],
        grad_back.astype(f32)[:, None],
        a_sum.reshape(-1),
        m_sum.reshape(-1),
    )


def solution(mesh):
    in_specs = (
        P(None, "dp", "seq", None),
        P(None, "dp", "seq"),
        P(("dp", "seq")),
        P(("dp", "seq")),
        P(None, "dp", "seq", None),
    )
    out_specs = (
        P(None, "dp", "seq", None),
        P(None, "dp", "seq", None),
        P(("dp", "seq")),
        P(("dp", "seq")),
    )
    one_each = mesh.shape["seq"] == 4 and mesh.shape["dp"] % 2 == 0
    return jax.shard_map(
        per_chip_sequence if one_each else per_device, mesh=mesh, in_specs=in_specs, out_specs=out_specs, check_vma=False
    )
```

```python
import functools
from functools import partial
import math

import jax
import jax.numpy as jnp
from jax import lax
from jax.experimental import pallas as pl
from jax.experimental.pallas import tpu as pltpu
from jax.sharding import PartitionSpec as P

D = 768
H = 12
HD = 64
FF = 3072


norm_eps = 1e-05
score_floor = -1e30
key_block = 512


def attention_layout():
    return [(D,), (D,), (D, 3 * D), (D,), (D,), (D, D), (D,)]


def mlp_layout():
    return [(D,), (D,), (D, FF), (FF,), (FF, D), (D,)]


def unpack_params(flat_vector, layout):
    offset = 0
    result = []
    for dims_entry in layout:
        amount = math.prod(dims_entry)
        result.append(lax.slice_in_dim(flat_vector, offset, offset + amount).reshape(dims_entry))
        offset += amount
    return result


def layer_norm(values, gain, shift):
    average = jnp.mean(values, axis=-1, keepdims=True)
    centred = values - average
    spread = jnp.mean(centred * centred, axis=-1, keepdims=True)
    return centred * lax.rsqrt(spread + norm_eps) * gain + shift


def gelu_tanh(values):
    return jax.nn.gelu(values, approximate=True)


def pack_grads(grad_list, total_size):
    flat_parts = [part_grad.reshape(-1) for part_grad in grad_list]
    used_total = sum((part_grad.size for part_grad in grad_list))
    flat_parts.append(jnp.zeros((total_size - used_total,), jnp.float32))
    return jnp.concatenate(flat_parts)


def fetch_params(attn_params, mlp_params):
    gathered = (
        lax.all_gather(attn_params, ("dp", "seq"), axis=0, tiled=True),
        lax.all_gather(mlp_params, ("dp", "seq"), axis=0, tiled=True),
    )
    return (
        unpack_params(gathered[0], attention_layout()),
        unpack_params(gathered[1], mlp_layout()),
    )


def send_grads(attn_list, mlp_list, attn_total, mlp_total):
    return (
        lax.psum_scatter(
            pack_grads(attn_list, attn_total), ("dp", "seq"), scatter_dimension=0, tiled=True
        ),
        lax.psum_scatter(
            pack_grads(mlp_list, mlp_total), ("dp", "seq"), scatter_dimension=0, tiled=True
        ),
    )


def fold_keys(key_rows, key_segs, fold_step, start_carry):
    return fold_step(
        start_carry,
        (
            lax.all_gather(key_rows, "seq", axis=0, tiled=True),
            lax.all_gather(key_segs, "seq", axis=0, tiled=True),
        ),
        jnp.int32(0),
    )


def over_blocks(block_step, carry_now, key_piece, key_start):
    piece_rows = key_piece[0].shape[0]
    step_rows = math.gcd(piece_rows, key_block)

    def loop_step(index_block, carry_in):
        offset = index_block * step_rows
        sub_piece = tuple(
            (lax.dynamic_slice_in_dim(member, offset, step_rows, 0) for member in key_piece)
        )
        return block_step(carry_in, sub_piece, offset)

    return lax.fori_loop(0, piece_rows // step_rows, loop_step, carry_now)


def block_scores(query_heads, query_segs, query_pos, kv_rows, key_segs, key_start):
    key_heads = kv_rows[:, :D].reshape(-1, H, HD)
    scores = jnp.einsum(
        "qhd,khd->hqk", query_heads, key_heads, preferred_element_type=jnp.float32
    ) * (1.0 / math.sqrt(HD))
    key_pos = key_start + jnp.arange(kv_rows.shape[0], dtype=jnp.int32)
    allowed = (query_segs[:, None] == key_segs[None, :]) & (key_pos[None, :] <= query_pos[:, None])
    return (jnp.where(allowed[None], scores, score_floor), key_heads)


MESH = pl.DeviceIdType.MESH
LANES = 128

def pad_rows(rows):
    return -(-rows // 16) * 16


class Gather:
    def __init__(self, dp_size, seq_size, own, slots, send_sems, recv_sems):
        self.n = seq_size
        self.bits = list(range(1, dp_size.bit_length() - 1))
        self.dp = lax.axis_index("dp")
        self.z = lax.axis_index("seq")
        self.own, self.slots = own, slots
        self.rows = own.shape[0]
        half = self.rows // 32 * 16
        self.parts = [(0, half), (half, self.rows - half)]
        self.orders = [self.bits, self.bits[::-1]]
        self.send_sems, self.recv_sems = send_sems, recv_sems
        self.started = []

    def peers(self):
        out = [(self.dp, lax.rem(self.z + k, self.n)) for k in range(1, self.n)]
        return out + [(self.dp ^ (1 << b), self.z) for b in [0] + self.bits]

    def place(self, i):
        last = self.n - 1
        high = self.z > last - self.z
        near = jnp.where(high, last - self.z, self.z)
        step = (i // 2) if i % 2 == 0 else -((i + 1) // 2)
        found = jnp.where(i <= 2 * near, near + step, i)
        return jnp.where(high, last - found, found)

    def view(self, mask, i, part):
        index = (self.dp ^ mask) * self.n + self.place(i)
        if part is None:
            return self.slots.at[index]
        start, size = self.parts[part]
        return self.slots.at[index, pl.ds(start, size)]

    def source(self, mask, i, part):
        if mask == 0 and i == 0:
            if part is None:
                return self.own
            start, size = self.parts[part]
            return self.own.at[pl.ds(start, size)]
        return self.view(mask, i, part)

    def recv_sem(self, sibling, part, mask, i):
        part = 0 if part is None else part
        count = 1 << len(self.bits)
        return self.recv_sems.at[((sibling * 2 + part) * count + (mask >> 1)) * self.n + self.place(i)]

    def send(self, mask, i, part, to, recv_sem, when=None):
        index = len(self.started)
        self.started.append((part, when))

        def start():
            pltpu.make_async_remote_copy(
                src_ref=self.source(mask, i, part), dst_ref=self.view(mask, i, part),
                send_sem=self.send_sems.at[index], recv_sem=recv_sem, device_id=to, device_id_type=MESH,
            ).start()

        if when is None:
            start()
        else:
            pl.when(when())(start)

    def wait(self, sibling, part, mask, i):
        view = self.view(mask ^ sibling, i, part)
        pltpu.make_async_remote_copy(
            src_ref=view, dst_ref=view, send_sem=self.send_sems.at[0],
            recv_sem=self.recv_sem(sibling, part, mask, i),
            device_id=(self.dp, self.z), device_id_type=MESH,
        ).wait_recv()

    def along(self, i, up):
        if i == 0:
            to = self.z + 1 if up else self.z - 1
        else:
            to = jnp.where(self.place(i) < self.z, self.z + 1, self.z - 1)

        def when():
            if i == 0:
                return (self.z < self.n - 1) if up else (self.z > 0)
            below = self.place(i) < self.z
            return (below & (self.z < self.n - 1)) | (jnp.logical_not(below) & (self.z > 0))

        self.send(0, i, None, (self.dp, to), self.recv_sem(0, None, 0, i), when)

    def forward(self, part, mask, i, seq=True):
        if mask == 0 and seq:
            self.along(i, True)
        for p in (0, 1) if part is None else (part,):
            order = self.orders[p]
            last = max([order.index(b) for b in self.bits if mask >> b & 1], default=-1)
            for b in order[last + 1 :]:
                self.send(mask, i, p, (self.dp ^ (1 << b), self.z), self.recv_sem(0, p, mask | 1 << b, i))
        self.send(mask, i, part, (self.dp ^ 1, self.z), self.recv_sem(1, part, mask, i))

    def begin_seq(self):
        self.along(0, True)
        self.along(0, False)

    def begin_bits(self):
        self.forward(None, 0, 0, False)

    def begin(self):
        self.begin_seq()
        self.begin_bits()

    def events(self):
        out = []
        for i in range(1, self.n):
            out.append((i, None, 0, i))
        for i in range(self.n):
            for level in range(len(self.bits)):
                for low in range(1 << level):
                    for p in (0, 1):
                        order = self.orders[p]
                        mask = 1 << order[level]
                        for n in range(level):
                            if low >> n & 1:
                                mask |= 1 << order[n]
                        out.append((i + level + 1, p, mask, i))
        out.sort(key=lambda e: e[0])
        return [e[1:] for e in out]

    def step(self, event):
        part, mask, i = event
        self.wait(0, part, mask, i)
        self.forward(part, mask, i)

    def finish_sibling(self):
        for part, mask, i in [(None, 0, 0)] + self.events():
            self.wait(1, part, mask, i)

    def finish_sends(self):
        for index, (part, when) in enumerate(self.started):

            def wait(index=index, part=part):
                start, size = (0, self.rows) if part is None else self.parts[part]
                view = self.slots.at[0, pl.ds(start, size)]
                pltpu.make_async_remote_copy(
                    src_ref=view, dst_ref=view, send_sem=self.send_sems.at[index], recv_sem=self.recv_sems.at[0],
                    device_id=(self.dp, self.z), device_id_type=MESH,
                ).wait_send()

            if when is None:
                wait()
            else:
                pl.when(when())(wait)


def gather_counts(dp_size, seq_size):
    bits = dp_size.bit_length() - 2
    masks = 1 << bits
    recv = 4 * masks * seq_size
    send = seq_size + 1 + seq_size * 2 * (masks - 1) + seq_size * (1 + 2 * (masks - 1))
    return send, recv


def gather_kernel(dp_size, seq_size, a_own, m_own, a_slots, m_slots, a_send, a_recv, m_send, m_recv, own_sems):
    ga = Gather(dp_size, seq_size, a_own, a_slots, a_send, a_recv)
    gm = Gather(dp_size, seq_size, m_own, m_slots, m_send, m_recv)
    barrier = pltpu.get_barrier_semaphore()
    peers = ga.peers()
    for peer in peers:
        pl.semaphore_signal(barrier, inc=1, device_id=peer, device_id_type=MESH)
    pl.semaphore_wait(barrier, len(peers))
    ca = pltpu.make_async_copy(a_own, a_slots.at[ga.dp * ga.n + ga.z], own_sems.at[0])
    cm = pltpu.make_async_copy(m_own, m_slots.at[ga.dp * ga.n + ga.z], own_sems.at[1])
    ca.start()
    cm.start()
    ga.begin()
    gm.begin()
    for e in ga.events():
        ga.step(e)
    for e in gm.events():
        gm.step(e)
    ca.wait()
    cm.wait()
    ga.finish_sibling()
    gm.finish_sibling()
    ga.finish_sends()
    gm.finish_sends()


def to_rows(flat):
    rows = flat.shape[0] // LANES
    return jnp.pad(flat.reshape(rows, LANES), ((0, pad_rows(rows) - rows), (0, 0)))


def gather_params(attn, mlp, dp_size, seq_size):
    a, m = to_rows(attn), to_rows(mlp)
    devices = dp_size * seq_size
    send, recv = gather_counts(dp_size, seq_size)
    return pl.pallas_call(
        functools.partial(gather_kernel, dp_size, seq_size),
        out_shape=[jax.ShapeDtypeStruct((devices,) + a.shape, jnp.bfloat16), jax.ShapeDtypeStruct((devices,) + m.shape, jnp.bfloat16)],
        in_specs=[pl.BlockSpec(memory_space=pl.ANY)] * 2,
        out_specs=[pl.BlockSpec(memory_space=pl.ANY)] * 2,
        scratch_shapes=[pltpu.SemaphoreType.DMA((send,)), pltpu.SemaphoreType.DMA((recv,)),
                        pltpu.SemaphoreType.DMA((send,)), pltpu.SemaphoreType.DMA((recv,)), pltpu.SemaphoreType.DMA((2,))],
        compiler_params=pltpu.CompilerParams(collective_id=0, has_side_effects=True),
    )(a, m)


def per_device(inputs, segments, attn_params, mlp_params, cotangent):
    micro_count = inputs.shape[0]
    local_rows = inputs.shape[2]
    seq_length = local_rows * lax.axis_size("seq")
    attn_total = attn_params.shape[0] * lax.axis_size(("dp", "seq"))
    mlp_total = mlp_params.shape[0] * lax.axis_size(("dp", "seq"))
    query_pos = lax.axis_index("seq") * local_rows + jnp.arange(local_rows, dtype=jnp.int32)
    score_scale = 1.0 / math.sqrt(HD)
    out_rows = []
    grad_rows = []
    attn_sums = None
    mlp_sums = None
    shard_sums = None
    attn_slots, mlp_slots = gather_params(attn_params, mlp_params, lax.axis_size("dp"), lax.axis_size("seq"))
    attn_set = unpack_params(
        attn_slots[:, : attn_params.shape[0] // LANES].reshape(-1), attention_layout()
    )
    mlp_set = unpack_params(
        mlp_slots[:, : mlp_params.shape[0] // LANES].reshape(-1), mlp_layout()
    )
    for micro_index in range(micro_count):
        gain_one, shift_one, w_qkv, bias_query, bias_value, w_proj, bias_proj = attn_set
        gain_two, shift_two, w_up, bias_up, w_down, bias_down = mlp_set
        input_rows = inputs[micro_index, 0].astype(jnp.float32)
        query_segs = segments[micro_index, 0]
        normed_one, norm_one_back = jax.vjp(
            layer_norm, input_rows, gain_one.astype(jnp.float32), shift_one.astype(jnp.float32)
        )
        normed_one_low = normed_one.astype(jnp.bfloat16)
        merged_rows = jnp.dot(normed_one_low, w_qkv, preferred_element_type=jnp.float32)
        query_low = (merged_rows[:, :D] + bias_query.astype(jnp.float32)).astype(jnp.bfloat16)
        kv_local = jnp.concatenate(
            [merged_rows[:, D : 2 * D], merged_rows[:, 2 * D :] + bias_value.astype(jnp.float32)],
            axis=1,
        ).astype(jnp.bfloat16)
        query_heads = query_low.reshape(local_rows, H, HD)

        def max_step(carry_in, sub_piece, key_start):
            scores, key_heads = block_scores(
                query_heads, query_segs, query_pos, sub_piece[0], sub_piece[1], key_start
            )
            running_top, running_total = carry_in
            new_top = jnp.maximum(running_top, jnp.max(scores, axis=-1))
            new_total = running_total * jnp.exp(running_top - new_top) + jnp.sum(
                jnp.exp(scores - new_top[..., None]), axis=-1
            )
            return (new_top, new_total)

        top_start = jnp.full((H, local_rows), score_floor, jnp.float32)
        row_top, row_total = fold_keys(
            kv_local,
            query_segs,
            partial(over_blocks, max_step),
            (top_start, jnp.zeros((H, local_rows), jnp.float32)),
        )
        log_total = row_top + jnp.log(row_total)

        def value_step(carry_in, sub_piece, key_start):
            scores, key_heads = block_scores(
                query_heads, query_segs, query_pos, sub_piece[0], sub_piece[1], key_start
            )
            probs = jnp.exp(scores - log_total[..., None])
            probs_low = probs.astype(jnp.bfloat16)
            probs_rest = (probs - probs_low.astype(jnp.float32)).astype(jnp.bfloat16)
            value_heads = sub_piece[0][:, D:].reshape(-1, H, HD)
            main_part, rest_part = carry_in
            main_part = main_part + jnp.einsum(
                "hqk,khd->qhd", probs_low, value_heads, preferred_element_type=jnp.float32
            )
            rest_part = rest_part + jnp.einsum(
                "hqk,khd->qhd", probs_rest, value_heads, preferred_element_type=jnp.float32
            )
            return (main_part, rest_part)

        zero_heads = jnp.zeros((local_rows, H, HD), jnp.float32)
        main_sum, rest_sum = fold_keys(
            kv_local, query_segs, partial(over_blocks, value_step), (zero_heads, zero_heads)
        )
        attended_low = main_sum.reshape(local_rows, D).astype(jnp.bfloat16)
        attended_full = main_sum + rest_sum
        middle = (
            input_rows
            + jnp.dot(attended_low, w_proj, preferred_element_type=jnp.float32)
            + bias_proj.astype(jnp.float32)
        )
        normed_two, norm_two_back = jax.vjp(
            layer_norm, middle, gain_two.astype(jnp.float32), shift_two.astype(jnp.float32)
        )
        normed_two_low = normed_two.astype(jnp.bfloat16)
        hidden = jnp.dot(normed_two_low, w_up, preferred_element_type=jnp.float32) + bias_up.astype(
            jnp.float32
        )
        active, gelu_back = jax.vjp(gelu_tanh, hidden)
        active_low = active.astype(jnp.bfloat16)
        result = (
            middle
            + jnp.dot(active_low, w_down, preferred_element_type=jnp.float32)
            + bias_down.astype(jnp.float32)
        )
        out_rows.append(result.astype(jnp.bfloat16))
        w_qkv, w_proj = (attn_set[2], attn_set[5])
        w_up, w_down = (mlp_set[2], mlp_set[4])
        cot_low = cotangent[micro_index, 0]
        cot_rows = cot_low.astype(jnp.float32)
        grad_w_down = jnp.einsum(
            "rf,rd->fd", active_low, cot_low, preferred_element_type=jnp.float32
        )
        grad_b_down = jnp.sum(cot_rows, axis=0)
        grad_active = jnp.einsum("rd,fd->rf", cot_low, w_down, preferred_element_type=jnp.float32)
        grad_hidden = gelu_back(grad_active)[0].astype(jnp.bfloat16)
        grad_w_up = jnp.einsum(
            "rd,rf->df", normed_two_low, grad_hidden, preferred_element_type=jnp.float32
        )
        grad_b_up = jnp.sum(grad_hidden.astype(jnp.float32), axis=0)
        grad_normed_two = jnp.einsum(
            "rf,df->rd", grad_hidden, w_up, preferred_element_type=jnp.float32
        )
        grad_middle_norm, grad_gain_two, grad_shift_two = norm_two_back(grad_normed_two)
        grad_middle = cot_rows + grad_middle_norm
        grad_branch = grad_middle.astype(jnp.bfloat16)
        grad_w_proj = jnp.einsum(
            "rd,re->de", attended_low, grad_branch, preferred_element_type=jnp.float32
        )
        grad_b_proj = jnp.sum(grad_branch.astype(jnp.float32), axis=0)
        grad_attended = jnp.einsum(
            "re,de->rd", grad_branch, w_proj, preferred_element_type=jnp.float32
        ).astype(jnp.bfloat16)
        grad_heads = grad_attended.reshape(local_rows, H, HD)
        row_delta = jnp.einsum("qhd,qhd->hq", grad_heads.astype(jnp.float32), attended_full)

        def grad_step(carry_in, sub_piece, key_start):
            scores, key_heads = block_scores(
                query_heads, query_segs, query_pos, sub_piece[0], sub_piece[1], key_start
            )
            value_heads = sub_piece[0][:, D:].reshape(-1, H, HD)
            probs = jnp.exp(scores - log_total[..., None])
            grad_probs = jnp.einsum(
                "qhd,khd->hqk", grad_heads, value_heads, preferred_element_type=jnp.float32
            )
            grad_scores = (probs * (grad_probs - row_delta[..., None])).astype(jnp.bfloat16)
            query_part, kv_part = carry_in
            query_part = (
                query_part
                + jnp.einsum(
                    "hqk,khd->qhd", grad_scores, key_heads, preferred_element_type=jnp.float32
                )
                * score_scale
            )
            key_grad = (
                jnp.einsum(
                    "hqk,qhd->khd", grad_scores, query_heads, preferred_element_type=jnp.float32
                )
                * score_scale
            )
            value_grad = jnp.einsum(
                "hqk,qhd->khd",
                probs.astype(jnp.bfloat16),
                grad_heads,
                preferred_element_type=jnp.float32,
            )
            block_grads = jnp.concatenate(
                [key_grad.reshape(-1, D), value_grad.reshape(-1, D)], axis=1
            )
            kv_part = lax.dynamic_update_slice_in_dim(kv_part, block_grads, key_start, 0)
            return (query_part, kv_part)

        query_sum, kv_sums = fold_keys(
            kv_local,
            query_segs,
            partial(over_blocks, grad_step),
            (zero_heads, jnp.zeros((seq_length, 2 * D), jnp.float32)),
        )
        kv_grads = lax.psum_scatter(
            kv_sums.astype(jnp.bfloat16), "seq", scatter_dimension=0, tiled=True
        ).astype(jnp.float32)
        grad_merged = jnp.concatenate([query_sum.reshape(local_rows, D), kv_grads], axis=1).astype(
            jnp.bfloat16
        )
        grad_merged_wide = grad_merged.astype(jnp.float32)
        grad_w_qkv = jnp.einsum(
            "rd,re->de", normed_one_low, grad_merged, preferred_element_type=jnp.float32
        )
        grad_b_query = jnp.sum(grad_merged_wide[:, :D], axis=0)
        grad_b_value = jnp.sum(grad_merged_wide[:, 2 * D :], axis=0)
        grad_normed_one = jnp.einsum(
            "re,de->rd", grad_merged, w_qkv, preferred_element_type=jnp.float32
        )
        grad_input_norm, grad_gain_one, grad_shift_one = norm_one_back(grad_normed_one)
        grad_rows.append(grad_middle + grad_input_norm)
        attn_list = [
            grad_gain_one,
            grad_shift_one,
            grad_w_qkv,
            grad_b_query,
            grad_b_value,
            grad_w_proj,
            grad_b_proj,
        ]
        mlp_list = [grad_gain_two, grad_shift_two, grad_w_up, grad_b_up, grad_w_down, grad_b_down]
        attn_sums = (
            attn_list
            if attn_sums is None
            else [left_sum + right_sum for left_sum, right_sum in zip(attn_sums, attn_list)]
        )
        mlp_sums = (
            mlp_list
            if mlp_sums is None
            else [left_sum + right_sum for left_sum, right_sum in zip(mlp_sums, mlp_list)]
        )
    shard_sums = send_grads(attn_sums, mlp_sums, attn_total, mlp_total)
    outputs = jnp.stack(out_rows)[:, None]
    input_grad = jnp.stack(grad_rows)[:, None]
    return (outputs, input_grad, shard_sums[0], shard_sums[1])


HALF_HEADS = H // 2
HALF_COLS = D // 2
ROW_D = D // LANES
ROW_FF = FF // LANES
ROW_QKV = 3 * ROW_D
ROW_HALF = HALF_COLS // LANES
FF_STEP = 512
VMEM_LIMIT = 63 * 2**20
A_FIRST = 7
PUMP = (4, 3, 3)

ATTN_QKV = 2 * ROW_D
ATTN_BQ = ATTN_QKV + D * ROW_QKV
ATTN_BV = ATTN_BQ + ROW_D
ATTN_PROJ = ATTN_BV + ROW_D
ATTN_BPROJ = ATTN_PROJ + D * ROW_D
MLP_UP = 2 * ROW_D
MLP_BUP = MLP_UP + D * ROW_FF
MLP_DOWN = MLP_BUP + ROW_FF
MLP_BDOWN = MLP_DOWN + FF * ROW_D

f32 = jnp.float32
bf16 = jnp.bfloat16


def dot_nn(left, right):
    return jnp.dot(left, right, preferred_element_type=f32)


def dot_nt(left, right):
    return lax.dot_general(left, right, (((1,), (1,)), ((), ())), preferred_element_type=f32)


def dot_tn(left, right):
    return lax.dot_general(left, right, (((0,), (0,)), ((), ())), preferred_element_type=f32)


def remote(src, dst, send_sem, recv_sem, to):
    return pltpu.make_async_remote_copy(
        src_ref=src, dst_ref=dst, send_sem=send_sem, recv_sem=recv_sem, device_id=to, device_id_type=MESH
    )


class Place:
    def __init__(self, seq_size):
        self.n = seq_size
        self.dp = lax.axis_index("dp")
        self.z = lax.axis_index("seq")
        self.core = lax.rem(self.dp, 2)
        self.base = self.dp - self.core
        self.sibling = (self.base + 1 - self.core, self.z)

    def line_peers(self):
        out = [self.sibling]
        for k in range(1, self.n):
            other = lax.rem(self.z + k, self.n)
            out += [(self.base, other), (self.base + 1, other)]
        return out

    def own_block(self, j):
        return 1 - self.core + 2 * j

    def other_block(self, j):
        return self.core + 2 * j

    def worker(self, micro):
        return (self.base + 1 - lax.rem(self.z, 2), 2 * micro + self.core)

    def home(self, j):
        return (self.base + lax.rem(self.z, 2), self.own_block(j)), self.z // 2


def greet(peers):
    barrier = pltpu.get_barrier_semaphore()
    for peer in peers:
        pl.semaphore_signal(barrier, inc=1, device_id=peer, device_id_type=MESH)
    pl.semaphore_wait(barrier, len(peers))


def unflatten(slots, flat, rows):
    def body(s, carry):
        flat[pl.ds(s * rows, rows), :] = slots[s, :rows, :].astype(f32)
        return carry

    lax.fori_loop(0, slots.shape[0], body, 0)


def flatten(flat, slots, rows):
    def body(s, carry):
        slots[s, :rows, :] = flat[pl.ds(s * rows, rows), :].astype(bf16)
        return carry

    lax.fori_loop(0, slots.shape[0], body, 0)


def load_matrix(flat, start, stride, columns, out, step):
    def body(i, carry):
        rows = pl.ds(pl.multiple_of(i * step, step), step)
        for j in range(columns):
            piece = flat[pl.ds(start + j + i * (step * stride), step, stride=stride), :]
            out[rows, j * LANES : (j + 1) * LANES] = piece.astype(bf16)
        return carry

    lax.fori_loop(0, out.shape[0] // step, body, 0)


def load_vector(flat, start, blocks):
    return jnp.concatenate([flat[pl.ds(start + j, 1), :] for j in range(blocks)], axis=1)


def store_vector(flat, start, value):
    for j in range(value.shape[1] // LANES):
        flat[pl.ds(start + j, 1), :] = value[:, j * LANES : (j + 1) * LANES]


def norm_parts(values):
    average = jnp.mean(values, axis=-1, keepdims=True)
    centred = values - average
    spread = jnp.mean(centred * centred, axis=-1, keepdims=True)
    scale = lax.rsqrt(spread + norm_eps)
    return centred * scale, scale


def norm_back(normal, scale, grad, gain):
    scaled = grad * gain
    return scale * (
        scaled
        - jnp.mean(scaled, axis=-1, keepdims=True)
        - normal * jnp.mean(scaled * normal, axis=-1, keepdims=True)
    )


def keep_allowed(scores, seg_col, seg_all, b, i, block):
    parts = []
    for r in range(block // LANES):
        row = seg_all[i, r : r + 1, :]
        allowed = seg_col[b * block : (b + 1) * block, :] == row
        if b == i:
            key_pos = lax.broadcasted_iota(jnp.int32, (block, LANES), 0)
            query_pos = lax.broadcasted_iota(jnp.int32, (block, LANES), 1) + r * LANES
            allowed = allowed & (key_pos <= query_pos)
        parts.append(jnp.where(allowed, scores[:, r * LANES : (r + 1) * LANES], score_floor))
    return jnp.concatenate(parts, axis=1)


def segment_columns(seg_all, seg_col, block):
    for t in range(seg_all.shape[0]):
        for r in range(block // LANES):
            row = jnp.broadcast_to(seg_all[t, r : r + 1, :], (LANES, LANES))
            seg_col[pl.ds(t * block + r * LANES, LANES), :] = row.T


def forward_kernel(
    dp_size, seq_size, a_rows,
    x_in, seg_in, cot_in, a_own, m_own,
    m_slots, cot_own, x_own, n1, wqkv, w_proj, vec, qt, kt, qh, kh, vh, seg_all, lse, att,
    a_slots, flat, x_all, vt, seg_col, scores, ot, att_out,
    a_send, a_recv, m_send, m_recv, own_sems, move_send, move_recv, cot_sems, swap_sems,
):
    place = Place(seq_size)
    block = x_in.shape[1]
    ga = Gather(dp_size, seq_size, a_own, a_slots, a_send, a_recv)
    gm = Gather(dp_size, seq_size, m_own, m_slots, m_send, m_recv)
    greet(place.line_peers() + [(place.dp ^ (1 << b), place.z) for b in ga.bits])

    mine = place.dp * seq_size + place.z
    own_copies = [
        pltpu.make_async_copy(a_own, a_slots.at[mine], own_sems.at[0]),
        pltpu.make_async_copy(m_own, m_slots.at[mine], own_sems.at[1]),
    ]
    ga.begin()
    sent = []
    for micro in range(2):
        to = place.worker(micro)
        sent.append(
            remote(seg_in.at[micro], seg_all.at[place.z], move_send.at[1, micro], move_recv.at[1, place.z], to)
        )
        sent.append(
            remote(x_in.at[micro], x_all.at[place.z], move_send.at[0, micro], move_recv.at[0, place.z], to)
        )
    for copy in sent:
        copy.start()
    gm.begin_bits()
    for copy in own_copies:
        copy.start()

    def arrival(t, kind):
        ref = (x_all, seg_all)[kind].at[t]
        return remote(ref, ref, move_send.at[kind, 0], move_recv.at[kind, t], place.sibling)

    events = ga.events()
    for event in events[:A_FIRST]:
        ga.step(event)
    gm.begin_seq()
    for event in events[A_FIRST:]:
        ga.step(event)
    for j in range(2):
        t = place.own_block(j)
        for kind in range(2):
            ref = (x_all, seg_all)[kind].at[t]
            arrival(t, kind).wait_recv()
            copy = remote(ref, ref, move_send.at[kind, 2 + j], move_recv.at[kind, t], place.sibling)
            copy.start()
            sent.append(copy)
    for micro in range(2):
        copy = remote(
            cot_in.at[micro], cot_own.at[place.z // 2], cot_sems.at[0, micro], cot_sems.at[1, place.z // 2],
            place.worker(micro),
        )
        copy.start()
        sent.append(copy)

    m_events = gm.events()
    pumped = [0]

    def pump(count):
        for event in m_events[pumped[0] : pumped[0] + count]:
            gm.step(event)
        pumped[0] += count

    pump(PUMP[0])
    own_copies[0].wait()
    ga.finish_sibling()
    unflatten(a_slots, flat, a_rows)
    pump(PUMP[1])
    for section in range(3):
        load_matrix(
            flat, ATTN_QKV + section * ROW_D + place.core * ROW_HALF, ROW_QKV, ROW_HALF, wqkv.at[section], LANES
        )
    load_matrix(flat, ATTN_PROJ, ROW_D, ROW_D, w_proj, LANES)
    gain = load_vector(flat, 0, ROW_D)
    shift = load_vector(flat, ROW_D, ROW_D)
    vec[...] = jnp.zeros_like(vec)
    vec[0:1, :] = gain
    vec[1:2, :] = load_vector(flat, ATTN_BPROJ, ROW_D)
    bias_query = load_vector(flat, ATTN_BQ + place.core * ROW_HALF, ROW_HALF)
    bias_value = load_vector(flat, ATTN_BV + place.core * ROW_HALF, ROW_HALF)
    pump(PUMP[2])
    for j in range(2):
        for kind in range(2):
            arrival(place.other_block(j), kind).wait_recv()
        x_own[j] = x_all[place.own_block(j)]
    segment_columns(seg_all, seg_col, block)

    def project(t, carry):
        rows = pl.ds(pl.multiple_of(t * block, block), block)
        normal, _ = norm_parts(x_all[t].astype(f32))
        low = (normal * gain + shift).astype(bf16)
        n1[rows, :] = low
        query = (dot_nn(low, wqkv[0]) + bias_query).astype(bf16).astype(f32) * (1.0 / math.sqrt(HD))
        key = dot_nn(low, wqkv[1])
        value = dot_nn(low, wqkv[2]) + bias_value
        for result, across, heads in ((query, qt, qh), (key, kt, kh), (value, vt, vh)):
            across[:, rows] = result.T.astype(bf16)
            rounded = result.astype(bf16)
            for h in range(HALF_HEADS):
                heads[h, rows, :] = rounded[:, h * HD : (h + 1) * HD]
        return carry

    lax.fori_loop(0, seq_size, project, 0)
    lse[...] = jnp.zeros_like(lse)

    rest = len(m_events) - pumped[0]
    per_head = -(-rest // HALF_HEADS)

    def one_head(h, carry):
        for c in range(HALF_HEADS):

            @pl.when(h == c)
            def _():
                pump(per_head)

        head_rows = pl.ds(pl.multiple_of(h * HD, HD), HD)
        for i in range(seq_size):
            columns = slice(i * block, (i + 1) * block)
            query = qt[head_rows, columns]
            top = jnp.full((1, block), -jnp.inf, f32)
            for b in range(i + 1):
                rows = slice(b * block, (b + 1) * block)
                piece = keep_allowed(dot_nn(kh[h, rows, :], query), seg_col, seg_all, b, i, block)
                scores[rows, :] = piece
                top = jnp.maximum(top, jnp.max(piece, axis=0, keepdims=True))
            total = jnp.zeros((1, block), f32)
            for b in range(i + 1):
                rows = slice(b * block, (b + 1) * block)
                piece = jnp.exp(scores[rows, :] - top)
                scores[rows, :] = piece
                total = total + jnp.sum(piece, axis=0, keepdims=True)
            inverse = 1.0 / total
            result = jnp.zeros((HD, block), f32)
            for b in range(i + 1):
                rows = slice(b * block, (b + 1) * block)
                result = result + dot_nn(vt[head_rows, rows], (scores[rows, :] * inverse).astype(bf16))
            ot[head_rows, columns] = result
            lse[pl.ds(h, 1), columns] = top + jnp.log(total)
        return carry

    lax.fori_loop(0, HALF_HEADS, one_head, 0)

    for j in range(2):
        columns = pl.ds(pl.multiple_of(place.other_block(j) * block, block), block)
        att_out[j] = ot[:, columns].T.astype(bf16)
        copy = remote(
            att_out.at[j], att.at[place.core, j], swap_sems.at[0, j], swap_sems.at[1, j], place.sibling
        )
        copy.start()
        sent.append(copy)
    for j in range(2):
        columns = pl.ds(pl.multiple_of(place.own_block(j) * block, block), block)
        att[place.core, j] = ot[:, columns].T.astype(bf16)
    for j in range(2):
        ref = att.at[1 - place.core, j]
        remote(ref, ref, swap_sems.at[0, j], swap_sems.at[1, j], place.sibling).wait_recv()
        ref = cot_own.at[j]
        remote(ref, ref, cot_sems.at[0, j], cot_sems.at[1, j], place.sibling).wait_recv()
    own_copies[1].wait()
    gm.finish_sibling()
    for copy in sent:
        copy.wait_send()
    ga.finish_sends()
    gm.finish_sends()


def mlp_kernel(
    m_rows,
    m_slots, x_own, cot, att, w_proj, vec,
    out, d_mid, d_att, g_slots, g_proj, g_bias,
    flat, w_up, w_down, mid, n2, d_n2, total, b_up, gb_up, sem,
):
    rows_all = x_own.shape[0]
    half = rows_all // 2
    copy = pltpu.make_async_copy(m_slots, g_slots, sem)
    copy.start()
    blocks = [slice(0, half), slice(half, rows_all)]
    for rows in blocks:
        mid[rows, :] = (
            x_own[rows, :].astype(f32)
            + dot_nn(att[0, rows, :], w_proj[:HALF_COLS, :])
            + dot_nn(att[1, rows, :], w_proj[HALF_COLS:, :])
            + vec[1:2, :]
        )
    copy.wait()
    unflatten(g_slots, flat, m_rows)
    load_matrix(flat, MLP_UP, ROW_FF, ROW_FF, w_up, 64)
    load_matrix(flat, MLP_DOWN, ROW_D, ROW_D, w_down, LANES)
    gain = load_vector(flat, 0, ROW_D)
    shift = load_vector(flat, ROW_D, ROW_D)
    b_down = load_vector(flat, MLP_BDOWN, ROW_D)
    b_up[...] = load_vector(flat, MLP_BUP, ROW_FF)
    for rows in blocks:
        normal, _ = norm_parts(mid[rows, :])
        n2[rows, :] = (normal * gain + shift).astype(bf16)
    total[...] = jnp.zeros_like(total)
    d_n2[...] = jnp.zeros_like(d_n2)
    inner = math.sqrt(2.0 / math.pi)

    def step(f, carry):
        start = pl.multiple_of(f * FF_STEP, FF_STEP)
        columns = pl.ds(start, FF_STEP)
        hidden = dot_nn(n2[...], w_up[:, columns]) + b_up[:, columns]
        square = hidden * hidden
        tanh = jnp.tanh(inner * (hidden + 0.044715 * (square * hidden)))
        cdf = 0.5 * (1.0 + tanh)
        active = (hidden * cdf).astype(bf16)
        slope = cdf + (0.5 * inner) * hidden * (1.0 - tanh * tanh) * (1.0 + (3 * 0.044715) * square)
        d_hidden = dot_nt(cot[...], w_down[columns, :]) * slope
        low = d_hidden.astype(bf16)
        gb_up[:, columns] = jnp.sum(low.astype(f32), axis=0, keepdims=True)
        total[...] += dot_nn(active, w_down[columns, :])
        d_n2[...] += dot_nt(low, w_up[:, columns])
        g_down = dot_tn(active, cot[...])
        for j in range(ROW_D):
            flat[pl.ds(MLP_DOWN + j + f * (FF_STEP * ROW_D), FF_STEP, stride=ROW_D), :] = g_down[
                :, j * LANES : (j + 1) * LANES
            ]
        g_up = dot_tn(n2[...], low)
        for j in range(FF_STEP // LANES):
            flat[pl.ds(MLP_UP + j + f * (FF_STEP // LANES), D, stride=ROW_FF), :] = g_up[
                :, j * LANES : (j + 1) * LANES
            ]
        return carry

    lax.fori_loop(0, FF // FF_STEP, step, 0)

    gain_sum = jnp.zeros((1, D), f32)
    shift_sum = jnp.zeros((1, D), f32)
    down_sum = jnp.zeros((1, D), f32)
    proj_sum = jnp.zeros((1, D), f32)
    for rows in blocks:
        out[rows, :] = (mid[rows, :] + total[rows, :] + b_down).astype(bf16)
        normal, scale = norm_parts(mid[rows, :])
        grad = d_n2[rows, :]
        cot_rows = cot[rows, :].astype(f32)
        gain_sum += jnp.sum(grad * normal, axis=0, keepdims=True)
        shift_sum += jnp.sum(grad, axis=0, keepdims=True)
        down_sum += jnp.sum(cot_rows, axis=0, keepdims=True)
        d_rows = cot_rows + norm_back(normal, scale, grad, gain)
        d_mid[rows, :] = d_rows
        low = d_rows.astype(bf16)
        n2[rows, :] = low
        proj_sum += jnp.sum(low.astype(f32), axis=0, keepdims=True)
        for c in range(2):
            d_att[c, rows, :] = dot_nt(low, w_proj[c * HALF_COLS : (c + 1) * HALF_COLS, :]).astype(bf16)
    for c in range(2):
        g_part = dot_tn(att[c], n2[...])
        for j in range(ROW_D):
            g_proj[pl.ds(c * HALF_COLS * ROW_D + j, HALF_COLS, stride=ROW_D), :] = g_part[
                :, j * LANES : (j + 1) * LANES
            ]
    g_bias[...] = proj_sum
    store_vector(flat, 0, gain_sum)
    store_vector(flat, ROW_D, shift_sum)
    store_vector(flat, MLP_BUP, gb_up[...])
    store_vector(flat, MLP_BDOWN, down_sum)
    used = MLP_BDOWN + ROW_D
    flat[used:, :] = jnp.zeros((flat.shape[0] - used, LANES), f32)
    flatten(flat, g_slots, m_rows)


def backward_kernel(
    dp_size, seq_size, a_rows,
    out_own, m_grads, d_mid, d_att, g_proj, g_bias, x_own, n1, wqkv, vec, qt, kt, qh, kh, vh, seg_all, lse,
    out_back, grad_back, a_out, m_out,
    flat, d_all, dt, dh, seg_col, p_piece, d_piece, dk, dv, dqt, dm, d_n1, d_n1_in, g_out, core_out,
    move_sems, swap_sems, norm_sems, proj_sem, *refs,
):
    place = Place(seq_size)
    block = x_own.shape[1]
    count = len(refs) // 2
    sm = make_scatter(dp_size, seq_size, m_out, refs[:count])
    sa = make_scatter(dp_size, seq_size, a_out, refs[count:])
    greet(place.line_peers() + [(place.dp ^ (1 << b), place.z) for b in sm.bits])
    sent = []
    for j in range(2):
        t = place.own_block(j)
        src = d_att.at[1 - place.core, pl.ds(j * block, block)]
        copy = remote(src, d_all.at[t], swap_sems.at[0, j], swap_sems.at[1, j], place.sibling)
        copy.start()
        sent.append(copy)
    sm.begin(m_grads)
    for j in range(2):
        to, micro = place.home(j)
        copy = remote(
            out_own.at[pl.ds(j * block, block)], out_back.at[micro], move_sems.at[0, j], move_sems.at[1, micro], to
        )
        copy.start()
        sent.append(copy)
    flat[...] = jnp.zeros_like(flat)
    proj_copy = pltpu.make_async_copy(g_proj, flat.at[pl.ds(ATTN_PROJ, D * ROW_D)], proj_sem)
    proj_copy.start()
    for j in range(2):
        d_all[place.own_block(j)] = d_att[place.core, j * block : (j + 1) * block, :]
    segment_columns(seg_all, seg_col, block)
    for j in range(2):
        ref = d_all.at[place.other_block(j)]
        remote(ref, ref, swap_sems.at[0, j], swap_sems.at[1, j], place.sibling).wait_recv()

    def spread(t, carry):
        rows = pl.ds(pl.multiple_of(t * block, block), block)
        piece = d_all[t]
        dt[:, rows] = piece.astype(f32).T.astype(bf16)
        for h in range(HALF_HEADS):
            dh[h, rows, :] = piece[:, h * HD : (h + 1) * HD]
        return carry

    lax.fori_loop(0, seq_size, spread, 0)

    m_events = sm.events()
    first = len(m_events) - len([e for e in m_events if e[0] != "c"])
    pumped = [0]

    def pump(count):
        for event in m_events[pumped[0] : pumped[0] + count]:
            sm.step(event)
        pumped[0] += count

    pump(first)
    per_head = -(-(len(m_events) - first) // HALF_HEADS)

    def one_pair(pair, carry):
        for side in range(2):
            for c in range(HALF_HEADS // 2):

                @pl.when(pair == c)
                def _():
                    begin = first + (2 * c + side) * per_head
                    for event in m_events[begin : begin + per_head]:
                        sm.step(event)

            h = 2 * pair + side
            head_rows = pl.ds(pl.multiple_of(h * HD, HD), HD)
            for i in range(seq_size):
                columns = slice(i * block, (i + 1) * block)
                query = qt[head_rows, columns]
                d_query = dt[head_rows, columns]
                level = lse[pl.ds(h, 1), columns]
                delta = jnp.zeros((1, block), f32)
                for b in range(i + 1):
                    rows = slice(b * block, (b + 1) * block)
                    probs = jnp.exp(
                        keep_allowed(dot_nn(kh[h, rows, :], query), seg_col, seg_all, b, i, block) - level
                    )
                    d_probs = dot_nn(vh[h, rows, :], d_query)
                    delta = delta + jnp.sum(probs * d_probs, axis=0, keepdims=True)
                    p_piece[rows, :] = probs
                    d_piece[rows, :] = d_probs
                result = jnp.zeros((HD, block), f32)
                for b in range(i + 1):
                    rows = slice(b * block, (b + 1) * block)
                    probs = p_piece[rows, :]
                    d_scores = (probs * (d_piece[rows, :] - delta)).astype(bf16)
                    key_part = dot_nn(d_scores, qh[h, columns, :])
                    value_part = dot_nn(probs.astype(bf16), dh[h, columns, :])
                    if b == i:
                        dk[side, rows, :] = key_part
                        dv[side, rows, :] = value_part
                    else:
                        dk[side, rows, :] += key_part
                        dv[side, rows, :] += value_part
                    result = result + dot_nn(kt[head_rows, rows], d_scores)
                dqt[head_rows, columns] = result * (1.0 / math.sqrt(HD))
        lanes = pl.ds(pl.multiple_of(pair * LANES, LANES), LANES)
        for section, part in ((1, dk), (2, dv)):
            dm[section, :, lanes] = jnp.concatenate([part[0], part[1]], axis=1).astype(bf16)
        return carry

    lax.fori_loop(0, HALF_HEADS // 2, one_pair, 0)
    pumped[0] = len(m_events)

    query_sum = jnp.zeros((1, HALF_COLS), f32)
    value_sum = jnp.zeros((1, HALF_COLS), f32)
    for t in range(seq_size):
        rows = slice(t * block, (t + 1) * block)
        low = dqt[:, rows].T.astype(bf16)
        dm[0, rows, :] = low
        query_sum += jnp.sum(low.astype(f32), axis=0, keepdims=True)
        value_sum += jnp.sum(dm[2, rows, :].astype(f32), axis=0, keepdims=True)

    def to_norm(t):
        rows = pl.ds(pl.multiple_of(t * block, block), block)
        return dot_nt(dm[0, rows, :], wqkv[0]) + dot_nt(dm[1, rows, :], wqkv[1]) + dot_nt(dm[2, rows, :], wqkv[2])

    for j in range(2):
        d_n1[j] = to_norm(place.other_block(j))
        copy = remote(d_n1.at[j], d_n1_in.at[j], norm_sems.at[0, j], norm_sems.at[1, j], place.sibling)
        copy.start()
        sent.append(copy)
    proj_copy.wait()
    for section in range(3):
        part = dot_tn(n1[...], dm[section])
        for j in range(ROW_HALF):
            start = ATTN_QKV + section * ROW_D + place.core * ROW_HALF + j
            flat[pl.ds(start, D, stride=ROW_QKV), :] = part[:, j * LANES : (j + 1) * LANES]
    store_vector(flat, ATTN_BQ + place.core * ROW_HALF, query_sum)
    store_vector(flat, ATTN_BV + place.core * ROW_HALF, value_sum)
    store_vector(flat, ATTN_BPROJ, g_bias[...])
    gain = vec[0:1, :]
    gain_sum = jnp.zeros((1, D), f32)
    shift_sum = jnp.zeros((1, D), f32)
    for j in range(2):
        grad = to_norm(place.own_block(j))
        ref = d_n1_in.at[j]
        remote(ref, ref, norm_sems.at[0, j], norm_sems.at[1, j], place.sibling).wait_recv()
        grad = grad + d_n1_in[j]
        normal, scale = norm_parts(x_own[j].astype(f32))
        gain_sum += jnp.sum(grad * normal, axis=0, keepdims=True)
        shift_sum += jnp.sum(grad, axis=0, keepdims=True)
        g_out[j] = (d_mid[j * block : (j + 1) * block, :] + norm_back(normal, scale, grad, gain)).astype(bf16)
    store_vector(flat, 0, gain_sum)
    store_vector(flat, ROW_D, shift_sum)
    sa.begin_flat(flat, a_rows, core_out)
    for j in range(2):
        to, micro = place.home(j)
        copy = remote(g_out.at[j], grad_back.at[micro], move_sems.at[2, j], move_sems.at[3, micro], to)
        copy.start()
        sent.append(copy)
    for event in sa.events():
        sa.step(event)
    sm.finish()
    sa.finish()
    for micro in range(2):
        for kind, ref in ((1, out_back), (3, grad_back)):
            remote(
                ref.at[micro], ref.at[micro], move_sems.at[0, micro], move_sems.at[kind, micro], place.sibling
            ).wait_recv()
    for copy in sent:
        copy.wait_send()


class Scatter:
    def __init__(self, dp_size, seq_size, out, acc, core_in, level_in, seq_in, load_sems, send_sems, recv_sems):
        self.n = seq_size
        self.bits = list(range(1, dp_size.bit_length() - 1))
        self.masks = [m << 1 for m in range(1 << len(self.bits))]
        self.dp = lax.axis_index("dp")
        self.z = lax.axis_index("seq")
        self.out, self.acc = out, acc
        self.loads = []
        self.core_in, self.level_in, self.seq_in = core_in, level_in, seq_in
        rows = acc.shape[2]
        half = rows // 32 * 16
        self.parts = [(0, half), (half, rows - half)]
        self.orders = [self.bits[::-1], self.bits]
        self.load_sems, self.send_sems, self.recv_sems = load_sems, send_sems, recv_sems
        self.started = []
        self.indices = {}

    def index(self, *key):
        return self.indices.setdefault(key, len(self.indices))

    def slot(self, mask, k):
        return (self.dp ^ mask) * self.n + lax.rem(self.z + k, self.n)

    def send(self, src, dst, to, key, part=None):
        remote(src, dst, self.send_sems.at[len(self.started)], self.recv_sems.at[self.index(*key)], to).start()
        self.started.append(part)

    def wait(self, ref, key):
        remote(ref, ref, self.send_sems.at[0], self.recv_sems.at[self.index(*key)], (self.dp, self.z)).wait_recv()

    def turn(self):
        return list(range(1, self.n)) + [0]

    def begin(self, slots):
        for k in self.turn():
            for mask in self.masks[::-1]:
                i = self.masks.index(mask)
                load = pltpu.make_async_copy(
                    slots.at[self.slot(mask, k)], self.acc.at[i, k], self.load_sems.at[i, k]
                )
                load.start()
                self.loads.append(load)
                self.send(
                    slots.at[self.slot(mask ^ 1, k)], self.core_in.at[i, k], (self.dp ^ 1, self.z), ("c", i, k)
                )

    def begin_flat(self, flat, rows, core_out):
        for k in self.turn():
            for mask in self.masks[::-1]:
                i = self.masks.index(mask)
                for target, which in ((core_out, mask ^ 1), (self.acc, mask)):
                    target[i, k, :rows, :] = flat[pl.ds(self.slot(which, k) * rows, rows), :].astype(bf16)
                    target[i, k, rows:, :] = jnp.zeros((target.shape[2] - rows, LANES), bf16)
                self.send(core_out.at[i, k], self.core_in.at[i, k], (self.dp ^ 1, self.z), ("c", i, k))

    def cell(self, part, level, mask):
        free = [b for b in self.bits if b not in self.orders[part][: level + 1]]
        return sum(1 << n for n, b in enumerate(free) if mask >> b & 1)

    def pass_on(self, part, level, mask, k):
        order = self.orders[part]
        i = self.masks.index(mask)
        start, size = self.parts[part]
        src = self.acc.at[i, k, pl.ds(start, size)]
        if level == len(order):
            if k:
                to = (self.dp, lax.rem(self.z + k, self.n))
                self.send(src, self.seq_in[part].at[k - 1], to, ("z", part, k), part)
            return
        bit = 1 << order[level]
        if mask & bit:
            rest = mask ^ bit
            dst = self.level_in[part][level].at[self.cell(part, level, rest), k]
            self.send(src, dst, (self.dp ^ bit, self.z), ("l", part, level, rest, k), part)

    def events(self):
        out = []
        for turn, k in enumerate(self.turn()):
            for mask in self.masks[::-1]:
                out.append((turn * 0.1, ("c", mask, k)))
            for level in range(len(self.bits)):
                for part in (0, 1):
                    past = self.orders[part][: level + 1]
                    for mask in self.masks[::-1]:
                        if not any(mask >> b & 1 for b in past):
                            out.append((turn + (level + 1) * 1.0 + 0.5, ("l", part, level, mask, k)))
        out.sort(key=lambda e: e[0])
        return [e[1] for e in out]

    def step(self, event):
        if event[0] == "c":
            _, mask, k = event
            i = self.masks.index(mask)
            if self.loads:
                pltpu.make_async_copy(self.acc.at[i, k], self.acc.at[i, k], self.load_sems.at[i, k]).wait()
            self.wait(self.core_in.at[i, k], ("c", i, k))
            self.acc[i, k] = (self.acc[i, k].astype(f32) + self.core_in[i, k].astype(f32)).astype(bf16)
            for part in (0, 1):
                self.pass_on(part, 0, mask, k)
            return
        _, part, level, mask, k = event
        i = self.masks.index(mask)
        start, size = self.parts[part]
        cell = self.level_in[part][level].at[self.cell(part, level, mask), k]
        self.wait(cell, ("l", part, level, mask, k))
        rows = pl.ds(start, size)
        self.acc[i, k, rows] = (self.acc[i, k, rows].astype(f32) + cell[...].astype(f32)).astype(bf16)
        self.pass_on(part, level + 1, mask, k)

    def finish(self):
        used = self.out.shape[0]
        for part in (0, 1):
            start, size = self.parts[part]
            size = min(size, used - start)
            total = self.acc[0, 0, pl.ds(start, size)].astype(f32)
            for k in range(1, self.n):
                self.wait(self.seq_in[part].at[k - 1], ("z", part, k))
                total = total + self.seq_in[part][k - 1, :size].astype(f32)
            self.out[start : start + size, :] = total
        for index, part in enumerate(self.started):
            start, size = (0, self.acc.shape[2]) if part is None else self.parts[part]
            ref = self.acc.at[0, 0, pl.ds(start, size)]
            remote(ref, ref, self.send_sems.at[index], self.recv_sems.at[0], (self.dp, self.z)).wait_send()


def scatter_scratch(dp_size, seq_size, rows):
    bits = dp_size.bit_length() - 2
    masks = 1 << bits
    half = rows // 32 * 16
    sizes = [half, rows - half]
    shapes = [
        pltpu.VMEM((masks, seq_size, rows, LANES), bf16),
        pltpu.VMEM((masks, seq_size, rows, LANES), bf16),
    ]
    for size in sizes:
        for level in range(bits):
            shapes.append(pltpu.VMEM((masks >> (level + 1), seq_size, size, LANES), bf16))
    for size in sizes:
        shapes.append(pltpu.VMEM((seq_size - 1, size, LANES), bf16))
    count = masks * seq_size + 2 * (masks - 1) * seq_size + 2 * (seq_size - 1)
    shapes += [
        pltpu.SemaphoreType.DMA((masks, seq_size)),
        pltpu.SemaphoreType.DMA((count,)),
        pltpu.SemaphoreType.DMA((count,)),
    ]
    return shapes


def make_scatter(dp_size, seq_size, out, refs):
    bits = dp_size.bit_length() - 2
    acc, core_in, *rest = refs
    level_in = [rest[:bits], rest[bits : 2 * bits]]
    rest = rest[2 * bits :]
    return Scatter(dp_size, seq_size, out, acc, core_in, level_in, rest[:2], *rest[2:])


ANY = pl.BlockSpec(memory_space=pl.ANY)
LOCAL = pl.BlockSpec(memory_space=pltpu.VMEM)


def shape_of(dims, dtype):
    return jax.ShapeDtypeStruct(dims, dtype)


def per_chip_sequence(inputs, segments, attn_params, mlp_params, cotangent):
    dp_size, n = lax.axis_size("dp"), lax.axis_size("seq")
    devices = dp_size * n
    block = inputs.shape[2]
    length = n * block
    a_rows, m_rows = attn_params.shape[0] // LANES, mlp_params.shape[0] // LANES
    a_own, m_own = to_rows(attn_params), to_rows(mlp_params)
    a_pad, m_pad = a_own.shape[0], m_own.shape[0]
    seg_rows = jnp.pad(segments.reshape(2, block // LANES, LANES), ((0, 0), (0, 8 - block // LANES), (0, 0)))
    send, recv = gather_counts(dp_size, n)
    dma = pltpu.SemaphoreType.DMA
    across = shape_of((HALF_COLS, length), bf16)
    heads = shape_of((HALF_HEADS, length, HD), bf16)
    own = shape_of((2, block, D), bf16)
    (
        m_slots, cot_own, x_own, n1, wqkv, w_proj, vec, qt, kt, qh, kh, vh, seg_all, lse, att,
    ) = pl.pallas_call(
        functools.partial(forward_kernel, dp_size, n, a_rows),
        out_shape=[
            shape_of((devices, m_pad, LANES), bf16), own, own, shape_of((length, D), bf16),
            shape_of((3, D, HALF_COLS), bf16), shape_of((D, D), bf16), shape_of((8, D), f32),
            across, across, heads, heads, heads,
            shape_of((n, 8, LANES), jnp.int32), shape_of((8, length), f32), shape_of((2, 2, block, HALF_COLS), bf16),
        ],
        in_specs=[ANY] * 5,
        out_specs=[ANY] * 2 + [LOCAL] * 13,
        scratch_shapes=[
            pltpu.VMEM((devices, a_pad, LANES), bf16),
            pltpu.VMEM((devices * a_rows, LANES), f32),
            pltpu.VMEM((n, block, D), bf16),
            pltpu.VMEM((HALF_COLS, length), bf16),
            pltpu.VMEM((length, LANES), jnp.int32),
            pltpu.VMEM((length, block), f32),
            pltpu.VMEM((HALF_COLS, length), f32),
            pltpu.VMEM((2, block, HALF_COLS), bf16),
            dma((send,)), dma((recv,)), dma((send,)), dma((recv,)), dma((2,)),
            dma((2, 4)), dma((2, n)), dma((2, 2)), dma((2, 2)),
        ],
        compiler_params=pltpu.CompilerParams(collective_id=0, has_side_effects=True, vmem_limit_bytes=VMEM_LIMIT),
    )(inputs[:, 0], seg_rows, cotangent[:, 0], a_own, m_own)

    tokens = 2 * block
    out_own, d_mid, d_att, m_grads, g_proj, g_bias = pl.pallas_call(
        functools.partial(mlp_kernel, m_rows),
        out_shape=[
            shape_of((tokens, D), bf16), shape_of((tokens, D), f32), shape_of((2, tokens, HALF_COLS), bf16),
            shape_of((devices, m_pad, LANES), bf16), shape_of((D * ROW_D, LANES), f32), shape_of((1, D), f32),
        ],
        in_specs=[ANY] + [LOCAL] * 5,
        out_specs=[LOCAL] * 6,
        scratch_shapes=[
            pltpu.VMEM((devices * m_rows, LANES), f32),
            pltpu.VMEM((D, FF), bf16), pltpu.VMEM((FF, D), bf16),
            pltpu.VMEM((tokens, D), f32), pltpu.VMEM((tokens, D), bf16),
            pltpu.VMEM((tokens, D), f32), pltpu.VMEM((tokens, D), f32),
            pltpu.VMEM((1, FF), f32), pltpu.VMEM((1, FF), f32),
            dma(()),
        ],
        compiler_params=pltpu.CompilerParams(vmem_limit_bytes=VMEM_LIMIT),
    )(m_slots, x_own.reshape(tokens, D), cot_own.reshape(tokens, D), att.reshape(2, tokens, HALF_COLS), w_proj, vec)

    masks = dp_size // 2
    out_back, grad_back, a_sum, m_sum = pl.pallas_call(
        functools.partial(backward_kernel, dp_size, n, a_rows),
        out_shape=[own, own, shape_of((a_rows, LANES), f32), shape_of((m_rows, LANES), f32)],
        in_specs=[ANY] * 2 + [LOCAL] * 2 + [ANY] + [LOCAL] * 12,
        out_specs=[ANY] * 2 + [LOCAL] * 2,
        scratch_shapes=[
            pltpu.VMEM((devices * a_rows, LANES), f32),
            pltpu.VMEM((n, block, HALF_COLS), bf16),
            pltpu.VMEM((HALF_COLS, length), bf16),
            pltpu.VMEM((HALF_HEADS, length, HD), bf16),
            pltpu.VMEM((length, LANES), jnp.int32),
            pltpu.VMEM((length, block), f32),
            pltpu.VMEM((length, block), f32),
            pltpu.VMEM((2, length, HD), f32),
            pltpu.VMEM((2, length, HD), f32),
            pltpu.VMEM((HALF_COLS, length), f32),
            pltpu.VMEM((3, length, HALF_COLS), bf16),
            pltpu.VMEM((2, block, D), f32),
            pltpu.VMEM((2, block, D), f32),
            pltpu.VMEM((2, block, D), bf16),
            pltpu.VMEM((masks, n, a_pad, LANES), bf16),
            dma((4, 2)), dma((2, 2)), dma((2, 2)), dma(()),
        ]
        + scatter_scratch(dp_size, n, m_pad)
        + scatter_scratch(dp_size, n, a_pad),
        compiler_params=pltpu.CompilerParams(collective_id=1, has_side_effects=True, vmem_limit_bytes=VMEM_LIMIT),
    )(out_own, m_grads, d_mid, d_att, g_proj, g_bias, x_own, n1, wqkv, vec, qt, kt, qh, kh, vh, seg_all, lse)
    return (
        out_back[:, None],
        grad_back.astype(f32)[:, None],
        a_sum.reshape(-1),
        m_sum.reshape(-1),
    )


def solution(mesh):
    in_specs = (
        P(None, "dp", "seq", None),
        P(None, "dp", "seq"),
        P(("dp", "seq")),
        P(("dp", "seq")),
        P(None, "dp", "seq", None),
    )
    out_specs = (
        P(None, "dp", "seq", None),
        P(None, "dp", "seq", None),
        P(("dp", "seq")),
        P(("dp", "seq")),
    )
    one_each = mesh.shape["seq"] == 4 and mesh.shape["dp"] % 2 == 0
    return jax.shard_map(
        per_chip_sequence if one_each else per_device, mesh=mesh, in_specs=in_specs, out_specs=out_specs, check_vma=False
    )
```

```python
import functools
from functools import partial
import math

import jax
import jax.numpy as jnp
from jax import lax
from jax.experimental import pallas as pl
from jax.experimental.pallas import tpu as pltpu
from jax.sharding import PartitionSpec as P

D = 768
H = 12
HD = 64
FF = 3072


norm_eps = 1e-05
score_floor = -1e30
key_block = 512


def attention_layout():
    return [(D,), (D,), (D, 3 * D), (D,), (D,), (D, D), (D,)]


def mlp_layout():
    return [(D,), (D,), (D, FF), (FF,), (FF, D), (D,)]


def unpack_params(flat_vector, layout):
    offset = 0
    result = []
    for dims_entry in layout:
        amount = math.prod(dims_entry)
        result.append(lax.slice_in_dim(flat_vector, offset, offset + amount).reshape(dims_entry))
        offset += amount
    return result


def layer_norm(values, gain, shift):
    average = jnp.mean(values, axis=-1, keepdims=True)
    centred = values - average
    spread = jnp.mean(centred * centred, axis=-1, keepdims=True)
    return centred * lax.rsqrt(spread + norm_eps) * gain + shift


def gelu_tanh(values):
    return jax.nn.gelu(values, approximate=True)


def pack_grads(grad_list, total_size):
    flat_parts = [part_grad.reshape(-1) for part_grad in grad_list]
    used_total = sum((part_grad.size for part_grad in grad_list))
    flat_parts.append(jnp.zeros((total_size - used_total,), jnp.float32))
    return jnp.concatenate(flat_parts)


def fetch_params(attn_params, mlp_params):
    gathered = (
        lax.all_gather(attn_params, ("dp", "seq"), axis=0, tiled=True),
        lax.all_gather(mlp_params, ("dp", "seq"), axis=0, tiled=True),
    )
    return (
        unpack_params(gathered[0], attention_layout()),
        unpack_params(gathered[1], mlp_layout()),
    )


def send_grads(attn_list, mlp_list, attn_total, mlp_total):
    return (
        lax.psum_scatter(
            pack_grads(attn_list, attn_total), ("dp", "seq"), scatter_dimension=0, tiled=True
        ),
        lax.psum_scatter(
            pack_grads(mlp_list, mlp_total), ("dp", "seq"), scatter_dimension=0, tiled=True
        ),
    )


def fold_keys(key_rows, key_segs, fold_step, start_carry):
    return fold_step(
        start_carry,
        (
            lax.all_gather(key_rows, "seq", axis=0, tiled=True),
            lax.all_gather(key_segs, "seq", axis=0, tiled=True),
        ),
        jnp.int32(0),
    )


def over_blocks(block_step, carry_now, key_piece, key_start):
    piece_rows = key_piece[0].shape[0]
    step_rows = math.gcd(piece_rows, key_block)

    def loop_step(index_block, carry_in):
        offset = index_block * step_rows
        sub_piece = tuple(
            (lax.dynamic_slice_in_dim(member, offset, step_rows, 0) for member in key_piece)
        )
        return block_step(carry_in, sub_piece, offset)

    return lax.fori_loop(0, piece_rows // step_rows, loop_step, carry_now)


def block_scores(query_heads, query_segs, query_pos, kv_rows, key_segs, key_start):
    key_heads = kv_rows[:, :D].reshape(-1, H, HD)
    scores = jnp.einsum(
        "qhd,khd->hqk", query_heads, key_heads, preferred_element_type=jnp.float32
    ) * (1.0 / math.sqrt(HD))
    key_pos = key_start + jnp.arange(kv_rows.shape[0], dtype=jnp.int32)
    allowed = (query_segs[:, None] == key_segs[None, :]) & (key_pos[None, :] <= query_pos[:, None])
    return (jnp.where(allowed[None], scores, score_floor), key_heads)


MESH = pl.DeviceIdType.MESH
LANES = 128

def pad_rows(rows):
    return -(-rows // 16) * 16


def nearest(z, n, i):
    last = n - 1
    high = z > last - z
    near = jnp.where(high, last - z, z)
    step = (i // 2) if i % 2 == 0 else -((i + 1) // 2)
    found = jnp.where(i <= 2 * near, near + step, i)
    return jnp.where(high, last - found, found)


class Gather:
    def __init__(self, dp_size, seq_size, own, slots, send_sems, recv_sems):
        self.n = seq_size
        self.bits = list(range(1, dp_size.bit_length() - 1))
        self.dp = lax.axis_index("dp")
        self.z = lax.axis_index("seq")
        self.own, self.slots = own, slots
        self.rows = own.shape[0]
        half = self.rows // 32 * 16
        self.parts = [(0, half), (half, self.rows - half)]
        self.orders = [self.bits, self.bits[::-1]]
        self.send_sems, self.recv_sems = send_sems, recv_sems
        self.started = []

    def peers(self):
        out = [(self.dp, lax.rem(self.z + k, self.n)) for k in range(1, self.n)]
        return out + [(self.dp ^ (1 << b), self.z) for b in [0] + self.bits]

    def place(self, i):
        return nearest(self.z, self.n, i)

    def view(self, mask, i, part):
        index = (self.dp ^ mask) * self.n + self.place(i)
        start, size = self.parts[part]
        return self.slots.at[index, pl.ds(start, size)]

    def source(self, mask, i, part):
        if mask == 0 and i == 0:
            start, size = self.parts[part]
            return self.own.at[pl.ds(start, size)]
        return self.view(mask, i, part)

    def recv_sem(self, sibling, part, mask, i):
        count = 1 << len(self.bits)
        return self.recv_sems.at[((sibling * 2 + part) * count + (mask >> 1)) * self.n + self.place(i)]

    def send(self, mask, i, part, to, recv_sem, when=None):
        index = len(self.started)
        self.started.append((part, when))

        def start():
            pltpu.make_async_remote_copy(
                src_ref=self.source(mask, i, part), dst_ref=self.view(mask, i, part),
                send_sem=self.send_sems.at[index], recv_sem=recv_sem, device_id=to, device_id_type=MESH,
            ).start()

        if when is None:
            start()
        else:
            pl.when(when())(start)

    def wait(self, sibling, part, mask, i):
        view = self.view(mask ^ sibling, i, part)
        pltpu.make_async_remote_copy(
            src_ref=view, dst_ref=view, send_sem=self.send_sems.at[0],
            recv_sem=self.recv_sem(sibling, part, mask, i),
            device_id=(self.dp, self.z), device_id_type=MESH,
        ).wait_recv()

    def along(self, i, part, up):
        if i == 0:
            to = self.z + 1 if up else self.z - 1
        else:
            to = jnp.where(self.place(i) < self.z, self.z + 1, self.z - 1)

        def when():
            if i == 0:
                return (self.z < self.n - 1) if up else (self.z > 0)
            below = self.place(i) < self.z
            return (below & (self.z < self.n - 1)) | (jnp.logical_not(below) & (self.z > 0))

        self.send(0, i, part, (self.dp, to), self.recv_sem(0, part, 0, i), when)

    def forward(self, part, mask, i):
        if mask == 0 and i:
            self.along(i, part, True)
        order = self.orders[part]
        for level in range(len(order)):
            if not any(mask >> b & 1 for b in order[level:]):
                bit = 1 << order[level]
                self.send(mask, i, part, (self.dp ^ bit, self.z), self.recv_sem(0, part, mask | bit, i))
        self.send(mask, i, part, (self.dp ^ 1, self.z), self.recv_sem(1, part, mask, i))

    def begin_seq(self):
        for part in (0, 1):
            for up in (True, False):
                self.along(0, part, up)

    def begin_bits(self):
        for level in range(len(self.bits)):
            for part in (0, 1):
                bit = 1 << self.orders[part][level]
                self.send(0, 0, part, (self.dp ^ bit, self.z), self.recv_sem(0, part, bit, 0))
        for part in (0, 1):
            self.send(0, 0, part, (self.dp ^ 1, self.z), self.recv_sem(1, part, 0, 0))

    def begin(self):
        self.begin_seq()
        self.begin_bits()

    def events(self, begin=0, seq_gap=1, level_gap=1):
        out = []
        for i in range(self.n):
            for part in (0, 1):
                at = begin + (i + 0.5 * part - 0.5) * seq_gap if i else 0
                if i:
                    out.append((at, (part, 0, i)))
                order = self.orders[part]
                for level in range(len(order)):
                    for low in range(1 << level):
                        mask = 1 << order[level]
                        for n in range(level):
                            if low >> n & 1:
                                mask |= 1 << order[n]
                        out.append((at + (level + 1) * level_gap, (part, mask, i)))
        return sorted(out, key=lambda e: e[0])

    def step(self, event):
        part, mask, i = event
        self.wait(0, part, mask, i)
        self.forward(part, mask, i)

    def finish_sibling(self):
        for part, mask, i in [(0, 0, 0), (1, 0, 0)] + [event for _, event in self.events()]:
            self.wait(1, part, mask, i)

    def finish_sends(self):
        for index, (part, when) in enumerate(self.started):

            def wait(index=index, part=part):
                start, size = self.parts[part]
                view = self.slots.at[0, pl.ds(start, size)]
                pltpu.make_async_remote_copy(
                    src_ref=view, dst_ref=view, send_sem=self.send_sems.at[index], recv_sem=self.recv_sems.at[0],
                    device_id=(self.dp, self.z), device_id_type=MESH,
                ).wait_send()

            if when is None:
                wait()
            else:
                pl.when(when())(wait)


def gather_counts(dp_size, seq_size):
    bits = dp_size.bit_length() - 2
    masks = 1 << bits
    recv = 4 * masks * seq_size
    send = 2 * (seq_size + 1 + seq_size * (masks - 1) + seq_size * masks)
    return send, recv


def gather_kernel(dp_size, seq_size, a_own, m_own, a_slots, m_slots, a_send, a_recv, m_send, m_recv, own_sems):
    ga = Gather(dp_size, seq_size, a_own, a_slots, a_send, a_recv)
    gm = Gather(dp_size, seq_size, m_own, m_slots, m_send, m_recv)
    barrier = pltpu.get_barrier_semaphore()
    peers = ga.peers()
    for peer in peers:
        pl.semaphore_signal(barrier, inc=1, device_id=peer, device_id_type=MESH)
    pl.semaphore_wait(barrier, len(peers))
    ca = pltpu.make_async_copy(a_own, a_slots.at[ga.dp * ga.n + ga.z], own_sems.at[0])
    cm = pltpu.make_async_copy(m_own, m_slots.at[ga.dp * ga.n + ga.z], own_sems.at[1])
    ca.start()
    cm.start()
    ga.begin()
    gm.begin()
    for _, event in ga.events():
        ga.step(event)
    for _, event in gm.events():
        gm.step(event)
    ca.wait()
    cm.wait()
    ga.finish_sibling()
    gm.finish_sibling()
    ga.finish_sends()
    gm.finish_sends()


def to_rows(flat):
    rows = flat.shape[0] // LANES
    return jnp.pad(flat.reshape(rows, LANES), ((0, pad_rows(rows) - rows), (0, 0)))


def gather_params(attn, mlp, dp_size, seq_size):
    a, m = to_rows(attn), to_rows(mlp)
    devices = dp_size * seq_size
    send, recv = gather_counts(dp_size, seq_size)
    return pl.pallas_call(
        functools.partial(gather_kernel, dp_size, seq_size),
        out_shape=[jax.ShapeDtypeStruct((devices,) + a.shape, jnp.bfloat16), jax.ShapeDtypeStruct((devices,) + m.shape, jnp.bfloat16)],
        in_specs=[pl.BlockSpec(memory_space=pl.ANY)] * 2,
        out_specs=[pl.BlockSpec(memory_space=pl.ANY)] * 2,
        scratch_shapes=[pltpu.SemaphoreType.DMA((send,)), pltpu.SemaphoreType.DMA((recv,)),
                        pltpu.SemaphoreType.DMA((send,)), pltpu.SemaphoreType.DMA((recv,)), pltpu.SemaphoreType.DMA((2,))],
        compiler_params=pltpu.CompilerParams(collective_id=0, has_side_effects=True),
    )(a, m)


def per_device(inputs, segments, attn_params, mlp_params, cotangent):
    micro_count = inputs.shape[0]
    local_rows = inputs.shape[2]
    seq_length = local_rows * lax.axis_size("seq")
    attn_total = attn_params.shape[0] * lax.axis_size(("dp", "seq"))
    mlp_total = mlp_params.shape[0] * lax.axis_size(("dp", "seq"))
    query_pos = lax.axis_index("seq") * local_rows + jnp.arange(local_rows, dtype=jnp.int32)
    score_scale = 1.0 / math.sqrt(HD)
    out_rows = []
    grad_rows = []
    attn_sums = None
    mlp_sums = None
    shard_sums = None
    attn_slots, mlp_slots = gather_params(attn_params, mlp_params, lax.axis_size("dp"), lax.axis_size("seq"))
    attn_set = unpack_params(
        attn_slots[:, : attn_params.shape[0] // LANES].reshape(-1), attention_layout()
    )
    mlp_set = unpack_params(
        mlp_slots[:, : mlp_params.shape[0] // LANES].reshape(-1), mlp_layout()
    )
    for micro_index in range(micro_count):
        gain_one, shift_one, w_qkv, bias_query, bias_value, w_proj, bias_proj = attn_set
        gain_two, shift_two, w_up, bias_up, w_down, bias_down = mlp_set
        input_rows = inputs[micro_index, 0].astype(jnp.float32)
        query_segs = segments[micro_index, 0]
        normed_one, norm_one_back = jax.vjp(
            layer_norm, input_rows, gain_one.astype(jnp.float32), shift_one.astype(jnp.float32)
        )
        normed_one_low = normed_one.astype(jnp.bfloat16)
        merged_rows = jnp.dot(normed_one_low, w_qkv, preferred_element_type=jnp.float32)
        query_low = (merged_rows[:, :D] + bias_query.astype(jnp.float32)).astype(jnp.bfloat16)
        kv_local = jnp.concatenate(
            [merged_rows[:, D : 2 * D], merged_rows[:, 2 * D :] + bias_value.astype(jnp.float32)],
            axis=1,
        ).astype(jnp.bfloat16)
        query_heads = query_low.reshape(local_rows, H, HD)

        def max_step(carry_in, sub_piece, key_start):
            scores, key_heads = block_scores(
                query_heads, query_segs, query_pos, sub_piece[0], sub_piece[1], key_start
            )
            running_top, running_total = carry_in
            new_top = jnp.maximum(running_top, jnp.max(scores, axis=-1))
            new_total = running_total * jnp.exp(running_top - new_top) + jnp.sum(
                jnp.exp(scores - new_top[..., None]), axis=-1
            )
            return (new_top, new_total)

        top_start = jnp.full((H, local_rows), score_floor, jnp.float32)
        row_top, row_total = fold_keys(
            kv_local,
            query_segs,
            partial(over_blocks, max_step),
            (top_start, jnp.zeros((H, local_rows), jnp.float32)),
        )
        log_total = row_top + jnp.log(row_total)

        def value_step(carry_in, sub_piece, key_start):
            scores, key_heads = block_scores(
                query_heads, query_segs, query_pos, sub_piece[0], sub_piece[1], key_start
            )
            probs = jnp.exp(scores - log_total[..., None])
            probs_low = probs.astype(jnp.bfloat16)
            probs_rest = (probs - probs_low.astype(jnp.float32)).astype(jnp.bfloat16)
            value_heads = sub_piece[0][:, D:].reshape(-1, H, HD)
            main_part, rest_part = carry_in
            main_part = main_part + jnp.einsum(
                "hqk,khd->qhd", probs_low, value_heads, preferred_element_type=jnp.float32
            )
            rest_part = rest_part + jnp.einsum(
                "hqk,khd->qhd", probs_rest, value_heads, preferred_element_type=jnp.float32
            )
            return (main_part, rest_part)

        zero_heads = jnp.zeros((local_rows, H, HD), jnp.float32)
        main_sum, rest_sum = fold_keys(
            kv_local, query_segs, partial(over_blocks, value_step), (zero_heads, zero_heads)
        )
        attended_low = main_sum.reshape(local_rows, D).astype(jnp.bfloat16)
        attended_full = main_sum + rest_sum
        middle = (
            input_rows
            + jnp.dot(attended_low, w_proj, preferred_element_type=jnp.float32)
            + bias_proj.astype(jnp.float32)
        )
        normed_two, norm_two_back = jax.vjp(
            layer_norm, middle, gain_two.astype(jnp.float32), shift_two.astype(jnp.float32)
        )
        normed_two_low = normed_two.astype(jnp.bfloat16)
        hidden = jnp.dot(normed_two_low, w_up, preferred_element_type=jnp.float32) + bias_up.astype(
            jnp.float32
        )
        active, gelu_back = jax.vjp(gelu_tanh, hidden)
        active_low = active.astype(jnp.bfloat16)
        result = (
            middle
            + jnp.dot(active_low, w_down, preferred_element_type=jnp.float32)
            + bias_down.astype(jnp.float32)
        )
        out_rows.append(result.astype(jnp.bfloat16))
        w_qkv, w_proj = (attn_set[2], attn_set[5])
        w_up, w_down = (mlp_set[2], mlp_set[4])
        cot_low = cotangent[micro_index, 0]
        cot_rows = cot_low.astype(jnp.float32)
        grad_w_down = jnp.einsum(
            "rf,rd->fd", active_low, cot_low, preferred_element_type=jnp.float32
        )
        grad_b_down = jnp.sum(cot_rows, axis=0)
        grad_active = jnp.einsum("rd,fd->rf", cot_low, w_down, preferred_element_type=jnp.float32)
        grad_hidden = gelu_back(grad_active)[0].astype(jnp.bfloat16)
        grad_w_up = jnp.einsum(
            "rd,rf->df", normed_two_low, grad_hidden, preferred_element_type=jnp.float32
        )
        grad_b_up = jnp.sum(grad_hidden.astype(jnp.float32), axis=0)
        grad_normed_two = jnp.einsum(
            "rf,df->rd", grad_hidden, w_up, preferred_element_type=jnp.float32
        )
        grad_middle_norm, grad_gain_two, grad_shift_two = norm_two_back(grad_normed_two)
        grad_middle = cot_rows + grad_middle_norm
        grad_branch = grad_middle.astype(jnp.bfloat16)
        grad_w_proj = jnp.einsum(
            "rd,re->de", attended_low, grad_branch, preferred_element_type=jnp.float32
        )
        grad_b_proj = jnp.sum(grad_branch.astype(jnp.float32), axis=0)
        grad_attended = jnp.einsum(
            "re,de->rd", grad_branch, w_proj, preferred_element_type=jnp.float32
        ).astype(jnp.bfloat16)
        grad_heads = grad_attended.reshape(local_rows, H, HD)
        row_delta = jnp.einsum("qhd,qhd->hq", grad_heads.astype(jnp.float32), attended_full)

        def grad_step(carry_in, sub_piece, key_start):
            scores, key_heads = block_scores(
                query_heads, query_segs, query_pos, sub_piece[0], sub_piece[1], key_start
            )
            value_heads = sub_piece[0][:, D:].reshape(-1, H, HD)
            probs = jnp.exp(scores - log_total[..., None])
            grad_probs = jnp.einsum(
                "qhd,khd->hqk", grad_heads, value_heads, preferred_element_type=jnp.float32
            )
            grad_scores = (probs * (grad_probs - row_delta[..., None])).astype(jnp.bfloat16)
            query_part, kv_part = carry_in
            query_part = (
                query_part
                + jnp.einsum(
                    "hqk,khd->qhd", grad_scores, key_heads, preferred_element_type=jnp.float32
                )
                * score_scale
            )
            key_grad = (
                jnp.einsum(
                    "hqk,qhd->khd", grad_scores, query_heads, preferred_element_type=jnp.float32
                )
                * score_scale
            )
            value_grad = jnp.einsum(
                "hqk,qhd->khd",
                probs.astype(jnp.bfloat16),
                grad_heads,
                preferred_element_type=jnp.float32,
            )
            block_grads = jnp.concatenate(
                [key_grad.reshape(-1, D), value_grad.reshape(-1, D)], axis=1
            )
            kv_part = lax.dynamic_update_slice_in_dim(kv_part, block_grads, key_start, 0)
            return (query_part, kv_part)

        query_sum, kv_sums = fold_keys(
            kv_local,
            query_segs,
            partial(over_blocks, grad_step),
            (zero_heads, jnp.zeros((seq_length, 2 * D), jnp.float32)),
        )
        kv_grads = lax.psum_scatter(
            kv_sums.astype(jnp.bfloat16), "seq", scatter_dimension=0, tiled=True
        ).astype(jnp.float32)
        grad_merged = jnp.concatenate([query_sum.reshape(local_rows, D), kv_grads], axis=1).astype(
            jnp.bfloat16
        )
        grad_merged_wide = grad_merged.astype(jnp.float32)
        grad_w_qkv = jnp.einsum(
            "rd,re->de", normed_one_low, grad_merged, preferred_element_type=jnp.float32
        )
        grad_b_query = jnp.sum(grad_merged_wide[:, :D], axis=0)
        grad_b_value = jnp.sum(grad_merged_wide[:, 2 * D :], axis=0)
        grad_normed_one = jnp.einsum(
            "re,de->rd", grad_merged, w_qkv, preferred_element_type=jnp.float32
        )
        grad_input_norm, grad_gain_one, grad_shift_one = norm_one_back(grad_normed_one)
        grad_rows.append(grad_middle + grad_input_norm)
        attn_list = [
            grad_gain_one,
            grad_shift_one,
            grad_w_qkv,
            grad_b_query,
            grad_b_value,
            grad_w_proj,
            grad_b_proj,
        ]
        mlp_list = [grad_gain_two, grad_shift_two, grad_w_up, grad_b_up, grad_w_down, grad_b_down]
        attn_sums = (
            attn_list
            if attn_sums is None
            else [left_sum + right_sum for left_sum, right_sum in zip(attn_sums, attn_list)]
        )
        mlp_sums = (
            mlp_list
            if mlp_sums is None
            else [left_sum + right_sum for left_sum, right_sum in zip(mlp_sums, mlp_list)]
        )
    shard_sums = send_grads(attn_sums, mlp_sums, attn_total, mlp_total)
    outputs = jnp.stack(out_rows)[:, None]
    input_grad = jnp.stack(grad_rows)[:, None]
    return (outputs, input_grad, shard_sums[0], shard_sums[1])


HALF_HEADS = H // 2
HALF_COLS = D // 2
ROW_D = D // LANES
ROW_FF = FF // LANES
ROW_QKV = 3 * ROW_D
ROW_HALF = HALF_COLS // LANES
FF_STEP = 512
VMEM_LIMIT = 63 * 2**20

A_TIMES = (3.0, 6.0, 4.0)
M_TIMES = (12.0, 9.0, 6.0)
M_OWN = 8.0
M_SEQ = 0.0
M_BITS = 4.0
SEND_X = 6.0
SHARE_X = 28.0
SEND_COT = 45.0
FORWARD_START = 30.0
HEAD_FORWARD = 3.3
BACKWARD_START = 8.0
HEAD_BACKWARD = 5.8

ATTN_QKV = 2 * ROW_D
ATTN_BQ = ATTN_QKV + D * ROW_QKV
ATTN_BV = ATTN_BQ + ROW_D
ATTN_PROJ = ATTN_BV + ROW_D
ATTN_BPROJ = ATTN_PROJ + D * ROW_D
MLP_UP = 2 * ROW_D
MLP_BUP = MLP_UP + D * ROW_FF
MLP_DOWN = MLP_BUP + ROW_FF
MLP_BDOWN = MLP_DOWN + FF * ROW_D

f32 = jnp.float32
bf16 = jnp.bfloat16


def dot_nn(left, right):
    return jnp.dot(left, right, preferred_element_type=f32)


def dot_nt(left, right):
    return lax.dot_general(left, right, (((1,), (1,)), ((), ())), preferred_element_type=f32)


def dot_tn(left, right):
    return lax.dot_general(left, right, (((0,), (0,)), ((), ())), preferred_element_type=f32)


def remote(src, dst, send_sem, recv_sem, to):
    return pltpu.make_async_remote_copy(
        src_ref=src, dst_ref=dst, send_sem=send_sem, recv_sem=recv_sem, device_id=to, device_id_type=MESH
    )


class Place:
    def __init__(self, seq_size):
        self.n = seq_size
        self.dp = lax.axis_index("dp")
        self.z = lax.axis_index("seq")
        self.core = lax.rem(self.dp, 2)
        self.base = self.dp - self.core
        self.sibling = (self.base + 1 - self.core, self.z)

    def line_peers(self):
        out = [self.sibling]
        for k in range(1, self.n):
            other = lax.rem(self.z + k, self.n)
            out += [(self.base, other), (self.base + 1, other)]
        return out

    def own_block(self, j):
        return 1 - self.core + 2 * j

    def other_block(self, j):
        return self.core + 2 * j

    def worker(self, micro):
        return (self.base + 1 - lax.rem(self.z, 2), 2 * micro + self.core)

    def home(self, j):
        return (self.base + lax.rem(self.z, 2), self.own_block(j)), self.z // 2


def split_heads(piece, heads, rows):
    lane = lax.broadcasted_iota(jnp.int32, (piece.shape[0], LANES), 1)
    for h in range(HALF_HEADS):
        pair = piece[:, h // 2 * LANES : (h // 2 + 1) * LANES]
        heads[h, rows, :] = jnp.where(lane // HD == h % 2, pair, jnp.zeros_like(pair))


class Action:
    def step(self, action):
        action()


class Steps:
    def __init__(self, timed):
        self.queue = sorted(timed, key=lambda e: e[0])

    def take(self, time):
        out = [event for at, event in self.queue if at <= time]
        self.queue = [e for e in self.queue if e[0] > time]
        return out

    def until(self, time):
        for owner, event in self.take(time):
            owner.step(event)

    def plan(self, start, points):
        out = {}
        for point, length in points:
            out[point] = self.take(start)
            start += length
        return out


def handle(plan, index):
    for turn, events in enumerate(plan):
        if events:

            @pl.when(index == turn)
            def _():
                for owner, event in events:
                    owner.step(event)


def greet(peers):
    barrier = pltpu.get_barrier_semaphore()
    for peer in peers:
        pl.semaphore_signal(barrier, inc=1, device_id=peer, device_id_type=MESH)
    pl.semaphore_wait(barrier, len(peers))


def unflatten(slots, flat, rows):
    def body(s, carry):
        flat[pl.ds(s * rows, rows), :] = slots[s, :rows, :].astype(f32)
        return carry

    lax.fori_loop(0, slots.shape[0], body, 0)


def load_matrix(flat, start, stride, columns, out, step):
    def body(i, carry):
        rows = pl.ds(pl.multiple_of(i * step, step), step)
        for j in range(columns):
            piece = flat[pl.ds(start + j + i * (step * stride), step, stride=stride), :]
            out[rows, j * LANES : (j + 1) * LANES] = piece.astype(bf16)
        return carry

    lax.fori_loop(0, out.shape[0] // step, body, 0)


def load_vector(flat, start, blocks):
    return jnp.concatenate([flat[pl.ds(start + j, 1), :] for j in range(blocks)], axis=1)


def store_vector(flat, start, value):
    for j in range(value.shape[1] // LANES):
        flat[pl.ds(start + j, 1), :] = value[:, j * LANES : (j + 1) * LANES]


def norm_parts(values):
    average = jnp.mean(values, axis=-1, keepdims=True)
    centred = values - average
    spread = jnp.mean(centred * centred, axis=-1, keepdims=True)
    scale = lax.rsqrt(spread + norm_eps)
    return centred * scale, scale


def norm_back(normal, scale, grad, gain):
    scaled = grad * gain
    return scale * (
        scaled
        - jnp.mean(scaled, axis=-1, keepdims=True)
        - normal * jnp.mean(scaled * normal, axis=-1, keepdims=True)
    )


def keep_allowed(scores, seg_col, seg_all, b, i, block):
    parts = []
    for r in range(block // LANES):
        row = seg_all[i, r : r + 1, :]
        allowed = seg_col[b * block : (b + 1) * block, :] == row
        if b == i:
            key_pos = lax.broadcasted_iota(jnp.int32, (block, LANES), 0)
            query_pos = lax.broadcasted_iota(jnp.int32, (block, LANES), 1) + r * LANES
            allowed = allowed & (key_pos <= query_pos)
        parts.append(jnp.where(allowed, scores[:, r * LANES : (r + 1) * LANES], score_floor))
    return jnp.concatenate(parts, axis=1)


def segment_columns(seg_all, seg_col, block):
    for t in range(seg_all.shape[0]):
        for r in range(block // LANES):
            row = jnp.broadcast_to(seg_all[t, r : r + 1, :], (LANES, LANES))
            seg_col[pl.ds(t * block + r * LANES, LANES), :] = row.T


def forward_kernel(
    dp_size, seq_size, a_rows,
    x_in, seg_in, cot_in, a_own, m_own,
    m_slots, cot_own, n1_out, wqkv_out, qt_out, kt_out, qh_out, kh_out, vh_out,
    x_own, w_proj, vec, seg_all, lse, att,
    n1, wqkv, qt, kt, qh, kh, vh,
    a_slots, flat, x_all, vt, seg_col, scores, ot, att_out,
    a_send, a_recv, m_send, m_recv, own_sems, move_send, move_recv, cot_sems, swap_sems, keep_sems,
):
    place = Place(seq_size)
    block = x_in.shape[1]
    ga = Gather(dp_size, seq_size, a_own, a_slots, a_send, a_recv)
    gm = Gather(dp_size, seq_size, m_own, m_slots, m_send, m_recv)
    greet(place.line_peers() + [(place.dp ^ (1 << b), place.z) for b in ga.bits])

    mine = place.dp * seq_size + place.z
    own_copies = [
        pltpu.make_async_copy(a_own, a_slots.at[mine], own_sems.at[0]),
        pltpu.make_async_copy(m_own, m_slots.at[mine], own_sems.at[1]),
    ]
    ga.begin()
    for copy in own_copies:
        copy.start()
    sent = []

    def launch(copy):
        copy.start()
        sent.append(copy)

    def send_inputs():
        for micro in range(2):
            to = place.worker(micro)
            launch(remote(seg_in.at[micro], seg_all.at[place.z], move_send.at[1, micro], move_recv.at[1, place.z], to))
            launch(remote(x_in.at[micro], x_all.at[place.z], move_send.at[0, micro], move_recv.at[0, place.z], to))

    def arrival(t, kind):
        ref = (x_all, seg_all)[kind].at[t]
        return remote(ref, ref, move_send.at[kind, 0], move_recv.at[kind, t], place.sibling)

    def share_inputs():
        for j in range(2):
            t = place.own_block(j)
            for kind in range(2):
                ref = (x_all, seg_all)[kind].at[t]
                arrival(t, kind).wait_recv()
                launch(remote(ref, ref, move_send.at[kind, 2 + j], move_recv.at[kind, t], place.sibling))

    def send_cotangent():
        for micro in range(2):
            remote(
                cot_in.at[micro], cot_own.at[place.z // 2], cot_sems.at[0, micro], cot_sems.at[1, place.z // 2],
                place.worker(micro),
            ).start()

    timed = [(time, (ga, event)) for time, event in ga.events(*A_TIMES)]
    timed += [(time + (0 if event[2] else M_OWN), (gm, event)) for time, event in gm.events(*M_TIMES)]
    timed += [
        (at, (Action(), action))
        for at, action in (
            (SEND_X, send_inputs), (SHARE_X, share_inputs), (SEND_COT, send_cotangent),
            (M_SEQ, gm.begin_seq), (M_BITS, gm.begin_bits),
        )
    ]
    both = Steps(timed)
    both.until(FORWARD_START)
    own_copies[0].wait()
    ga.finish_sibling()
    unflatten(a_slots, flat, a_rows)
    both.until(FORWARD_START + 3)
    for section in range(3):
        load_matrix(
            flat, ATTN_QKV + section * ROW_D + place.core * ROW_HALF, ROW_QKV, ROW_HALF, wqkv.at[section], LANES
        )
    load_matrix(flat, ATTN_PROJ, ROW_D, ROW_D, w_proj, LANES)
    gain = load_vector(flat, 0, ROW_D)
    shift = load_vector(flat, ROW_D, ROW_D)
    vec[...] = jnp.zeros_like(vec)
    vec[0:1, :] = gain
    vec[1:2, :] = load_vector(flat, ATTN_BPROJ, ROW_D)
    bias_query = load_vector(flat, ATTN_BQ + place.core * ROW_HALF, ROW_HALF)
    bias_value = load_vector(flat, ATTN_BV + place.core * ROW_HALF, ROW_HALF)
    both.until(FORWARD_START + 7)
    for j in range(2):
        for kind in range(2):
            arrival(place.other_block(j), kind).wait_recv()
        x_own[j] = x_all[place.own_block(j)]
    segment_columns(seg_all, seg_col, block)

    def project(t, carry):
        rows = pl.ds(pl.multiple_of(t * block, block), block)
        normal, _ = norm_parts(x_all[t].astype(f32))
        low = (normal * gain + shift).astype(bf16)
        n1[rows, :] = low
        query = (dot_nn(low, wqkv[0]) + bias_query).astype(bf16).astype(f32) * (1.0 / math.sqrt(HD))
        key = dot_nn(low, wqkv[1])
        value = dot_nn(low, wqkv[2]) + bias_value
        for result, across, heads in ((query, qt, qh), (key, kt, kh), (value, vt, vh)):
            across[:, rows] = result.T.astype(bf16)
            split_heads(result.astype(bf16), heads, rows)
        return carry

    lax.fori_loop(0, seq_size, project, 0)
    keep = [
        pltpu.make_async_copy(src, dst, keep_sems.at[i])
        for i, (src, dst) in enumerate(
            [(n1, n1_out), (wqkv, wqkv_out), (qt, qt_out), (kt, kt_out), (qh, qh_out), (kh, kh_out), (vh, vh_out)]
        )
    ]
    for copy in keep:
        copy.start()
    lse[...] = jnp.zeros_like(lse)
    unit = HEAD_FORWARD / (seq_size * (seq_size + 1) // 2)
    points = [((h, i), unit * (i + 1)) for h in range(HALF_HEADS) for i in range(seq_size)]
    plan = both.plan(FORWARD_START + 12, points)

    def one_head(h, carry):
        head_rows = pl.ds(pl.multiple_of(h * HD, HD), HD)
        pair_rows = pl.ds(pl.multiple_of(h // 2 * LANES, LANES), LANES)
        for i in range(seq_size):
            handle([plan[c, i] for c in range(HALF_HEADS)], h)
            columns = slice(i * block, (i + 1) * block)
            query = qt[pair_rows, columns]
            top = jnp.full((1, block), -jnp.inf, f32)
            for b in range(i + 1):
                rows = slice(b * block, (b + 1) * block)
                piece = keep_allowed(dot_nn(kh[h, rows, :], query), seg_col, seg_all, b, i, block)
                scores[rows, :] = piece
                top = jnp.maximum(top, jnp.max(piece, axis=0, keepdims=True))
            total = jnp.zeros((1, block), f32)
            for b in range(i + 1):
                rows = slice(b * block, (b + 1) * block)
                piece = jnp.exp(scores[rows, :] - top)
                scores[rows, :] = piece
                total = total + jnp.sum(piece, axis=0, keepdims=True)
            inverse = 1.0 / total
            result = jnp.zeros((HD, block), f32)
            for b in range(i + 1):
                rows = slice(b * block, (b + 1) * block)
                result = result + dot_nn(vt[head_rows, rows], (scores[rows, :] * inverse).astype(bf16))
            ot[head_rows, columns] = result
            lse[pl.ds(h, 1), columns] = top + jnp.log(total)
        return carry

    lax.fori_loop(0, HALF_HEADS, one_head, 0)
    both.until(math.inf)

    for j in range(2):
        columns = pl.ds(pl.multiple_of(place.other_block(j) * block, block), block)
        att_out[j] = ot[:, columns].T.astype(bf16)
        copy = remote(
            att_out.at[j], att.at[place.core, j], swap_sems.at[0, j], swap_sems.at[1, j], place.sibling
        )
        copy.start()
        sent.append(copy)
    for j in range(2):
        columns = pl.ds(pl.multiple_of(place.own_block(j) * block, block), block)
        att[place.core, j] = ot[:, columns].T.astype(bf16)
    for j in range(2):
        ref = att.at[1 - place.core, j]
        remote(ref, ref, swap_sems.at[0, j], swap_sems.at[1, j], place.sibling).wait_recv()
        ref = cot_own.at[j]
        remote(ref, ref, cot_sems.at[0, j], cot_sems.at[1, j], place.sibling).wait()
    own_copies[1].wait()
    for copy in keep:
        copy.wait()
    gm.finish_sibling()
    for copy in sent:
        copy.wait_send()
    ga.finish_sends()
    gm.finish_sends()


def mlp_kernel(
    m_rows,
    m_slots, x_own, cot, att, w_proj, vec,
    g_out, out, d_mid, d_att, g_proj, g_bias,
    g_slots, flat, w_up, w_down, mid, n2, d_n2, total, b_up, gb_up, sem, out_sems,
):
    rows_all = x_own.shape[0]
    half = rows_all // 2
    copy = pltpu.make_async_copy(m_slots, g_slots, sem)
    copy.start()
    blocks = [slice(0, half), slice(half, rows_all)]
    for rows in blocks:
        mid[rows, :] = (
            x_own[rows, :].astype(f32)
            + dot_nn(att[0, rows, :], w_proj[:HALF_COLS, :])
            + dot_nn(att[1, rows, :], w_proj[HALF_COLS:, :])
            + vec[1:2, :]
        )
    copy.wait()
    unflatten(g_slots, flat, m_rows)
    load_matrix(flat, MLP_UP, ROW_FF, ROW_FF, w_up, 64)
    load_matrix(flat, MLP_DOWN, ROW_D, ROW_D, w_down, LANES)
    gain = load_vector(flat, 0, ROW_D)
    shift = load_vector(flat, ROW_D, ROW_D)
    b_down = load_vector(flat, MLP_BDOWN, ROW_D)
    b_up[...] = load_vector(flat, MLP_BUP, ROW_FF)
    for rows in blocks:
        normal, _ = norm_parts(mid[rows, :])
        n2[rows, :] = (normal * gain + shift).astype(bf16)
    total[...] = jnp.zeros_like(total)
    d_n2[...] = jnp.zeros_like(d_n2)
    inner = math.sqrt(2.0 / math.pi)

    def step(f, carry):
        start = pl.multiple_of(f * FF_STEP, FF_STEP)
        columns = pl.ds(start, FF_STEP)
        hidden = dot_nn(n2[...], w_up[:, columns]) + b_up[:, columns]
        square = hidden * hidden
        tanh = jnp.tanh(inner * (hidden + 0.044715 * (square * hidden)))
        cdf = 0.5 * (1.0 + tanh)
        active = (hidden * cdf).astype(bf16)
        slope = cdf + (0.5 * inner) * hidden * (1.0 - tanh * tanh) * (1.0 + (3 * 0.044715) * square)
        d_hidden = dot_nt(cot[...], w_down[columns, :]) * slope
        low = d_hidden.astype(bf16)
        gb_up[:, columns] = jnp.sum(low.astype(f32), axis=0, keepdims=True)
        total[...] += dot_nn(active, w_down[columns, :])
        d_n2[...] += dot_nt(low, w_up[:, columns])
        g_down = dot_tn(active, cot[...])
        for j in range(ROW_D):
            flat[pl.ds(MLP_DOWN + j + f * (FF_STEP * ROW_D), FF_STEP, stride=ROW_D), :] = g_down[
                :, j * LANES : (j + 1) * LANES
            ]
        g_up = dot_tn(n2[...], low)
        for j in range(FF_STEP // LANES):
            flat[pl.ds(MLP_UP + j + f * (FF_STEP // LANES), D, stride=ROW_FF), :] = g_up[
                :, j * LANES : (j + 1) * LANES
            ]
        return carry

    lax.fori_loop(0, FF // FF_STEP, step, 0)

    gain_sum = jnp.zeros((1, D), f32)
    shift_sum = jnp.zeros((1, D), f32)
    down_sum = jnp.zeros((1, D), f32)
    proj_sum = jnp.zeros((1, D), f32)
    for rows in blocks:
        out[rows, :] = (mid[rows, :] + total[rows, :] + b_down).astype(bf16)
        normal, scale = norm_parts(mid[rows, :])
        grad = d_n2[rows, :]
        cot_rows = cot[rows, :].astype(f32)
        gain_sum += jnp.sum(grad * normal, axis=0, keepdims=True)
        shift_sum += jnp.sum(grad, axis=0, keepdims=True)
        down_sum += jnp.sum(cot_rows, axis=0, keepdims=True)
        d_rows = cot_rows + norm_back(normal, scale, grad, gain)
        d_mid[rows, :] = d_rows
        low = d_rows.astype(bf16)
        n2[rows, :] = low
        proj_sum += jnp.sum(low.astype(f32), axis=0, keepdims=True)
        for c in range(2):
            d_att[c, rows, :] = dot_nt(low, w_proj[c * HALF_COLS : (c + 1) * HALF_COLS, :]).astype(bf16)
    for c in range(2):
        g_part = dot_tn(att[c], n2[...])
        for j in range(ROW_D):
            g_proj[pl.ds(c * HALF_COLS * ROW_D + j, HALF_COLS, stride=ROW_D), :] = g_part[
                :, j * LANES : (j + 1) * LANES
            ]
    g_bias[...] = proj_sum
    store_vector(flat, 0, gain_sum)
    store_vector(flat, ROW_D, shift_sum)
    store_vector(flat, MLP_BUP, gb_up[...])
    store_vector(flat, MLP_BDOWN, down_sum)
    used = MLP_BDOWN + ROW_D
    flat[used:, :] = jnp.zeros((flat.shape[0] - used, LANES), f32)
    group = g_slots.shape[0] // 4
    flush = []
    for part in range(4):
        slots = pl.ds(part * group, group)

        def body(s, carry, part=part):
            s = s + part * group
            g_slots[s, :m_rows, :] = flat[pl.ds(s * m_rows, m_rows), :].astype(bf16)
            return carry

        lax.fori_loop(0, group, body, 0)
        copy = pltpu.make_async_copy(g_slots.at[slots], g_out.at[slots], out_sems.at[part])
        copy.start()
        flush.append(copy)
    for copy in flush:
        copy.wait()


def backward_kernel(
    dp_size, seq_size, a_rows,
    out_own, m_grads, g_proj, n1_in, wqkv_in, qt_in, kt_in, qh_in, kh_in, vh_in, d_mid_in, x_own_in,
    d_att, g_bias, vec, seg_all, lse,
    out_back, grad_back, a_out, m_out,
    n1, wqkv, qt, kt, qh, kh, vh, d_mid, x_own,
    flat, d_all, dt, dh, seg_col, p_piece, d_piece, dk, dv, dqt, dm, d_n1, d_n1_in,
    move_sems, swap_sems, norm_sems, proj_sem, load_sems, *refs,
):
    place = Place(seq_size)
    block = x_own_in.shape[1]
    count = len(refs) // 2
    sm = make_scatter(dp_size, seq_size, m_out, refs[:count])
    sa = make_scatter(dp_size, seq_size, a_out, refs[count:])
    loads = [
        pltpu.make_async_copy(src, dst, load_sems.at[i])
        for i, (src, dst) in enumerate(
            [
                (qt_in, qt), (kt_in, kt), (qh_in, qh), (kh_in, kh), (vh_in, vh),
                (n1_in, n1), (wqkv_in, wqkv), (d_mid_in, d_mid), (x_own_in, x_own),
            ]
        )
    ]
    for copy in loads:
        copy.start()
    greet(place.line_peers() + [(place.dp ^ (1 << b), place.z) for b in sm.bits])
    sent = []
    for j in range(2):
        t = place.own_block(j)
        src = d_att.at[1 - place.core, pl.ds(j * block, block)]
        copy = remote(src, d_all.at[t], swap_sems.at[0, j], swap_sems.at[1, j], place.sibling)
        copy.start()
        sent.append(copy)
    sm.begin(m_grads)
    for j in range(2):
        to, micro = place.home(j)
        copy = remote(
            out_own.at[pl.ds(j * block, block)], out_back.at[micro], move_sems.at[0, j], move_sems.at[1, micro], to
        )
        copy.start()
        sent.append(copy)
    flat[...] = jnp.zeros_like(flat)
    proj_copy = pltpu.make_async_copy(g_proj, flat.at[pl.ds(ATTN_PROJ, D * ROW_D)], proj_sem)
    proj_copy.start()
    for j in range(2):
        d_all[place.own_block(j)] = d_att[place.core, j * block : (j + 1) * block, :]
    segment_columns(seg_all, seg_col, block)
    for j in range(2):
        ref = d_all.at[place.other_block(j)]
        remote(ref, ref, swap_sems.at[0, j], swap_sems.at[1, j], place.sibling).wait_recv()

    def spread(t, carry):
        rows = pl.ds(pl.multiple_of(t * block, block), block)
        piece = d_all[t]
        dt[:, rows] = piece.astype(f32).T.astype(bf16)
        split_heads(piece, dh, rows)
        return carry

    lax.fori_loop(0, seq_size, spread, 0)

    steps = Steps([(time, (sm, event)) for time, event in sm.events()])
    steps.until(BACKWARD_START)
    unit = HEAD_BACKWARD / (seq_size * (seq_size + 1) // 2)
    points = [
        ((i, side, pair), unit * (i + 1))
        for i in reversed(range(seq_size))
        for pair in range(HALF_HEADS // 2)
        for side in range(2)
    ]
    plan = steps.plan(BACKWARD_START, points)
    for copy in loads[:5]:
        copy.wait()

    def query_block(i):
        columns = slice(i * block, (i + 1) * block)

        def one_pair(pair, carry):
            pair_rows = pl.ds(pl.multiple_of(pair * LANES, LANES), LANES)
            for side in range(2):
                handle([plan[i, side, turn] for turn in range(HALF_HEADS // 2)], pair)
                h = 2 * pair + side
                head_rows = pl.ds(pl.multiple_of(h * HD, HD), HD)
                query = qt[pair_rows, columns]
                d_query = dt[pair_rows, columns]
                level = lse[pl.ds(h, 1), columns]
                delta = jnp.zeros((1, block), f32)
                for b in range(i + 1):
                    rows = slice(b * block, (b + 1) * block)
                    probs = jnp.exp(
                        keep_allowed(dot_nn(kh[h, rows, :], query), seg_col, seg_all, b, i, block) - level
                    )
                    d_probs = dot_nn(vh[h, rows, :], d_query)
                    delta = delta + jnp.sum(probs * d_probs, axis=0, keepdims=True)
                    p_piece[rows, :] = probs
                    d_piece[rows, :] = d_probs
                result = jnp.zeros((HD, block), f32)
                for b in range(i + 1):
                    rows = slice(b * block, (b + 1) * block)
                    probs = p_piece[rows, :]
                    d_scores = (probs * (d_piece[rows, :] - delta)).astype(bf16)
                    key_part = dot_nn(d_scores, qh[h, columns, :])
                    value_part = dot_nn(probs.astype(bf16), dh[h, columns, :])
                    if i == seq_size - 1 and side == 0:
                        dk[pair, rows, :] = key_part
                        dv[pair, rows, :] = value_part
                    else:
                        dk[pair, rows, :] += key_part
                        dv[pair, rows, :] += value_part
                    result = result + dot_nn(kt[head_rows, rows], d_scores)
                dqt[head_rows, columns] = result * (1.0 / math.sqrt(HD))
            return carry

        lax.fori_loop(0, HALF_HEADS // 2, one_pair, 0)
        dm[0, columns, :] = dqt[:, columns].T.astype(bf16)
        for section, part in ((1, dk), (2, dv)):
            for pair in range(HALF_HEADS // 2):
                dm[section, columns, pair * LANES : (pair + 1) * LANES] = part[pair, columns, :].astype(bf16)

    def to_norm(t):
        rows = pl.ds(pl.multiple_of(t * block, block), block)
        return dot_nt(dm[0, rows, :], wqkv[0]) + dot_nt(dm[1, rows, :], wqkv[1]) + dot_nt(dm[2, rows, :], wqkv[2])

    def share_norm(j):
        d_n1[j] = to_norm(place.other_block(j))
        copy = remote(d_n1.at[j], d_n1_in.at[j], norm_sems.at[0, j], norm_sems.at[1, j], place.sibling)
        copy.start()
        sent.append(copy)
        d_n1[2] = to_norm(place.own_block(j))

    def finish_input(j):
        ref = d_n1_in.at[j]
        remote(ref, ref, norm_sems.at[0, j], norm_sems.at[1, j], place.sibling).wait_recv()
        grad = d_n1[2] + d_n1_in[j]
        normal, scale = norm_parts(x_own[j].astype(f32))
        x_own[j] = (d_mid[j * block : (j + 1) * block, :] + norm_back(normal, scale, grad, gain)).astype(bf16)
        to, micro = place.home(j)
        copy = remote(x_own.at[j], grad_back.at[micro], move_sems.at[2, j], move_sems.at[3, micro], to)
        copy.start()
        sent.append(copy)
        return jnp.sum(grad * normal, axis=0, keepdims=True), jnp.sum(grad, axis=0, keepdims=True)

    gain = vec[0:1, :]
    query_block(3)
    query_block(2)
    for copy in loads[5:]:
        copy.wait()
    share_norm(1)
    query_block(1)
    gain_sum, shift_sum = finish_input(1)
    query_block(0)
    share_norm(0)
    now = BACKWARD_START + HALF_HEADS * HEAD_BACKWARD
    steps.until(now)
    proj_copy.wait()
    for section in range(3):
        part = dot_tn(n1[...], dm[section])
        for j in range(ROW_HALF):
            start = ATTN_QKV + section * ROW_D + place.core * ROW_HALF + j
            flat[pl.ds(start, D, stride=ROW_QKV), :] = part[:, j * LANES : (j + 1) * LANES]
    steps.until(now + 5)
    more_gain, more_shift = finish_input(0)
    store_vector(flat, 0, gain_sum + more_gain)
    store_vector(flat, ROW_D, shift_sum + more_shift)
    for section, start in ((0, ATTN_BQ), (2, ATTN_BV)):
        total = jnp.sum(dm[section].astype(f32), axis=0, keepdims=True)
        store_vector(flat, start + place.core * ROW_HALF, total)
    store_vector(flat, ATTN_BPROJ, g_bias[...])
    sa.begin_flat(flat, a_rows, sm.core_in)
    steps.until(math.inf)
    for _, event in sa.events():
        sa.step(event)
    sm.finish()
    sa.finish()
    for micro in range(2):
        for kind, ref in ((1, out_back), (3, grad_back)):
            remote(
                ref.at[micro], ref.at[micro], move_sems.at[0, micro], move_sems.at[kind, micro], place.sibling
            ).wait_recv()
    for copy in sent:
        copy.wait_send()


class Scatter:
    def __init__(self, dp_size, seq_size, out, acc, core_in, level_in, seq_in, load_sems, send_sems, recv_sems, seq_sems):
        self.n = seq_size
        self.bits = list(range(1, dp_size.bit_length() - 1))
        self.masks = [m << 1 for m in range(1 << len(self.bits))]
        self.dp = lax.axis_index("dp")
        self.z = lax.axis_index("seq")
        self.out, self.acc = out, acc
        self.loads = []
        self.core_in, self.level_in, self.seq_in = core_in, level_in, seq_in
        rows = acc.shape[2]
        half = rows // 32 * 16
        self.parts = [(0, half), (half, rows - half)]
        self.orders = [self.bits[::-1], self.bits]
        self.load_sems, self.send_sems, self.recv_sems, self.seq_sems = load_sems, send_sems, recv_sems, seq_sems
        self.started = []
        self.indices = {}

    def index(self, *key):
        return self.indices.setdefault(key, len(self.indices))

    def slot(self, mask, k):
        return (self.dp ^ mask) * self.n + nearest(self.z, self.n, k)

    def send(self, src, dst, to, key, part=None):
        sem = self.recv_sems.at[self.index(*key)] if isinstance(key, tuple) else key
        remote(src, dst, self.send_sems.at[len(self.started)], sem, to).start()
        self.started.append(part)

    def wait(self, ref, key):
        remote(ref, ref, self.send_sems.at[0], self.recv_sems.at[self.index(*key)], (self.dp, self.z)).wait_recv()

    def turn(self):
        return list(range(self.n))[::-1]

    def begin(self, slots):
        for k in self.turn():
            for mask in self.masks[::-1]:
                i = self.masks.index(mask)
                load = pltpu.make_async_copy(
                    slots.at[self.slot(mask, k)], self.acc.at[i, k], self.load_sems.at[i, k]
                )
                load.start()
                self.loads.append(load)
                self.send(
                    slots.at[self.slot(mask ^ 1, k)], self.core_in.at[i, k], (self.dp ^ 1, self.z), ("c", i, k)
                )

    def begin_flat(self, flat, rows, core_out):
        whole = self.acc.shape[2]
        for k in self.turn():
            for mask in self.masks[::-1]:
                i = self.masks.index(mask)
                for target, which in ((core_out, mask ^ 1), (self.acc, mask)):
                    target[i, k, :rows, :] = flat[pl.ds(self.slot(which, k) * rows, rows), :].astype(bf16)
                    target[i, k, rows:whole, :] = jnp.zeros((whole - rows, LANES), bf16)
                self.send(core_out.at[i, k, pl.ds(0, whole)], self.core_in.at[i, k], (self.dp ^ 1, self.z), ("c", i, k))

    def cell(self, part, level, mask):
        free = [b for b in self.bits if b not in self.orders[part][: level + 1]]
        return sum(1 << n for n, b in enumerate(free) if mask >> b & 1)

    def pass_on(self, part, level, mask, k):
        order = self.orders[part]
        i = self.masks.index(mask)
        start, size = self.parts[part]
        src = self.acc.at[i, k, pl.ds(start, size)]
        if level == len(order):
            return
        bit = 1 << order[level]
        if mask & bit:
            rest = mask ^ bit
            dst = self.level_in[part][level].at[self.cell(part, level, rest), k]
            self.send(src, dst, (self.dp ^ bit, self.z), ("l", part, level, rest, k), part)

    def events(self, begin=6.0, gap=9.6, level_gap=(9.0, 19.0), seq_gap=0.5):
        out = []
        for turn, k in enumerate(self.turn()):
            at = begin + max(0, turn - 1) * gap
            for mask in self.masks[::-1]:
                out.append((at, ("c", mask, k)))
            at = begin + turn * gap
            for level in range(len(self.bits)):
                for part in (0, 1):
                    past = self.orders[part][: level + 1]
                    for mask in self.masks[::-1]:
                        if not any(mask >> b & 1 for b in past):
                            out.append((at + level_gap[min(level, 1)], ("l", part, level, mask, k)))
            if k:
                for part in (0, 1):
                    out.append((at + level_gap[min(len(self.bits) - 1, 1)] + seq_gap, ("z", part, k)))
        return sorted(out, key=lambda e: e[0])

    def step(self, event):
        if event[0] == "c":
            _, mask, k = event
            i = self.masks.index(mask)
            if self.loads:
                pltpu.make_async_copy(self.acc.at[i, k], self.acc.at[i, k], self.load_sems.at[i, k]).wait()
            self.wait(self.core_in.at[i, k], ("c", i, k))
            self.acc[i, k] = (self.acc[i, k].astype(f32) + self.core_in[i, k].astype(f32)).astype(bf16)
            for part in (0, 1):
                self.pass_on(part, 0, mask, k)
            return
        if event[0] == "z":
            _, part, k = event
            self.along(part, k)
            return
        _, part, level, mask, k = event
        i = self.masks.index(mask)
        start, size = self.parts[part]
        cell = self.level_in[part][level].at[self.cell(part, level, mask), k]
        self.wait(cell, ("l", part, level, mask, k))
        rows = pl.ds(start, size)
        self.acc[i, k, rows] = (self.acc[i, k, rows].astype(f32) + cell[...].astype(f32)).astype(bf16)
        self.pass_on(part, level + 1, mask, k)

    def from_side(self, part, place, side):
        index = place if side == 0 else self.n
        ref = self.seq_in[part].at[index]
        remote(ref, ref, self.send_sems.at[0], self.seq_sems.at[part, index], (self.dp, self.z)).wait_recv()
        return self.seq_in[part][index].astype(f32)

    def along(self, part, k):
        place = nearest(self.z, self.n, k)
        up = place > self.z
        start, size = self.parts[part]
        rows = pl.ds(start, size)

        @pl.when((up & (self.z > 0)) | (jnp.logical_not(up) & (self.z < self.n - 1)))
        def _():
            self.acc[0, k, rows] = (self.acc[0, k, rows].astype(f32) + self.from_side(part, place, 0)).astype(bf16)

        to = jnp.where(up, self.z + 1, self.z - 1)
        index = jnp.where((to == place) & jnp.logical_not(up), self.n, place)
        self.send(
            self.acc.at[0, k, rows], self.seq_in[part].at[index], (self.dp, to), self.seq_sems.at[part, index], part
        )

    def finish(self):
        used = self.out.shape[0]
        for part in (0, 1):
            start, size = self.parts[part]
            kept = min(size, used - start)
            rows = slice(start, start + kept)
            self.out[rows, :] = self.acc[0, 0, pl.ds(start, kept)].astype(f32)
            for side, there in ((0, self.z > 0), (1, self.z < self.n - 1)):

                @pl.when(there)
                def _():
                    self.out[rows, :] += self.from_side(part, self.z, side)[:kept]

        for index, part in enumerate(self.started):
            start, size = (0, self.acc.shape[2]) if part is None else self.parts[part]
            ref = self.acc.at[0, 0, pl.ds(start, size)]
            remote(ref, ref, self.send_sems.at[index], self.recv_sems.at[0], (self.dp, self.z)).wait_send()


def scatter_scratch(dp_size, seq_size, rows):
    bits = dp_size.bit_length() - 2
    masks = 1 << bits
    half = rows // 32 * 16
    sizes = [half, rows - half]
    shapes = [
        pltpu.VMEM((masks, seq_size, rows, LANES), bf16),
        pltpu.VMEM((masks, seq_size, rows, LANES), bf16),
    ]
    for size in sizes:
        for level in range(bits):
            shapes.append(pltpu.VMEM((masks >> (level + 1), seq_size, size, LANES), bf16))
    for size in sizes:
        shapes.append(pltpu.VMEM((seq_size + 1, size, LANES), bf16))
    count = masks * seq_size + 2 * (masks - 1) * seq_size + 2 * (seq_size - 1)
    shapes += [
        pltpu.SemaphoreType.DMA((masks, seq_size)),
        pltpu.SemaphoreType.DMA((count,)),
        pltpu.SemaphoreType.DMA((count,)),
        pltpu.SemaphoreType.DMA((2, seq_size + 1)),
    ]
    return shapes


def make_scatter(dp_size, seq_size, out, refs):
    bits = dp_size.bit_length() - 2
    acc, core_in, *rest = refs
    level_in = [rest[:bits], rest[bits : 2 * bits]]
    rest = rest[2 * bits :]
    return Scatter(dp_size, seq_size, out, acc, core_in, level_in, rest[:2], *rest[2:])


ANY = pl.BlockSpec(memory_space=pl.ANY)
LOCAL = pl.BlockSpec(memory_space=pltpu.VMEM)


def shape_of(dims, dtype):
    return jax.ShapeDtypeStruct(dims, dtype)


def per_chip_sequence(inputs, segments, attn_params, mlp_params, cotangent):
    dp_size, n = lax.axis_size("dp"), lax.axis_size("seq")
    devices = dp_size * n
    block = inputs.shape[2]
    length = n * block
    a_rows, m_rows = attn_params.shape[0] // LANES, mlp_params.shape[0] // LANES
    a_own, m_own = to_rows(attn_params), to_rows(mlp_params)
    a_pad, m_pad = a_own.shape[0], m_own.shape[0]
    seg_rows = jnp.pad(segments.reshape(2, block // LANES, LANES), ((0, 0), (0, 8 - block // LANES), (0, 0)))
    send, recv = gather_counts(dp_size, n)
    dma = pltpu.SemaphoreType.DMA
    across = shape_of((HALF_COLS, length), bf16)
    heads = shape_of((HALF_HEADS, length, LANES), bf16)
    own = shape_of((2, block, D), bf16)
    kept = [
        shape_of((length, D), bf16), shape_of((3, D, HALF_COLS), bf16), across, across, heads, heads, heads,
    ]
    (
        m_slots, cot_own, n1, wqkv, qt, kt, qh, kh, vh, x_own, w_proj, vec, seg_all, lse, att,
    ) = pl.pallas_call(
        functools.partial(forward_kernel, dp_size, n, a_rows),
        out_shape=[shape_of((devices, m_pad, LANES), bf16), own]
        + kept
        + [
            own, shape_of((D, D), bf16), shape_of((8, D), f32),
            shape_of((n, 8, LANES), jnp.int32), shape_of((8, length), f32), shape_of((2, 2, block, HALF_COLS), bf16),
        ],
        in_specs=[ANY] * 5,
        out_specs=[ANY] * 9 + [LOCAL] * 6,
        scratch_shapes=[pltpu.VMEM(like.shape, like.dtype) for like in kept]
        + [
            pltpu.VMEM((devices, a_pad, LANES), bf16),
            pltpu.VMEM((devices * a_rows, LANES), f32),
            pltpu.VMEM((n, block, D), bf16),
            pltpu.VMEM((HALF_COLS, length), bf16),
            pltpu.VMEM((length, LANES), jnp.int32),
            pltpu.VMEM((length, block), f32),
            pltpu.VMEM((HALF_COLS, length), f32),
            pltpu.VMEM((2, block, HALF_COLS), bf16),
            dma((send,)), dma((recv,)), dma((send,)), dma((recv,)), dma((2,)),
            dma((2, 4)), dma((2, n)), dma((2, 2)), dma((2, 2)), dma((len(kept),)),
        ],
        compiler_params=pltpu.CompilerParams(collective_id=0, has_side_effects=True, vmem_limit_bytes=VMEM_LIMIT),
    )(inputs[:, 0], seg_rows, cotangent[:, 0], a_own, m_own)

    tokens = 2 * block
    m_grads, out_own, d_mid, d_att, g_proj, g_bias = pl.pallas_call(
        functools.partial(mlp_kernel, m_rows),
        out_shape=[
            shape_of((devices, m_pad, LANES), bf16),
            shape_of((tokens, D), bf16), shape_of((tokens, D), f32), shape_of((2, tokens, HALF_COLS), bf16),
            shape_of((D * ROW_D, LANES), f32), shape_of((1, D), f32),
        ],
        in_specs=[ANY] + [LOCAL] * 5,
        out_specs=[ANY] + [LOCAL] * 5,
        scratch_shapes=[
            pltpu.VMEM((devices, m_pad, LANES), bf16),
            pltpu.VMEM((devices * m_rows, LANES), f32),
            pltpu.VMEM((D, FF), bf16), pltpu.VMEM((FF, D), bf16),
            pltpu.VMEM((tokens, D), f32), pltpu.VMEM((tokens, D), bf16),
            pltpu.VMEM((tokens, D), f32), pltpu.VMEM((tokens, D), f32),
            pltpu.VMEM((1, FF), f32), pltpu.VMEM((1, FF), f32),
            dma(()), dma((4,)),
        ],
        compiler_params=pltpu.CompilerParams(vmem_limit_bytes=VMEM_LIMIT),
    )(m_slots, x_own.reshape(tokens, D), cot_own.reshape(tokens, D), att.reshape(2, tokens, HALF_COLS), w_proj, vec)

    out_back, grad_back, a_sum, m_sum = pl.pallas_call(
        functools.partial(backward_kernel, dp_size, n, a_rows),
        out_shape=[own, own, shape_of((a_rows, LANES), f32), shape_of((m_rows, LANES), f32)],
        in_specs=[ANY] * 12 + [LOCAL] * 5,
        out_specs=[ANY] * 2 + [LOCAL] * 2,
        scratch_shapes=[pltpu.VMEM(like.shape, like.dtype) for like in kept]
        + [
            pltpu.VMEM((tokens, D), f32),
            pltpu.VMEM((2, block, D), bf16),
            pltpu.VMEM((devices * a_rows, LANES), f32),
            pltpu.VMEM((n, block, HALF_COLS), bf16),
            pltpu.VMEM((HALF_COLS, length), bf16),
            pltpu.VMEM((HALF_HEADS, length, LANES), bf16),
            pltpu.VMEM((length, LANES), jnp.int32),
            pltpu.VMEM((length, block), f32),
            pltpu.VMEM((length, block), f32),
            pltpu.VMEM((HALF_HEADS // 2, length, LANES), f32),
            pltpu.VMEM((HALF_HEADS // 2, length, LANES), f32),
            pltpu.VMEM((HALF_COLS, length), f32),
            pltpu.VMEM((3, length, HALF_COLS), bf16),
            pltpu.VMEM((3, block, D), f32),
            pltpu.VMEM((2, block, D), f32),
            dma((4, 2)), dma((2, 2)), dma((2, 2)), dma(()), dma((9,)),
        ]
        + scatter_scratch(dp_size, n, m_pad)
        + scatter_scratch(dp_size, n, a_pad),
        compiler_params=pltpu.CompilerParams(collective_id=1, has_side_effects=True, vmem_limit_bytes=VMEM_LIMIT),
    )(
        out_own, m_grads, g_proj, n1, wqkv, qt, kt, qh, kh, vh, d_mid, x_own,
        d_att, g_bias, vec, seg_all, lse,
    )
    return (
        out_back[:, None],
        grad_back.astype(f32)[:, None],
        a_sum.reshape(-1),
        m_sum.reshape(-1),
    )


def solution(mesh):
    in_specs = (
        P(None, "dp", "seq", None),
        P(None, "dp", "seq"),
        P(("dp", "seq")),
        P(("dp", "seq")),
        P(None, "dp", "seq", None),
    )
    out_specs = (
        P(None, "dp", "seq", None),
        P(None, "dp", "seq", None),
        P(("dp", "seq")),
        P(("dp", "seq")),
    )
    one_each = mesh.shape["seq"] == 4 and mesh.shape["dp"] % 2 == 0
    return jax.shard_map(
        per_chip_sequence if one_each else per_device, mesh=mesh, in_specs=in_specs, out_specs=out_specs, check_vma=False
    )
```

```python
import functools
from functools import partial
import math

import jax
import jax.numpy as jnp
from jax import lax
from jax.experimental import pallas as pl
from jax.experimental.pallas import tpu as pltpu
from jax.sharding import PartitionSpec as P

D = 768
H = 12
HD = 64
FF = 3072


norm_eps = 1e-05
score_floor = -1e30
key_block = 512


def attention_layout():
    return [(D,), (D,), (D, 3 * D), (D,), (D,), (D, D), (D,)]


def mlp_layout():
    return [(D,), (D,), (D, FF), (FF,), (FF, D), (D,)]


def unpack_params(flat_vector, layout):
    offset = 0
    result = []
    for dims_entry in layout:
        amount = math.prod(dims_entry)
        result.append(lax.slice_in_dim(flat_vector, offset, offset + amount).reshape(dims_entry))
        offset += amount
    return result


def layer_norm(values, gain, shift):
    average = jnp.mean(values, axis=-1, keepdims=True)
    centred = values - average
    spread = jnp.mean(centred * centred, axis=-1, keepdims=True)
    return centred * lax.rsqrt(spread + norm_eps) * gain + shift


def gelu_tanh(values):
    return jax.nn.gelu(values, approximate=True)


def pack_grads(grad_list, total_size):
    flat_parts = [part_grad.reshape(-1) for part_grad in grad_list]
    used_total = sum((part_grad.size for part_grad in grad_list))
    flat_parts.append(jnp.zeros((total_size - used_total,), jnp.float32))
    return jnp.concatenate(flat_parts)


def fetch_params(attn_params, mlp_params):
    gathered = (
        lax.all_gather(attn_params, ("dp", "seq"), axis=0, tiled=True),
        lax.all_gather(mlp_params, ("dp", "seq"), axis=0, tiled=True),
    )
    return (
        unpack_params(gathered[0], attention_layout()),
        unpack_params(gathered[1], mlp_layout()),
    )


def send_grads(attn_list, mlp_list, attn_total, mlp_total):
    return (
        lax.psum_scatter(
            pack_grads(attn_list, attn_total), ("dp", "seq"), scatter_dimension=0, tiled=True
        ),
        lax.psum_scatter(
            pack_grads(mlp_list, mlp_total), ("dp", "seq"), scatter_dimension=0, tiled=True
        ),
    )


def fold_keys(key_rows, key_segs, fold_step, start_carry):
    return fold_step(
        start_carry,
        (
            lax.all_gather(key_rows, "seq", axis=0, tiled=True),
            lax.all_gather(key_segs, "seq", axis=0, tiled=True),
        ),
        jnp.int32(0),
    )


def over_blocks(block_step, carry_now, key_piece, key_start):
    piece_rows = key_piece[0].shape[0]
    step_rows = math.gcd(piece_rows, key_block)

    def loop_step(index_block, carry_in):
        offset = index_block * step_rows
        sub_piece = tuple(
            (lax.dynamic_slice_in_dim(member, offset, step_rows, 0) for member in key_piece)
        )
        return block_step(carry_in, sub_piece, offset)

    return lax.fori_loop(0, piece_rows // step_rows, loop_step, carry_now)


def block_scores(query_heads, query_segs, query_pos, kv_rows, key_segs, key_start):
    key_heads = kv_rows[:, :D].reshape(-1, H, HD)
    scores = jnp.einsum(
        "qhd,khd->hqk", query_heads, key_heads, preferred_element_type=jnp.float32
    ) * (1.0 / math.sqrt(HD))
    key_pos = key_start + jnp.arange(kv_rows.shape[0], dtype=jnp.int32)
    allowed = (query_segs[:, None] == key_segs[None, :]) & (key_pos[None, :] <= query_pos[:, None])
    return (jnp.where(allowed[None], scores, score_floor), key_heads)


MESH = pl.DeviceIdType.MESH
LANES = 128

def pad_rows(rows):
    return -(-rows // 16) * 16


def nearest(z, n, i):
    last = n - 1
    high = z > last - z
    near = jnp.where(high, last - z, z)
    step = (i // 2) if i % 2 == 0 else -((i + 1) // 2)
    found = jnp.where(i <= 2 * near, near + step, i)
    return jnp.where(high, last - found, found)


class Gather:
    def __init__(self, dp_size, seq_size, own, slots, send_sems, recv_sems):
        self.n = seq_size
        self.bits = list(range(1, dp_size.bit_length() - 1))
        self.dp = lax.axis_index("dp")
        self.z = lax.axis_index("seq")
        self.own, self.slots = own, slots
        self.rows = own.shape[0]
        half = self.rows // 32 * 16
        self.parts = [(0, half), (half, self.rows - half)]
        self.orders = [self.bits, self.bits[::-1]]
        self.send_sems, self.recv_sems = send_sems, recv_sems
        self.started = []

    def peers(self):
        out = [(self.dp, lax.rem(self.z + k, self.n)) for k in range(1, self.n)]
        return out + [(self.dp ^ (1 << b), self.z) for b in [0] + self.bits]

    def place(self, i):
        return nearest(self.z, self.n, i)

    def view(self, mask, i, part):
        index = (self.dp ^ mask) * self.n + self.place(i)
        start, size = self.parts[part]
        return self.slots.at[index, pl.ds(start, size)]

    def source(self, mask, i, part):
        if mask == 0 and i == 0:
            start, size = self.parts[part]
            return self.own.at[pl.ds(start, size)]
        return self.view(mask, i, part)

    def recv_sem(self, sibling, part, mask, i):
        count = 1 << len(self.bits)
        return self.recv_sems.at[((sibling * 2 + part) * count + (mask >> 1)) * self.n + self.place(i)]

    def send(self, mask, i, part, to, recv_sem, when=None):
        index = len(self.started)
        self.started.append((part, when))

        def start():
            pltpu.make_async_remote_copy(
                src_ref=self.source(mask, i, part), dst_ref=self.view(mask, i, part),
                send_sem=self.send_sems.at[index], recv_sem=recv_sem, device_id=to, device_id_type=MESH,
            ).start()

        if when is None:
            start()
        else:
            pl.when(when())(start)

    def wait(self, sibling, part, mask, i):
        view = self.view(mask ^ sibling, i, part)
        pltpu.make_async_remote_copy(
            src_ref=view, dst_ref=view, send_sem=self.send_sems.at[0],
            recv_sem=self.recv_sem(sibling, part, mask, i),
            device_id=(self.dp, self.z), device_id_type=MESH,
        ).wait_recv()

    def along(self, i, part, up):
        if i == 0:
            to = self.z + 1 if up else self.z - 1
        else:
            to = jnp.where(self.place(i) < self.z, self.z + 1, self.z - 1)

        def when():
            if i == 0:
                return (self.z < self.n - 1) if up else (self.z > 0)
            below = self.place(i) < self.z
            return (below & (self.z < self.n - 1)) | (jnp.logical_not(below) & (self.z > 0))

        self.send(0, i, part, (self.dp, to), self.recv_sem(0, part, 0, i), when)

    def forward(self, part, mask, i):
        if mask == 0 and i:
            self.along(i, part, True)
        order = self.orders[part]
        for level in range(len(order)):
            if not any(mask >> b & 1 for b in order[level:]):
                bit = 1 << order[level]
                self.send(mask, i, part, (self.dp ^ bit, self.z), self.recv_sem(0, part, mask | bit, i))
        self.send(mask, i, part, (self.dp ^ 1, self.z), self.recv_sem(1, part, mask, i))

    def begin_seq(self):
        for part in (0, 1):
            for up in (True, False):
                self.along(0, part, up)

    def begin_bits(self):
        for level in range(len(self.bits)):
            for part in (0, 1):
                bit = 1 << self.orders[part][level]
                self.send(0, 0, part, (self.dp ^ bit, self.z), self.recv_sem(0, part, bit, 0))
        for part in (0, 1):
            self.send(0, 0, part, (self.dp ^ 1, self.z), self.recv_sem(1, part, 0, 0))

    def begin(self):
        self.begin_seq()
        self.begin_bits()

    def events(self, begin=0, seq_gap=1, level_gap=1):
        out = []
        for i in range(self.n):
            for part in (0, 1):
                at = begin + (i + 0.5 * part - 0.5) * seq_gap if i else 0
                if i:
                    out.append((at, (part, 0, i)))
                order = self.orders[part]
                for level in range(len(order)):
                    for low in range(1 << level):
                        mask = 1 << order[level]
                        for n in range(level):
                            if low >> n & 1:
                                mask |= 1 << order[n]
                        out.append((at + (level + 1) * level_gap, (part, mask, i)))
        return sorted(out, key=lambda e: e[0])

    def step(self, event):
        part, mask, i = event
        self.wait(0, part, mask, i)
        self.forward(part, mask, i)

    def finish_sibling(self):
        for part, mask, i in [(0, 0, 0), (1, 0, 0)] + [event for _, event in self.events()]:
            self.wait(1, part, mask, i)

    def finish_sends(self):
        for index, (part, when) in enumerate(self.started):

            def wait(index=index, part=part):
                start, size = self.parts[part]
                view = self.slots.at[0, pl.ds(start, size)]
                pltpu.make_async_remote_copy(
                    src_ref=view, dst_ref=view, send_sem=self.send_sems.at[index], recv_sem=self.recv_sems.at[0],
                    device_id=(self.dp, self.z), device_id_type=MESH,
                ).wait_send()

            if when is None:
                wait()
            else:
                pl.when(when())(wait)


def gather_counts(dp_size, seq_size):
    bits = dp_size.bit_length() - 2
    masks = 1 << bits
    recv = 4 * masks * seq_size
    send = 2 * (seq_size + 1 + seq_size * (masks - 1) + seq_size * masks)
    return send, recv


def gather_kernel(dp_size, seq_size, a_own, m_own, a_slots, m_slots, a_send, a_recv, m_send, m_recv, own_sems):
    ga = Gather(dp_size, seq_size, a_own, a_slots, a_send, a_recv)
    gm = Gather(dp_size, seq_size, m_own, m_slots, m_send, m_recv)
    barrier = pltpu.get_barrier_semaphore()
    peers = ga.peers()
    for peer in peers:
        pl.semaphore_signal(barrier, inc=1, device_id=peer, device_id_type=MESH)
    pl.semaphore_wait(barrier, len(peers))
    ca = pltpu.make_async_copy(a_own, a_slots.at[ga.dp * ga.n + ga.z], own_sems.at[0])
    cm = pltpu.make_async_copy(m_own, m_slots.at[ga.dp * ga.n + ga.z], own_sems.at[1])
    ca.start()
    cm.start()
    ga.begin()
    gm.begin()
    for _, event in ga.events():
        ga.step(event)
    for _, event in gm.events():
        gm.step(event)
    ca.wait()
    cm.wait()
    ga.finish_sibling()
    gm.finish_sibling()
    ga.finish_sends()
    gm.finish_sends()


def to_rows(flat):
    rows = flat.shape[0] // LANES
    return jnp.pad(flat.reshape(rows, LANES), ((0, pad_rows(rows) - rows), (0, 0)))


def gather_params(attn, mlp, dp_size, seq_size):
    a, m = to_rows(attn), to_rows(mlp)
    devices = dp_size * seq_size
    send, recv = gather_counts(dp_size, seq_size)
    return pl.pallas_call(
        functools.partial(gather_kernel, dp_size, seq_size),
        out_shape=[jax.ShapeDtypeStruct((devices,) + a.shape, jnp.bfloat16), jax.ShapeDtypeStruct((devices,) + m.shape, jnp.bfloat16)],
        in_specs=[pl.BlockSpec(memory_space=pl.ANY)] * 2,
        out_specs=[pl.BlockSpec(memory_space=pl.ANY)] * 2,
        scratch_shapes=[pltpu.SemaphoreType.DMA((send,)), pltpu.SemaphoreType.DMA((recv,)),
                        pltpu.SemaphoreType.DMA((send,)), pltpu.SemaphoreType.DMA((recv,)), pltpu.SemaphoreType.DMA((2,))],
        compiler_params=pltpu.CompilerParams(collective_id=0, has_side_effects=True),
    )(a, m)


def per_device(inputs, segments, attn_params, mlp_params, cotangent):
    micro_count = inputs.shape[0]
    local_rows = inputs.shape[2]
    seq_length = local_rows * lax.axis_size("seq")
    attn_total = attn_params.shape[0] * lax.axis_size(("dp", "seq"))
    mlp_total = mlp_params.shape[0] * lax.axis_size(("dp", "seq"))
    query_pos = lax.axis_index("seq") * local_rows + jnp.arange(local_rows, dtype=jnp.int32)
    score_scale = 1.0 / math.sqrt(HD)
    out_rows = []
    grad_rows = []
    attn_sums = None
    mlp_sums = None
    shard_sums = None
    attn_slots, mlp_slots = gather_params(attn_params, mlp_params, lax.axis_size("dp"), lax.axis_size("seq"))
    attn_set = unpack_params(
        attn_slots[:, : attn_params.shape[0] // LANES].reshape(-1), attention_layout()
    )
    mlp_set = unpack_params(
        mlp_slots[:, : mlp_params.shape[0] // LANES].reshape(-1), mlp_layout()
    )
    for micro_index in range(micro_count):
        gain_one, shift_one, w_qkv, bias_query, bias_value, w_proj, bias_proj = attn_set
        gain_two, shift_two, w_up, bias_up, w_down, bias_down = mlp_set
        input_rows = inputs[micro_index, 0].astype(jnp.float32)
        query_segs = segments[micro_index, 0]
        normed_one, norm_one_back = jax.vjp(
            layer_norm, input_rows, gain_one.astype(jnp.float32), shift_one.astype(jnp.float32)
        )
        normed_one_low = normed_one.astype(jnp.bfloat16)
        merged_rows = jnp.dot(normed_one_low, w_qkv, preferred_element_type=jnp.float32)
        query_low = (merged_rows[:, :D] + bias_query.astype(jnp.float32)).astype(jnp.bfloat16)
        kv_local = jnp.concatenate(
            [merged_rows[:, D : 2 * D], merged_rows[:, 2 * D :] + bias_value.astype(jnp.float32)],
            axis=1,
        ).astype(jnp.bfloat16)
        query_heads = query_low.reshape(local_rows, H, HD)

        def max_step(carry_in, sub_piece, key_start):
            scores, key_heads = block_scores(
                query_heads, query_segs, query_pos, sub_piece[0], sub_piece[1], key_start
            )
            running_top, running_total = carry_in
            new_top = jnp.maximum(running_top, jnp.max(scores, axis=-1))
            new_total = running_total * jnp.exp(running_top - new_top) + jnp.sum(
                jnp.exp(scores - new_top[..., None]), axis=-1
            )
            return (new_top, new_total)

        top_start = jnp.full((H, local_rows), score_floor, jnp.float32)
        row_top, row_total = fold_keys(
            kv_local,
            query_segs,
            partial(over_blocks, max_step),
            (top_start, jnp.zeros((H, local_rows), jnp.float32)),
        )
        log_total = row_top + jnp.log(row_total)

        def value_step(carry_in, sub_piece, key_start):
            scores, key_heads = block_scores(
                query_heads, query_segs, query_pos, sub_piece[0], sub_piece[1], key_start
            )
            probs = jnp.exp(scores - log_total[..., None])
            probs_low = probs.astype(jnp.bfloat16)
            probs_rest = (probs - probs_low.astype(jnp.float32)).astype(jnp.bfloat16)
            value_heads = sub_piece[0][:, D:].reshape(-1, H, HD)
            main_part, rest_part = carry_in
            main_part = main_part + jnp.einsum(
                "hqk,khd->qhd", probs_low, value_heads, preferred_element_type=jnp.float32
            )
            rest_part = rest_part + jnp.einsum(
                "hqk,khd->qhd", probs_rest, value_heads, preferred_element_type=jnp.float32
            )
            return (main_part, rest_part)

        zero_heads = jnp.zeros((local_rows, H, HD), jnp.float32)
        main_sum, rest_sum = fold_keys(
            kv_local, query_segs, partial(over_blocks, value_step), (zero_heads, zero_heads)
        )
        attended_low = main_sum.reshape(local_rows, D).astype(jnp.bfloat16)
        attended_full = main_sum + rest_sum
        middle = (
            input_rows
            + jnp.dot(attended_low, w_proj, preferred_element_type=jnp.float32)
            + bias_proj.astype(jnp.float32)
        )
        normed_two, norm_two_back = jax.vjp(
            layer_norm, middle, gain_two.astype(jnp.float32), shift_two.astype(jnp.float32)
        )
        normed_two_low = normed_two.astype(jnp.bfloat16)
        hidden = jnp.dot(normed_two_low, w_up, preferred_element_type=jnp.float32) + bias_up.astype(
            jnp.float32
        )
        active, gelu_back = jax.vjp(gelu_tanh, hidden)
        active_low = active.astype(jnp.bfloat16)
        result = (
            middle
            + jnp.dot(active_low, w_down, preferred_element_type=jnp.float32)
            + bias_down.astype(jnp.float32)
        )
        out_rows.append(result.astype(jnp.bfloat16))
        w_qkv, w_proj = (attn_set[2], attn_set[5])
        w_up, w_down = (mlp_set[2], mlp_set[4])
        cot_low = cotangent[micro_index, 0]
        cot_rows = cot_low.astype(jnp.float32)
        grad_w_down = jnp.einsum(
            "rf,rd->fd", active_low, cot_low, preferred_element_type=jnp.float32
        )
        grad_b_down = jnp.sum(cot_rows, axis=0)
        grad_active = jnp.einsum("rd,fd->rf", cot_low, w_down, preferred_element_type=jnp.float32)
        grad_hidden = gelu_back(grad_active)[0].astype(jnp.bfloat16)
        grad_w_up = jnp.einsum(
            "rd,rf->df", normed_two_low, grad_hidden, preferred_element_type=jnp.float32
        )
        grad_b_up = jnp.sum(grad_hidden.astype(jnp.float32), axis=0)
        grad_normed_two = jnp.einsum(
            "rf,df->rd", grad_hidden, w_up, preferred_element_type=jnp.float32
        )
        grad_middle_norm, grad_gain_two, grad_shift_two = norm_two_back(grad_normed_two)
        grad_middle = cot_rows + grad_middle_norm
        grad_branch = grad_middle.astype(jnp.bfloat16)
        grad_w_proj = jnp.einsum(
            "rd,re->de", attended_low, grad_branch, preferred_element_type=jnp.float32
        )
        grad_b_proj = jnp.sum(grad_branch.astype(jnp.float32), axis=0)
        grad_attended = jnp.einsum(
            "re,de->rd", grad_branch, w_proj, preferred_element_type=jnp.float32
        ).astype(jnp.bfloat16)
        grad_heads = grad_attended.reshape(local_rows, H, HD)
        row_delta = jnp.einsum("qhd,qhd->hq", grad_heads.astype(jnp.float32), attended_full)

        def grad_step(carry_in, sub_piece, key_start):
            scores, key_heads = block_scores(
                query_heads, query_segs, query_pos, sub_piece[0], sub_piece[1], key_start
            )
            value_heads = sub_piece[0][:, D:].reshape(-1, H, HD)
            probs = jnp.exp(scores - log_total[..., None])
            grad_probs = jnp.einsum(
                "qhd,khd->hqk", grad_heads, value_heads, preferred_element_type=jnp.float32
            )
            grad_scores = (probs * (grad_probs - row_delta[..., None])).astype(jnp.bfloat16)
            query_part, kv_part = carry_in
            query_part = (
                query_part
                + jnp.einsum(
                    "hqk,khd->qhd", grad_scores, key_heads, preferred_element_type=jnp.float32
                )
                * score_scale
            )
            key_grad = (
                jnp.einsum(
                    "hqk,qhd->khd", grad_scores, query_heads, preferred_element_type=jnp.float32
                )
                * score_scale
            )
            value_grad = jnp.einsum(
                "hqk,qhd->khd",
                probs.astype(jnp.bfloat16),
                grad_heads,
                preferred_element_type=jnp.float32,
            )
            block_grads = jnp.concatenate(
                [key_grad.reshape(-1, D), value_grad.reshape(-1, D)], axis=1
            )
            kv_part = lax.dynamic_update_slice_in_dim(kv_part, block_grads, key_start, 0)
            return (query_part, kv_part)

        query_sum, kv_sums = fold_keys(
            kv_local,
            query_segs,
            partial(over_blocks, grad_step),
            (zero_heads, jnp.zeros((seq_length, 2 * D), jnp.float32)),
        )
        kv_grads = lax.psum_scatter(
            kv_sums.astype(jnp.bfloat16), "seq", scatter_dimension=0, tiled=True
        ).astype(jnp.float32)
        grad_merged = jnp.concatenate([query_sum.reshape(local_rows, D), kv_grads], axis=1).astype(
            jnp.bfloat16
        )
        grad_merged_wide = grad_merged.astype(jnp.float32)
        grad_w_qkv = jnp.einsum(
            "rd,re->de", normed_one_low, grad_merged, preferred_element_type=jnp.float32
        )
        grad_b_query = jnp.sum(grad_merged_wide[:, :D], axis=0)
        grad_b_value = jnp.sum(grad_merged_wide[:, 2 * D :], axis=0)
        grad_normed_one = jnp.einsum(
            "re,de->rd", grad_merged, w_qkv, preferred_element_type=jnp.float32
        )
        grad_input_norm, grad_gain_one, grad_shift_one = norm_one_back(grad_normed_one)
        grad_rows.append(grad_middle + grad_input_norm)
        attn_list = [
            grad_gain_one,
            grad_shift_one,
            grad_w_qkv,
            grad_b_query,
            grad_b_value,
            grad_w_proj,
            grad_b_proj,
        ]
        mlp_list = [grad_gain_two, grad_shift_two, grad_w_up, grad_b_up, grad_w_down, grad_b_down]
        attn_sums = (
            attn_list
            if attn_sums is None
            else [left_sum + right_sum for left_sum, right_sum in zip(attn_sums, attn_list)]
        )
        mlp_sums = (
            mlp_list
            if mlp_sums is None
            else [left_sum + right_sum for left_sum, right_sum in zip(mlp_sums, mlp_list)]
        )
    shard_sums = send_grads(attn_sums, mlp_sums, attn_total, mlp_total)
    outputs = jnp.stack(out_rows)[:, None]
    input_grad = jnp.stack(grad_rows)[:, None]
    return (outputs, input_grad, shard_sums[0], shard_sums[1])


HALF_HEADS = H // 2
HALF_COLS = D // 2
ROW_D = D // LANES
ROW_FF = FF // LANES
ROW_QKV = 3 * ROW_D
ROW_HALF = HALF_COLS // LANES
FF_STEP = 512
HEAD = 16
MARGIN = 32
VMEM_LIMIT = 63 * 2**20

A_TIMES = (3.0, 6.0, 4.0)
M_TIMES = (12.0, 9.0, 6.0)
M_OWN = 8.0
M_SEQ = 0.0
M_BITS = 4.0
SEND_X = (6.0, 6.0, 6.0, 6.0)
SHARE_X = 28.0
SEND_COT = (45.0, 45.0)
FORWARD_START = 30.0
HEAD_FORWARD = 3.3
BACKWARD_FIRST = 6.5
BACKWARD_START = 8.0
A_BACK = (6.0, 5.0, (5.0, 10.0), 1.0)
HEAD_BACKWARD = 5.8

ATTN_QKV = 2 * ROW_D
ATTN_BQ = ATTN_QKV + D * ROW_QKV
ATTN_BV = ATTN_BQ + ROW_D
ATTN_PROJ = ATTN_BV + ROW_D
ATTN_BPROJ = ATTN_PROJ + D * ROW_D
MLP_UP = 2 * ROW_D
MLP_BUP = MLP_UP + D * ROW_FF
MLP_DOWN = MLP_BUP + ROW_FF
MLP_BDOWN = MLP_DOWN + FF * ROW_D

f32 = jnp.float32
bf16 = jnp.bfloat16


def dot_nn(left, right):
    return jnp.dot(left, right, preferred_element_type=f32)


def dot_nt(left, right):
    return lax.dot_general(left, right, (((1,), (1,)), ((), ())), preferred_element_type=f32)


def dot_tn(left, right):
    return lax.dot_general(left, right, (((0,), (0,)), ((), ())), preferred_element_type=f32)


def remote(src, dst, send_sem, recv_sem, to):
    return pltpu.make_async_remote_copy(
        src_ref=src, dst_ref=dst, send_sem=send_sem, recv_sem=recv_sem, device_id=to, device_id_type=MESH
    )


class Place:
    def __init__(self, seq_size):
        self.n = seq_size
        self.dp = lax.axis_index("dp")
        self.z = lax.axis_index("seq")
        self.core = lax.rem(self.dp, 2)
        self.base = self.dp - self.core
        self.sibling = (self.base + 1 - self.core, self.z)

    def line_peers(self):
        out = [self.sibling]
        for k in range(1, self.n):
            other = lax.rem(self.z + k, self.n)
            out += [(self.base, other), (self.base + 1, other)]
        return out

    def own_block(self, j):
        return 1 - self.core + 2 * j

    def other_block(self, j):
        return self.core + 2 * j

    def worker(self, micro):
        return (self.base + 1 - lax.rem(self.z, 2), 2 * micro + self.core)

    def home(self, j):
        return (self.base + lax.rem(self.z, 2), self.own_block(j)), self.z // 2


def split_heads(piece, heads, rows):
    lane = lax.broadcasted_iota(jnp.int32, (piece.shape[0], LANES), 1)
    for h in range(HALF_HEADS):
        pair = piece[:, h // 2 * LANES : (h // 2 + 1) * LANES]
        heads[h, rows, :] = jnp.where(lane // HD == h % 2, pair, jnp.zeros_like(pair))


class Action:
    def step(self, action):
        action()


class Steps:
    def __init__(self, timed):
        self.queue = sorted(timed, key=lambda e: e[0])

    def take(self, time):
        out = [event for at, event in self.queue if at <= time]
        self.queue = [e for e in self.queue if e[0] > time]
        return out

    def until(self, time):
        for owner, event in self.take(time):
            owner.step(event)

    def plan(self, start, points):
        out = {}
        for point, length in points:
            out[point] = self.take(start)
            start += length
        return out


def handle(plan, index):
    for turn, events in enumerate(plan):
        if events:

            @pl.when(index == turn)
            def _():
                for owner, event in events:
                    owner.step(event)


def greet(peers):
    barrier = pltpu.get_barrier_semaphore()
    for peer in peers:
        pl.semaphore_signal(barrier, inc=1, device_id=peer, device_id_type=MESH)
    pl.semaphore_wait(barrier, len(peers))


class Layout:
    def __init__(self, rows, devices, matrices, tail):
        self.rows, self.tail = rows, tail
        self.whole = sum(count * columns for _, count, columns in matrices) // devices
        self.slot_rows = self.whole + HEAD + tail
        self.regions = []
        first = 0
        for start, count, columns in matrices:
            shards = count * columns // self.whole
            self.regions.append((start, columns, self.whole // columns, first, shards))
            first += shards
        assert first == devices
        for s in range(devices):
            start, columns, height, first, _ = self.region(s)
            shift = start + self.whole * (s - first) - rows * s
            assert shift <= HEAD and shift + self.whole >= rows - tail and shift >= -MARGIN

    def region(self, s):
        return [r for r in self.regions if r[3] <= s < r[3] + r[4]][0]

    def shift(self, s, region):
        start, _, _, first, _ = region
        return start - self.whole * first + (self.whole - self.rows) * s

    def piece(self, row):
        s, q = row // self.rows, row % self.rows
        if q < HEAD:
            return s, self.whole + q
        assert q >= self.rows - self.tail
        return s, self.whole + HEAD + q - (self.rows - self.tail)

    def lacking(self, region):
        out = []
        start, columns, height, first, shards = region
        for s in range(first, first + shards):
            shift = self.shift(s, region)
            for q in range(self.whole):
                if not 0 <= shift + q < self.rows:
                    out.append(((s - first) * height + q // columns, q % columns) + self.piece(s * self.rows + shift + q))
        return out

    def beyond(self):
        out = []
        for s in range(sum(r[4] for r in self.regions)):
            shift = self.shift(s, self.region(s))
            for q in list(range(max(shift, 0))) + list(range(shift + self.whole, self.rows)):
                row = s * self.rows + q
                for start, columns, height, first, shards in self.regions:
                    if start <= row < start + shards * self.whole:
                        i, j = (row - start) // columns, (row - start) % columns
                        out.append(self.piece(row) + (first + i // height, j * height + i % height))
        return out

    def branch(self, s, action):
        for region in self.regions:
            pl.when((s >= region[3]) & (s < region[3] + region[4]))(functools.partial(action, region))

    def pack(self, own, wide, slot, s):
        edge = jnp.zeros((MARGIN, LANES), f32)
        wide[:MARGIN, :] = edge
        wide[MARGIN + own.shape[0] :, :] = edge
        wide[MARGIN : MARGIN + own.shape[0], :] = own[...].astype(f32)

        def fill(region):
            _, columns, height, _, _ = region
            for j in range(columns):
                piece = wide[pl.ds(MARGIN + self.shift(s, region) + j, height, stride=columns), :]
                slot[j * height : (j + 1) * height, :] = piece.astype(bf16)

        self.branch(s, fill)
        slot[self.whole : self.whole + HEAD, :] = own[:HEAD, :]
        last = wide[MARGIN + self.rows - self.tail : MARGIN + self.rows, :]
        slot[self.whole + HEAD :, :] = last.astype(bf16)

    def unpack(self, slot, wide, out, s):
        def fill(region):
            _, columns, height, _, _ = region
            shift = self.shift(s, region)
            for j in range(columns):
                wide[pl.ds(MARGIN + shift + j, height, stride=columns), :] = slot[j * height : (j + 1) * height, :]
            out[...] = wide[MARGIN : MARGIN + self.rows, :]
            row = lax.broadcasted_iota(jnp.int32, (HEAD, LANES), 0)
            out[:HEAD, :] = jnp.where(row < shift, slot[self.whole : self.whole + HEAD, :], out[:HEAD, :])
            begin = self.rows - self.tail
            row = lax.broadcasted_iota(jnp.int32, (self.tail, LANES), 0) + begin
            last = slot[self.whole + HEAD :, :]
            out[begin:, :] = jnp.where(row >= shift + self.whole, last, out[begin:, :])

        self.branch(s, fill)

    def vector(self, slots, row, blocks):
        parts = []
        for j in range(blocks):
            s, q = self.piece(row + j)
            aligned = q // 16 * 16
            parts.append(slots[s, aligned : aligned + 16, :].astype(f32)[q - aligned : q - aligned + 1, :])
        return jnp.concatenate(parts, axis=1)

    def put_vectors(self, slots, entries):
        areas = {}
        for row, value in entries:
            for j in range(value.shape[1] // LANES):
                s, at = self.piece(row + j)
                begin = self.whole if at < self.whole + HEAD else self.whole + HEAD
                areas.setdefault((s, begin), {})[at - begin] = value[:, j * LANES : (j + 1) * LANES]
        zero = jnp.zeros((1, LANES), f32)
        for (s, begin), rows in areas.items():
            size = HEAD if begin == self.whole else self.tail
            tile = jnp.concatenate([rows.get(n, zero) for n in range(size)], axis=0)
            slots[s, begin : begin + size, :] = tile.astype(bf16)


def load_matrix(slots, layout, which, base, out):
    region = layout.regions[which]
    _, columns, height, first, shards = region

    def body(s, carry):
        rows = pl.ds(pl.multiple_of(s * height, height), height)
        for j in range(columns):
            out[rows, j * LANES : (j + 1) * LANES] = slots[s + first - base, j * height : (j + 1) * height, :]
        return carry

    lax.fori_loop(0, shards, body, 0)
    for i, j, s, q in layout.lacking(region):
        out[i : i + 1, j * LANES : (j + 1) * LANES] = slots[s - base, q : q + 1, :]


def attn_layout(rows, devices):
    return Layout(rows, devices, [(ATTN_QKV, D, ROW_QKV), (ATTN_PROJ, D, ROW_D)], 16)


def mlp_layout_of(rows, devices):
    return Layout(rows, devices, [(MLP_UP, D, ROW_FF), (MLP_DOWN, FF, ROW_D)], 32)


def norm_parts(values):
    average = jnp.mean(values, axis=-1, keepdims=True)
    centred = values - average
    spread = jnp.mean(centred * centred, axis=-1, keepdims=True)
    scale = lax.rsqrt(spread + norm_eps)
    return centred * scale, scale


def norm_back(normal, scale, grad, gain):
    scaled = grad * gain
    return scale * (
        scaled
        - jnp.mean(scaled, axis=-1, keepdims=True)
        - normal * jnp.mean(scaled * normal, axis=-1, keepdims=True)
    )


def keep_allowed(scores, seg_col, seg_all, b, i, block):
    parts = []
    for r in range(block // LANES):
        row = seg_all[i, r : r + 1, :]
        allowed = seg_col[b * block : (b + 1) * block, :] == row
        if b == i:
            key_pos = lax.broadcasted_iota(jnp.int32, (block, LANES), 0)
            query_pos = lax.broadcasted_iota(jnp.int32, (block, LANES), 1) + r * LANES
            allowed = allowed & (key_pos <= query_pos)
        parts.append(jnp.where(allowed, scores[:, r * LANES : (r + 1) * LANES], score_floor))
    return jnp.concatenate(parts, axis=1)


def segment_columns(seg_all, seg_col, block):
    for t in range(seg_all.shape[0]):
        for r in range(block // LANES):
            row = jnp.broadcast_to(seg_all[t, r : r + 1, :], (LANES, LANES))
            seg_col[pl.ds(t * block + r * LANES, LANES), :] = row.T


def forward_kernel(
    dp_size, seq_size, a_layout, m_layout,
    x_in, seg_in, cot_in, a_raw, m_raw,
    m_slots, cot_own, n1_out, wqkv_out, qt_out, kt_out, qh_out, kh_out, vh_out,
    x_own, w_proj, vec, seg_all, lse, att,
    n1, wqkv, qt, kt, qh, kh, vh,
    a_slots, a_own, m_own, a_wide, m_wide, x_all, vt, seg_col, scores, ot, att_out,
    a_send, a_recv, m_send, m_recv, own_sems, move_send, move_recv, cot_sems, swap_sems, keep_sems,
):
    place = Place(seq_size)
    block = x_in.shape[1]
    ga = Gather(dp_size, seq_size, a_own, a_slots, a_send, a_recv)
    gm = Gather(dp_size, seq_size, m_own, m_slots, m_send, m_recv)
    mine = place.dp * seq_size + place.z
    a_layout.pack(a_raw, a_wide, a_own, mine)
    greet(place.line_peers() + [(place.dp ^ (1 << b), place.z) for b in ga.bits])

    own_copies = [
        pltpu.make_async_copy(a_own, a_slots.at[mine], own_sems.at[0]),
        pltpu.make_async_copy(m_own, m_slots.at[mine], own_sems.at[1]),
    ]
    ga.begin()
    m_layout.pack(m_raw, m_wide, m_own, mine)
    for copy in own_copies:
        copy.start()
    sent = []

    def launch(copy):
        copy.start()
        sent.append(copy)

    def send_segments():
        for micro in range(2):
            launch(
                remote(
                    seg_in.at[micro], seg_all.at[place.z], move_send.at[2, micro], move_recv.at[2, place.z],
                    place.worker(micro),
                )
            )

    def send_inputs(micro, half):
        rows = pl.ds(half * (block // 2), block // 2)
        launch(
            remote(
                x_in.at[micro, rows], x_all.at[place.z, rows], move_send.at[half, micro], move_recv.at[half, place.z],
                place.worker(micro),
            )
        )

    def moved(t, kind):
        return seg_all.at[t] if kind == 2 else x_all.at[t, pl.ds(kind * (block // 2), block // 2)]

    def arrival(t, kind):
        ref = moved(t, kind)
        return remote(ref, ref, move_send.at[kind, 0], move_recv.at[kind, t], place.sibling)

    def share_inputs():
        for j in range(2):
            t = place.own_block(j)
            for kind in range(3):
                ref = moved(t, kind)
                arrival(t, kind).wait_recv()
                launch(remote(ref, ref, move_send.at[kind, 2 + j], move_recv.at[kind, t], place.sibling))

    def send_cotangent(micro):
        remote(
            cot_in.at[micro], cot_own.at[place.z // 2], cot_sems.at[0, micro], cot_sems.at[1, place.z // 2],
            place.worker(micro),
        ).start()

    timed = [(time, (ga, event)) for time, event in ga.events(*A_TIMES)]
    timed += [(time + (0 if event[2] else M_OWN), (gm, event)) for time, event in gm.events(*M_TIMES)]
    timed += [
        (at, (Action(), action))
        for at, action in (
            (SEND_X[0], send_segments), (SHARE_X, share_inputs), (M_SEQ, gm.begin_seq), (M_BITS, gm.begin_bits),
        )
    ]
    timed += [
        (SEND_X[n], (Action(), functools.partial(send_inputs, 1 - n // 2, n % 2))) for n in range(4)
    ]
    timed += [(SEND_COT[n], (Action(), functools.partial(send_cotangent, 1 - n))) for n in range(2)]
    both = Steps(timed)
    both.until(FORWARD_START)
    own_copies[0].wait()
    ga.finish_sibling()
    height = a_layout.regions[0][2]

    def take_columns(s, carry):
        rows = pl.ds(pl.multiple_of(s * height, height), height)
        for section in range(3):
            for j in range(ROW_HALF):
                block_at = section * ROW_D + place.core * ROW_HALF + j
                piece = a_slots[s, pl.ds(pl.multiple_of(block_at * height, height), height), :]
                wqkv[section, rows, j * LANES : (j + 1) * LANES] = piece
        return carry

    lax.fori_loop(0, a_layout.regions[0][4], take_columns, 0)
    for core in range(2):

        @pl.when(place.core == core)
        def _():
            for i, j, s, q in a_layout.lacking(a_layout.regions[0]):
                section, at = j // ROW_D, j % ROW_D - core * ROW_HALF
                if 0 <= at < ROW_HALF:
                    wqkv[section, i : i + 1, at * LANES : (at + 1) * LANES] = a_slots[s, q : q + 1, :]

    load_matrix(a_slots, a_layout, 1, 0, w_proj)
    gain = a_layout.vector(a_slots, 0, ROW_D)
    shift = a_layout.vector(a_slots, ROW_D, ROW_D)
    vec[...] = jnp.zeros_like(vec)
    vec[0:1, :] = gain
    vec[1:2, :] = a_layout.vector(a_slots, ATTN_BPROJ, ROW_D)
    first_half = place.core == 0
    bias_query = a_layout.vector(a_slots, ATTN_BQ, ROW_D)
    bias_query = jnp.where(first_half, bias_query[:, :HALF_COLS], bias_query[:, HALF_COLS:])
    bias_value = a_layout.vector(a_slots, ATTN_BV, ROW_D)
    bias_value = jnp.where(first_half, bias_value[:, :HALF_COLS], bias_value[:, HALF_COLS:])
    both.until(FORWARD_START + 2)
    for j in range(2):
        for kind in range(3):
            arrival(place.other_block(j), kind).wait_recv()
        x_own[j] = x_all[place.own_block(j)]
    segment_columns(seg_all, seg_col, block)

    def project(t, carry):
        rows = pl.ds(pl.multiple_of(t * block, block), block)
        normal, _ = norm_parts(x_all[t].astype(f32))
        low = (normal * gain + shift).astype(bf16)
        n1[rows, :] = low
        query = (dot_nn(low, wqkv[0]) + bias_query).astype(bf16).astype(f32) * (1.0 / math.sqrt(HD))
        key = dot_nn(low, wqkv[1])
        value = dot_nn(low, wqkv[2]) + bias_value
        for result, across, heads in ((query, qt, qh), (key, kt, kh), (value, vt, vh)):
            across[:, rows] = result.T.astype(bf16)
            split_heads(result.astype(bf16), heads, rows)
        return carry

    lax.fori_loop(0, seq_size, project, 0)
    keep = [
        pltpu.make_async_copy(src, dst, keep_sems.at[i])
        for i, (src, dst) in enumerate(
            [(n1, n1_out), (wqkv, wqkv_out), (qt, qt_out), (kt, kt_out), (qh, qh_out), (kh, kh_out), (vh, vh_out)]
        )
    ]
    for copy in keep:
        copy.start()
    lse[...] = jnp.zeros_like(lse)
    unit = HEAD_FORWARD / (seq_size * (seq_size + 1) // 2)
    points = [((h, i), unit * (i + 1)) for h in range(HALF_HEADS) for i in range(seq_size)]
    plan = both.plan(FORWARD_START + 7, points)

    def one_head(h, carry):
        head_rows = pl.ds(pl.multiple_of(h * HD, HD), HD)
        pair_rows = pl.ds(pl.multiple_of(h // 2 * LANES, LANES), LANES)
        for i in range(seq_size):
            handle([plan[c, i] for c in range(HALF_HEADS)], h)
            columns = slice(i * block, (i + 1) * block)
            query = qt[pair_rows, columns]
            top = jnp.full((1, block), -jnp.inf, f32)
            for b in range(i + 1):
                rows = slice(b * block, (b + 1) * block)
                piece = keep_allowed(dot_nn(kh[h, rows, :], query), seg_col, seg_all, b, i, block)
                scores[rows, :] = piece
                top = jnp.maximum(top, jnp.max(piece, axis=0, keepdims=True))
            total = jnp.zeros((1, block), f32)
            for b in range(i + 1):
                rows = slice(b * block, (b + 1) * block)
                piece = jnp.exp(scores[rows, :] - top)
                scores[rows, :] = piece
                total = total + jnp.sum(piece, axis=0, keepdims=True)
            inverse = 1.0 / total
            result = jnp.zeros((HD, block), f32)
            for b in range(i + 1):
                rows = slice(b * block, (b + 1) * block)
                result = result + dot_nn(vt[head_rows, rows], (scores[rows, :] * inverse).astype(bf16))
            ot[head_rows, columns] = result
            lse[pl.ds(h, 1), columns] = top + jnp.log(total)
        return carry

    lax.fori_loop(0, HALF_HEADS, one_head, 0)
    both.until(math.inf)

    for j in range(2):
        columns = pl.ds(pl.multiple_of(place.other_block(j) * block, block), block)
        att_out[j] = ot[:, columns].T.astype(bf16)
        copy = remote(
            att_out.at[j], att.at[place.core, j], swap_sems.at[0, j], swap_sems.at[1, j], place.sibling
        )
        copy.start()
        sent.append(copy)
    for j in range(2):
        columns = pl.ds(pl.multiple_of(place.own_block(j) * block, block), block)
        att[place.core, j] = ot[:, columns].T.astype(bf16)
    for j in range(2):
        ref = att.at[1 - place.core, j]
        remote(ref, ref, swap_sems.at[0, j], swap_sems.at[1, j], place.sibling).wait_recv()
        ref = cot_own.at[j]
        remote(ref, ref, cot_sems.at[0, j], cot_sems.at[1, j], place.sibling).wait()
    own_copies[1].wait()
    for copy in keep:
        copy.wait()
    gm.finish_sibling()
    for copy in sent:
        copy.wait_send()
    ga.finish_sends()
    gm.finish_sends()


def backward_kernel(
    dp_size, seq_size, a_layout, m_layout,
    m_slots, x_own_in, n1_in, wqkv_in, qt_in, kt_in, qh_in, kh_in, vh_in, cot_in, att_in, w_proj_in,
    vec, seg_all, lse,
    out_back, grad_back, a_out, m_out,
    g_slots, a_slots, x_own, out_own, d_mid, d_att, d_all, d_n1_in, g_bias, a_wide, m_wide,
    move_sems, swap_sems, norm_sems, load_sems, *refs,
):
    place = Place(seq_size)
    block = x_own.shape[1]
    length = seq_size * block
    mine = place.dp * seq_size + place.z
    count = len(refs) // 2
    sm = make_scatter(dp_size, seq_size, g_slots, refs[:count])
    sa = make_scatter(dp_size, seq_size, a_slots, refs[count:])
    slots_copy = pltpu.make_async_copy(m_slots, g_slots, load_sems.at[1])
    slots_copy.start()
    greet(place.line_peers() + [(place.dp ^ (1 << b), place.z) for b in sm.bits])
    a_slots[...] = jnp.zeros_like(a_slots)
    def mlp(cot, att, w_proj, w_up, w_down, mid, n2, d_n2, total, b_up, gb_up):
        blocks = [slice(j * block, (j + 1) * block) for j in range(2)]
        first_loads = [
            pltpu.make_async_copy(src, dst, load_sems.at[i])
            for i, src, dst in ((0, x_own_in, x_own), (9, att_in, att), (10, w_proj_in, w_proj), (11, cot_in, cot))
        ]
        for copy in first_loads:
            copy.start()
        for copy in first_loads:
            copy.wait()
        for j, rows in enumerate(blocks):
            mid[rows, :] = (
                x_own[j].astype(f32)
                + dot_nn(att[0, rows, :], w_proj[:HALF_COLS, :])
                + dot_nn(att[1, rows, :], w_proj[HALF_COLS:, :])
                + vec[1:2, :]
            )
        slots_copy.wait()
        load_matrix(g_slots, m_layout, 0, 0, w_up)
        load_matrix(g_slots, m_layout, 1, 0, w_down)
        gain = m_layout.vector(g_slots, 0, ROW_D)
        shift = m_layout.vector(g_slots, ROW_D, ROW_D)
        b_down = m_layout.vector(g_slots, MLP_BDOWN, ROW_D)
        b_up[...] = m_layout.vector(g_slots, MLP_BUP, ROW_FF)
        for rows in blocks:
            normal, _ = norm_parts(mid[rows, :])
            n2[rows, :] = (normal * gain + shift).astype(bf16)
        total[...] = jnp.zeros_like(total)
        d_n2[...] = jnp.zeros_like(d_n2)
        inner = math.sqrt(2.0 / math.pi)
        _, _, up_height, up_first, up_shards = m_layout.regions[0]
        _, _, down_height, down_first, _ = m_layout.regions[1]
        turns = FF // FF_STEP // 2

        def step(u, carry):
            for v in range(turns):
                start = pl.multiple_of((u * turns + v) * FF_STEP, FF_STEP)
                columns = pl.ds(start, FF_STEP)
                hidden = dot_nn(n2[...], w_up[:, columns]) + b_up[:, columns]
                square = hidden * hidden
                tanh = jnp.tanh(inner * (hidden + 0.044715 * (square * hidden)))
                cdf = 0.5 * (1.0 + tanh)
                active = (hidden * cdf).astype(bf16)
                slope = cdf + (0.5 * inner) * hidden * (1.0 - tanh * tanh) * (1.0 + (3 * 0.044715) * square)
                low = (dot_nt(cot[...], w_down[columns, :]) * slope).astype(bf16)
                gb_up[:, columns] = jnp.sum(low.astype(f32), axis=0, keepdims=True)
                total[...] += dot_nn(active, w_down[columns, :])
                d_n2[...] += dot_nt(low, w_up[:, columns])
                g_down = dot_tn(active, cot[...]).astype(bf16)
                begin = v * FF_STEP
                for t in range(begin // down_height, (begin + FF_STEP - 1) // down_height + 1):
                    top = max(begin, t * down_height)
                    end = min(begin + FF_STEP, (t + 1) * down_height)
                    slot = down_first + u * (turns * FF_STEP // down_height) + t
                    for j in range(ROW_D):
                        at = j * down_height + top - t * down_height
                        g_slots[slot, at : at + end - top, :] = g_down[
                            top - begin : end - begin, j * LANES : (j + 1) * LANES
                        ]
                g_up = dot_tn(n2[...], low).astype(bf16)
                for j in range(FF_STEP // LANES):
                    at = ((u * turns + v) * (FF_STEP // LANES) + j) * up_height
                    rows = pl.ds(pl.multiple_of(at, up_height), up_height)
                    for s in range(up_shards):
                        g_slots[up_first + s, rows, :] = g_up[
                            s * up_height : (s + 1) * up_height, j * LANES : (j + 1) * LANES
                        ]
            return carry

        lax.fori_loop(0, 2, step, 0)

        gain_sum = jnp.zeros((1, D), f32)
        shift_sum = jnp.zeros((1, D), f32)
        down_sum = jnp.zeros((1, D), f32)
        proj_sum = jnp.zeros((1, D), f32)
        for rows in blocks:
            normal, scale = norm_parts(mid[rows, :])
            grad = d_n2[rows, :]
            cot_rows = cot[rows, :].astype(f32)
            gain_sum += jnp.sum(grad * normal, axis=0, keepdims=True)
            shift_sum += jnp.sum(grad, axis=0, keepdims=True)
            down_sum += jnp.sum(cot_rows, axis=0, keepdims=True)
            d_rows = cot_rows + norm_back(normal, scale, grad, gain)
            d_mid[rows, :] = d_rows
            low = d_rows.astype(bf16)
            n2[rows, :] = low
            proj_sum += jnp.sum(low.astype(f32), axis=0, keepdims=True)
        m_layout.put_vectors(
            g_slots, [(0, gain_sum), (ROW_D, shift_sum), (MLP_BUP, gb_up[...]), (MLP_BDOWN, down_sum)]
        )
        for s, q, there, at in m_layout.beyond():
            g_slots[s, q : q + 1, :] = g_slots[there, at : at + 1, :]
        sm.begin()
        for c in range(2):
            for rows in blocks:
                d_att[c, rows, :] = dot_nt(n2[rows, :], w_proj[c * HALF_COLS : (c + 1) * HALF_COLS, :]).astype(bf16)
        for j in range(2):
            src = d_att.at[1 - place.core, pl.ds(j * block, block)]
            remote(
                src, d_all.at[place.own_block(j)], swap_sems.at[0, j], swap_sems.at[1, j], place.sibling
            ).start()
        steps.until(BACKWARD_FIRST)
        for j, rows in enumerate(blocks):
            out_own[rows, :] = (mid[rows, :] + total[rows, :] + b_down).astype(bf16)
            to, micro = place.home(j)
            remote(
                out_own.at[pl.ds(j * block, block)], out_back.at[micro], move_sems.at[0, j], move_sems.at[1, micro], to
            ).start()
        g_bias[...] = proj_sum
        _, _, height, first, shards = a_layout.regions[1]
        for c in range(2):
            g_part = dot_tn(att[c], n2[...]).astype(bf16)
            for t in range(shards // 2):
                for j in range(ROW_D):
                    a_slots[first + c * (shards // 2) + t, j * height : (j + 1) * height, :] = g_part[
                        t * height : (t + 1) * height, j * LANES : (j + 1) * LANES
                    ]

    tokens = 2 * block
    steps = Steps([(time, (sm, event)) for time, event in sm.events()])
    pl.run_scoped(
        mlp,
        pltpu.VMEM((tokens, D), bf16), pltpu.VMEM((2, tokens, HALF_COLS), bf16), pltpu.VMEM((D, D), bf16),
        pltpu.VMEM((D, FF), bf16), pltpu.VMEM((FF, D), bf16),
        pltpu.VMEM((tokens, D), f32), pltpu.VMEM((tokens, D), bf16),
        pltpu.VMEM((tokens, D), f32), pltpu.VMEM((tokens, D), f32),
        pltpu.VMEM((1, FF), f32), pltpu.VMEM((1, FF), f32),
    )

    def attention(
        n1, wqkv, qt, kt, qh, kh, vh, dt, dh, seg_col, p_piece, d_piece, dk, dv, dqt, dm, d_n1
    ):
        loads = [
            pltpu.make_async_copy(src, dst, load_sems.at[2 + i])
            for i, (src, dst) in enumerate(
                [(qt_in, qt), (kt_in, kt), (qh_in, qh), (kh_in, kh), (vh_in, vh), (n1_in, n1), (wqkv_in, wqkv)]
            )
        ]
        for copy in loads:
            copy.start()
        for j in range(2):
            d_all[place.own_block(j)] = d_att[place.core, j * block : (j + 1) * block, :]
        segment_columns(seg_all, seg_col, block)
        steps.until(BACKWARD_START - 3)
        for j in range(2):
            ref = d_all.at[place.other_block(j)]
            remote(ref, ref, swap_sems.at[0, j], swap_sems.at[1, j], place.sibling).wait_recv()

        def spread(t, carry):
            rows = pl.ds(pl.multiple_of(t * block, block), block)
            piece = d_all[t]
            dt[:, rows] = piece.astype(f32).T.astype(bf16)
            split_heads(piece, dh, rows)
            return carry

        lax.fori_loop(0, seq_size, spread, 0)
        steps.until(BACKWARD_START)
        unit = HEAD_BACKWARD / (seq_size * (seq_size + 1) // 2)
        points = [
            ((i, side, pair), unit * (i + 1))
            for i in reversed(range(seq_size))
            for pair in range(HALF_HEADS // 2)
            for side in range(2)
        ]
        plan = steps.plan(BACKWARD_START, points)
        for copy in loads[:5]:
            copy.wait()

        def query_block(i):
            columns = slice(i * block, (i + 1) * block)

            def one_pair(pair, carry):
                pair_rows = pl.ds(pl.multiple_of(pair * LANES, LANES), LANES)
                for side in range(2):
                    handle([plan[i, side, turn] for turn in range(HALF_HEADS // 2)], pair)
                    h = 2 * pair + side
                    head_rows = pl.ds(pl.multiple_of(h * HD, HD), HD)
                    query = qt[pair_rows, columns]
                    d_query = dt[pair_rows, columns]
                    level = lse[pl.ds(h, 1), columns]
                    delta = jnp.zeros((1, block), f32)
                    for b in range(i + 1):
                        rows = slice(b * block, (b + 1) * block)
                        probs = jnp.exp(
                            keep_allowed(dot_nn(kh[h, rows, :], query), seg_col, seg_all, b, i, block) - level
                        )
                        d_probs = dot_nn(vh[h, rows, :], d_query)
                        delta = delta + jnp.sum(probs * d_probs, axis=0, keepdims=True)
                        p_piece[rows, :] = probs
                        d_piece[rows, :] = d_probs
                    result = jnp.zeros((HD, block), f32)
                    for b in range(i + 1):
                        rows = slice(b * block, (b + 1) * block)
                        probs = p_piece[rows, :]
                        d_scores = (probs * (d_piece[rows, :] - delta)).astype(bf16)
                        key_part = dot_nn(d_scores, qh[h, columns, :])
                        value_part = dot_nn(probs.astype(bf16), dh[h, columns, :])
                        if i == seq_size - 1 and side == 0:
                            dk[pair, rows, :] = key_part
                            dv[pair, rows, :] = value_part
                        else:
                            dk[pair, rows, :] += key_part
                            dv[pair, rows, :] += value_part
                        result = result + dot_nn(kt[head_rows, rows], d_scores)
                    dqt[head_rows, :] = result * (1.0 / math.sqrt(HD))
                return carry

            lax.fori_loop(0, HALF_HEADS // 2, one_pair, 0)
            dm[0, columns, :] = dqt[...].T.astype(bf16)
            for section, part in ((1, dk), (2, dv)):
                for pair in range(HALF_HEADS // 2):
                    dm[section, columns, pair * LANES : (pair + 1) * LANES] = part[pair, columns, :].astype(bf16)

        def to_norm(t):
            rows = pl.ds(pl.multiple_of(t * block, block), block)
            return (
                dot_nt(dm[0, rows, :], wqkv[0]) + dot_nt(dm[1, rows, :], wqkv[1]) + dot_nt(dm[2, rows, :], wqkv[2])
            )

        def share_norm(j):
            d_n1[j] = to_norm(place.other_block(j))
            remote(d_n1.at[j], d_n1_in.at[j], norm_sems.at[0, j], norm_sems.at[1, j], place.sibling).start()

        def finish_input(j):
            ref = d_n1_in.at[j]
            remote(ref, ref, norm_sems.at[0, j], norm_sems.at[1, j], place.sibling).wait_recv()
            grad = to_norm(place.own_block(j)) + d_n1_in[j]
            normal, scale = norm_parts(x_own[j].astype(f32))
            x_own[j] = (d_mid[j * block : (j + 1) * block, :] + norm_back(normal, scale, grad, gain)).astype(bf16)
            to, micro = place.home(j)
            remote(x_own.at[j], grad_back.at[micro], move_sems.at[2, j], move_sems.at[3, micro], to).start()
            return jnp.sum(grad * normal, axis=0, keepdims=True), jnp.sum(grad, axis=0, keepdims=True)

        gain = vec[0:1, :]
        query_block(3)
        query_block(2)
        for copy in loads[5:]:
            copy.wait()
        share_norm(1)
        query_block(1)
        gain_sum, shift_sum = finish_input(1)
        query_block(0)
        share_norm(0)
        now = BACKWARD_START + HALF_HEADS * HEAD_BACKWARD
        steps.until(now)
        _, _, height, first, shards = a_layout.regions[0]
        for section in range(3):
            part = dot_tn(n1[...], dm[section]).astype(bf16)
            for j in range(ROW_HALF):
                at = (section * ROW_D + place.core * ROW_HALF + j) * height
                rows = pl.ds(pl.multiple_of(at, height), height)
                for s in range(shards):
                    a_slots[first + s, rows, :] = part[s * height : (s + 1) * height, j * LANES : (j + 1) * LANES]
        steps.until(now + 4)
        more_gain, more_shift = finish_input(0)
        sums = []
        for section in (0, 2):
            half = jnp.sum(dm[section].astype(f32), axis=0, keepdims=True)
            zero = jnp.zeros_like(half)
            first_half = place.core == 0
            sums.append(
                jnp.concatenate([jnp.where(first_half, half, zero), jnp.where(first_half, zero, half)], axis=1)
            )
        a_layout.put_vectors(
            a_slots,
            [
                (0, gain_sum + more_gain), (ROW_D, shift_sum + more_shift),
                (ATTN_BQ, sums[0]), (ATTN_BV, sums[1]), (ATTN_BPROJ, g_bias[...]),
            ],
        )
        for s, q, there, at in a_layout.beyond():
            a_slots[s, q : q + 1, :] = a_slots[there, at : at + 1, :]
        sa.begin()
        Steps(steps.queue + [(now + time, (sa, event)) for time, event in sa.events(*A_BACK)]).until(math.inf)
        sm.finish()
        m_layout.unpack(sm.out, m_wide, m_out, mine)
        sa.finish()
        a_layout.unpack(sa.out, a_wide, a_out, mine)
        for micro in range(2):
            for kind, ref in ((1, out_back), (3, grad_back)):
                remote(
                    ref.at[micro], ref.at[micro], move_sems.at[0, micro], move_sems.at[kind, micro], place.sibling
                ).wait_recv()
        for j in range(2):
            for ref, sem in (
                (d_all, swap_sems.at[0, j]), (out_back, move_sems.at[0, j]),
                (d_n1_in, norm_sems.at[0, j]), (grad_back, move_sems.at[2, j]),
            ):
                remote(ref.at[0], ref.at[0], sem, sem, place.sibling).wait_send()

    pl.run_scoped(
        attention,
        *[
            pltpu.VMEM(ref.shape, ref.dtype)
            for ref in (n1_in, wqkv_in, qt_in, kt_in, qh_in, kh_in, vh_in)
        ],
        pltpu.VMEM((HALF_COLS, length), bf16),
        pltpu.VMEM((HALF_HEADS, length, LANES), bf16),
        pltpu.VMEM((length, LANES), jnp.int32),
        pltpu.VMEM((length, block), f32),
        pltpu.VMEM((length, block), f32),
        pltpu.VMEM((HALF_HEADS // 2, length, LANES), f32),
        pltpu.VMEM((HALF_HEADS // 2, length, LANES), f32),
        pltpu.VMEM((HALF_COLS, block), f32),
        pltpu.VMEM((3, length, HALF_COLS), bf16),
        pltpu.VMEM((2, block, D), f32),
    )


class Scatter:
    def __init__(self, dp_size, seq_size, slots, out, core_in, level_in, seq_in, send_sems, recv_sems, seq_sems):
        self.n = seq_size
        self.bits = list(range(1, dp_size.bit_length() - 1))
        self.masks = [m << 1 for m in range(1 << len(self.bits))]
        self.dp = lax.axis_index("dp")
        self.z = lax.axis_index("seq")
        self.slots, self.out = slots, out
        self.core_in, self.level_in, self.seq_in = core_in, level_in, seq_in
        rows = slots.shape[1]
        half = rows // 32 * 16
        self.parts = [(0, half), (half, rows - half)]
        self.orders = [self.bits[::-1], self.bits]
        self.send_sems, self.recv_sems, self.seq_sems = send_sems, recv_sems, seq_sems
        self.started = []
        self.indices = {}

    def index(self, *key):
        return self.indices.setdefault(key, len(self.indices))

    def slot(self, mask, k):
        return (self.dp ^ mask) * self.n + nearest(self.z, self.n, k)

    def send(self, src, dst, to, key, part=None):
        sem = self.recv_sems.at[self.index(*key)] if isinstance(key, tuple) else key
        remote(src, dst, self.send_sems.at[len(self.started)], sem, to).start()
        self.started.append(part)

    def wait(self, ref, key):
        remote(ref, ref, self.send_sems.at[0], self.recv_sems.at[self.index(*key)], (self.dp, self.z)).wait_recv()

    def turn(self):
        return list(range(self.n))[::-1]

    def begin(self):
        for k in self.turn():
            for mask in self.masks[::-1]:
                i = self.masks.index(mask)
                self.send(
                    self.slots.at[self.slot(mask ^ 1, k)], self.core_in.at[i, k], (self.dp ^ 1, self.z), ("c", i, k)
                )

    def add(self, mask, k, part, term):
        start, size = (0, self.slots.shape[1]) if part is None else self.parts[part]
        rows = pl.ds(start, size)
        index = self.slot(mask, k)
        self.slots[index, rows, :] = (self.slots[index, rows, :].astype(f32) + term.astype(f32)).astype(bf16)

    def view(self, mask, k, part):
        start, size = self.parts[part]
        return self.slots.at[self.slot(mask, k), pl.ds(start, size)]

    def cell(self, part, level, mask):
        free = [b for b in self.bits if b not in self.orders[part][: level + 1]]
        return sum(1 << n for n, b in enumerate(free) if mask >> b & 1)

    def pass_on(self, part, level, mask, k):
        order = self.orders[part]
        src = self.view(mask, k, part)
        if level == len(order):
            return
        bit = 1 << order[level]
        if mask & bit:
            rest = mask ^ bit
            dst = self.level_in[part][level].at[self.cell(part, level, rest), k]
            self.send(src, dst, (self.dp ^ bit, self.z), ("l", part, level, rest, k), part)

    def events(self, begin=6.0, gap=9.6, level_gap=(9.0, 19.0), seq_gap=0.5):
        out = []
        for turn, k in enumerate(self.turn()):
            at = begin + max(0, turn - 1) * gap
            for mask in self.masks[::-1]:
                out.append((at, ("c", mask, k)))
            at = begin + turn * gap
            for level in range(len(self.bits)):
                for part in (0, 1):
                    past = self.orders[part][: level + 1]
                    for mask in self.masks[::-1]:
                        if not any(mask >> b & 1 for b in past):
                            out.append((at + level_gap[min(level, 1)], ("l", part, level, mask, k)))
            if k:
                for part in (0, 1):
                    out.append((at + level_gap[min(len(self.bits) - 1, 1)] + seq_gap, ("z", part, k)))
        return sorted(out, key=lambda e: e[0])

    def step(self, event):
        if event[0] == "c":
            _, mask, k = event
            i = self.masks.index(mask)
            self.wait(self.core_in.at[i, k], ("c", i, k))
            self.add(mask, k, None, self.core_in[i, k])
            for part in (0, 1):
                self.pass_on(part, 0, mask, k)
            return
        if event[0] == "z":
            _, part, k = event
            self.along(part, k)
            return
        _, part, level, mask, k = event
        index = self.cell(part, level, mask)
        self.wait(self.level_in[part][level].at[index, k], ("l", part, level, mask, k))
        self.add(mask, k, part, self.level_in[part][level][index, k])
        self.pass_on(part, level + 1, mask, k)

    def from_side(self, part, place, side):
        index = place if side == 0 else self.n
        ref = self.seq_in[part].at[index]
        remote(ref, ref, self.send_sems.at[0], self.seq_sems.at[part, index], (self.dp, self.z)).wait_recv()
        return self.seq_in[part][index].astype(f32)

    def along(self, part, k):
        place = nearest(self.z, self.n, k)
        up = place > self.z

        @pl.when((up & (self.z > 0)) | (jnp.logical_not(up) & (self.z < self.n - 1)))
        def _():
            self.add(0, k, part, self.from_side(part, place, 0))

        to = jnp.where(up, self.z + 1, self.z - 1)
        index = jnp.where((to == place) & jnp.logical_not(up), self.n, place)
        self.send(
            self.view(0, k, part), self.seq_in[part].at[index], (self.dp, to), self.seq_sems.at[part, index], part
        )

    def finish(self):
        index = self.slot(0, 0)
        for part in (0, 1):
            start, size = self.parts[part]
            rows = slice(start, start + size)
            self.out[rows, :] = self.slots[index, rows, :].astype(f32)
            for side, there in ((0, self.z > 0), (1, self.z < self.n - 1)):

                @pl.when(there)
                def _():
                    self.out[rows, :] += self.from_side(part, self.z, side)

        for index, part in enumerate(self.started):
            start, size = (0, self.slots.shape[1]) if part is None else self.parts[part]
            ref = self.slots.at[0, pl.ds(start, size)]
            remote(ref, ref, self.send_sems.at[index], self.recv_sems.at[0], (self.dp, self.z)).wait_send()


def scatter_scratch(dp_size, seq_size, rows):
    bits = dp_size.bit_length() - 2
    masks = 1 << bits
    half = rows // 32 * 16
    sizes = [half, rows - half]
    shapes = [pltpu.VMEM((masks, seq_size, rows, LANES), bf16), pltpu.VMEM((rows, LANES), f32)]
    for size in sizes:
        for level in range(bits):
            shapes.append(pltpu.VMEM((masks >> (level + 1), seq_size, size, LANES), bf16))
    for size in sizes:
        shapes.append(pltpu.VMEM((seq_size + 1, size, LANES), bf16))
    count = masks * seq_size + 2 * (masks - 1) * seq_size + 2 * (seq_size - 1)
    shapes += [
        pltpu.SemaphoreType.DMA((count,)),
        pltpu.SemaphoreType.DMA((count,)),
        pltpu.SemaphoreType.DMA((2, seq_size + 1)),
    ]
    return shapes


def make_scatter(dp_size, seq_size, slots, refs):
    bits = dp_size.bit_length() - 2
    core_in, total, *rest = refs
    level_in = [rest[:bits], rest[bits : 2 * bits]]
    rest = rest[2 * bits :]
    return Scatter(dp_size, seq_size, slots, total, core_in, level_in, rest[:2], *rest[2:])


ANY = pl.BlockSpec(memory_space=pl.ANY)
LOCAL = pl.BlockSpec(memory_space=pltpu.VMEM)


def shape_of(dims, dtype):
    return jax.ShapeDtypeStruct(dims, dtype)


def per_chip_sequence(inputs, segments, attn_params, mlp_params, cotangent):
    dp_size, n = lax.axis_size("dp"), lax.axis_size("seq")
    devices = dp_size * n
    block = inputs.shape[2]
    length = n * block
    tokens = 2 * block
    a_layout = attn_layout(attn_params.shape[0] // LANES, devices)
    m_layout = mlp_layout_of(mlp_params.shape[0] // LANES, devices)
    a_raw, m_raw = to_rows(attn_params), to_rows(mlp_params)
    a_rows, m_rows = a_layout.slot_rows, m_layout.slot_rows
    wide = [pltpu.VMEM((raw.shape[0] + 2 * MARGIN, LANES), f32) for raw in (a_raw, m_raw)]
    seg_rows = jnp.pad(segments.reshape(2, block // LANES, LANES), ((0, 0), (0, 8 - block // LANES), (0, 0)))
    send, recv = gather_counts(dp_size, n)
    dma = pltpu.SemaphoreType.DMA
    across = shape_of((HALF_COLS, length), bf16)
    heads = shape_of((HALF_HEADS, length, LANES), bf16)
    own = shape_of((2, block, D), bf16)
    kept = [
        shape_of((length, D), bf16), shape_of((3, D, HALF_COLS), bf16), across, across, heads, heads, heads,
    ]
    (
        m_slots, cot_own, n1, wqkv, qt, kt, qh, kh, vh, x_own, w_proj, vec, seg_all, lse, att,
    ) = pl.pallas_call(
        functools.partial(forward_kernel, dp_size, n, a_layout, m_layout),
        out_shape=[shape_of((devices, m_rows, LANES), bf16), own]
        + kept
        + [
            own, shape_of((D, D), bf16), shape_of((8, D), f32),
            shape_of((n, 8, LANES), jnp.int32), shape_of((8, length), f32), shape_of((2, 2, block, HALF_COLS), bf16),
        ],
        in_specs=[ANY] * 3 + [LOCAL] * 2,
        out_specs=[ANY] * 9 + [LOCAL] * 6,
        scratch_shapes=[pltpu.VMEM(like.shape, like.dtype) for like in kept]
        + [
            pltpu.VMEM((devices, a_rows, LANES), bf16),
            pltpu.VMEM((a_rows, LANES), bf16),
            pltpu.VMEM((m_rows, LANES), bf16),
        ]
        + wide
        + [
            pltpu.VMEM((n, block, D), bf16),
            pltpu.VMEM((HALF_COLS, length), bf16),
            pltpu.VMEM((length, LANES), jnp.int32),
            pltpu.VMEM((length, block), f32),
            pltpu.VMEM((HALF_COLS, length), f32),
            pltpu.VMEM((2, block, HALF_COLS), bf16),
            dma((send,)), dma((recv,)), dma((send,)), dma((recv,)), dma((2,)),
            dma((3, 4)), dma((3, n)), dma((2, 2)), dma((2, 2)), dma((len(kept),)),
        ],
        compiler_params=pltpu.CompilerParams(collective_id=0, has_side_effects=True, vmem_limit_bytes=VMEM_LIMIT),
    )(inputs[:, 0], seg_rows, cotangent[:, 0], a_raw, m_raw)

    out_back, grad_back, a_sum, m_sum = pl.pallas_call(
        functools.partial(backward_kernel, dp_size, n, a_layout, m_layout),
        out_shape=[own, own, shape_of((a_layout.rows, LANES), f32), shape_of((m_layout.rows, LANES), f32)],
        in_specs=[ANY] * 12 + [LOCAL] * 3,
        out_specs=[ANY] * 2 + [LOCAL] * 2,
        scratch_shapes=[
            pltpu.VMEM((devices, m_rows, LANES), bf16),
            pltpu.VMEM((devices, a_rows, LANES), bf16),
            pltpu.VMEM((2, block, D), bf16),
            pltpu.VMEM((tokens, D), bf16),
            pltpu.VMEM((tokens, D), f32),
            pltpu.VMEM((2, tokens, HALF_COLS), bf16),
            pltpu.VMEM((n, block, HALF_COLS), bf16),
            pltpu.VMEM((2, block, D), f32),
            pltpu.VMEM((1, D), f32),
        ]
        + wide
        + [dma((4, 2)), dma((2, 2)), dma((2, 2)), dma((12,))]
        + scatter_scratch(dp_size, n, m_rows)
        + scatter_scratch(dp_size, n, a_rows),
        compiler_params=pltpu.CompilerParams(collective_id=1, has_side_effects=True, vmem_limit_bytes=VMEM_LIMIT),
    )(
        m_slots, x_own, n1, wqkv, qt, kt, qh, kh, vh,
        cot_own.reshape(tokens, D), att.reshape(2, tokens, HALF_COLS), w_proj, vec, seg_all, lse,
    )
    return (
        out_back[:, None],
        grad_back.astype(f32)[:, None],
        a_sum.reshape(-1),
        m_sum.reshape(-1),
    )


def solution(mesh):
    in_specs = (
        P(None, "dp", "seq", None),
        P(None, "dp", "seq"),
        P(("dp", "seq")),
        P(("dp", "seq")),
        P(None, "dp", "seq", None),
    )
    out_specs = (
        P(None, "dp", "seq", None),
        P(None, "dp", "seq", None),
        P(("dp", "seq")),
        P(("dp", "seq")),
    )
    one_each = mesh.shape["seq"] == 4 and mesh.shape["dp"] % 2 == 0
    return jax.shard_map(
        per_chip_sequence if one_each else per_device, mesh=mesh, in_specs=in_specs, out_specs=out_specs, check_vma=False
    )
```

```python
import functools
from functools import partial
import math

import jax
import jax.numpy as jnp
from jax import lax
from jax.experimental import pallas as pl
from jax.experimental.pallas import tpu as pltpu
from jax.sharding import PartitionSpec as P

D = 768
H = 12
HD = 64
FF = 3072


norm_eps = 1e-05
score_floor = -1e30
key_block = 512


def attention_layout():
    return [(D,), (D,), (D, 3 * D), (D,), (D,), (D, D), (D,)]


def mlp_layout():
    return [(D,), (D,), (D, FF), (FF,), (FF, D), (D,)]


def unpack_params(flat_vector, layout):
    offset = 0
    result = []
    for dims_entry in layout:
        amount = math.prod(dims_entry)
        result.append(lax.slice_in_dim(flat_vector, offset, offset + amount).reshape(dims_entry))
        offset += amount
    return result


def layer_norm(values, gain, shift):
    average = jnp.mean(values, axis=-1, keepdims=True)
    centred = values - average
    spread = jnp.mean(centred * centred, axis=-1, keepdims=True)
    return centred * lax.rsqrt(spread + norm_eps) * gain + shift


def gelu_tanh(values):
    return jax.nn.gelu(values, approximate=True)


def pack_grads(grad_list, total_size):
    flat_parts = [part_grad.reshape(-1) for part_grad in grad_list]
    used_total = sum((part_grad.size for part_grad in grad_list))
    flat_parts.append(jnp.zeros((total_size - used_total,), jnp.float32))
    return jnp.concatenate(flat_parts)


def fetch_params(attn_params, mlp_params):
    gathered = (
        lax.all_gather(attn_params, ("dp", "seq"), axis=0, tiled=True),
        lax.all_gather(mlp_params, ("dp", "seq"), axis=0, tiled=True),
    )
    return (
        unpack_params(gathered[0], attention_layout()),
        unpack_params(gathered[1], mlp_layout()),
    )


def send_grads(attn_list, mlp_list, attn_total, mlp_total):
    return (
        lax.psum_scatter(
            pack_grads(attn_list, attn_total), ("dp", "seq"), scatter_dimension=0, tiled=True
        ),
        lax.psum_scatter(
            pack_grads(mlp_list, mlp_total), ("dp", "seq"), scatter_dimension=0, tiled=True
        ),
    )


def fold_keys(key_rows, key_segs, fold_step, start_carry):
    return fold_step(
        start_carry,
        (
            lax.all_gather(key_rows, "seq", axis=0, tiled=True),
            lax.all_gather(key_segs, "seq", axis=0, tiled=True),
        ),
        jnp.int32(0),
    )


def over_blocks(block_step, carry_now, key_piece, key_start):
    piece_rows = key_piece[0].shape[0]
    step_rows = math.gcd(piece_rows, key_block)

    def loop_step(index_block, carry_in):
        offset = index_block * step_rows
        sub_piece = tuple(
            (lax.dynamic_slice_in_dim(member, offset, step_rows, 0) for member in key_piece)
        )
        return block_step(carry_in, sub_piece, offset)

    return lax.fori_loop(0, piece_rows // step_rows, loop_step, carry_now)


def block_scores(query_heads, query_segs, query_pos, kv_rows, key_segs, key_start):
    key_heads = kv_rows[:, :D].reshape(-1, H, HD)
    scores = jnp.einsum(
        "qhd,khd->hqk", query_heads, key_heads, preferred_element_type=jnp.float32
    ) * (1.0 / math.sqrt(HD))
    key_pos = key_start + jnp.arange(kv_rows.shape[0], dtype=jnp.int32)
    allowed = (query_segs[:, None] == key_segs[None, :]) & (key_pos[None, :] <= query_pos[:, None])
    return (jnp.where(allowed[None], scores, score_floor), key_heads)


MESH = pl.DeviceIdType.MESH
LANES = 128

def pad_rows(rows):
    return -(-rows // 16) * 16


def nearest(z, n, i):
    last = n - 1
    high = z > last - z
    near = jnp.where(high, last - z, z)
    step = (i // 2) if i % 2 == 0 else -((i + 1) // 2)
    found = jnp.where(i <= 2 * near, near + step, i)
    return jnp.where(high, last - found, found)


class Gather:
    def __init__(self, dp_size, seq_size, own, slots, send_sems, recv_sems):
        self.n = seq_size
        self.bits = list(range(1, dp_size.bit_length() - 1))
        self.dp = lax.axis_index("dp")
        self.z = lax.axis_index("seq")
        self.own, self.slots = own, slots
        self.rows = own.shape[0]
        half = self.rows // 32 * 16
        self.parts = [(0, half), (half, self.rows - half)]
        self.orders = [self.bits, self.bits[::-1]]
        self.send_sems, self.recv_sems = send_sems, recv_sems
        self.started = []

    def peers(self):
        out = [(self.dp, lax.rem(self.z + k, self.n)) for k in range(1, self.n)]
        return out + [(self.dp ^ (1 << b), self.z) for b in [0] + self.bits]

    def place(self, i):
        return nearest(self.z, self.n, i)

    def view(self, mask, i, part):
        index = (self.dp ^ mask) * self.n + self.place(i)
        start, size = self.parts[part]
        return self.slots.at[index, pl.ds(start, size)]

    def source(self, mask, i, part):
        if mask == 0 and i == 0:
            start, size = self.parts[part]
            return self.own.at[pl.ds(start, size)]
        return self.view(mask, i, part)

    def recv_sem(self, sibling, part, mask, i):
        count = 1 << len(self.bits)
        return self.recv_sems.at[((sibling * 2 + part) * count + (mask >> 1)) * self.n + self.place(i)]

    def send(self, mask, i, part, to, recv_sem, when=None):
        index = len(self.started)
        self.started.append((part, when))

        def start():
            pltpu.make_async_remote_copy(
                src_ref=self.source(mask, i, part), dst_ref=self.view(mask, i, part),
                send_sem=self.send_sems.at[index], recv_sem=recv_sem, device_id=to, device_id_type=MESH,
            ).start()

        if when is None:
            start()
        else:
            pl.when(when())(start)

    def wait(self, sibling, part, mask, i):
        view = self.view(mask ^ sibling, i, part)
        pltpu.make_async_remote_copy(
            src_ref=view, dst_ref=view, send_sem=self.send_sems.at[0],
            recv_sem=self.recv_sem(sibling, part, mask, i),
            device_id=(self.dp, self.z), device_id_type=MESH,
        ).wait_recv()

    def along(self, i, part, up):
        if i == 0:
            to = self.z + 1 if up else self.z - 1
        else:
            to = jnp.where(self.place(i) < self.z, self.z + 1, self.z - 1)

        def when():
            if i == 0:
                return (self.z < self.n - 1) if up else (self.z > 0)
            below = self.place(i) < self.z
            return (below & (self.z < self.n - 1)) | (jnp.logical_not(below) & (self.z > 0))

        self.send(0, i, part, (self.dp, to), self.recv_sem(0, part, 0, i), when)

    def forward(self, part, mask, i):
        if mask == 0 and i:
            self.along(i, part, True)
        order = self.orders[part]
        for level in range(len(order)):
            if not any(mask >> b & 1 for b in order[level:]):
                bit = 1 << order[level]
                self.send(mask, i, part, (self.dp ^ bit, self.z), self.recv_sem(0, part, mask | bit, i))
        self.send(mask, i, part, (self.dp ^ 1, self.z), self.recv_sem(1, part, mask, i))

    def begin_seq(self, part):
        for up in (True, False):
            self.along(0, part, up)

    def begin_bits(self):
        for level in range(len(self.bits)):
            for part in (0, 1):
                bit = 1 << self.orders[part][level]
                self.send(0, 0, part, (self.dp ^ bit, self.z), self.recv_sem(0, part, bit, 0))
        for part in (0, 1):
            self.send(0, 0, part, (self.dp ^ 1, self.z), self.recv_sem(1, part, 0, 0))

    def begin(self):
        self.begin_seq(0)
        self.begin_seq(1)
        self.begin_bits()

    def events(self, seq_times=None, own=0.0, level_gap=1.0):
        if seq_times is None:
            seq_times = [(i + 1.0, i + 1.5) for i in range(self.n - 1)]
        out = []
        for i in range(self.n):
            for part in (0, 1):
                at = seq_times[i - 1][part] if i else own
                if i:
                    out.append((at, (part, 0, i)))
                order = self.orders[part]
                for level in range(len(order)):
                    for low in range(1 << level):
                        mask = 1 << order[level]
                        for n in range(level):
                            if low >> n & 1:
                                mask |= 1 << order[n]
                        out.append((at + (level + 1) * level_gap, (part, mask, i)))
        return sorted(out, key=lambda e: e[0])

    def step(self, event):
        part, mask, i = event
        self.wait(0, part, mask, i)
        self.forward(part, mask, i)

    def finish_sibling(self):
        for part, mask, i in [(0, 0, 0), (1, 0, 0)] + [event for _, event in self.events()]:
            self.wait(1, part, mask, i)

    def finish_sends(self):
        for index, (part, when) in enumerate(self.started):

            def wait(index=index, part=part):
                start, size = self.parts[part]
                view = self.slots.at[0, pl.ds(start, size)]
                pltpu.make_async_remote_copy(
                    src_ref=view, dst_ref=view, send_sem=self.send_sems.at[index], recv_sem=self.recv_sems.at[0],
                    device_id=(self.dp, self.z), device_id_type=MESH,
                ).wait_send()

            if when is None:
                wait()
            else:
                pl.when(when())(wait)


def gather_counts(dp_size, seq_size):
    bits = dp_size.bit_length() - 2
    masks = 1 << bits
    recv = 4 * masks * seq_size
    send = 2 * (seq_size + 1 + seq_size * (masks - 1) + seq_size * masks)
    return send, recv


def gather_kernel(dp_size, seq_size, a_own, m_own, a_slots, m_slots, a_send, a_recv, m_send, m_recv, own_sems):
    ga = Gather(dp_size, seq_size, a_own, a_slots, a_send, a_recv)
    gm = Gather(dp_size, seq_size, m_own, m_slots, m_send, m_recv)
    barrier = pltpu.get_barrier_semaphore()
    peers = ga.peers()
    for peer in peers:
        pl.semaphore_signal(barrier, inc=1, device_id=peer, device_id_type=MESH)
    pl.semaphore_wait(barrier, len(peers))
    ca = pltpu.make_async_copy(a_own, a_slots.at[ga.dp * ga.n + ga.z], own_sems.at[0])
    cm = pltpu.make_async_copy(m_own, m_slots.at[ga.dp * ga.n + ga.z], own_sems.at[1])
    ca.start()
    cm.start()
    ga.begin()
    gm.begin()
    for _, event in ga.events():
        ga.step(event)
    for _, event in gm.events():
        gm.step(event)
    ca.wait()
    cm.wait()
    ga.finish_sibling()
    gm.finish_sibling()
    ga.finish_sends()
    gm.finish_sends()


def to_rows(flat):
    rows = flat.shape[0] // LANES
    return jnp.pad(flat.reshape(rows, LANES), ((0, pad_rows(rows) - rows), (0, 0)))


def gather_params(attn, mlp, dp_size, seq_size):
    a, m = to_rows(attn), to_rows(mlp)
    devices = dp_size * seq_size
    send, recv = gather_counts(dp_size, seq_size)
    return pl.pallas_call(
        functools.partial(gather_kernel, dp_size, seq_size),
        out_shape=[jax.ShapeDtypeStruct((devices,) + a.shape, jnp.bfloat16), jax.ShapeDtypeStruct((devices,) + m.shape, jnp.bfloat16)],
        in_specs=[pl.BlockSpec(memory_space=pl.ANY)] * 2,
        out_specs=[pl.BlockSpec(memory_space=pl.ANY)] * 2,
        scratch_shapes=[pltpu.SemaphoreType.DMA((send,)), pltpu.SemaphoreType.DMA((recv,)),
                        pltpu.SemaphoreType.DMA((send,)), pltpu.SemaphoreType.DMA((recv,)), pltpu.SemaphoreType.DMA((2,))],
        compiler_params=pltpu.CompilerParams(collective_id=0, has_side_effects=True),
    )(a, m)


def per_device(inputs, segments, attn_params, mlp_params, cotangent):
    micro_count = inputs.shape[0]
    local_rows = inputs.shape[2]
    seq_length = local_rows * lax.axis_size("seq")
    attn_total = attn_params.shape[0] * lax.axis_size(("dp", "seq"))
    mlp_total = mlp_params.shape[0] * lax.axis_size(("dp", "seq"))
    query_pos = lax.axis_index("seq") * local_rows + jnp.arange(local_rows, dtype=jnp.int32)
    score_scale = 1.0 / math.sqrt(HD)
    out_rows = []
    grad_rows = []
    attn_sums = None
    mlp_sums = None
    shard_sums = None
    attn_slots, mlp_slots = gather_params(attn_params, mlp_params, lax.axis_size("dp"), lax.axis_size("seq"))
    attn_set = unpack_params(
        attn_slots[:, : attn_params.shape[0] // LANES].reshape(-1), attention_layout()
    )
    mlp_set = unpack_params(
        mlp_slots[:, : mlp_params.shape[0] // LANES].reshape(-1), mlp_layout()
    )
    for micro_index in range(micro_count):
        gain_one, shift_one, w_qkv, bias_query, bias_value, w_proj, bias_proj = attn_set
        gain_two, shift_two, w_up, bias_up, w_down, bias_down = mlp_set
        input_rows = inputs[micro_index, 0].astype(jnp.float32)
        query_segs = segments[micro_index, 0]
        normed_one, norm_one_back = jax.vjp(
            layer_norm, input_rows, gain_one.astype(jnp.float32), shift_one.astype(jnp.float32)
        )
        normed_one_low = normed_one.astype(jnp.bfloat16)
        merged_rows = jnp.dot(normed_one_low, w_qkv, preferred_element_type=jnp.float32)
        query_low = (merged_rows[:, :D] + bias_query.astype(jnp.float32)).astype(jnp.bfloat16)
        kv_local = jnp.concatenate(
            [merged_rows[:, D : 2 * D], merged_rows[:, 2 * D :] + bias_value.astype(jnp.float32)],
            axis=1,
        ).astype(jnp.bfloat16)
        query_heads = query_low.reshape(local_rows, H, HD)

        def max_step(carry_in, sub_piece, key_start):
            scores, key_heads = block_scores(
                query_heads, query_segs, query_pos, sub_piece[0], sub_piece[1], key_start
            )
            running_top, running_total = carry_in
            new_top = jnp.maximum(running_top, jnp.max(scores, axis=-1))
            new_total = running_total * jnp.exp(running_top - new_top) + jnp.sum(
                jnp.exp(scores - new_top[..., None]), axis=-1
            )
            return (new_top, new_total)

        top_start = jnp.full((H, local_rows), score_floor, jnp.float32)
        row_top, row_total = fold_keys(
            kv_local,
            query_segs,
            partial(over_blocks, max_step),
            (top_start, jnp.zeros((H, local_rows), jnp.float32)),
        )
        log_total = row_top + jnp.log(row_total)

        def value_step(carry_in, sub_piece, key_start):
            scores, key_heads = block_scores(
                query_heads, query_segs, query_pos, sub_piece[0], sub_piece[1], key_start
            )
            probs = jnp.exp(scores - log_total[..., None])
            probs_low = probs.astype(jnp.bfloat16)
            probs_rest = (probs - probs_low.astype(jnp.float32)).astype(jnp.bfloat16)
            value_heads = sub_piece[0][:, D:].reshape(-1, H, HD)
            main_part, rest_part = carry_in
            main_part = main_part + jnp.einsum(
                "hqk,khd->qhd", probs_low, value_heads, preferred_element_type=jnp.float32
            )
            rest_part = rest_part + jnp.einsum(
                "hqk,khd->qhd", probs_rest, value_heads, preferred_element_type=jnp.float32
            )
            return (main_part, rest_part)

        zero_heads = jnp.zeros((local_rows, H, HD), jnp.float32)
        main_sum, rest_sum = fold_keys(
            kv_local, query_segs, partial(over_blocks, value_step), (zero_heads, zero_heads)
        )
        attended_low = main_sum.reshape(local_rows, D).astype(jnp.bfloat16)
        attended_full = main_sum + rest_sum
        middle = (
            input_rows
            + jnp.dot(attended_low, w_proj, preferred_element_type=jnp.float32)
            + bias_proj.astype(jnp.float32)
        )
        normed_two, norm_two_back = jax.vjp(
            layer_norm, middle, gain_two.astype(jnp.float32), shift_two.astype(jnp.float32)
        )
        normed_two_low = normed_two.astype(jnp.bfloat16)
        hidden = jnp.dot(normed_two_low, w_up, preferred_element_type=jnp.float32) + bias_up.astype(
            jnp.float32
        )
        active, gelu_back = jax.vjp(gelu_tanh, hidden)
        active_low = active.astype(jnp.bfloat16)
        result = (
            middle
            + jnp.dot(active_low, w_down, preferred_element_type=jnp.float32)
            + bias_down.astype(jnp.float32)
        )
        out_rows.append(result.astype(jnp.bfloat16))
        w_qkv, w_proj = (attn_set[2], attn_set[5])
        w_up, w_down = (mlp_set[2], mlp_set[4])
        cot_low = cotangent[micro_index, 0]
        cot_rows = cot_low.astype(jnp.float32)
        grad_w_down = jnp.einsum(
            "rf,rd->fd", active_low, cot_low, preferred_element_type=jnp.float32
        )
        grad_b_down = jnp.sum(cot_rows, axis=0)
        grad_active = jnp.einsum("rd,fd->rf", cot_low, w_down, preferred_element_type=jnp.float32)
        grad_hidden = gelu_back(grad_active)[0].astype(jnp.bfloat16)
        grad_w_up = jnp.einsum(
            "rd,rf->df", normed_two_low, grad_hidden, preferred_element_type=jnp.float32
        )
        grad_b_up = jnp.sum(grad_hidden.astype(jnp.float32), axis=0)
        grad_normed_two = jnp.einsum(
            "rf,df->rd", grad_hidden, w_up, preferred_element_type=jnp.float32
        )
        grad_middle_norm, grad_gain_two, grad_shift_two = norm_two_back(grad_normed_two)
        grad_middle = cot_rows + grad_middle_norm
        grad_branch = grad_middle.astype(jnp.bfloat16)
        grad_w_proj = jnp.einsum(
            "rd,re->de", attended_low, grad_branch, preferred_element_type=jnp.float32
        )
        grad_b_proj = jnp.sum(grad_branch.astype(jnp.float32), axis=0)
        grad_attended = jnp.einsum(
            "re,de->rd", grad_branch, w_proj, preferred_element_type=jnp.float32
        ).astype(jnp.bfloat16)
        grad_heads = grad_attended.reshape(local_rows, H, HD)
        row_delta = jnp.einsum("qhd,qhd->hq", grad_heads.astype(jnp.float32), attended_full)

        def grad_step(carry_in, sub_piece, key_start):
            scores, key_heads = block_scores(
                query_heads, query_segs, query_pos, sub_piece[0], sub_piece[1], key_start
            )
            value_heads = sub_piece[0][:, D:].reshape(-1, H, HD)
            probs = jnp.exp(scores - log_total[..., None])
            grad_probs = jnp.einsum(
                "qhd,khd->hqk", grad_heads, value_heads, preferred_element_type=jnp.float32
            )
            grad_scores = (probs * (grad_probs - row_delta[..., None])).astype(jnp.bfloat16)
            query_part, kv_part = carry_in
            query_part = (
                query_part
                + jnp.einsum(
                    "hqk,khd->qhd", grad_scores, key_heads, preferred_element_type=jnp.float32
                )
                * score_scale
            )
            key_grad = (
                jnp.einsum(
                    "hqk,qhd->khd", grad_scores, query_heads, preferred_element_type=jnp.float32
                )
                * score_scale
            )
            value_grad = jnp.einsum(
                "hqk,qhd->khd",
                probs.astype(jnp.bfloat16),
                grad_heads,
                preferred_element_type=jnp.float32,
            )
            block_grads = jnp.concatenate(
                [key_grad.reshape(-1, D), value_grad.reshape(-1, D)], axis=1
            )
            kv_part = lax.dynamic_update_slice_in_dim(kv_part, block_grads, key_start, 0)
            return (query_part, kv_part)

        query_sum, kv_sums = fold_keys(
            kv_local,
            query_segs,
            partial(over_blocks, grad_step),
            (zero_heads, jnp.zeros((seq_length, 2 * D), jnp.float32)),
        )
        kv_grads = lax.psum_scatter(
            kv_sums.astype(jnp.bfloat16), "seq", scatter_dimension=0, tiled=True
        ).astype(jnp.float32)
        grad_merged = jnp.concatenate([query_sum.reshape(local_rows, D), kv_grads], axis=1).astype(
            jnp.bfloat16
        )
        grad_merged_wide = grad_merged.astype(jnp.float32)
        grad_w_qkv = jnp.einsum(
            "rd,re->de", normed_one_low, grad_merged, preferred_element_type=jnp.float32
        )
        grad_b_query = jnp.sum(grad_merged_wide[:, :D], axis=0)
        grad_b_value = jnp.sum(grad_merged_wide[:, 2 * D :], axis=0)
        grad_normed_one = jnp.einsum(
            "re,de->rd", grad_merged, w_qkv, preferred_element_type=jnp.float32
        )
        grad_input_norm, grad_gain_one, grad_shift_one = norm_one_back(grad_normed_one)
        grad_rows.append(grad_middle + grad_input_norm)
        attn_list = [
            grad_gain_one,
            grad_shift_one,
            grad_w_qkv,
            grad_b_query,
            grad_b_value,
            grad_w_proj,
            grad_b_proj,
        ]
        mlp_list = [grad_gain_two, grad_shift_two, grad_w_up, grad_b_up, grad_w_down, grad_b_down]
        attn_sums = (
            attn_list
            if attn_sums is None
            else [left_sum + right_sum for left_sum, right_sum in zip(attn_sums, attn_list)]
        )
        mlp_sums = (
            mlp_list
            if mlp_sums is None
            else [left_sum + right_sum for left_sum, right_sum in zip(mlp_sums, mlp_list)]
        )
    shard_sums = send_grads(attn_sums, mlp_sums, attn_total, mlp_total)
    outputs = jnp.stack(out_rows)[:, None]
    input_grad = jnp.stack(grad_rows)[:, None]
    return (outputs, input_grad, shard_sums[0], shard_sums[1])


HALF_HEADS = H // 2
HALF_COLS = D // 2
ROW_D = D // LANES
ROW_FF = FF // LANES
ROW_QKV = 3 * ROW_D
ROW_HALF = HALF_COLS // LANES
FF_STEP = 512
HEAD = 16
MARGIN = 32
VMEM_LIMIT = 63 * 2**20

A_SEQ = ((6.0, 9.0), (12.0, 15.0), (18.0, 21.0))
A_OWN = (1.0, 6.1)
M_SEQ = ((16.5, 21.0), (25.5, 30.0), (34.5, 39.0))
M_OWN = (8.0, 8.6)
M_BEGIN = (0.0, -1.1, 4.0)
SEND_X = (6.0, 6.0, 6.0, 6.0)
SHARE_X = 24.5
SEND_COT = (45.0, 45.0)
FORWARD_START = 36.1
PROJECT = 4.0
HEAD_FORWARD = 2.9
BACKWARD_FIRST = 6.5
BACKWARD_START = 8.0
M_BACK = (6.0, 9.6, (9.0, 19.0), 0.5)
A_BACK = (6.0, 5.0, (5.0, 10.0), 1.0)
HEAD_BACKWARD = 5.8

ATTN_QKV = 2 * ROW_D
ATTN_BQ = ATTN_QKV + D * ROW_QKV
ATTN_BV = ATTN_BQ + ROW_D
ATTN_PROJ = ATTN_BV + ROW_D
ATTN_BPROJ = ATTN_PROJ + D * ROW_D
MLP_UP = 2 * ROW_D
MLP_BUP = MLP_UP + D * ROW_FF
MLP_DOWN = MLP_BUP + ROW_FF
MLP_BDOWN = MLP_DOWN + FF * ROW_D

f32 = jnp.float32
bf16 = jnp.bfloat16


def dot_nn(left, right):
    return jnp.dot(left, right, preferred_element_type=f32)


def dot_nt(left, right):
    return lax.dot_general(left, right, (((1,), (1,)), ((), ())), preferred_element_type=f32)


def dot_tn(left, right):
    return lax.dot_general(left, right, (((0,), (0,)), ((), ())), preferred_element_type=f32)


def remote(src, dst, send_sem, recv_sem, to):
    return pltpu.make_async_remote_copy(
        src_ref=src, dst_ref=dst, send_sem=send_sem, recv_sem=recv_sem, device_id=to, device_id_type=MESH
    )


class Place:
    def __init__(self, seq_size):
        self.n = seq_size
        self.dp = lax.axis_index("dp")
        self.z = lax.axis_index("seq")
        self.core = lax.rem(self.dp, 2)
        self.base = self.dp - self.core
        self.sibling = (self.base + 1 - self.core, self.z)

    def line_peers(self):
        out = [self.sibling]
        for k in range(1, self.n):
            other = lax.rem(self.z + k, self.n)
            out += [(self.base, other), (self.base + 1, other)]
        return out

    def own_block(self, j):
        return 1 - self.core + 2 * j

    def other_block(self, j):
        return self.core + 2 * j

    def worker(self, micro):
        return (self.base + 1 - lax.rem(self.z, 2), 2 * micro + self.core)

    def home(self, j):
        return (self.base + lax.rem(self.z, 2), self.own_block(j)), self.z // 2


def split_heads(piece, heads, rows):
    lane = lax.broadcasted_iota(jnp.int32, (piece.shape[0], LANES), 1)
    for h in range(HALF_HEADS):
        pair = piece[:, h // 2 * LANES : (h // 2 + 1) * LANES]
        heads[h, rows, :] = jnp.where(lane // HD == h % 2, pair, jnp.zeros_like(pair))


class Action:
    def step(self, action):
        action()


class Steps:
    def __init__(self, timed):
        self.queue = sorted(timed, key=lambda e: e[0])

    def take(self, time):
        out = [event for at, event in self.queue if at <= time]
        self.queue = [e for e in self.queue if e[0] > time]
        return out

    def until(self, time):
        for owner, event in self.take(time):
            owner.step(event)

    def plan(self, start, points):
        out = {}
        for point, length in points:
            out[point] = self.take(start)
            start += length
        return out


def handle(plan, index):
    for turn, events in enumerate(plan):
        if events:

            @pl.when(index == turn)
            def _():
                for owner, event in events:
                    owner.step(event)


def greet(peers):
    barrier = pltpu.get_barrier_semaphore()
    for peer in peers:
        pl.semaphore_signal(barrier, inc=1, device_id=peer, device_id_type=MESH)
    pl.semaphore_wait(barrier, len(peers))


class Layout:
    def __init__(self, rows, devices, matrices, tail):
        self.rows, self.tail = rows, tail
        self.whole = sum(count * columns for _, count, columns in matrices) // devices
        self.slot_rows = self.whole + HEAD + tail
        self.regions = []
        first = 0
        for start, count, columns in matrices:
            shards = count * columns // self.whole
            self.regions.append((start, columns, self.whole // columns, first, shards))
            first += shards
        assert first == devices
        for s in range(devices):
            start, columns, height, first, _ = self.region(s)
            shift = start + self.whole * (s - first) - rows * s
            assert shift <= HEAD and shift + self.whole >= rows - tail and shift >= -MARGIN

    def region(self, s):
        return [r for r in self.regions if r[3] <= s < r[3] + r[4]][0]

    def shift(self, s, region):
        start, _, _, first, _ = region
        return start - self.whole * first + (self.whole - self.rows) * s

    def piece(self, row):
        s, q = row // self.rows, row % self.rows
        if q < HEAD:
            return s, self.whole + q
        assert q >= self.rows - self.tail
        return s, self.whole + HEAD + q - (self.rows - self.tail)

    def lacking(self, region):
        out = []
        start, columns, height, first, shards = region
        for s in range(first, first + shards):
            shift = self.shift(s, region)
            for q in range(self.whole):
                if not 0 <= shift + q < self.rows:
                    out.append(((s - first) * height + q // columns, q % columns) + self.piece(s * self.rows + shift + q))
        return out

    def beyond(self):
        out = []
        for s in range(sum(r[4] for r in self.regions)):
            shift = self.shift(s, self.region(s))
            for q in list(range(max(shift, 0))) + list(range(shift + self.whole, self.rows)):
                row = s * self.rows + q
                for start, columns, height, first, shards in self.regions:
                    if start <= row < start + shards * self.whole:
                        i, j = (row - start) // columns, (row - start) % columns
                        out.append(self.piece(row) + (first + i // height, j * height + i % height))
        return out

    def branch(self, s, action):
        for region in self.regions:
            pl.when((s >= region[3]) & (s < region[3] + region[4]))(functools.partial(action, region))

    def pack(self, own, wide, slot, s):
        edge = jnp.zeros((MARGIN, LANES), f32)
        wide[:MARGIN, :] = edge
        wide[MARGIN + own.shape[0] :, :] = edge
        wide[MARGIN : MARGIN + own.shape[0], :] = own[...].astype(f32)

        def fill(region):
            _, columns, height, _, _ = region
            for j in range(columns):
                piece = wide[pl.ds(MARGIN + self.shift(s, region) + j, height, stride=columns), :]
                slot[j * height : (j + 1) * height, :] = piece.astype(bf16)

        self.branch(s, fill)
        slot[self.whole : self.whole + HEAD, :] = own[:HEAD, :]
        last = wide[MARGIN + self.rows - self.tail : MARGIN + self.rows, :]
        slot[self.whole + HEAD :, :] = last.astype(bf16)

    def unpack(self, slot, wide, out, s):
        def fill(region):
            _, columns, height, _, _ = region
            shift = self.shift(s, region)
            for j in range(columns):
                wide[pl.ds(MARGIN + shift + j, height, stride=columns), :] = slot[j * height : (j + 1) * height, :]
            out[...] = wide[MARGIN : MARGIN + self.rows, :]
            row = lax.broadcasted_iota(jnp.int32, (HEAD, LANES), 0)
            out[:HEAD, :] = jnp.where(row < shift, slot[self.whole : self.whole + HEAD, :], out[:HEAD, :])
            begin = self.rows - self.tail
            row = lax.broadcasted_iota(jnp.int32, (self.tail, LANES), 0) + begin
            last = slot[self.whole + HEAD :, :]
            out[begin:, :] = jnp.where(row >= shift + self.whole, last, out[begin:, :])

        self.branch(s, fill)

    def vector(self, slots, row, blocks):
        parts = []
        for j in range(blocks):
            s, q = self.piece(row + j)
            aligned = q // 16 * 16
            parts.append(slots[s, aligned : aligned + 16, :].astype(f32)[q - aligned : q - aligned + 1, :])
        return jnp.concatenate(parts, axis=1)

    def put_vectors(self, slots, entries):
        areas = {}
        for row, value in entries:
            for j in range(value.shape[1] // LANES):
                s, at = self.piece(row + j)
                begin = self.whole if at < self.whole + HEAD else self.whole + HEAD
                areas.setdefault((s, begin), {})[at - begin] = value[:, j * LANES : (j + 1) * LANES]
        zero = jnp.zeros((1, LANES), f32)
        for (s, begin), rows in areas.items():
            size = HEAD if begin == self.whole else self.tail
            tile = jnp.concatenate([rows.get(n, zero) for n in range(size)], axis=0)
            slots[s, begin : begin + size, :] = tile.astype(bf16)


def load_matrix(slots, layout, which, base, out):
    region = layout.regions[which]
    _, columns, height, first, shards = region

    def body(s, carry):
        rows = pl.ds(pl.multiple_of(s * height, height), height)
        for j in range(columns):
            out[rows, j * LANES : (j + 1) * LANES] = slots[s + first - base, j * height : (j + 1) * height, :]
        return carry

    lax.fori_loop(0, shards, body, 0)
    for i, j, s, q in layout.lacking(region):
        out[i : i + 1, j * LANES : (j + 1) * LANES] = slots[s - base, q : q + 1, :]


def attn_layout(rows, devices):
    return Layout(rows, devices, [(ATTN_QKV, D, ROW_QKV), (ATTN_PROJ, D, ROW_D)], 16)


def mlp_layout_of(rows, devices):
    return Layout(rows, devices, [(MLP_UP, D, ROW_FF), (MLP_DOWN, FF, ROW_D)], 32)


def norm_parts(values):
    average = jnp.mean(values, axis=-1, keepdims=True)
    centred = values - average
    spread = jnp.mean(centred * centred, axis=-1, keepdims=True)
    scale = lax.rsqrt(spread + norm_eps)
    return centred * scale, scale


def norm_back(normal, scale, grad, gain):
    scaled = grad * gain
    return scale * (
        scaled
        - jnp.mean(scaled, axis=-1, keepdims=True)
        - normal * jnp.mean(scaled * normal, axis=-1, keepdims=True)
    )


def keep_allowed(scores, seg_col, seg_all, b, i, block):
    parts = []
    for r in range(block // LANES):
        row = seg_all[i, r : r + 1, :]
        allowed = seg_col[b * block : (b + 1) * block, :] == row
        if b == i:
            key_pos = lax.broadcasted_iota(jnp.int32, (block, LANES), 0)
            query_pos = lax.broadcasted_iota(jnp.int32, (block, LANES), 1) + r * LANES
            allowed = allowed & (key_pos <= query_pos)
        parts.append(jnp.where(allowed, scores[:, r * LANES : (r + 1) * LANES], score_floor))
    return jnp.concatenate(parts, axis=1)


def segment_columns(seg_all, seg_col, block):
    for t in range(seg_all.shape[0]):
        for r in range(block // LANES):
            row = jnp.broadcast_to(seg_all[t, r : r + 1, :], (LANES, LANES))
            seg_col[pl.ds(t * block + r * LANES, LANES), :] = row.T


def forward_kernel(
    dp_size, seq_size, a_layout, m_layout,
    x_in, seg_in, cot_in, a_raw, m_raw,
    m_slots, cot_own, n1_out, wqkv_out, qt_out, kt_out, qh_out, kh_out, vh_out,
    x_own, w_proj, vec, seg_all, lse, att,
    n1, wqkv, qt, kt, qh, kh, vh,
    a_slots, a_own, m_own, a_wide, m_wide, x_all, plain, vt, seg_col, scores, ot, att_out,
    a_send, a_recv, m_send, m_recv, own_sems, move_send, move_recv, cot_sems, swap_sems, keep_sems,
):
    place = Place(seq_size)
    block = x_in.shape[1]
    ga = Gather(dp_size, seq_size, a_own, a_slots, a_send, a_recv)
    gm = Gather(dp_size, seq_size, m_own, m_slots, m_send, m_recv)
    mine = place.dp * seq_size + place.z
    a_layout.pack(a_raw, a_wide, a_own, mine)
    greet(place.line_peers() + [(place.dp ^ (1 << b), place.z) for b in ga.bits])

    own_copies = [
        pltpu.make_async_copy(a_own, a_slots.at[mine], own_sems.at[0]),
        pltpu.make_async_copy(m_own, m_slots.at[mine], own_sems.at[1]),
    ]
    ga.begin()
    m_layout.pack(m_raw, m_wide, m_own, mine)
    for copy in own_copies:
        copy.start()
    sent = []

    def launch(copy):
        copy.start()
        sent.append(copy)

    def send_segments():
        for micro in range(2):
            launch(
                remote(
                    seg_in.at[micro], seg_all.at[place.z], move_send.at[2, micro], move_recv.at[2, place.z],
                    place.worker(micro),
                )
            )

    def send_inputs(micro, half):
        rows = pl.ds(half * (block // 2), block // 2)
        launch(
            remote(
                x_in.at[micro, rows], x_all.at[place.z, rows], move_send.at[half, micro], move_recv.at[half, place.z],
                place.worker(micro),
            )
        )

    def moved(t, kind):
        return seg_all.at[t] if kind == 2 else x_all.at[t, pl.ds(kind * (block // 2), block // 2)]

    def arrival(t, kind):
        ref = moved(t, kind)
        return remote(ref, ref, move_send.at[kind, 0], move_recv.at[kind, t], place.sibling)

    def share_inputs():
        for j in range(2):
            t = place.own_block(j)
            for kind in range(3):
                ref = moved(t, kind)
                arrival(t, kind).wait_recv()
                launch(remote(ref, ref, move_send.at[kind, 2 + j], move_recv.at[kind, t], place.sibling))

    def send_cotangent(micro):
        remote(
            cot_in.at[micro], cot_own.at[place.z // 2], cot_sems.at[0, micro], cot_sems.at[1, place.z // 2],
            place.worker(micro),
        ).start()

    timed = [(time, (ga, event)) for time, event in ga.events(A_SEQ, *A_OWN)]
    timed += [(time, (gm, event)) for time, event in gm.events(M_SEQ, *M_OWN)]
    timed += [
        (at, (Action(), action))
        for at, action in (
            (SEND_X[0], send_segments), (SHARE_X, share_inputs), (M_BEGIN[2], gm.begin_bits),
            (M_BEGIN[0], functools.partial(gm.begin_seq, 0)), (M_BEGIN[1], functools.partial(gm.begin_seq, 1)),
        )
    ]
    timed += [
        (SEND_X[n], (Action(), functools.partial(send_inputs, 1 - n // 2, n % 2))) for n in range(4)
    ]
    timed += [(SEND_COT[n], (Action(), functools.partial(send_cotangent, 1 - n))) for n in range(2)]
    both = Steps(timed)
    both.until(FORWARD_START)
    own_copies[0].wait()
    ga.finish_sibling()
    height = a_layout.regions[0][2]

    def take_columns(s, carry):
        rows = pl.ds(pl.multiple_of(s * height, height), height)
        for section in range(3):
            for j in range(ROW_HALF):
                block_at = section * ROW_D + place.core * ROW_HALF + j
                piece = a_slots[s, pl.ds(pl.multiple_of(block_at * height, height), height), :]
                wqkv[section, rows, j * LANES : (j + 1) * LANES] = piece
        return carry

    lax.fori_loop(0, a_layout.regions[0][4], take_columns, 0)
    for core in range(2):

        @pl.when(place.core == core)
        def _():
            for i, j, s, q in a_layout.lacking(a_layout.regions[0]):
                section, at = j // ROW_D, j % ROW_D - core * ROW_HALF
                if 0 <= at < ROW_HALF:
                    wqkv[section, i : i + 1, at * LANES : (at + 1) * LANES] = a_slots[s, q : q + 1, :]

    load_matrix(a_slots, a_layout, 1, 0, w_proj)
    gain = a_layout.vector(a_slots, 0, ROW_D)
    shift = a_layout.vector(a_slots, ROW_D, ROW_D)
    vec[...] = jnp.zeros_like(vec)
    vec[0:1, :] = gain
    vec[1:2, :] = a_layout.vector(a_slots, ATTN_BPROJ, ROW_D)
    first_half = place.core == 0
    bias_query = a_layout.vector(a_slots, ATTN_BQ, ROW_D)
    bias_query = jnp.where(first_half, bias_query[:, :HALF_COLS], bias_query[:, HALF_COLS:])
    bias_value = a_layout.vector(a_slots, ATTN_BV, ROW_D)
    bias_value = jnp.where(first_half, bias_value[:, :HALF_COLS], bias_value[:, HALF_COLS:])
    both.until(FORWARD_START + 2)
    for j in range(2):
        for kind in range(3):
            arrival(place.other_block(j), kind).wait_recv()
        x_own[j] = x_all[place.own_block(j)]
    segment_columns(seg_all, seg_col, block)

    project_plan = both.plan(FORWARD_START + 2, [(t, PROJECT / seq_size) for t in range(seq_size)])

    def project(t, carry):
        handle([project_plan[turn] for turn in range(seq_size)], t)
        rows = pl.ds(pl.multiple_of(t * block, block), block)
        normal, _ = norm_parts(x_all[t].astype(f32))
        low = (normal * gain + shift).astype(bf16)
        n1[rows, :] = low
        query = (dot_nn(low, wqkv[0]) + bias_query).astype(bf16).astype(f32) * (1.0 / math.sqrt(HD))
        key = dot_nn(low, wqkv[1]).astype(bf16)
        value = dot_nn(low, wqkv[2]) + bias_value
        qt[:, rows] = query.T.astype(bf16)
        split_heads(key, kh, rows)
        vt[:, rows] = value.T.astype(bf16)
        plain[0, rows, :] = query.astype(bf16)
        plain[1, rows, :] = key
        plain[2, rows, :] = value.astype(bf16)
        return carry

    def other_forms(t, carry):
        rows = pl.ds(pl.multiple_of(t * block, block), block)
        split_heads(plain[0, rows, :], qh, rows)
        split_heads(plain[2, rows, :], vh, rows)
        kt[:, rows] = plain[1, rows, :].astype(f32).T.astype(bf16)
        return carry

    lax.fori_loop(0, seq_size, project, 0)
    keep = [
        pltpu.make_async_copy(src, dst, keep_sems.at[i])
        for i, (src, dst) in enumerate([(n1, n1_out), (wqkv, wqkv_out), (qt, qt_out), (kh, kh_out)])
    ]
    for copy in keep:
        copy.start()
    lse[...] = jnp.zeros_like(lse)
    unit = HEAD_FORWARD / (seq_size * (seq_size + 1) // 2)
    points = [((h, i), unit * (i + 1)) for h in range(HALF_HEADS) for i in range(seq_size)]
    plan = both.plan(FORWARD_START + 2 + PROJECT, points)

    def one_head(h, carry):
        head_rows = pl.ds(pl.multiple_of(h * HD, HD), HD)
        pair_rows = pl.ds(pl.multiple_of(h // 2 * LANES, LANES), LANES)
        for i in range(seq_size):
            handle([plan[c, i] for c in range(HALF_HEADS)], h)
            columns = slice(i * block, (i + 1) * block)
            query = qt[pair_rows, columns]
            top = jnp.full((1, block), -jnp.inf, f32)
            for b in range(i + 1):
                rows = slice(b * block, (b + 1) * block)
                piece = keep_allowed(dot_nn(kh[h, rows, :], query), seg_col, seg_all, b, i, block)
                scores[rows, :] = piece
                top = jnp.maximum(top, jnp.max(piece, axis=0, keepdims=True))
            total = jnp.zeros((1, block), f32)
            for b in range(i + 1):
                rows = slice(b * block, (b + 1) * block)
                piece = jnp.exp(scores[rows, :] - top)
                scores[rows, :] = piece
                total = total + jnp.sum(piece, axis=0, keepdims=True)
            inverse = 1.0 / total
            result = jnp.zeros((HD, block), f32)
            for b in range(i + 1):
                rows = slice(b * block, (b + 1) * block)
                result = result + dot_nn(vt[head_rows, rows], (scores[rows, :] * inverse).astype(bf16))
            ot[head_rows, columns] = result
            lse[pl.ds(h, 1), columns] = top + jnp.log(total)
        return carry

    lax.fori_loop(0, HALF_HEADS, one_head, 0)
    both.until(FORWARD_START + 3 + PROJECT + HALF_HEADS * HEAD_FORWARD)

    for j in range(2):
        columns = pl.ds(pl.multiple_of(place.other_block(j) * block, block), block)
        att_out[j] = ot[:, columns].T.astype(bf16)
        copy = remote(
            att_out.at[j], att.at[place.core, j], swap_sems.at[0, j], swap_sems.at[1, j], place.sibling
        )
        copy.start()
        sent.append(copy)
    for j in range(2):
        columns = pl.ds(pl.multiple_of(place.own_block(j) * block, block), block)
        att[place.core, j] = ot[:, columns].T.astype(bf16)
    lax.fori_loop(0, seq_size, other_forms, 0)
    keep += [
        pltpu.make_async_copy(src, dst, keep_sems.at[4 + i])
        for i, (src, dst) in enumerate([(kt, kt_out), (qh, qh_out), (vh, vh_out)])
    ]
    for copy in keep[4:]:
        copy.start()
    both.until(math.inf)
    for j in range(2):
        ref = att.at[1 - place.core, j]
        remote(ref, ref, swap_sems.at[0, j], swap_sems.at[1, j], place.sibling).wait_recv()
        ref = cot_own.at[j]
        remote(ref, ref, cot_sems.at[0, j], cot_sems.at[1, j], place.sibling).wait()
    own_copies[1].wait()
    for copy in keep:
        copy.wait()
    gm.finish_sibling()
    for copy in sent:
        copy.wait_send()
    ga.finish_sends()
    gm.finish_sends()


def backward_kernel(
    dp_size, seq_size, a_layout, m_layout,
    m_slots, x_own_in, n1_in, wqkv_in, qt_in, kt_in, qh_in, kh_in, vh_in, cot_in, att_in, w_proj_in,
    vec, seg_all, lse,
    out_back, grad_back, a_out, m_out,
    g_slots, a_slots, x_own, out_own, d_mid, d_att, d_all, d_n1_in, g_bias, a_wide, m_wide,
    move_sems, swap_sems, norm_sems, load_sems, *refs,
):
    place = Place(seq_size)
    block = x_own.shape[1]
    length = seq_size * block
    mine = place.dp * seq_size + place.z
    count = len(refs) // 2
    sm = make_scatter(dp_size, seq_size, g_slots, refs[:count])
    sa = make_scatter(dp_size, seq_size, a_slots, refs[count:])
    slots_copy = pltpu.make_async_copy(m_slots, g_slots, load_sems.at[1])
    slots_copy.start()
    greet(place.line_peers() + [(place.dp ^ (1 << b), place.z) for b in sm.bits])
    a_slots[...] = jnp.zeros_like(a_slots)
    def mlp(cot, att, w_proj, w_up, w_down, mid, n2, d_n2, total, b_up, gb_up):
        blocks = [slice(j * block, (j + 1) * block) for j in range(2)]
        first_loads = [
            pltpu.make_async_copy(src, dst, load_sems.at[i])
            for i, src, dst in ((0, x_own_in, x_own), (9, att_in, att), (10, w_proj_in, w_proj), (11, cot_in, cot))
        ]
        for copy in first_loads:
            copy.start()
        for copy in first_loads:
            copy.wait()
        for j, rows in enumerate(blocks):
            mid[rows, :] = (
                x_own[j].astype(f32)
                + dot_nn(att[0, rows, :], w_proj[:HALF_COLS, :])
                + dot_nn(att[1, rows, :], w_proj[HALF_COLS:, :])
                + vec[1:2, :]
            )
        slots_copy.wait()
        load_matrix(g_slots, m_layout, 0, 0, w_up)
        load_matrix(g_slots, m_layout, 1, 0, w_down)
        gain = m_layout.vector(g_slots, 0, ROW_D)
        shift = m_layout.vector(g_slots, ROW_D, ROW_D)
        b_down = m_layout.vector(g_slots, MLP_BDOWN, ROW_D)
        b_up[...] = m_layout.vector(g_slots, MLP_BUP, ROW_FF)
        for rows in blocks:
            normal, _ = norm_parts(mid[rows, :])
            n2[rows, :] = (normal * gain + shift).astype(bf16)
        total[...] = jnp.zeros_like(total)
        d_n2[...] = jnp.zeros_like(d_n2)
        inner = math.sqrt(2.0 / math.pi)
        _, _, up_height, up_first, up_shards = m_layout.regions[0]
        _, _, down_height, down_first, _ = m_layout.regions[1]
        turns = FF // FF_STEP // 2

        def step(u, carry):
            for v in range(turns):
                start = pl.multiple_of((u * turns + v) * FF_STEP, FF_STEP)
                columns = pl.ds(start, FF_STEP)
                hidden = dot_nn(n2[...], w_up[:, columns]) + b_up[:, columns]
                square = hidden * hidden
                tanh = jnp.tanh(inner * (hidden + 0.044715 * (square * hidden)))
                cdf = 0.5 * (1.0 + tanh)
                active = (hidden * cdf).astype(bf16)
                slope = cdf + (0.5 * inner) * hidden * (1.0 - tanh * tanh) * (1.0 + (3 * 0.044715) * square)
                low = (dot_nt(cot[...], w_down[columns, :]) * slope).astype(bf16)
                gb_up[:, columns] = jnp.sum(low.astype(f32), axis=0, keepdims=True)
                total[...] += dot_nn(active, w_down[columns, :])
                d_n2[...] += dot_nt(low, w_up[:, columns])
                g_down = dot_tn(active, cot[...]).astype(bf16)
                begin = v * FF_STEP
                for t in range(begin // down_height, (begin + FF_STEP - 1) // down_height + 1):
                    top = max(begin, t * down_height)
                    end = min(begin + FF_STEP, (t + 1) * down_height)
                    slot = down_first + u * (turns * FF_STEP // down_height) + t
                    for j in range(ROW_D):
                        at = j * down_height + top - t * down_height
                        g_slots[slot, at : at + end - top, :] = g_down[
                            top - begin : end - begin, j * LANES : (j + 1) * LANES
                        ]
                g_up = dot_tn(n2[...], low).astype(bf16)
                for j in range(FF_STEP // LANES):
                    at = ((u * turns + v) * (FF_STEP // LANES) + j) * up_height
                    rows = pl.ds(pl.multiple_of(at, up_height), up_height)
                    for s in range(up_shards):
                        g_slots[up_first + s, rows, :] = g_up[
                            s * up_height : (s + 1) * up_height, j * LANES : (j + 1) * LANES
                        ]
            return carry

        lax.fori_loop(0, 2, step, 0)

        gain_sum = jnp.zeros((1, D), f32)
        shift_sum = jnp.zeros((1, D), f32)
        down_sum = jnp.zeros((1, D), f32)
        proj_sum = jnp.zeros((1, D), f32)
        for rows in blocks:
            normal, scale = norm_parts(mid[rows, :])
            grad = d_n2[rows, :]
            cot_rows = cot[rows, :].astype(f32)
            gain_sum += jnp.sum(grad * normal, axis=0, keepdims=True)
            shift_sum += jnp.sum(grad, axis=0, keepdims=True)
            down_sum += jnp.sum(cot_rows, axis=0, keepdims=True)
            d_rows = cot_rows + norm_back(normal, scale, grad, gain)
            d_mid[rows, :] = d_rows
            low = d_rows.astype(bf16)
            n2[rows, :] = low
            proj_sum += jnp.sum(low.astype(f32), axis=0, keepdims=True)
        m_layout.put_vectors(
            g_slots, [(0, gain_sum), (ROW_D, shift_sum), (MLP_BUP, gb_up[...]), (MLP_BDOWN, down_sum)]
        )
        for s, q, there, at in m_layout.beyond():
            g_slots[s, q : q + 1, :] = g_slots[there, at : at + 1, :]
        sm.begin()
        for c in range(2):
            for rows in blocks:
                d_att[c, rows, :] = dot_nt(n2[rows, :], w_proj[c * HALF_COLS : (c + 1) * HALF_COLS, :]).astype(bf16)
        for j in range(2):
            src = d_att.at[1 - place.core, pl.ds(j * block, block)]
            remote(
                src, d_all.at[place.own_block(j)], swap_sems.at[0, j], swap_sems.at[1, j], place.sibling
            ).start()
        steps.until(BACKWARD_FIRST)
        for j, rows in enumerate(blocks):
            out_own[rows, :] = (mid[rows, :] + total[rows, :] + b_down).astype(bf16)
            to, micro = place.home(j)
            remote(
                out_own.at[pl.ds(j * block, block)], out_back.at[micro], move_sems.at[0, j], move_sems.at[1, micro], to
            ).start()
        g_bias[...] = proj_sum
        _, _, height, first, shards = a_layout.regions[1]
        for c in range(2):
            g_part = dot_tn(att[c], n2[...]).astype(bf16)
            for t in range(shards // 2):
                for j in range(ROW_D):
                    a_slots[first + c * (shards // 2) + t, j * height : (j + 1) * height, :] = g_part[
                        t * height : (t + 1) * height, j * LANES : (j + 1) * LANES
                    ]

    tokens = 2 * block
    steps = Steps([(time, (sm, event)) for time, event in sm.events(*M_BACK)])
    pl.run_scoped(
        mlp,
        pltpu.VMEM((tokens, D), bf16), pltpu.VMEM((2, tokens, HALF_COLS), bf16), pltpu.VMEM((D, D), bf16),
        pltpu.VMEM((D, FF), bf16), pltpu.VMEM((FF, D), bf16),
        pltpu.VMEM((tokens, D), f32), pltpu.VMEM((tokens, D), bf16),
        pltpu.VMEM((tokens, D), f32), pltpu.VMEM((tokens, D), f32),
        pltpu.VMEM((1, FF), f32), pltpu.VMEM((1, FF), f32),
    )

    def attention(
        n1, wqkv, qt, kt, qh, kh, vh, dt, dh, seg_col, p_piece, d_piece, dk, dv, dqt, dm, d_n1
    ):
        loads = [
            pltpu.make_async_copy(src, dst, load_sems.at[2 + i])
            for i, (src, dst) in enumerate(
                [(qt_in, qt), (kt_in, kt), (qh_in, qh), (kh_in, kh), (vh_in, vh), (n1_in, n1), (wqkv_in, wqkv)]
            )
        ]
        for copy in loads:
            copy.start()
        for j in range(2):
            d_all[place.own_block(j)] = d_att[place.core, j * block : (j + 1) * block, :]
        segment_columns(seg_all, seg_col, block)
        steps.until(BACKWARD_START - 3)
        for j in range(2):
            ref = d_all.at[place.other_block(j)]
            remote(ref, ref, swap_sems.at[0, j], swap_sems.at[1, j], place.sibling).wait_recv()

        def spread(t, carry):
            rows = pl.ds(pl.multiple_of(t * block, block), block)
            piece = d_all[t]
            dt[:, rows] = piece.astype(f32).T.astype(bf16)
            split_heads(piece, dh, rows)
            return carry

        lax.fori_loop(0, seq_size, spread, 0)
        steps.until(BACKWARD_START)
        unit = HEAD_BACKWARD / (seq_size * (seq_size + 1) // 2)
        points = [
            ((i, side, pair), unit * (i + 1))
            for i in reversed(range(seq_size))
            for pair in range(HALF_HEADS // 2)
            for side in range(2)
        ]
        plan = steps.plan(BACKWARD_START, points)
        for copy in loads[:5]:
            copy.wait()

        def query_block(i):
            columns = slice(i * block, (i + 1) * block)

            def one_pair(pair, carry):
                pair_rows = pl.ds(pl.multiple_of(pair * LANES, LANES), LANES)
                for side in range(2):
                    handle([plan[i, side, turn] for turn in range(HALF_HEADS // 2)], pair)
                    h = 2 * pair + side
                    head_rows = pl.ds(pl.multiple_of(h * HD, HD), HD)
                    query = qt[pair_rows, columns]
                    d_query = dt[pair_rows, columns]
                    level = lse[pl.ds(h, 1), columns]
                    delta = jnp.zeros((1, block), f32)
                    for b in range(i + 1):
                        rows = slice(b * block, (b + 1) * block)
                        probs = jnp.exp(
                            keep_allowed(dot_nn(kh[h, rows, :], query), seg_col, seg_all, b, i, block) - level
                        )
                        d_probs = dot_nn(vh[h, rows, :], d_query)
                        delta = delta + jnp.sum(probs * d_probs, axis=0, keepdims=True)
                        p_piece[rows, :] = probs
                        d_piece[rows, :] = d_probs
                    result = jnp.zeros((HD, block), f32)
                    for b in range(i + 1):
                        rows = slice(b * block, (b + 1) * block)
                        probs = p_piece[rows, :]
                        d_scores = (probs * (d_piece[rows, :] - delta)).astype(bf16)
                        key_part = dot_nn(d_scores, qh[h, columns, :])
                        value_part = dot_nn(probs.astype(bf16), dh[h, columns, :])
                        if i == seq_size - 1 and side == 0:
                            dk[pair, rows, :] = key_part
                            dv[pair, rows, :] = value_part
                        else:
                            dk[pair, rows, :] += key_part
                            dv[pair, rows, :] += value_part
                        result = result + dot_nn(kt[head_rows, rows], d_scores)
                    dqt[head_rows, :] = result * (1.0 / math.sqrt(HD))
                return carry

            lax.fori_loop(0, HALF_HEADS // 2, one_pair, 0)
            dm[0, columns, :] = dqt[...].T.astype(bf16)
            for section, part in ((1, dk), (2, dv)):
                for pair in range(HALF_HEADS // 2):
                    dm[section, columns, pair * LANES : (pair + 1) * LANES] = part[pair, columns, :].astype(bf16)

        def to_norm(t):
            rows = pl.ds(pl.multiple_of(t * block, block), block)
            return (
                dot_nt(dm[0, rows, :], wqkv[0]) + dot_nt(dm[1, rows, :], wqkv[1]) + dot_nt(dm[2, rows, :], wqkv[2])
            )

        def share_norm(j):
            d_n1[j] = to_norm(place.other_block(j))
            remote(d_n1.at[j], d_n1_in.at[j], norm_sems.at[0, j], norm_sems.at[1, j], place.sibling).start()

        def finish_input(j):
            ref = d_n1_in.at[j]
            remote(ref, ref, norm_sems.at[0, j], norm_sems.at[1, j], place.sibling).wait_recv()
            grad = to_norm(place.own_block(j)) + d_n1_in[j]
            normal, scale = norm_parts(x_own[j].astype(f32))
            x_own[j] = (d_mid[j * block : (j + 1) * block, :] + norm_back(normal, scale, grad, gain)).astype(bf16)
            to, micro = place.home(j)
            remote(x_own.at[j], grad_back.at[micro], move_sems.at[2, j], move_sems.at[3, micro], to).start()
            return jnp.sum(grad * normal, axis=0, keepdims=True), jnp.sum(grad, axis=0, keepdims=True)

        gain = vec[0:1, :]
        query_block(3)
        query_block(2)
        for copy in loads[5:]:
            copy.wait()
        share_norm(1)
        query_block(1)
        gain_sum, shift_sum = finish_input(1)
        query_block(0)
        share_norm(0)
        now = BACKWARD_START + HALF_HEADS * HEAD_BACKWARD
        steps.until(now)
        _, _, height, first, shards = a_layout.regions[0]
        for section in range(3):
            part = dot_tn(n1[...], dm[section]).astype(bf16)
            for j in range(ROW_HALF):
                at = (section * ROW_D + place.core * ROW_HALF + j) * height
                rows = pl.ds(pl.multiple_of(at, height), height)
                for s in range(shards):
                    a_slots[first + s, rows, :] = part[s * height : (s + 1) * height, j * LANES : (j + 1) * LANES]
        steps.until(now + 4)
        more_gain, more_shift = finish_input(0)
        sums = []
        for section in (0, 2):
            half = jnp.sum(dm[section].astype(f32), axis=0, keepdims=True)
            zero = jnp.zeros_like(half)
            first_half = place.core == 0
            sums.append(
                jnp.concatenate([jnp.where(first_half, half, zero), jnp.where(first_half, zero, half)], axis=1)
            )
        a_layout.put_vectors(
            a_slots,
            [
                (0, gain_sum + more_gain), (ROW_D, shift_sum + more_shift),
                (ATTN_BQ, sums[0]), (ATTN_BV, sums[1]), (ATTN_BPROJ, g_bias[...]),
            ],
        )
        for s, q, there, at in a_layout.beyond():
            a_slots[s, q : q + 1, :] = a_slots[there, at : at + 1, :]
        sa.begin()
        Steps(steps.queue + [(now + time, (sa, event)) for time, event in sa.events(*A_BACK)]).until(math.inf)
        sm.finish()
        m_layout.unpack(sm.out, m_wide, m_out, mine)
        sa.finish()
        a_layout.unpack(sa.out, a_wide, a_out, mine)
        for micro in range(2):
            for kind, ref in ((1, out_back), (3, grad_back)):
                remote(
                    ref.at[micro], ref.at[micro], move_sems.at[0, micro], move_sems.at[kind, micro], place.sibling
                ).wait_recv()
        for j in range(2):
            for ref, sem in (
                (d_all, swap_sems.at[0, j]), (out_back, move_sems.at[0, j]),
                (d_n1_in, norm_sems.at[0, j]), (grad_back, move_sems.at[2, j]),
            ):
                remote(ref.at[0], ref.at[0], sem, sem, place.sibling).wait_send()

    pl.run_scoped(
        attention,
        *[
            pltpu.VMEM(ref.shape, ref.dtype)
            for ref in (n1_in, wqkv_in, qt_in, kt_in, qh_in, kh_in, vh_in)
        ],
        pltpu.VMEM((HALF_COLS, length), bf16),
        pltpu.VMEM((HALF_HEADS, length, LANES), bf16),
        pltpu.VMEM((length, LANES), jnp.int32),
        pltpu.VMEM((length, block), f32),
        pltpu.VMEM((length, block), f32),
        pltpu.VMEM((HALF_HEADS // 2, length, LANES), f32),
        pltpu.VMEM((HALF_HEADS // 2, length, LANES), f32),
        pltpu.VMEM((HALF_COLS, block), f32),
        pltpu.VMEM((3, length, HALF_COLS), bf16),
        pltpu.VMEM((2, block, D), f32),
    )


class Scatter:
    def __init__(self, dp_size, seq_size, slots, out, core_in, level_in, seq_in, send_sems, recv_sems, seq_sems):
        self.n = seq_size
        self.bits = list(range(1, dp_size.bit_length() - 1))
        self.masks = [m << 1 for m in range(1 << len(self.bits))]
        self.dp = lax.axis_index("dp")
        self.z = lax.axis_index("seq")
        self.slots, self.out = slots, out
        self.core_in, self.level_in, self.seq_in = core_in, level_in, seq_in
        rows = slots.shape[1]
        half = rows // 32 * 16
        self.parts = [(0, half), (half, rows - half)]
        self.orders = [self.bits[::-1], self.bits]
        self.send_sems, self.recv_sems, self.seq_sems = send_sems, recv_sems, seq_sems
        self.started = []
        self.indices = {}

    def index(self, *key):
        return self.indices.setdefault(key, len(self.indices))

    def slot(self, mask, k):
        return (self.dp ^ mask) * self.n + nearest(self.z, self.n, k)

    def send(self, src, dst, to, key, part=None):
        sem = self.recv_sems.at[self.index(*key)] if isinstance(key, tuple) else key
        remote(src, dst, self.send_sems.at[len(self.started)], sem, to).start()
        self.started.append(part)

    def wait(self, ref, key):
        remote(ref, ref, self.send_sems.at[0], self.recv_sems.at[self.index(*key)], (self.dp, self.z)).wait_recv()

    def turn(self):
        return list(range(self.n))[::-1]

    def begin(self):
        for k in self.turn():
            for mask in self.masks[::-1]:
                i = self.masks.index(mask)
                self.send(
                    self.slots.at[self.slot(mask ^ 1, k)], self.core_in.at[i, k], (self.dp ^ 1, self.z), ("c", i, k)
                )

    def add(self, mask, k, part, term):
        start, size = (0, self.slots.shape[1]) if part is None else self.parts[part]
        rows = pl.ds(start, size)
        index = self.slot(mask, k)
        self.slots[index, rows, :] = (self.slots[index, rows, :].astype(f32) + term.astype(f32)).astype(bf16)

    def view(self, mask, k, part):
        start, size = self.parts[part]
        return self.slots.at[self.slot(mask, k), pl.ds(start, size)]

    def cell(self, part, level, mask):
        free = [b for b in self.bits if b not in self.orders[part][: level + 1]]
        return sum(1 << n for n, b in enumerate(free) if mask >> b & 1)

    def pass_on(self, part, level, mask, k):
        order = self.orders[part]
        src = self.view(mask, k, part)
        if level == len(order):
            return
        bit = 1 << order[level]
        if mask & bit:
            rest = mask ^ bit
            dst = self.level_in[part][level].at[self.cell(part, level, rest), k]
            self.send(src, dst, (self.dp ^ bit, self.z), ("l", part, level, rest, k), part)

    def events(self, begin=6.0, gap=9.6, level_gap=(9.0, 19.0), seq_gap=0.5):
        out = []
        for turn, k in enumerate(self.turn()):
            at = begin + max(0, turn - 1) * gap
            for mask in self.masks[::-1]:
                out.append((at, ("c", mask, k)))
            at = begin + turn * gap
            for level in range(len(self.bits)):
                for part in (0, 1):
                    past = self.orders[part][: level + 1]
                    for mask in self.masks[::-1]:
                        if not any(mask >> b & 1 for b in past):
                            out.append((at + level_gap[min(level, 1)], ("l", part, level, mask, k)))
            if k:
                for part in (0, 1):
                    out.append((at + level_gap[min(len(self.bits) - 1, 1)] + seq_gap, ("z", part, k)))
        return sorted(out, key=lambda e: e[0])

    def step(self, event):
        if event[0] == "c":
            _, mask, k = event
            i = self.masks.index(mask)
            self.wait(self.core_in.at[i, k], ("c", i, k))
            self.add(mask, k, None, self.core_in[i, k])
            for part in (0, 1):
                self.pass_on(part, 0, mask, k)
            return
        if event[0] == "z":
            _, part, k = event
            self.along(part, k)
            return
        _, part, level, mask, k = event
        index = self.cell(part, level, mask)
        self.wait(self.level_in[part][level].at[index, k], ("l", part, level, mask, k))
        self.add(mask, k, part, self.level_in[part][level][index, k])
        self.pass_on(part, level + 1, mask, k)

    def from_side(self, part, place, side):
        index = place if side == 0 else self.n
        ref = self.seq_in[part].at[index]
        remote(ref, ref, self.send_sems.at[0], self.seq_sems.at[part, index], (self.dp, self.z)).wait_recv()
        return self.seq_in[part][index].astype(f32)

    def along(self, part, k):
        place = nearest(self.z, self.n, k)
        up = place > self.z

        @pl.when((up & (self.z > 0)) | (jnp.logical_not(up) & (self.z < self.n - 1)))
        def _():
            self.add(0, k, part, self.from_side(part, place, 0))

        to = jnp.where(up, self.z + 1, self.z - 1)
        index = jnp.where((to == place) & jnp.logical_not(up), self.n, place)
        self.send(
            self.view(0, k, part), self.seq_in[part].at[index], (self.dp, to), self.seq_sems.at[part, index], part
        )

    def finish(self):
        index = self.slot(0, 0)
        for part in (0, 1):
            start, size = self.parts[part]
            rows = slice(start, start + size)
            self.out[rows, :] = self.slots[index, rows, :].astype(f32)
            for side, there in ((0, self.z > 0), (1, self.z < self.n - 1)):

                @pl.when(there)
                def _():
                    self.out[rows, :] += self.from_side(part, self.z, side)

        for index, part in enumerate(self.started):
            start, size = (0, self.slots.shape[1]) if part is None else self.parts[part]
            ref = self.slots.at[0, pl.ds(start, size)]
            remote(ref, ref, self.send_sems.at[index], self.recv_sems.at[0], (self.dp, self.z)).wait_send()


def scatter_scratch(dp_size, seq_size, rows):
    bits = dp_size.bit_length() - 2
    masks = 1 << bits
    half = rows // 32 * 16
    sizes = [half, rows - half]
    shapes = [pltpu.VMEM((masks, seq_size, rows, LANES), bf16), pltpu.VMEM((rows, LANES), f32)]
    for size in sizes:
        for level in range(bits):
            shapes.append(pltpu.VMEM((masks >> (level + 1), seq_size, size, LANES), bf16))
    for size in sizes:
        shapes.append(pltpu.VMEM((seq_size + 1, size, LANES), bf16))
    count = masks * seq_size + 2 * (masks - 1) * seq_size + 2 * (seq_size - 1)
    shapes += [
        pltpu.SemaphoreType.DMA((count,)),
        pltpu.SemaphoreType.DMA((count,)),
        pltpu.SemaphoreType.DMA((2, seq_size + 1)),
    ]
    return shapes


def make_scatter(dp_size, seq_size, slots, refs):
    bits = dp_size.bit_length() - 2
    core_in, total, *rest = refs
    level_in = [rest[:bits], rest[bits : 2 * bits]]
    rest = rest[2 * bits :]
    return Scatter(dp_size, seq_size, slots, total, core_in, level_in, rest[:2], *rest[2:])


def deliver_kernel(out_in, grad_in, a_in, m_in, out, grad, a_out, m_out, sems):
    copies = [
        pltpu.make_async_copy(src, dst, sems.at[i])
        for i, (src, dst) in enumerate([(out_in, out), (a_in, a_out), (m_in, m_out)])
    ]
    for copy in copies:
        copy.start()
    grad[...] = grad_in[...].astype(f32)
    for copy in copies:
        copy.wait()


ANY = pl.BlockSpec(memory_space=pl.ANY)
LOCAL = pl.BlockSpec(memory_space=pltpu.VMEM)


def shape_of(dims, dtype):
    return jax.ShapeDtypeStruct(dims, dtype)


def per_chip_sequence(inputs, segments, attn_params, mlp_params, cotangent):
    dp_size, n = lax.axis_size("dp"), lax.axis_size("seq")
    devices = dp_size * n
    block = inputs.shape[2]
    length = n * block
    tokens = 2 * block
    a_layout = attn_layout(attn_params.shape[0] // LANES, devices)
    m_layout = mlp_layout_of(mlp_params.shape[0] // LANES, devices)
    a_raw, m_raw = attn_params.reshape(-1, LANES), mlp_params.reshape(-1, LANES)
    a_rows, m_rows = a_layout.slot_rows, m_layout.slot_rows
    wide = [pltpu.VMEM((raw.shape[0] + 2 * MARGIN, LANES), f32) for raw in (a_raw, m_raw)]
    seg_rows = segments.reshape(2, block // LANES, LANES)
    send, recv = gather_counts(dp_size, n)
    dma = pltpu.SemaphoreType.DMA
    across = shape_of((HALF_COLS, length), bf16)
    heads = shape_of((HALF_HEADS, length, LANES), bf16)
    own = shape_of((2, block, D), bf16)
    kept = [
        shape_of((length, D), bf16), shape_of((3, D, HALF_COLS), bf16), across, across, heads, heads, heads,
    ]
    (
        m_slots, cot_own, n1, wqkv, qt, kt, qh, kh, vh, x_own, w_proj, vec, seg_all, lse, att,
    ) = pl.pallas_call(
        functools.partial(forward_kernel, dp_size, n, a_layout, m_layout),
        out_shape=[shape_of((devices, m_rows, LANES), bf16), own]
        + kept
        + [
            own, shape_of((D, D), bf16), shape_of((8, D), f32),
            shape_of((n, block // LANES, LANES), jnp.int32), shape_of((8, length), f32), shape_of((2, 2, block, HALF_COLS), bf16),
        ],
        in_specs=[ANY] * 3 + [LOCAL] * 2,
        out_specs=[ANY] * 9 + [LOCAL] * 6,
        scratch_shapes=[pltpu.VMEM(like.shape, like.dtype) for like in kept]
        + [
            pltpu.VMEM((devices, a_rows, LANES), bf16),
            pltpu.VMEM((a_rows, LANES), bf16),
            pltpu.VMEM((m_rows, LANES), bf16),
        ]
        + wide
        + [
            pltpu.VMEM((n, block, D), bf16),
            pltpu.VMEM((3, length, HALF_COLS), bf16),
            pltpu.VMEM((HALF_COLS, length), bf16),
            pltpu.VMEM((length, LANES), jnp.int32),
            pltpu.VMEM((length, block), f32),
            pltpu.VMEM((HALF_COLS, length), f32),
            pltpu.VMEM((2, block, HALF_COLS), bf16),
            dma((send,)), dma((recv,)), dma((send,)), dma((recv,)), dma((2,)),
            dma((3, 4)), dma((3, n)), dma((2, 2)), dma((2, 2)), dma((len(kept),)),
        ],
        compiler_params=pltpu.CompilerParams(collective_id=0, has_side_effects=True, vmem_limit_bytes=VMEM_LIMIT),
    )(inputs[:, 0], seg_rows, cotangent[:, 0], a_raw, m_raw)

    out_back, grad_back, a_sum, m_sum = pl.pallas_call(
        functools.partial(backward_kernel, dp_size, n, a_layout, m_layout),
        out_shape=[own, own, shape_of((a_layout.rows, LANES), f32), shape_of((m_layout.rows, LANES), f32)],
        in_specs=[ANY] * 12 + [LOCAL] * 3,
        out_specs=[ANY] * 2 + [LOCAL] * 2,
        scratch_shapes=[
            pltpu.VMEM((devices, m_rows, LANES), bf16),
            pltpu.VMEM((devices, a_rows, LANES), bf16),
            pltpu.VMEM((2, block, D), bf16),
            pltpu.VMEM((tokens, D), bf16),
            pltpu.VMEM((tokens, D), f32),
            pltpu.VMEM((2, tokens, HALF_COLS), bf16),
            pltpu.VMEM((n, block, HALF_COLS), bf16),
            pltpu.VMEM((2, block, D), f32),
            pltpu.VMEM((1, D), f32),
        ]
        + wide
        + [dma((4, 2)), dma((2, 2)), dma((2, 2)), dma((12,))]
        + scatter_scratch(dp_size, n, m_rows)
        + scatter_scratch(dp_size, n, a_rows),
        compiler_params=pltpu.CompilerParams(collective_id=1, has_side_effects=True, vmem_limit_bytes=VMEM_LIMIT),
    )(
        m_slots, x_own, n1, wqkv, qt, kt, qh, kh, vh,
        cot_own.reshape(tokens, D), att.reshape(2, tokens, HALF_COLS), w_proj, vec, seg_all, lse,
    )
    out, grad, a_sum, m_sum = pl.pallas_call(
        deliver_kernel,
        out_shape=[own, shape_of(own.shape, f32), shape_of(a_sum.shape, f32), shape_of(m_sum.shape, f32)],
        in_specs=[ANY, LOCAL, ANY, ANY],
        out_specs=[ANY, LOCAL, ANY, ANY],
        scratch_shapes=[dma((3,))],
        compiler_params=pltpu.CompilerParams(vmem_limit_bytes=16 * 2**20),
    )(out_back, grad_back, a_sum, m_sum)
    return out[:, None], grad[:, None], a_sum.reshape(-1), m_sum.reshape(-1)


def solution(mesh):
    in_specs = (
        P(None, "dp", "seq", None),
        P(None, "dp", "seq"),
        P(("dp", "seq")),
        P(("dp", "seq")),
        P(None, "dp", "seq", None),
    )
    out_specs = (
        P(None, "dp", "seq", None),
        P(None, "dp", "seq", None),
        P(("dp", "seq")),
        P(("dp", "seq")),
    )
    one_each = mesh.shape["seq"] == 4 and mesh.shape["dp"] % 2 == 0
    return jax.shard_map(
        per_chip_sequence if one_each else per_device, mesh=mesh, in_specs=in_specs, out_specs=out_specs, check_vma=False
    )
```

```python
import functools
from functools import partial
import math

import jax
import jax.numpy as jnp
from jax import lax
from jax.experimental import pallas as pl
from jax.experimental.pallas import tpu as pltpu
from jax.sharding import PartitionSpec as P

D = 768
H = 12
HD = 64
FF = 3072


norm_eps = 1e-05
score_floor = -1e30
key_block = 512


def attention_layout():
    return [(D,), (D,), (D, 3 * D), (D,), (D,), (D, D), (D,)]


def mlp_layout():
    return [(D,), (D,), (D, FF), (FF,), (FF, D), (D,)]


def unpack_params(flat_vector, layout):
    offset = 0
    result = []
    for dims_entry in layout:
        amount = math.prod(dims_entry)
        result.append(lax.slice_in_dim(flat_vector, offset, offset + amount).reshape(dims_entry))
        offset += amount
    return result


def layer_norm(values, gain, shift):
    average = jnp.mean(values, axis=-1, keepdims=True)
    centred = values - average
    spread = jnp.mean(centred * centred, axis=-1, keepdims=True)
    return centred * lax.rsqrt(spread + norm_eps) * gain + shift


def gelu_tanh(values):
    return jax.nn.gelu(values, approximate=True)


def pack_grads(grad_list, total_size):
    flat_parts = [part_grad.reshape(-1) for part_grad in grad_list]
    used_total = sum((part_grad.size for part_grad in grad_list))
    flat_parts.append(jnp.zeros((total_size - used_total,), jnp.float32))
    return jnp.concatenate(flat_parts)


def fetch_params(attn_params, mlp_params):
    gathered = (
        lax.all_gather(attn_params, ("dp", "seq"), axis=0, tiled=True),
        lax.all_gather(mlp_params, ("dp", "seq"), axis=0, tiled=True),
    )
    return (
        unpack_params(gathered[0], attention_layout()),
        unpack_params(gathered[1], mlp_layout()),
    )


def send_grads(attn_list, mlp_list, attn_total, mlp_total):
    return (
        lax.psum_scatter(
            pack_grads(attn_list, attn_total), ("dp", "seq"), scatter_dimension=0, tiled=True
        ),
        lax.psum_scatter(
            pack_grads(mlp_list, mlp_total), ("dp", "seq"), scatter_dimension=0, tiled=True
        ),
    )


def fold_keys(key_rows, key_segs, fold_step, start_carry):
    return fold_step(
        start_carry,
        (
            lax.all_gather(key_rows, "seq", axis=0, tiled=True),
            lax.all_gather(key_segs, "seq", axis=0, tiled=True),
        ),
        jnp.int32(0),
    )


def over_blocks(block_step, carry_now, key_piece, key_start):
    piece_rows = key_piece[0].shape[0]
    step_rows = math.gcd(piece_rows, key_block)

    def loop_step(index_block, carry_in):
        offset = index_block * step_rows
        sub_piece = tuple(
            (lax.dynamic_slice_in_dim(member, offset, step_rows, 0) for member in key_piece)
        )
        return block_step(carry_in, sub_piece, offset)

    return lax.fori_loop(0, piece_rows // step_rows, loop_step, carry_now)


def block_scores(query_heads, query_segs, query_pos, kv_rows, key_segs, key_start):
    key_heads = kv_rows[:, :D].reshape(-1, H, HD)
    scores = jnp.einsum(
        "qhd,khd->hqk", query_heads, key_heads, preferred_element_type=jnp.float32
    ) * (1.0 / math.sqrt(HD))
    key_pos = key_start + jnp.arange(kv_rows.shape[0], dtype=jnp.int32)
    allowed = (query_segs[:, None] == key_segs[None, :]) & (key_pos[None, :] <= query_pos[:, None])
    return (jnp.where(allowed[None], scores, score_floor), key_heads)


MESH = pl.DeviceIdType.MESH
LANES = 128

def pad_rows(rows):
    return -(-rows // 16) * 16


def nearest(z, n, i):
    last = n - 1
    high = z > last - z
    near = jnp.where(high, last - z, z)
    step = (i // 2) if i % 2 == 0 else -((i + 1) // 2)
    found = jnp.where(i <= 2 * near, near + step, i)
    return jnp.where(high, last - found, found)


class Gather:
    def __init__(self, dp_size, seq_size, own, slots, send_sems, recv_sems):
        self.n = seq_size
        self.bits = list(range(1, dp_size.bit_length() - 1))
        self.dp = lax.axis_index("dp")
        self.z = lax.axis_index("seq")
        self.own, self.slots = own, slots
        self.rows = own.shape[0]
        half = self.rows // 32 * 16
        self.parts = [(0, half), (half, self.rows - half)]
        self.orders = [self.bits, self.bits[::-1]]
        self.send_sems, self.recv_sems = send_sems, recv_sems
        self.started = []

    def peers(self):
        out = [(self.dp, lax.rem(self.z + k, self.n)) for k in range(1, self.n)]
        return out + [(self.dp ^ (1 << b), self.z) for b in [0] + self.bits]

    def place(self, i):
        return nearest(self.z, self.n, i)

    def view(self, mask, i, part):
        index = (self.dp ^ mask) * self.n + self.place(i)
        start, size = self.parts[part]
        return self.slots.at[index, pl.ds(start, size)]

    def source(self, mask, i, part):
        if mask == 0 and i == 0:
            start, size = self.parts[part]
            return self.own.at[pl.ds(start, size)]
        return self.view(mask, i, part)

    def recv_sem(self, sibling, part, mask, i):
        count = 1 << len(self.bits)
        return self.recv_sems.at[((sibling * 2 + part) * count + (mask >> 1)) * self.n + self.place(i)]

    def send(self, mask, i, part, to, recv_sem, when=None):
        index = len(self.started)
        self.started.append((part, when))

        def start():
            pltpu.make_async_remote_copy(
                src_ref=self.source(mask, i, part), dst_ref=self.view(mask, i, part),
                send_sem=self.send_sems.at[index], recv_sem=recv_sem, device_id=to, device_id_type=MESH,
            ).start()

        if when is None:
            start()
        else:
            pl.when(when())(start)

    def wait(self, sibling, part, mask, i):
        view = self.view(mask ^ sibling, i, part)
        pltpu.make_async_remote_copy(
            src_ref=view, dst_ref=view, send_sem=self.send_sems.at[0],
            recv_sem=self.recv_sem(sibling, part, mask, i),
            device_id=(self.dp, self.z), device_id_type=MESH,
        ).wait_recv()

    def along(self, i, part, up):
        if i == 0:
            to = self.z + 1 if up else self.z - 1
        else:
            to = jnp.where(self.place(i) < self.z, self.z + 1, self.z - 1)

        def when():
            if i == 0:
                return (self.z < self.n - 1) if up else (self.z > 0)
            below = self.place(i) < self.z
            return (below & (self.z < self.n - 1)) | (jnp.logical_not(below) & (self.z > 0))

        self.send(0, i, part, (self.dp, to), self.recv_sem(0, part, 0, i), when)

    def forward(self, part, mask, i):
        if mask == 0 and i:
            self.along(i, part, True)
        order = self.orders[part]
        for level in range(len(order)):
            if not any(mask >> b & 1 for b in order[level:]):
                bit = 1 << order[level]
                self.send(mask, i, part, (self.dp ^ bit, self.z), self.recv_sem(0, part, mask | bit, i))
        self.send(mask, i, part, (self.dp ^ 1, self.z), self.recv_sem(1, part, mask, i))

    def begin_seq(self, part):
        for up in (True, False):
            self.along(0, part, up)

    def begin_bits(self):
        for level in range(len(self.bits)):
            for part in (0, 1):
                bit = 1 << self.orders[part][level]
                self.send(0, 0, part, (self.dp ^ bit, self.z), self.recv_sem(0, part, bit, 0))
        for part in (0, 1):
            self.send(0, 0, part, (self.dp ^ 1, self.z), self.recv_sem(1, part, 0, 0))

    def begin(self):
        self.begin_seq(0)
        self.begin_seq(1)
        self.begin_bits()

    def events(self, seq_times=None, own=0.0, level_gap=1.0):
        if seq_times is None:
            seq_times = [(i + 1.0, i + 1.5) for i in range(self.n - 1)]
        out = []
        for i in range(self.n):
            for part in (0, 1):
                at = seq_times[i - 1][part] if i else own
                if i:
                    out.append((at, (part, 0, i)))
                order = self.orders[part]
                for level in range(len(order)):
                    for low in range(1 << level):
                        mask = 1 << order[level]
                        for n in range(level):
                            if low >> n & 1:
                                mask |= 1 << order[n]
                        out.append((at + (level + 1) * level_gap, (part, mask, i)))
        return sorted(out, key=lambda e: e[0])

    def step(self, event):
        part, mask, i = event
        self.wait(0, part, mask, i)
        self.forward(part, mask, i)

    def finish_sibling(self):
        for part, mask, i in [(0, 0, 0), (1, 0, 0)] + [event for _, event in self.events()]:
            self.wait(1, part, mask, i)

    def finish_sends(self):
        for index, (part, when) in enumerate(self.started):

            def wait(index=index, part=part):
                start, size = self.parts[part]
                view = self.slots.at[0, pl.ds(start, size)]
                pltpu.make_async_remote_copy(
                    src_ref=view, dst_ref=view, send_sem=self.send_sems.at[index], recv_sem=self.recv_sems.at[0],
                    device_id=(self.dp, self.z), device_id_type=MESH,
                ).wait_send()

            if when is None:
                wait()
            else:
                pl.when(when())(wait)


def gather_counts(dp_size, seq_size):
    bits = dp_size.bit_length() - 2
    masks = 1 << bits
    recv = 4 * masks * seq_size
    send = 2 * (seq_size + 1 + seq_size * (masks - 1) + seq_size * masks)
    return send, recv


def gather_kernel(dp_size, seq_size, a_own, m_own, a_slots, m_slots, a_send, a_recv, m_send, m_recv, own_sems):
    ga = Gather(dp_size, seq_size, a_own, a_slots, a_send, a_recv)
    gm = Gather(dp_size, seq_size, m_own, m_slots, m_send, m_recv)
    barrier = pltpu.get_barrier_semaphore()
    peers = ga.peers()
    for peer in peers:
        pl.semaphore_signal(barrier, inc=1, device_id=peer, device_id_type=MESH)
    pl.semaphore_wait(barrier, len(peers))
    ca = pltpu.make_async_copy(a_own, a_slots.at[ga.dp * ga.n + ga.z], own_sems.at[0])
    cm = pltpu.make_async_copy(m_own, m_slots.at[ga.dp * ga.n + ga.z], own_sems.at[1])
    ca.start()
    cm.start()
    ga.begin()
    gm.begin()
    for _, event in ga.events():
        ga.step(event)
    for _, event in gm.events():
        gm.step(event)
    ca.wait()
    cm.wait()
    ga.finish_sibling()
    gm.finish_sibling()
    ga.finish_sends()
    gm.finish_sends()


def to_rows(flat):
    rows = flat.shape[0] // LANES
    return jnp.pad(flat.reshape(rows, LANES), ((0, pad_rows(rows) - rows), (0, 0)))


def gather_params(attn, mlp, dp_size, seq_size):
    a, m = to_rows(attn), to_rows(mlp)
    devices = dp_size * seq_size
    send, recv = gather_counts(dp_size, seq_size)
    return pl.pallas_call(
        functools.partial(gather_kernel, dp_size, seq_size),
        out_shape=[jax.ShapeDtypeStruct((devices,) + a.shape, jnp.bfloat16), jax.ShapeDtypeStruct((devices,) + m.shape, jnp.bfloat16)],
        in_specs=[pl.BlockSpec(memory_space=pl.ANY)] * 2,
        out_specs=[pl.BlockSpec(memory_space=pl.ANY)] * 2,
        scratch_shapes=[pltpu.SemaphoreType.DMA((send,)), pltpu.SemaphoreType.DMA((recv,)),
                        pltpu.SemaphoreType.DMA((send,)), pltpu.SemaphoreType.DMA((recv,)), pltpu.SemaphoreType.DMA((2,))],
        compiler_params=pltpu.CompilerParams(collective_id=0, has_side_effects=True),
    )(a, m)


def per_device(inputs, segments, attn_params, mlp_params, cotangent):
    micro_count = inputs.shape[0]
    local_rows = inputs.shape[2]
    seq_length = local_rows * lax.axis_size("seq")
    attn_total = attn_params.shape[0] * lax.axis_size(("dp", "seq"))
    mlp_total = mlp_params.shape[0] * lax.axis_size(("dp", "seq"))
    query_pos = lax.axis_index("seq") * local_rows + jnp.arange(local_rows, dtype=jnp.int32)
    score_scale = 1.0 / math.sqrt(HD)
    out_rows = []
    grad_rows = []
    attn_sums = None
    mlp_sums = None
    shard_sums = None
    attn_slots, mlp_slots = gather_params(attn_params, mlp_params, lax.axis_size("dp"), lax.axis_size("seq"))
    attn_set = unpack_params(
        attn_slots[:, : attn_params.shape[0] // LANES].reshape(-1), attention_layout()
    )
    mlp_set = unpack_params(
        mlp_slots[:, : mlp_params.shape[0] // LANES].reshape(-1), mlp_layout()
    )
    for micro_index in range(micro_count):
        gain_one, shift_one, w_qkv, bias_query, bias_value, w_proj, bias_proj = attn_set
        gain_two, shift_two, w_up, bias_up, w_down, bias_down = mlp_set
        input_rows = inputs[micro_index, 0].astype(jnp.float32)
        query_segs = segments[micro_index, 0]
        normed_one, norm_one_back = jax.vjp(
            layer_norm, input_rows, gain_one.astype(jnp.float32), shift_one.astype(jnp.float32)
        )
        normed_one_low = normed_one.astype(jnp.bfloat16)
        merged_rows = jnp.dot(normed_one_low, w_qkv, preferred_element_type=jnp.float32)
        query_low = (merged_rows[:, :D] + bias_query.astype(jnp.float32)).astype(jnp.bfloat16)
        kv_local = jnp.concatenate(
            [merged_rows[:, D : 2 * D], merged_rows[:, 2 * D :] + bias_value.astype(jnp.float32)],
            axis=1,
        ).astype(jnp.bfloat16)
        query_heads = query_low.reshape(local_rows, H, HD)

        def max_step(carry_in, sub_piece, key_start):
            scores, key_heads = block_scores(
                query_heads, query_segs, query_pos, sub_piece[0], sub_piece[1], key_start
            )
            running_top, running_total = carry_in
            new_top = jnp.maximum(running_top, jnp.max(scores, axis=-1))
            new_total = running_total * jnp.exp(running_top - new_top) + jnp.sum(
                jnp.exp(scores - new_top[..., None]), axis=-1
            )
            return (new_top, new_total)

        top_start = jnp.full((H, local_rows), score_floor, jnp.float32)
        row_top, row_total = fold_keys(
            kv_local,
            query_segs,
            partial(over_blocks, max_step),
            (top_start, jnp.zeros((H, local_rows), jnp.float32)),
        )
        log_total = row_top + jnp.log(row_total)

        def value_step(carry_in, sub_piece, key_start):
            scores, key_heads = block_scores(
                query_heads, query_segs, query_pos, sub_piece[0], sub_piece[1], key_start
            )
            probs = jnp.exp(scores - log_total[..., None])
            probs_low = probs.astype(jnp.bfloat16)
            probs_rest = (probs - probs_low.astype(jnp.float32)).astype(jnp.bfloat16)
            value_heads = sub_piece[0][:, D:].reshape(-1, H, HD)
            main_part, rest_part = carry_in
            main_part = main_part + jnp.einsum(
                "hqk,khd->qhd", probs_low, value_heads, preferred_element_type=jnp.float32
            )
            rest_part = rest_part + jnp.einsum(
                "hqk,khd->qhd", probs_rest, value_heads, preferred_element_type=jnp.float32
            )
            return (main_part, rest_part)

        zero_heads = jnp.zeros((local_rows, H, HD), jnp.float32)
        main_sum, rest_sum = fold_keys(
            kv_local, query_segs, partial(over_blocks, value_step), (zero_heads, zero_heads)
        )
        attended_low = main_sum.reshape(local_rows, D).astype(jnp.bfloat16)
        attended_full = main_sum + rest_sum
        middle = (
            input_rows
            + jnp.dot(attended_low, w_proj, preferred_element_type=jnp.float32)
            + bias_proj.astype(jnp.float32)
        )
        normed_two, norm_two_back = jax.vjp(
            layer_norm, middle, gain_two.astype(jnp.float32), shift_two.astype(jnp.float32)
        )
        normed_two_low = normed_two.astype(jnp.bfloat16)
        hidden = jnp.dot(normed_two_low, w_up, preferred_element_type=jnp.float32) + bias_up.astype(
            jnp.float32
        )
        active, gelu_back = jax.vjp(gelu_tanh, hidden)
        active_low = active.astype(jnp.bfloat16)
        result = (
            middle
            + jnp.dot(active_low, w_down, preferred_element_type=jnp.float32)
            + bias_down.astype(jnp.float32)
        )
        out_rows.append(result.astype(jnp.bfloat16))
        w_qkv, w_proj = (attn_set[2], attn_set[5])
        w_up, w_down = (mlp_set[2], mlp_set[4])
        cot_low = cotangent[micro_index, 0]
        cot_rows = cot_low.astype(jnp.float32)
        grad_w_down = jnp.einsum(
            "rf,rd->fd", active_low, cot_low, preferred_element_type=jnp.float32
        )
        grad_b_down = jnp.sum(cot_rows, axis=0)
        grad_active = jnp.einsum("rd,fd->rf", cot_low, w_down, preferred_element_type=jnp.float32)
        grad_hidden = gelu_back(grad_active)[0].astype(jnp.bfloat16)
        grad_w_up = jnp.einsum(
            "rd,rf->df", normed_two_low, grad_hidden, preferred_element_type=jnp.float32
        )
        grad_b_up = jnp.sum(grad_hidden.astype(jnp.float32), axis=0)
        grad_normed_two = jnp.einsum(
            "rf,df->rd", grad_hidden, w_up, preferred_element_type=jnp.float32
        )
        grad_middle_norm, grad_gain_two, grad_shift_two = norm_two_back(grad_normed_two)
        grad_middle = cot_rows + grad_middle_norm
        grad_branch = grad_middle.astype(jnp.bfloat16)
        grad_w_proj = jnp.einsum(
            "rd,re->de", attended_low, grad_branch, preferred_element_type=jnp.float32
        )
        grad_b_proj = jnp.sum(grad_branch.astype(jnp.float32), axis=0)
        grad_attended = jnp.einsum(
            "re,de->rd", grad_branch, w_proj, preferred_element_type=jnp.float32
        ).astype(jnp.bfloat16)
        grad_heads = grad_attended.reshape(local_rows, H, HD)
        row_delta = jnp.einsum("qhd,qhd->hq", grad_heads.astype(jnp.float32), attended_full)

        def grad_step(carry_in, sub_piece, key_start):
            scores, key_heads = block_scores(
                query_heads, query_segs, query_pos, sub_piece[0], sub_piece[1], key_start
            )
            value_heads = sub_piece[0][:, D:].reshape(-1, H, HD)
            probs = jnp.exp(scores - log_total[..., None])
            grad_probs = jnp.einsum(
                "qhd,khd->hqk", grad_heads, value_heads, preferred_element_type=jnp.float32
            )
            grad_scores = (probs * (grad_probs - row_delta[..., None])).astype(jnp.bfloat16)
            query_part, kv_part = carry_in
            query_part = (
                query_part
                + jnp.einsum(
                    "hqk,khd->qhd", grad_scores, key_heads, preferred_element_type=jnp.float32
                )
                * score_scale
            )
            key_grad = (
                jnp.einsum(
                    "hqk,qhd->khd", grad_scores, query_heads, preferred_element_type=jnp.float32
                )
                * score_scale
            )
            value_grad = jnp.einsum(
                "hqk,qhd->khd",
                probs.astype(jnp.bfloat16),
                grad_heads,
                preferred_element_type=jnp.float32,
            )
            block_grads = jnp.concatenate(
                [key_grad.reshape(-1, D), value_grad.reshape(-1, D)], axis=1
            )
            kv_part = lax.dynamic_update_slice_in_dim(kv_part, block_grads, key_start, 0)
            return (query_part, kv_part)

        query_sum, kv_sums = fold_keys(
            kv_local,
            query_segs,
            partial(over_blocks, grad_step),
            (zero_heads, jnp.zeros((seq_length, 2 * D), jnp.float32)),
        )
        kv_grads = lax.psum_scatter(
            kv_sums.astype(jnp.bfloat16), "seq", scatter_dimension=0, tiled=True
        ).astype(jnp.float32)
        grad_merged = jnp.concatenate([query_sum.reshape(local_rows, D), kv_grads], axis=1).astype(
            jnp.bfloat16
        )
        grad_merged_wide = grad_merged.astype(jnp.float32)
        grad_w_qkv = jnp.einsum(
            "rd,re->de", normed_one_low, grad_merged, preferred_element_type=jnp.float32
        )
        grad_b_query = jnp.sum(grad_merged_wide[:, :D], axis=0)
        grad_b_value = jnp.sum(grad_merged_wide[:, 2 * D :], axis=0)
        grad_normed_one = jnp.einsum(
            "re,de->rd", grad_merged, w_qkv, preferred_element_type=jnp.float32
        )
        grad_input_norm, grad_gain_one, grad_shift_one = norm_one_back(grad_normed_one)
        grad_rows.append(grad_middle + grad_input_norm)
        attn_list = [
            grad_gain_one,
            grad_shift_one,
            grad_w_qkv,
            grad_b_query,
            grad_b_value,
            grad_w_proj,
            grad_b_proj,
        ]
        mlp_list = [grad_gain_two, grad_shift_two, grad_w_up, grad_b_up, grad_w_down, grad_b_down]
        attn_sums = (
            attn_list
            if attn_sums is None
            else [left_sum + right_sum for left_sum, right_sum in zip(attn_sums, attn_list)]
        )
        mlp_sums = (
            mlp_list
            if mlp_sums is None
            else [left_sum + right_sum for left_sum, right_sum in zip(mlp_sums, mlp_list)]
        )
    shard_sums = send_grads(attn_sums, mlp_sums, attn_total, mlp_total)
    outputs = jnp.stack(out_rows)[:, None]
    input_grad = jnp.stack(grad_rows)[:, None]
    return (outputs, input_grad, shard_sums[0], shard_sums[1])


HALF_HEADS = H // 2
HALF_COLS = D // 2
ROW_D = D // LANES
ROW_FF = FF // LANES
ROW_QKV = 3 * ROW_D
ROW_HALF = HALF_COLS // LANES
FF_STEP = 512
HEAD = 16
MARGIN = 32
VMEM_LIMIT = 63 * 2**20

A_SEQ = ((6.0, 9.0), (12.0, 15.0), (18.0, 21.0))
A_OWN = (1.0, 6.1)
M_SEQ = ((16.5, 21.0), (25.5, 30.0), (34.5, 39.0))
M_OWN = (8.0, 8.6)
M_BEGIN = (0.0, -1.1, 4.0)
SEND_X = (6.0, 6.0, 6.0, 6.0)
SHARE_X = 24.5
SEND_COT = (45.0, 45.0)
FORWARD_START = 36.1
PROJECT = 4.0
HEAD_FORWARD = 2.9
BACKWARD_FIRST = 6.5
BACKWARD_START = 8.0
M_BACK = (6.0, 9.6, (9.0, 19.0), 0.5)
A_BACK = (-4.0, 4.0, (6.0, 13.0), 2.0)
HEAD_BACKWARD = 5.4

ATTN_QKV = 2 * ROW_D
ATTN_BQ = ATTN_QKV + D * ROW_QKV
ATTN_BV = ATTN_BQ + ROW_D
ATTN_PROJ = ATTN_BV + ROW_D
ATTN_BPROJ = ATTN_PROJ + D * ROW_D
MLP_UP = 2 * ROW_D
MLP_BUP = MLP_UP + D * ROW_FF
MLP_DOWN = MLP_BUP + ROW_FF
MLP_BDOWN = MLP_DOWN + FF * ROW_D

f32 = jnp.float32
bf16 = jnp.bfloat16


def dot_nn(left, right):
    return jnp.dot(left, right, preferred_element_type=f32)


def dot_nt(left, right):
    return lax.dot_general(left, right, (((1,), (1,)), ((), ())), preferred_element_type=f32)


def dot_tn(left, right):
    return lax.dot_general(left, right, (((0,), (0,)), ((), ())), preferred_element_type=f32)


def remote(src, dst, send_sem, recv_sem, to):
    return pltpu.make_async_remote_copy(
        src_ref=src, dst_ref=dst, send_sem=send_sem, recv_sem=recv_sem, device_id=to, device_id_type=MESH
    )


class Place:
    def __init__(self, seq_size):
        self.n = seq_size
        self.dp = lax.axis_index("dp")
        self.z = lax.axis_index("seq")
        self.core = lax.rem(self.dp, 2)
        self.base = self.dp - self.core
        self.sibling = (self.base + 1 - self.core, self.z)

    def line_peers(self):
        out = [self.sibling]
        for k in range(1, self.n):
            other = lax.rem(self.z + k, self.n)
            out += [(self.base, other), (self.base + 1, other)]
        return out

    def own_block(self, j):
        return 1 - self.core + 2 * j

    def other_block(self, j):
        return self.core + 2 * j

    def worker(self, micro):
        return (self.base + 1 - lax.rem(self.z, 2), 2 * micro + self.core)

    def home(self, j):
        return (self.base + lax.rem(self.z, 2), self.own_block(j)), self.z // 2


def split_heads(piece, heads, rows):
    lane = lax.broadcasted_iota(jnp.int32, (piece.shape[0], LANES), 1)
    for h in range(HALF_HEADS):
        pair = piece[:, h // 2 * LANES : (h // 2 + 1) * LANES]
        heads[h, rows, :] = jnp.where(lane // HD == h % 2, pair, jnp.zeros_like(pair))


class Action:
    def step(self, action):
        action()


class Steps:
    def __init__(self, timed):
        self.queue = sorted(timed, key=lambda e: e[0])

    def take(self, time):
        out = [event for at, event in self.queue if at <= time]
        self.queue = [e for e in self.queue if e[0] > time]
        return out

    def until(self, time):
        for owner, event in self.take(time):
            owner.step(event)

    def plan(self, start, points):
        out = {}
        for point, length in points:
            out[point] = self.take(start)
            start += length
        return out


def handle(plan, index):
    for turn, events in enumerate(plan):
        if events:

            @pl.when(index == turn)
            def _():
                for owner, event in events:
                    owner.step(event)


def greet(peers):
    barrier = pltpu.get_barrier_semaphore()
    for peer in peers:
        pl.semaphore_signal(barrier, inc=1, device_id=peer, device_id_type=MESH)
    pl.semaphore_wait(barrier, len(peers))


class Layout:
    def __init__(self, rows, devices, matrices, tail):
        self.rows, self.tail = rows, tail
        self.whole = sum(count * columns for _, count, columns in matrices) // devices
        self.slot_rows = self.whole + HEAD + tail
        self.regions = []
        first = 0
        for start, count, columns in matrices:
            shards = count * columns // self.whole
            self.regions.append((start, columns, self.whole // columns, first, shards))
            first += shards
        assert first == devices
        for s in range(devices):
            start, columns, height, first, _ = self.region(s)
            shift = start + self.whole * (s - first) - rows * s
            assert shift <= HEAD and shift + self.whole >= rows - tail and shift >= -MARGIN

    def region(self, s):
        return [r for r in self.regions if r[3] <= s < r[3] + r[4]][0]

    def shift(self, s, region):
        start, _, _, first, _ = region
        return start - self.whole * first + (self.whole - self.rows) * s

    def piece(self, row):
        s, q = row // self.rows, row % self.rows
        if q < HEAD:
            return s, self.whole + q
        assert q >= self.rows - self.tail
        return s, self.whole + HEAD + q - (self.rows - self.tail)

    def lacking(self, region):
        out = []
        start, columns, height, first, shards = region
        for s in range(first, first + shards):
            shift = self.shift(s, region)
            for q in range(self.whole):
                if not 0 <= shift + q < self.rows:
                    out.append(((s - first) * height + q // columns, q % columns) + self.piece(s * self.rows + shift + q))
        return out

    def beyond(self):
        out = []
        for s in range(sum(r[4] for r in self.regions)):
            shift = self.shift(s, self.region(s))
            for q in list(range(max(shift, 0))) + list(range(shift + self.whole, self.rows)):
                row = s * self.rows + q
                for start, columns, height, first, shards in self.regions:
                    if start <= row < start + shards * self.whole:
                        i, j = (row - start) // columns, (row - start) % columns
                        out.append(self.piece(row) + (first + i // height, j * height + i % height))
        return out

    def branch(self, s, action):
        for region in self.regions:
            pl.when((s >= region[3]) & (s < region[3] + region[4]))(functools.partial(action, region))

    def pack(self, own, wide, slot, s):
        wide[:MARGIN, :] = jnp.zeros((MARGIN, LANES), f32)
        wide[MARGIN + own.shape[0] :, :] = jnp.zeros((2 * MARGIN, LANES), f32)
        wide[MARGIN : MARGIN + own.shape[0], :] = own[...].astype(f32)

        def fill(region):
            _, columns, height, _, _ = region
            for j in range(columns):
                piece = wide[pl.ds(MARGIN + self.shift(s, region) + j, height, stride=columns), :]
                slot[j * height : (j + 1) * height, :] = piece.astype(bf16)

        self.branch(s, fill)
        slot[self.whole : self.whole + HEAD, :] = own[:HEAD, :]
        last = wide[MARGIN + self.rows - self.tail : MARGIN + self.rows, :]
        slot[self.whole + HEAD :, :] = last.astype(bf16)

    def unpack(self, slot, wide, out, s):
        def fill(region):
            _, columns, height, _, _ = region
            shift = self.shift(s, region)
            for j in range(columns):
                wide[pl.ds(MARGIN + shift + j, height, stride=columns), :] = slot[j * height : (j + 1) * height, :]
            out[...] = wide[MARGIN : MARGIN + self.rows, :]
            row = lax.broadcasted_iota(jnp.int32, (HEAD, LANES), 0)
            out[:HEAD, :] = jnp.where(row < shift, slot[self.whole : self.whole + HEAD, :], out[:HEAD, :])
            begin = self.rows - self.tail
            row = lax.broadcasted_iota(jnp.int32, (self.tail, LANES), 0) + begin
            last = slot[self.whole + HEAD :, :]
            out[begin:, :] = jnp.where(row >= shift + self.whole, last, out[begin:, :])

        self.branch(s, fill)

    def vector(self, slots, row, blocks):
        parts = []
        for j in range(blocks):
            s, q = self.piece(row + j)
            aligned = q // 16 * 16
            parts.append(slots[s, aligned : aligned + 16, :].astype(f32)[q - aligned : q - aligned + 1, :])
        return jnp.concatenate(parts, axis=1)

    def put_vectors(self, slots, entries):
        areas = {}
        for row, value in entries:
            for j in range(value.shape[1] // LANES):
                s, at = self.piece(row + j)
                begin = self.whole if at < self.whole + HEAD else self.whole + HEAD
                areas.setdefault((s, begin), {})[at - begin] = value[:, j * LANES : (j + 1) * LANES]
        zero = jnp.zeros((1, LANES), f32)
        for (s, begin), rows in areas.items():
            size = HEAD if begin == self.whole else self.tail
            tile = jnp.concatenate([rows.get(n, zero) for n in range(size)], axis=0)
            slots[s, begin : begin + size, :] = tile.astype(bf16)


def load_matrix(slots, layout, which, base, out):
    region = layout.regions[which]
    _, columns, height, first, shards = region

    def body(s, carry):
        rows = pl.ds(pl.multiple_of(s * height, height), height)
        for j in range(columns):
            out[rows, j * LANES : (j + 1) * LANES] = slots[s + first - base, j * height : (j + 1) * height, :]
        return carry

    lax.fori_loop(0, shards, body, 0)
    for i, j, s, q in layout.lacking(region):
        out[i : i + 1, j * LANES : (j + 1) * LANES] = slots[s - base, q : q + 1, :]


def attn_layout(rows, devices):
    return Layout(rows, devices, [(ATTN_QKV, D, ROW_QKV), (ATTN_PROJ, D, ROW_D)], 16)


def mlp_layout_of(rows, devices):
    return Layout(rows, devices, [(MLP_UP, D, ROW_FF), (MLP_DOWN, FF, ROW_D)], 32)


def norm_parts(values):
    average = jnp.mean(values, axis=-1, keepdims=True)
    centred = values - average
    spread = jnp.mean(centred * centred, axis=-1, keepdims=True)
    scale = lax.rsqrt(spread + norm_eps)
    return centred * scale, scale


def norm_back(normal, scale, grad, gain):
    scaled = grad * gain
    return scale * (
        scaled
        - jnp.mean(scaled, axis=-1, keepdims=True)
        - normal * jnp.mean(scaled * normal, axis=-1, keepdims=True)
    )


def keep_allowed(scores, seg_col, seg_all, b, i, block):
    parts = []
    for r in range(block // LANES):
        row = seg_all[i, r : r + 1, :]
        allowed = seg_col[b * block : (b + 1) * block, :] == row
        if b == i:
            key_pos = lax.broadcasted_iota(jnp.int32, (block, LANES), 0)
            query_pos = lax.broadcasted_iota(jnp.int32, (block, LANES), 1) + r * LANES
            allowed = allowed & (key_pos <= query_pos)
        parts.append(jnp.where(allowed, scores[:, r * LANES : (r + 1) * LANES], score_floor))
    return jnp.concatenate(parts, axis=1)


def segment_columns(seg_all, seg_col, block):
    for t in range(seg_all.shape[0]):
        for r in range(block // LANES):
            row = jnp.broadcast_to(seg_all[t, r : r + 1, :], (LANES, LANES))
            seg_col[pl.ds(t * block + r * LANES, LANES), :] = row.T


def forward_kernel(
    dp_size, seq_size, a_layout, m_layout,
    x_in, seg_in, cot_in, a_raw, m_raw,
    m_slots, cot_own, n1_out, wqkv_out, qt_out, kt_out, qh_out, kh_out, vh_out,
    x_own, w_proj, vec, seg_all, lse, att,
    n1, wqkv, qt, kt, qh, kh, vh,
    a_slots, a_own, m_own, a_wide, m_wide, x_all, plain, vt, seg_col, scores, ot, att_out,
    a_send, a_recv, m_send, m_recv, own_sems, move_send, move_recv, cot_sems, swap_sems, keep_sems,
):
    place = Place(seq_size)
    block = x_in.shape[1]
    ga = Gather(dp_size, seq_size, a_own, a_slots, a_send, a_recv)
    gm = Gather(dp_size, seq_size, m_own, m_slots, m_send, m_recv)
    mine = place.dp * seq_size + place.z
    a_layout.pack(a_raw, a_wide, a_own, mine)
    greet(place.line_peers() + [(place.dp ^ (1 << b), place.z) for b in ga.bits])

    own_copies = [
        pltpu.make_async_copy(a_own, a_slots.at[mine], own_sems.at[0]),
        pltpu.make_async_copy(m_own, m_slots.at[mine], own_sems.at[1]),
    ]
    ga.begin()
    m_layout.pack(m_raw, m_wide, m_own, mine)
    for copy in own_copies:
        copy.start()
    sent = []

    def launch(copy):
        copy.start()
        sent.append(copy)

    def send_segments():
        for micro in range(2):
            launch(
                remote(
                    seg_in.at[micro], seg_all.at[place.z], move_send.at[2, micro], move_recv.at[2, place.z],
                    place.worker(micro),
                )
            )

    def send_inputs(micro, half):
        rows = pl.ds(half * (block // 2), block // 2)
        launch(
            remote(
                x_in.at[micro, rows], x_all.at[place.z, rows], move_send.at[half, micro], move_recv.at[half, place.z],
                place.worker(micro),
            )
        )

    def moved(t, kind):
        return seg_all.at[t] if kind == 2 else x_all.at[t, pl.ds(kind * (block // 2), block // 2)]

    def arrival(t, kind):
        ref = moved(t, kind)
        return remote(ref, ref, move_send.at[kind, 0], move_recv.at[kind, t], place.sibling)

    def share_inputs():
        for j in range(2):
            t = place.own_block(j)
            for kind in range(3):
                ref = moved(t, kind)
                arrival(t, kind).wait_recv()
                launch(remote(ref, ref, move_send.at[kind, 2 + j], move_recv.at[kind, t], place.sibling))

    def send_cotangent(micro):
        remote(
            cot_in.at[micro], cot_own.at[place.z // 2], cot_sems.at[0, micro], cot_sems.at[1, place.z // 2],
            place.worker(micro),
        ).start()

    timed = [(time, (ga, event)) for time, event in ga.events(A_SEQ, *A_OWN)]
    timed += [(time, (gm, event)) for time, event in gm.events(M_SEQ, *M_OWN)]
    timed += [
        (at, (Action(), action))
        for at, action in (
            (SEND_X[0], send_segments), (SHARE_X, share_inputs), (M_BEGIN[2], gm.begin_bits),
            (M_BEGIN[0], functools.partial(gm.begin_seq, 0)), (M_BEGIN[1], functools.partial(gm.begin_seq, 1)),
        )
    ]
    timed += [
        (SEND_X[n], (Action(), functools.partial(send_inputs, 1 - n // 2, n % 2))) for n in range(4)
    ]
    timed += [(SEND_COT[n], (Action(), functools.partial(send_cotangent, 1 - n))) for n in range(2)]
    both = Steps(timed)
    both.until(FORWARD_START)
    own_copies[0].wait()
    ga.finish_sibling()
    height = a_layout.regions[0][2]

    def take_columns(s, carry):
        rows = pl.ds(pl.multiple_of(s * height, height), height)
        for section in range(3):
            for j in range(ROW_HALF):
                block_at = section * ROW_D + place.core * ROW_HALF + j
                piece = a_slots[s, pl.ds(pl.multiple_of(block_at * height, height), height), :]
                wqkv[section, rows, j * LANES : (j + 1) * LANES] = piece
        return carry

    lax.fori_loop(0, a_layout.regions[0][4], take_columns, 0)
    for core in range(2):

        @pl.when(place.core == core)
        def _():
            for i, j, s, q in a_layout.lacking(a_layout.regions[0]):
                section, at = j // ROW_D, j % ROW_D - core * ROW_HALF
                if 0 <= at < ROW_HALF:
                    wqkv[section, i : i + 1, at * LANES : (at + 1) * LANES] = a_slots[s, q : q + 1, :]

    load_matrix(a_slots, a_layout, 1, 0, w_proj)
    gain = a_layout.vector(a_slots, 0, ROW_D)
    shift = a_layout.vector(a_slots, ROW_D, ROW_D)
    vec[...] = jnp.zeros_like(vec)
    vec[0:1, :] = gain
    vec[1:2, :] = a_layout.vector(a_slots, ATTN_BPROJ, ROW_D)
    first_half = place.core == 0
    bias_query = a_layout.vector(a_slots, ATTN_BQ, ROW_D)
    bias_query = jnp.where(first_half, bias_query[:, :HALF_COLS], bias_query[:, HALF_COLS:])
    bias_value = a_layout.vector(a_slots, ATTN_BV, ROW_D)
    bias_value = jnp.where(first_half, bias_value[:, :HALF_COLS], bias_value[:, HALF_COLS:])
    both.until(FORWARD_START + 2)
    for j in range(2):
        for kind in range(3):
            arrival(place.other_block(j), kind).wait_recv()
        x_own[j] = x_all[place.own_block(j)]
    segment_columns(seg_all, seg_col, block)

    project_plan = both.plan(FORWARD_START + 2, [(t, PROJECT / seq_size) for t in range(seq_size)])

    def project(t, carry):
        handle([project_plan[turn] for turn in range(seq_size)], t)
        rows = pl.ds(pl.multiple_of(t * block, block), block)
        normal, _ = norm_parts(x_all[t].astype(f32))
        low = (normal * gain + shift).astype(bf16)
        n1[rows, :] = low
        query = (dot_nn(low, wqkv[0]) + bias_query).astype(bf16).astype(f32) * (1.0 / math.sqrt(HD))
        key = dot_nn(low, wqkv[1]).astype(bf16)
        value = dot_nn(low, wqkv[2]) + bias_value
        qt[:, rows] = query.T.astype(bf16)
        split_heads(key, kh, rows)
        vt[:, rows] = value.T.astype(bf16)
        plain[0, rows, :] = query.astype(bf16)
        plain[1, rows, :] = key
        plain[2, rows, :] = value.astype(bf16)
        return carry

    def other_forms(t, carry):
        rows = pl.ds(pl.multiple_of(t * block, block), block)
        split_heads(plain[0, rows, :], qh, rows)
        split_heads(plain[2, rows, :], vh, rows)
        kt[:, rows] = plain[1, rows, :].astype(f32).T.astype(bf16)
        return carry

    lax.fori_loop(0, seq_size, project, 0)
    keep = [
        pltpu.make_async_copy(src, dst, keep_sems.at[i])
        for i, (src, dst) in enumerate([(n1, n1_out), (wqkv, wqkv_out), (qt, qt_out), (kh, kh_out)])
    ]
    for copy in keep:
        copy.start()
    lse[...] = jnp.zeros_like(lse)
    unit = HEAD_FORWARD / (seq_size * (seq_size + 1) // 2)
    points = [((h, i), unit * (i + 1)) for h in range(HALF_HEADS) for i in range(seq_size)]
    plan = both.plan(FORWARD_START + 2 + PROJECT, points)

    def one_head(h, carry):
        head_rows = pl.ds(pl.multiple_of(h * HD, HD), HD)
        pair_rows = pl.ds(pl.multiple_of(h // 2 * LANES, LANES), LANES)
        for i in range(seq_size):
            handle([plan[c, i] for c in range(HALF_HEADS)], h)
            columns = slice(i * block, (i + 1) * block)
            query = qt[pair_rows, columns]
            top = jnp.full((1, block), -jnp.inf, f32)
            for b in range(i + 1):
                rows = slice(b * block, (b + 1) * block)
                piece = keep_allowed(dot_nn(kh[h, rows, :], query), seg_col, seg_all, b, i, block)
                scores[rows, :] = piece
                top = jnp.maximum(top, jnp.max(piece, axis=0, keepdims=True))
            total = jnp.zeros((1, block), f32)
            for b in range(i + 1):
                rows = slice(b * block, (b + 1) * block)
                piece = jnp.exp(scores[rows, :] - top)
                scores[rows, :] = piece
                total = total + jnp.sum(piece, axis=0, keepdims=True)
            inverse = 1.0 / total
            result = jnp.zeros((HD, block), f32)
            for b in range(i + 1):
                rows = slice(b * block, (b + 1) * block)
                result = result + dot_nn(vt[head_rows, rows], (scores[rows, :] * inverse).astype(bf16))
            ot[head_rows, columns] = result
            lse[pl.ds(h, 1), columns] = top + jnp.log(total)
        return carry

    lax.fori_loop(0, HALF_HEADS, one_head, 0)
    both.until(FORWARD_START + 3 + PROJECT + HALF_HEADS * HEAD_FORWARD)

    for j in range(2):
        columns = pl.ds(pl.multiple_of(place.other_block(j) * block, block), block)
        att_out[j] = ot[:, columns].T.astype(bf16)
        copy = remote(
            att_out.at[j], att.at[place.core, j], swap_sems.at[0, j], swap_sems.at[1, j], place.sibling
        )
        copy.start()
        sent.append(copy)
    for j in range(2):
        columns = pl.ds(pl.multiple_of(place.own_block(j) * block, block), block)
        att[place.core, j] = ot[:, columns].T.astype(bf16)
    lax.fori_loop(0, seq_size, other_forms, 0)
    keep += [
        pltpu.make_async_copy(src, dst, keep_sems.at[4 + i])
        for i, (src, dst) in enumerate([(kt, kt_out), (qh, qh_out), (vh, vh_out)])
    ]
    for copy in keep[4:]:
        copy.start()
    both.until(math.inf)
    for j in range(2):
        ref = att.at[1 - place.core, j]
        remote(ref, ref, swap_sems.at[0, j], swap_sems.at[1, j], place.sibling).wait_recv()
        ref = cot_own.at[j]
        remote(ref, ref, cot_sems.at[0, j], cot_sems.at[1, j], place.sibling).wait()
    own_copies[1].wait()
    for copy in keep:
        copy.wait()
    gm.finish_sibling()
    for copy in sent:
        copy.wait_send()
    ga.finish_sends()
    gm.finish_sends()


def backward_kernel(
    dp_size, seq_size, a_layout, m_layout,
    m_slots, x_own_in, n1_in, wqkv_in, qt_in, kt_in, qh_in, kh_in, vh_in, cot_in, att_in, w_proj_in,
    vec, seg_all, lse,
    out_back, grad_back, a_out, m_out,
    g_slots, a_slots, x_own, out_own, d_mid, d_att, d_all, d_n1_in, g_bias, a_wide, m_wide,
    move_sems, swap_sems, norm_sems, load_sems, *refs,
):
    place = Place(seq_size)
    block = x_own.shape[1]
    length = seq_size * block
    mine = place.dp * seq_size + place.z
    count = len(refs) // 2
    sm = make_scatter(dp_size, seq_size, g_slots, refs[:count])
    sa = make_scatter(dp_size, seq_size, a_slots, refs[count:])
    slots_copy = pltpu.make_async_copy(m_slots, g_slots, load_sems.at[1])
    slots_copy.start()
    greet(place.line_peers() + [(place.dp ^ (1 << b), place.z) for b in sm.bits])
    a_slots[...] = jnp.zeros_like(a_slots)
    def mlp(cot, att, w_proj, w_up, w_down, mid, n2, d_n2, total, b_up, gb_up):
        blocks = [slice(j * block, (j + 1) * block) for j in range(2)]
        first_loads = [
            pltpu.make_async_copy(src, dst, load_sems.at[i])
            for i, src, dst in ((0, x_own_in, x_own), (9, att_in, att), (10, w_proj_in, w_proj), (11, cot_in, cot))
        ]
        for copy in first_loads:
            copy.start()
        for copy in first_loads:
            copy.wait()
        for j, rows in enumerate(blocks):
            mid[rows, :] = (
                x_own[j].astype(f32)
                + dot_nn(att[0, rows, :], w_proj[:HALF_COLS, :])
                + dot_nn(att[1, rows, :], w_proj[HALF_COLS:, :])
                + vec[1:2, :]
            )
        slots_copy.wait()
        load_matrix(g_slots, m_layout, 0, 0, w_up)
        load_matrix(g_slots, m_layout, 1, 0, w_down)
        gain = m_layout.vector(g_slots, 0, ROW_D)
        shift = m_layout.vector(g_slots, ROW_D, ROW_D)
        b_down = m_layout.vector(g_slots, MLP_BDOWN, ROW_D)
        b_up[...] = m_layout.vector(g_slots, MLP_BUP, ROW_FF)
        for rows in blocks:
            normal, _ = norm_parts(mid[rows, :])
            n2[rows, :] = (normal * gain + shift).astype(bf16)
        total[...] = jnp.zeros_like(total)
        d_n2[...] = jnp.zeros_like(d_n2)
        inner = math.sqrt(2.0 / math.pi)
        _, _, up_height, up_first, up_shards = m_layout.regions[0]
        _, _, down_height, down_first, _ = m_layout.regions[1]
        turns = FF // FF_STEP // 2

        def step(u, carry):
            for v in range(turns):
                start = pl.multiple_of((u * turns + v) * FF_STEP, FF_STEP)
                columns = pl.ds(start, FF_STEP)
                hidden = dot_nn(n2[...], w_up[:, columns]) + b_up[:, columns]
                square = hidden * hidden
                tanh = jnp.tanh(inner * (hidden + 0.044715 * (square * hidden)))
                cdf = 0.5 * (1.0 + tanh)
                active = (hidden * cdf).astype(bf16)
                slope = cdf + (0.5 * inner) * hidden * (1.0 - tanh * tanh) * (1.0 + (3 * 0.044715) * square)
                low = (dot_nt(cot[...], w_down[columns, :]) * slope).astype(bf16)
                gb_up[:, columns] = jnp.sum(low.astype(f32), axis=0, keepdims=True)
                total[...] += dot_nn(active, w_down[columns, :])
                d_n2[...] += dot_nt(low, w_up[:, columns])
                g_down = dot_tn(active, cot[...]).astype(bf16)
                begin = v * FF_STEP
                for t in range(begin // down_height, (begin + FF_STEP - 1) // down_height + 1):
                    top = max(begin, t * down_height)
                    end = min(begin + FF_STEP, (t + 1) * down_height)
                    slot = down_first + u * (turns * FF_STEP // down_height) + t
                    for j in range(ROW_D):
                        at = j * down_height + top - t * down_height
                        g_slots[slot, at : at + end - top, :] = g_down[
                            top - begin : end - begin, j * LANES : (j + 1) * LANES
                        ]
                g_up = dot_tn(n2[...], low).astype(bf16)
                for j in range(FF_STEP // LANES):
                    at = ((u * turns + v) * (FF_STEP // LANES) + j) * up_height
                    rows = pl.ds(pl.multiple_of(at, up_height), up_height)
                    for s in range(up_shards):
                        g_slots[up_first + s, rows, :] = g_up[
                            s * up_height : (s + 1) * up_height, j * LANES : (j + 1) * LANES
                        ]
            return carry

        lax.fori_loop(0, 2, step, 0)

        gain_sum = jnp.zeros((1, D), f32)
        shift_sum = jnp.zeros((1, D), f32)
        down_sum = jnp.zeros((1, D), f32)
        proj_sum = jnp.zeros((1, D), f32)
        for rows in blocks:
            normal, scale = norm_parts(mid[rows, :])
            grad = d_n2[rows, :]
            cot_rows = cot[rows, :].astype(f32)
            gain_sum += jnp.sum(grad * normal, axis=0, keepdims=True)
            shift_sum += jnp.sum(grad, axis=0, keepdims=True)
            down_sum += jnp.sum(cot_rows, axis=0, keepdims=True)
            d_rows = cot_rows + norm_back(normal, scale, grad, gain)
            d_mid[rows, :] = d_rows
            low = d_rows.astype(bf16)
            n2[rows, :] = low
            proj_sum += jnp.sum(low.astype(f32), axis=0, keepdims=True)
        m_layout.put_vectors(
            g_slots, [(0, gain_sum), (ROW_D, shift_sum), (MLP_BUP, gb_up[...]), (MLP_BDOWN, down_sum)]
        )
        for s, q, there, at in m_layout.beyond():
            g_slots[s, q : q + 1, :] = g_slots[there, at : at + 1, :]
        sm.begin()
        for c in range(2):
            for rows in blocks:
                d_att[c, rows, :] = dot_nt(n2[rows, :], w_proj[c * HALF_COLS : (c + 1) * HALF_COLS, :]).astype(bf16)
        for j in range(2):
            src = d_att.at[1 - place.core, pl.ds(j * block, block)]
            remote(
                src, d_all.at[place.own_block(j)], swap_sems.at[0, j], swap_sems.at[1, j], place.sibling
            ).start()
        steps.until(BACKWARD_FIRST)
        for j, rows in enumerate(blocks):
            out_own[rows, :] = (mid[rows, :] + total[rows, :] + b_down).astype(bf16)
            to, micro = place.home(j)
            remote(
                out_own.at[pl.ds(j * block, block)], out_back.at[micro], move_sems.at[0, j], move_sems.at[1, micro], to
            ).start()
        g_bias[...] = proj_sum
        _, _, height, first, shards = a_layout.regions[1]
        for c in range(2):
            g_part = dot_tn(att[c], n2[...]).astype(bf16)
            for t in range(shards // 2):
                for j in range(ROW_D):
                    a_slots[first + c * (shards // 2) + t, j * height : (j + 1) * height, :] = g_part[
                        t * height : (t + 1) * height, j * LANES : (j + 1) * LANES
                    ]

    tokens = 2 * block
    steps = Steps([(time, (sm, event)) for time, event in sm.events(*M_BACK)])
    pl.run_scoped(
        mlp,
        pltpu.VMEM((tokens, D), bf16), pltpu.VMEM((2, tokens, HALF_COLS), bf16), pltpu.VMEM((D, D), bf16),
        pltpu.VMEM((D, FF), bf16), pltpu.VMEM((FF, D), bf16),
        pltpu.VMEM((tokens, D), f32), pltpu.VMEM((tokens, D), bf16),
        pltpu.VMEM((tokens, D), f32), pltpu.VMEM((tokens, D), f32),
        pltpu.VMEM((1, FF), f32), pltpu.VMEM((1, FF), f32),
    )

    def attention(
        n1, wqkv, qt, kt, qh, kh, vh, dt, dh, seg_col, p_piece, d_piece, dk, dv, dqt, dm, d_n1
    ):
        loads = [
            pltpu.make_async_copy(src, dst, load_sems.at[2 + i])
            for i, (src, dst) in enumerate(
                [(qt_in, qt), (kt_in, kt), (qh_in, qh), (kh_in, kh), (vh_in, vh), (n1_in, n1), (wqkv_in, wqkv)]
            )
        ]
        for copy in loads:
            copy.start()
        for j in range(2):
            d_all[place.own_block(j)] = d_att[place.core, j * block : (j + 1) * block, :]
        segment_columns(seg_all, seg_col, block)
        steps.until(BACKWARD_START - 3)
        for j in range(2):
            ref = d_all.at[place.other_block(j)]
            remote(ref, ref, swap_sems.at[0, j], swap_sems.at[1, j], place.sibling).wait_recv()

        def spread(t, carry):
            rows = pl.ds(pl.multiple_of(t * block, block), block)
            piece = d_all[t]
            dt[:, rows] = piece.astype(f32).T.astype(bf16)
            split_heads(piece, dh, rows)
            return carry

        lax.fori_loop(0, seq_size, spread, 0)
        steps.until(BACKWARD_START)
        unit = HEAD_BACKWARD / (seq_size * (seq_size + 1) // 2)
        points = [
            ((i, side, pair), unit * (i + 1))
            for i in reversed(range(seq_size))
            for pair in range(HALF_HEADS // 2)
            for side in range(2)
        ]
        plan = steps.plan(BACKWARD_START, points)
        for copy in loads[:5]:
            copy.wait()

        def query_block(i):
            columns = slice(i * block, (i + 1) * block)

            def one_pair(pair, carry):
                pair_rows = pl.ds(pl.multiple_of(pair * LANES, LANES), LANES)
                for side in range(2):
                    handle([plan[i, side, turn] for turn in range(HALF_HEADS // 2)], pair)
                    h = 2 * pair + side
                    head_rows = pl.ds(pl.multiple_of(h * HD, HD), HD)
                    query = qt[pair_rows, columns]
                    d_query = dt[pair_rows, columns]
                    level = lse[pl.ds(h, 1), columns]
                    delta = jnp.zeros((1, block), f32)
                    for b in range(i + 1):
                        rows = slice(b * block, (b + 1) * block)
                        probs = jnp.exp(
                            keep_allowed(dot_nn(kh[h, rows, :], query), seg_col, seg_all, b, i, block) - level
                        )
                        d_probs = dot_nn(vh[h, rows, :], d_query)
                        delta = delta + jnp.sum(probs * d_probs, axis=0, keepdims=True)
                        p_piece[rows, :] = probs
                        d_piece[rows, :] = d_probs
                    result = jnp.zeros((HD, block), f32)
                    for b in range(i + 1):
                        rows = slice(b * block, (b + 1) * block)
                        probs = p_piece[rows, :]
                        d_scores = (probs * (d_piece[rows, :] - delta)).astype(bf16)
                        key_part = dot_nn(d_scores, qh[h, columns, :])
                        value_part = dot_nn(probs.astype(bf16), dh[h, columns, :])
                        if i == seq_size - 1 and side == 0:
                            dk[pair, rows, :] = key_part
                            dv[pair, rows, :] = value_part
                        else:
                            dk[pair, rows, :] += key_part
                            dv[pair, rows, :] += value_part
                        result = result + dot_nn(kt[head_rows, rows], d_scores)
                    dqt[head_rows, :] = result * (1.0 / math.sqrt(HD))
                return carry

            lax.fori_loop(0, HALF_HEADS // 2, one_pair, 0)
            dm[0, columns, :] = dqt[...].T.astype(bf16)
            for section, part in ((1, dk), (2, dv)):
                for pair in range(HALF_HEADS // 2):
                    dm[section, columns, pair * LANES : (pair + 1) * LANES] = part[pair, columns, :].astype(bf16)

        def to_norm(t):
            rows = pl.ds(pl.multiple_of(t * block, block), block)
            return (
                dot_nt(dm[0, rows, :], wqkv[0]) + dot_nt(dm[1, rows, :], wqkv[1]) + dot_nt(dm[2, rows, :], wqkv[2])
            )

        def share_norm(j):
            d_n1[j] = to_norm(place.other_block(j))
            remote(d_n1.at[j], d_n1_in.at[j], norm_sems.at[0, j], norm_sems.at[1, j], place.sibling).start()

        def finish_input(j):
            ref = d_n1_in.at[j]
            remote(ref, ref, norm_sems.at[0, j], norm_sems.at[1, j], place.sibling).wait_recv()
            grad = to_norm(place.own_block(j)) + d_n1_in[j]
            normal, scale = norm_parts(x_own[j].astype(f32))
            x_own[j] = (d_mid[j * block : (j + 1) * block, :] + norm_back(normal, scale, grad, gain)).astype(bf16)
            to, micro = place.home(j)
            remote(x_own.at[j], grad_back.at[micro], move_sems.at[2, j], move_sems.at[3, micro], to).start()
            return jnp.sum(grad * normal, axis=0, keepdims=True), jnp.sum(grad, axis=0, keepdims=True)

        gain = vec[0:1, :]
        query_block(3)
        query_block(2)
        for copy in loads[5:]:
            copy.wait()
        share_norm(1)
        query_block(1)
        gain_sum, shift_sum = finish_input(1)
        query_block(0)
        share_norm(0)
        now = BACKWARD_START + HALF_HEADS * HEAD_BACKWARD
        steps.until(now)
        _, _, height, first, shards = a_layout.regions[0]
        for section in range(3):
            part = dot_tn(n1[...], dm[section]).astype(bf16)
            for j in range(ROW_HALF):
                at = (section * ROW_D + place.core * ROW_HALF + j) * height
                rows = pl.ds(pl.multiple_of(at, height), height)
                for s in range(shards):
                    a_slots[first + s, rows, :] = part[s * height : (s + 1) * height, j * LANES : (j + 1) * LANES]
        steps.until(now + 4)
        more_gain, more_shift = finish_input(0)
        sums = []
        for section in (0, 2):
            half = jnp.sum(dm[section].astype(f32), axis=0, keepdims=True)
            zero = jnp.zeros_like(half)
            first_half = place.core == 0
            sums.append(
                jnp.concatenate([jnp.where(first_half, half, zero), jnp.where(first_half, zero, half)], axis=1)
            )
        a_layout.put_vectors(
            a_slots,
            [
                (0, gain_sum + more_gain), (ROW_D, shift_sum + more_shift),
                (ATTN_BQ, sums[0]), (ATTN_BV, sums[1]), (ATTN_BPROJ, g_bias[...]),
            ],
        )
        for s, q, there, at in a_layout.beyond():
            a_slots[s, q : q + 1, :] = a_slots[there, at : at + 1, :]
        sa.begin()
        Steps(steps.queue + [(now + time, (sa, event)) for time, event in sa.events(*A_BACK)]).until(math.inf)
        sm.finish()
        m_layout.unpack(sm.out, m_wide, m_out, mine)
        sa.finish()
        a_layout.unpack(sa.out, a_wide, a_out, mine)
        for micro in range(2):
            for kind, ref in ((1, out_back), (3, grad_back)):
                remote(
                    ref.at[micro], ref.at[micro], move_sems.at[0, micro], move_sems.at[kind, micro], place.sibling
                ).wait_recv()
        for j in range(2):
            for ref, sem in (
                (d_all, swap_sems.at[0, j]), (out_back, move_sems.at[0, j]),
                (d_n1_in, norm_sems.at[0, j]), (grad_back, move_sems.at[2, j]),
            ):
                remote(ref.at[0], ref.at[0], sem, sem, place.sibling).wait_send()

    pl.run_scoped(
        attention,
        *[
            pltpu.VMEM(ref.shape, ref.dtype)
            for ref in (n1_in, wqkv_in, qt_in, kt_in, qh_in, kh_in, vh_in)
        ],
        pltpu.VMEM((HALF_COLS, length), bf16),
        pltpu.VMEM((HALF_HEADS, length, LANES), bf16),
        pltpu.VMEM((length, LANES), jnp.int32),
        pltpu.VMEM((length, block), f32),
        pltpu.VMEM((length, block), f32),
        pltpu.VMEM((HALF_HEADS // 2, length, LANES), f32),
        pltpu.VMEM((HALF_HEADS // 2, length, LANES), f32),
        pltpu.VMEM((HALF_COLS, block), f32),
        pltpu.VMEM((3, length, HALF_COLS), bf16),
        pltpu.VMEM((2, block, D), f32),
    )


class Scatter:
    def __init__(self, dp_size, seq_size, slots, out, core_in, level_in, seq_in, send_sems, recv_sems, seq_sems):
        self.n = seq_size
        self.bits = list(range(1, dp_size.bit_length() - 1))
        self.masks = [m << 1 for m in range(1 << len(self.bits))]
        self.dp = lax.axis_index("dp")
        self.z = lax.axis_index("seq")
        self.slots, self.out = slots, out
        self.core_in, self.level_in, self.seq_in = core_in, level_in, seq_in
        rows = slots.shape[1]
        half = rows // 32 * 16
        self.parts = [(0, half), (half, rows - half)]
        self.orders = [self.bits[::-1], self.bits]
        self.send_sems, self.recv_sems, self.seq_sems = send_sems, recv_sems, seq_sems
        self.started = []
        self.indices = {}

    def index(self, *key):
        return self.indices.setdefault(key, len(self.indices))

    def slot(self, mask, k):
        return (self.dp ^ mask) * self.n + nearest(self.z, self.n, k)

    def send(self, src, dst, to, key, part=None):
        sem = self.recv_sems.at[self.index(*key)] if isinstance(key, tuple) else key
        remote(src, dst, self.send_sems.at[len(self.started)], sem, to).start()
        self.started.append(part)

    def wait(self, ref, key):
        remote(ref, ref, self.send_sems.at[0], self.recv_sems.at[self.index(*key)], (self.dp, self.z)).wait_recv()

    def turn(self):
        return list(range(self.n))[::-1]

    def begin(self):
        for k in self.turn():
            for mask in self.masks[::-1]:
                i = self.masks.index(mask)
                self.send(
                    self.slots.at[self.slot(mask ^ 1, k)], self.core_in.at[i, k], (self.dp ^ 1, self.z), ("c", i, k)
                )

    def add(self, mask, k, part, term):
        start, size = (0, self.slots.shape[1]) if part is None else self.parts[part]
        rows = pl.ds(start, size)
        index = self.slot(mask, k)
        self.slots[index, rows, :] = (self.slots[index, rows, :].astype(f32) + term.astype(f32)).astype(bf16)

    def view(self, mask, k, part):
        start, size = self.parts[part]
        return self.slots.at[self.slot(mask, k), pl.ds(start, size)]

    def cell(self, part, level, mask):
        free = [b for b in self.bits if b not in self.orders[part][: level + 1]]
        return sum(1 << n for n, b in enumerate(free) if mask >> b & 1)

    def pass_on(self, part, level, mask, k):
        order = self.orders[part]
        src = self.view(mask, k, part)
        if level == len(order):
            return
        bit = 1 << order[level]
        if mask & bit:
            rest = mask ^ bit
            dst = self.level_in[part][level].at[self.cell(part, level, rest), k]
            self.send(src, dst, (self.dp ^ bit, self.z), ("l", part, level, rest, k), part)

    def events(self, begin=6.0, gap=9.6, level_gap=(9.0, 19.0), seq_gap=0.5):
        out = []
        for turn, k in enumerate(self.turn()):
            at = begin + max(0, turn - 1) * gap
            for mask in self.masks[::-1]:
                out.append((at, ("c", mask, k)))
            at = begin + turn * gap
            for level in range(len(self.bits)):
                for part in (0, 1):
                    past = self.orders[part][: level + 1]
                    for mask in self.masks[::-1]:
                        if not any(mask >> b & 1 for b in past):
                            out.append((at + level_gap[min(level, 1)], ("l", part, level, mask, k)))
            if k:
                for part in (0, 1):
                    out.append((at + level_gap[min(len(self.bits) - 1, 1)] + seq_gap, ("z", part, k)))
        return sorted(out, key=lambda e: e[0])

    def step(self, event):
        if event[0] == "c":
            _, mask, k = event
            i = self.masks.index(mask)
            self.wait(self.core_in.at[i, k], ("c", i, k))
            self.add(mask, k, None, self.core_in[i, k])
            for part in (0, 1):
                self.pass_on(part, 0, mask, k)
            return
        if event[0] == "z":
            _, part, k = event
            self.along(part, k)
            return
        _, part, level, mask, k = event
        index = self.cell(part, level, mask)
        self.wait(self.level_in[part][level].at[index, k], ("l", part, level, mask, k))
        self.add(mask, k, part, self.level_in[part][level][index, k])
        self.pass_on(part, level + 1, mask, k)

    def from_side(self, part, place, side):
        index = place if side == 0 else self.n
        ref = self.seq_in[part].at[index]
        remote(ref, ref, self.send_sems.at[0], self.seq_sems.at[part, index], (self.dp, self.z)).wait_recv()
        return self.seq_in[part][index].astype(f32)

    def along(self, part, k):
        place = nearest(self.z, self.n, k)
        up = place > self.z

        @pl.when((up & (self.z > 0)) | (jnp.logical_not(up) & (self.z < self.n - 1)))
        def _():
            self.add(0, k, part, self.from_side(part, place, 0))

        to = jnp.where(up, self.z + 1, self.z - 1)
        index = jnp.where((to == place) & jnp.logical_not(up), self.n, place)
        self.send(
            self.view(0, k, part), self.seq_in[part].at[index], (self.dp, to), self.seq_sems.at[part, index], part
        )

    def finish(self):
        index = self.slot(0, 0)
        for part in (0, 1):
            start, size = self.parts[part]
            rows = slice(start, start + size)
            self.out[rows, :] = self.slots[index, rows, :].astype(f32)
            for side, there in ((0, self.z > 0), (1, self.z < self.n - 1)):

                @pl.when(there)
                def _():
                    self.out[rows, :] += self.from_side(part, self.z, side)

        for index, part in enumerate(self.started):
            start, size = (0, self.slots.shape[1]) if part is None else self.parts[part]
            ref = self.slots.at[0, pl.ds(start, size)]
            remote(ref, ref, self.send_sems.at[index], self.recv_sems.at[0], (self.dp, self.z)).wait_send()


def scatter_scratch(dp_size, seq_size, rows):
    bits = dp_size.bit_length() - 2
    masks = 1 << bits
    half = rows // 32 * 16
    sizes = [half, rows - half]
    shapes = [pltpu.VMEM((masks, seq_size, rows, LANES), bf16), pltpu.VMEM((rows, LANES), f32)]
    for size in sizes:
        for level in range(bits):
            shapes.append(pltpu.VMEM((masks >> (level + 1), seq_size, size, LANES), bf16))
    for size in sizes:
        shapes.append(pltpu.VMEM((seq_size + 1, size, LANES), bf16))
    count = masks * seq_size + 2 * (masks - 1) * seq_size + 2 * (seq_size - 1)
    shapes += [
        pltpu.SemaphoreType.DMA((count,)),
        pltpu.SemaphoreType.DMA((count,)),
        pltpu.SemaphoreType.DMA((2, seq_size + 1)),
    ]
    return shapes


def make_scatter(dp_size, seq_size, slots, refs):
    bits = dp_size.bit_length() - 2
    core_in, total, *rest = refs
    level_in = [rest[:bits], rest[bits : 2 * bits]]
    rest = rest[2 * bits :]
    return Scatter(dp_size, seq_size, slots, total, core_in, level_in, rest[:2], *rest[2:])


def deliver_kernel(out_in, grad_in, a_in, m_in, out, grad, a_out, m_out, sems):
    copies = [
        pltpu.make_async_copy(src, dst, sems.at[i])
        for i, (src, dst) in enumerate([(out_in, out), (a_in, a_out), (m_in, m_out)])
    ]
    for copy in copies:
        copy.start()
    grad[...] = grad_in[...].astype(f32)
    for copy in copies:
        copy.wait()


ANY = pl.BlockSpec(memory_space=pl.ANY)
LOCAL = pl.BlockSpec(memory_space=pltpu.VMEM)


def shape_of(dims, dtype):
    return jax.ShapeDtypeStruct(dims, dtype)


def per_chip_sequence(inputs, segments, attn_params, mlp_params, cotangent):
    dp_size, n = lax.axis_size("dp"), lax.axis_size("seq")
    devices = dp_size * n
    block = inputs.shape[2]
    length = n * block
    tokens = 2 * block
    a_layout = attn_layout(attn_params.shape[0] // LANES, devices)
    m_layout = mlp_layout_of(mlp_params.shape[0] // LANES, devices)
    a_raw, m_raw = attn_params.reshape(-1, LANES), mlp_params.reshape(-1, LANES)
    a_rows, m_rows = a_layout.slot_rows, m_layout.slot_rows
    wide = [pltpu.VMEM((raw.shape[0] + 3 * MARGIN, LANES), f32) for raw in (a_raw, m_raw)]
    seg_rows = segments.reshape(2, block // LANES, LANES)
    send, recv = gather_counts(dp_size, n)
    dma = pltpu.SemaphoreType.DMA
    across = shape_of((HALF_COLS, length), bf16)
    heads = shape_of((HALF_HEADS, length, LANES), bf16)
    own = shape_of((2, block, D), bf16)
    kept = [
        shape_of((length, D), bf16), shape_of((3, D, HALF_COLS), bf16), across, across, heads, heads, heads,
    ]
    (
        m_slots, cot_own, n1, wqkv, qt, kt, qh, kh, vh, x_own, w_proj, vec, seg_all, lse, att,
    ) = pl.pallas_call(
        functools.partial(forward_kernel, dp_size, n, a_layout, m_layout),
        out_shape=[shape_of((devices, m_rows, LANES), bf16), own]
        + kept
        + [
            own, shape_of((D, D), bf16), shape_of((8, D), f32),
            shape_of((n, block // LANES, LANES), jnp.int32), shape_of((8, length), f32), shape_of((2, 2, block, HALF_COLS), bf16),
        ],
        in_specs=[ANY] * 3 + [LOCAL] * 2,
        out_specs=[ANY] * 9 + [LOCAL] * 6,
        scratch_shapes=[pltpu.VMEM(like.shape, like.dtype) for like in kept]
        + [
            pltpu.VMEM((devices, a_rows, LANES), bf16),
            pltpu.VMEM((a_rows, LANES), bf16),
            pltpu.VMEM((m_rows, LANES), bf16),
        ]
        + wide
        + [
            pltpu.VMEM((n, block, D), bf16),
            pltpu.VMEM((3, length, HALF_COLS), bf16),
            pltpu.VMEM((HALF_COLS, length), bf16),
            pltpu.VMEM((length, LANES), jnp.int32),
            pltpu.VMEM((length, block), f32),
            pltpu.VMEM((HALF_COLS, length), f32),
            pltpu.VMEM((2, block, HALF_COLS), bf16),
            dma((send,)), dma((recv,)), dma((send,)), dma((recv,)), dma((2,)),
            dma((3, 4)), dma((3, n)), dma((2, 2)), dma((2, 2)), dma((len(kept),)),
        ],
        compiler_params=pltpu.CompilerParams(collective_id=0, has_side_effects=True, vmem_limit_bytes=VMEM_LIMIT),
    )(inputs[:, 0], seg_rows, cotangent[:, 0], a_raw, m_raw)

    out_back, grad_back, a_sum, m_sum = pl.pallas_call(
        functools.partial(backward_kernel, dp_size, n, a_layout, m_layout),
        out_shape=[own, own, shape_of((a_layout.rows, LANES), f32), shape_of((m_layout.rows, LANES), f32)],
        in_specs=[ANY] * 12 + [LOCAL] * 3,
        out_specs=[ANY] * 2 + [LOCAL] * 2,
        scratch_shapes=[
            pltpu.VMEM((devices, m_rows, LANES), bf16),
            pltpu.VMEM((devices, a_rows, LANES), bf16),
            pltpu.VMEM((2, block, D), bf16),
            pltpu.VMEM((tokens, D), bf16),
            pltpu.VMEM((tokens, D), f32),
            pltpu.VMEM((2, tokens, HALF_COLS), bf16),
            pltpu.VMEM((n, block, HALF_COLS), bf16),
            pltpu.VMEM((2, block, D), f32),
            pltpu.VMEM((1, D), f32),
        ]
        + wide
        + [dma((4, 2)), dma((2, 2)), dma((2, 2)), dma((12,))]
        + scatter_scratch(dp_size, n, m_rows)
        + scatter_scratch(dp_size, n, a_rows),
        compiler_params=pltpu.CompilerParams(collective_id=1, has_side_effects=True, vmem_limit_bytes=VMEM_LIMIT),
    )(
        m_slots, x_own, n1, wqkv, qt, kt, qh, kh, vh,
        cot_own.reshape(tokens, D), att.reshape(2, tokens, HALF_COLS), w_proj, vec, seg_all, lse,
    )
    out, grad, a_sum, m_sum = pl.pallas_call(
        deliver_kernel,
        out_shape=[own, shape_of(own.shape, f32), shape_of(a_sum.shape, f32), shape_of(m_sum.shape, f32)],
        in_specs=[ANY, LOCAL, ANY, ANY],
        out_specs=[ANY, LOCAL, ANY, ANY],
        scratch_shapes=[dma((3,))],
        compiler_params=pltpu.CompilerParams(vmem_limit_bytes=16 * 2**20),
    )(out_back, grad_back, a_sum, m_sum)
    return out[:, None], grad[:, None], a_sum.reshape(-1), m_sum.reshape(-1)


def solution(mesh):
    in_specs = (
        P(None, "dp", "seq", None),
        P(None, "dp", "seq"),
        P(("dp", "seq")),
        P(("dp", "seq")),
        P(None, "dp", "seq", None),
    )
    out_specs = (
        P(None, "dp", "seq", None),
        P(None, "dp", "seq", None),
        P(("dp", "seq")),
        P(("dp", "seq")),
    )
    one_each = mesh.shape["seq"] == 4 and mesh.shape["dp"] % 2 == 0
    return jax.shard_map(
        per_chip_sequence if one_each else per_device, mesh=mesh, in_specs=in_specs, out_specs=out_specs, check_vma=False
    )
```
